32 devices in a mesh: dp: 8 (over y, x, core), mp: 4 (over z).
Axes of the slice: x: 2, y: 2, z: 4, core: 2. Of those that a mesh axis runs over, the one named last changes fastest.
Arguments:
- tokens: bfloat16 [12288, 768], P(('dp', 'mp')), may hold values from -6 to 6
- w_qkv: float32 [2, 3, 768, 768], P(None, None, 'dp', 'mp'), may hold values from -0.21875 to 0.21875
- b_qkv: float32 [2, 3, 768], P(None, None, 'mp'), may hold values from -3 to 3
- w_out: float32 [2, 768, 768], P(None, 'mp', 'dp'), may hold values from -0.875 to 0.875
- vectors: float32 [2, 6, 768], replicated
- w_in: float32 [2, 768, 3072], P(None, 'dp', 'mp'), may hold values from -0.21875 to 0.21875
- b_in: float32 [2, 3072], P(None, 'mp'), may hold values from -3 to 3
- w_back: float32 [2, 3072, 768], P(None, 'mp', 'dp'), may hold values from -0.15625 to 0.15625
- cotangent: bfloat16 [12288, 768], P(('dp', 'mp')), may hold values from -6 to 6
- lengths: int32 [8, 3], P('dp'), may hold values from 0 to 1536, as said below
- buckets: int32 [8], P('dp'), may hold values from 0 to 2, as said below
Outputs:
- output: bfloat16 [12288, 768], P(('dp', 'mp'))
- grad_tokens: float32 [12288, 768], P(('dp', 'mp'))
- grad_w_qkv: float32 [2, 3, 768, 768], P(None, None, 'dp', 'mp')
- grad_b_qkv: float32 [2, 3, 768], P(None, None, 'mp')
- grad_w_out: float32 [2, 768, 768], P(None, 'mp', 'dp')
- grad_vectors: float32 [2, 6, 768], replicated
- grad_w_in: float32 [2, 768, 3072], P(None, 'dp', 'mp')
- grad_b_in: float32 [2, 3072], P(None, 'mp')
- grad_w_back: float32 [2, 3072, 768], P(None, 'mp', 'dp')
The draws below stay inside these ranges and needn't reach their ends.
Inputs may be any that keep to these rules, and one draw needn't show every extreme that they name: `buckets`: some index of dp has bucket 2 in every draw. Row i describes slab i, held by index i // 1 of dp with bucket b: its first 3 - b entries are the lengths of its 3 - b sequences, each from half the slot 1536 // (3 - b) to the whole slot, one of them exactly the whole slot; the remaining entries are 0.
All inputs are finite; a program needn't handle non-finite values.
Results may differ from the reference program's by a relative error of at most 0.02.
Values may be sent and summed in bfloat16 or wider, within the bound.
A program may use at most 192 MiB of HBM per device.

```python
import jax
import jax.numpy as jnp
from jax import lax

D = 768
HEADS = 12
FF = 3072
HD = 64
LAYERS = 2
LEN_MAX = 1536
SLABS = 1
TOKENS = 12288
N_DP = 8


def bucket_plan(key):
    picked = jax.random.randint(jax.random.fold_in(key, 101), (N_DP,), 0, 3)
    forced = jax.random.randint(jax.random.fold_in(key, 102), (), 0, N_DP)
    return jnp.where(jnp.arange(N_DP) == forced, 2, picked).astype(jnp.int32)


def draw_buckets(key, part):
    plan = bucket_plan(key)
    return plan


def draw_lengths(key, part):
    plan = bucket_plan(key)
    key = jax.random.fold_in(key, 4)
    seq_count = jnp.repeat(3 - plan, SLABS)
    slot_len = LEN_MAX // seq_count
    half_slot = slot_len // 2
    spread = jax.random.randint(jax.random.fold_in(key, 1), (N_DP * SLABS, 3), 0, 1 << 20)
    drawn = half_slot[:, None] + spread % (slot_len - half_slot + 1)[:, None]
    chosen = jax.random.randint(jax.random.fold_in(key, 2), (N_DP * SLABS,), 0, 1 << 20) % seq_count
    member = jnp.arange(3)[None, :]
    drawn = jnp.where(member == chosen[:, None], slot_len[:, None], drawn)
    return jnp.where(member < seq_count[:, None], drawn, 0).astype(jnp.int32)


def draw_vectors(key, part):
    key = jax.random.fold_in(key, 5)
    biases = 0.3 * jax.random.normal(jax.random.fold_in(key, 1), (LAYERS, 6, D), jnp.float32)
    gains = jax.random.uniform(jax.random.fold_in(key, 2), (LAYERS, 6, D), jnp.float32, 0.6, 1.4)
    is_gain = (jnp.arange(6) == 1) | (jnp.arange(6) == 4)
    return jnp.where(is_gain[None, :, None], gains, biases)


def block_scale(stream_key, dims, cuts, smallest, top_value):
    def one(axis_at, shards_of):
        steps = jax.random.uniform(jax.random.fold_in(jax.random.fold_in(stream_key, 6), axis_at), (shards_of,), jnp.float32, smallest / len(cuts), top_value / len(cuts))
        return jnp.repeat(jnp.exp(steps), dims[axis_at] // shards_of).reshape((-1,) + (1,) * (len(dims) - axis_at - 1))

    factor_of = one(*cuts[0])
    for cut in cuts[1:]:
        factor_of = factor_of * one(*cut)
    return factor_of


def noise(stream_key, shape, scale, most, cuts=(), kind=jnp.bfloat16):
    level = block_scale(stream_key, shape, cuts, -0.22, 0.18) if cuts else 1.0
    values = jax.random.normal(stream_key, shape, jnp.float32) * scale * level
    return jnp.minimum(jnp.maximum(values, -most), most).astype(kind)


def setup_inputs(seed: int = 0) -> dict:
    seeds = jax.random.split(jax.random.key(seed), 12)
    return {
        "tokens": noise(seeds[0], (TOKENS, D), 1.0, 6.0, ((0, 32),)),
        "w_qkv": noise(seeds[1], (LAYERS, 3, D, D), D ** -0.5, 0.21875, ((2, 8), (3, 4)), jnp.float32),
        "b_qkv": noise(seeds[2], (LAYERS, 3, D), 0.5, 3.0, ((2, 4),), jnp.float32),
        "w_out": noise(seeds[3], (LAYERS, D, D), (D // 16) ** -0.5, 0.875, ((1, 4), (2, 8)), jnp.float32),
        "vectors": draw_vectors(jax.random.fold_in(seeds[11], 71), 0),
        "w_in": noise(seeds[5], (LAYERS, D, FF), D ** -0.5, 0.21875, ((1, 8), (2, 4)), jnp.float32),
        "b_in": noise(seeds[6], (LAYERS, FF), 0.5, 3.0, ((1, 4),), jnp.float32),
        "w_back": noise(seeds[7], (LAYERS, FF, D), (FF // 2) ** -0.5, 0.15625, ((1, 4), (2, 8)), jnp.float32),
        "cotangent": noise(seeds[8], (TOKENS, D), 1.0, 6.0, ((0, 32),)),
        "lengths": draw_lengths(jax.random.fold_in(seeds[11], 71), 0),
        "buckets": draw_buckets(jax.random.fold_in(seeds[11], 71), 0),
    }


EPSILON = 1e-06
NEGATIVE = -1e+30
HIGHEST = lax.Precision.HIGHEST

@jax.custom_vjp
def low(v):
    return lax.optimization_barrier(v.astype(jnp.bfloat16)).astype(jnp.float32)

@jax.custom_vjp
def low_back(v):
    return v

def low_keep(v):
    return (low(v), None)

def low_pass(kept, grad):
    return (grad,)

def back_keep(v):
    return (v, None)

def back_low(kept, grad):
    return (low(grad),)
low.defvjp(low_keep, low_pass)
low_back.defvjp(back_keep, back_low)

def rotary(turned, places):
    half_size = turned.shape[-1] // 2
    frequency = 10000.0 ** (-2.0 * jnp.arange(half_size, dtype=jnp.float32) / turned.shape[-1])
    angles = places.astype(jnp.float32)[:, None] * frequency[None, :]
    cosine = jnp.cos(angles)[:, None, :]
    sine_part = jnp.sin(angles)[:, None, :]
    first_half = turned[..., :half_size]
    second = turned[..., half_size:]
    return jnp.concatenate([first_half * cosine - second * sine_part, second * cosine + first_half * sine_part], axis=-1)

def layer_norm(summed, gain, shift):
    row_mean = lax.optimization_barrier(jnp.mean(summed, axis=-1, keepdims=True))
    centred = summed - row_mean
    variance = lax.optimization_barrier(jnp.mean(centred * centred, axis=-1, keepdims=True))
    return centred * lax.rsqrt(variance + EPSILON) * gain + shift

def slab_mask(bucket, seq_lengths, query_places, key_places):
    slot_len = LEN_MAX // (3 - bucket)
    query_seq = query_places // slot_len
    key_seq = key_places // slot_len
    choose = key_seq[:, None] == jnp.arange(3, dtype=jnp.int32)[None, :]
    key_limit = lax.optimization_barrier(jnp.sum(jnp.where(choose, seq_lengths[None, :], 0), axis=1))
    return (query_seq[:, None] == key_seq[None, :]) & (key_places - key_seq * slot_len < key_limit)[None, :]

def slab_attention(queries, key_heads, values, bucket, seq_lengths):
    places = jnp.arange(LEN_MAX, dtype=jnp.int32)
    raw_scores = low_back(jnp.einsum('qhd,khd->hqk', queries, key_heads, precision=HIGHEST))
    scores = raw_scores * HD ** (-0.5)
    visible = slab_mask(bucket, seq_lengths, places, places)
    scores = jnp.where(visible[None], scores, NEGATIVE)
    weights = low(jax.nn.softmax(scores, axis=-1))
    mixed_heads = jnp.einsum('hqk,khd->qhd', weights, values, precision=HIGHEST)
    return low(low_back(mixed_heads))

def network(stream, w_qkv, b_qkv, w_out, vectors, w_in, b_in, w_back, lengths, buckets):
    slab_count = lengths.shape[0]
    bucket_rows = jnp.repeat(buckets, SLABS)
    slot_rows = LEN_MAX // (3 - bucket_rows)
    positions = jnp.arange(LEN_MAX, dtype=jnp.int32)
    places = (positions[None, :] % slot_rows[:, None]).reshape(-1)
    row_count = stream.shape[0]
    slab_shape = (slab_count, LEN_MAX, HEADS, HD)
    attend_slab = jax.checkpoint(lambda element: slab_attention(element[0], element[1], element[2], element[3], element[4]))
    for layer_at in range(LAYERS):
        projected = low_back(jnp.einsum('td,jdc->tjc', low(stream), low(w_qkv[layer_at]), precision=HIGHEST)) + b_qkv[layer_at][None]
        queries = low(rotary(projected[:, 0].reshape(row_count, HEADS, HD), places))
        key_heads = low(rotary(projected[:, 1].reshape(row_count, HEADS, HD), places))
        values = low(projected[:, 2].reshape(row_count, HEADS, HD))
        mixed_heads = lax.map(attend_slab, (queries.reshape(slab_shape), key_heads.reshape(slab_shape), values.reshape(slab_shape), bucket_rows, lengths))
        mixed_heads = mixed_heads.reshape(row_count, D)
        attended = low_back(jnp.dot(mixed_heads, low(w_out[layer_at]), precision=HIGHEST)) + vectors[layer_at, 0]
        normed = layer_norm(stream + attended, vectors[layer_at, 1], vectors[layer_at, 2])
        inner_sum = low_back(jnp.dot(low(normed), low(w_in[layer_at]), precision=HIGHEST)) + b_in[layer_at]
        active = low(jax.nn.gelu(inner_sum, approximate=False))
        fed_back = low_back(jnp.dot(active, low(w_back[layer_at]), precision=HIGHEST)) + vectors[layer_at, 3]
        stream = layer_norm(normed + fed_back, vectors[layer_at, 4], vectors[layer_at, 5])
    return stream

def reference(tokens, w_qkv, b_qkv, w_out, vectors, w_in, b_in, w_back, cotangent, lengths, buckets):

    def forward(stream, proj_w, proj_b, out_w, vector_set, in_w, in_b, back_w):
        return network(stream, proj_w, proj_b, out_w, vector_set, in_w, in_b, back_w, lengths, buckets)
    result, pullback = jax.vjp(forward, tokens.astype(jnp.float32), w_qkv, b_qkv, w_out, vectors, w_in, b_in, w_back)
    grads = pullback(cotangent.astype(jnp.float32))
    return (result.astype(jnp.bfloat16), grads[0], grads[1], grads[2], grads[3], grads[4], grads[5], grads[6], grads[7])
```

```python
from functools import partial

import jax
import jax.numpy as jnp
from jax import lax
from jax.experimental import pallas as pl
from jax.experimental.pallas import tpu as pltpu
from jax.sharding import PartitionSpec as P

HD = 64
LEN_MAX = 1536
EPSILON = 1e-06
NEGATIVE = -1e30
F32 = jnp.float32
BF16 = jnp.bfloat16
LANES = 128
MP = 4
VMEM_LIMIT = 60 * 1024 * 1024


def nn(a, b):
    return lax.dot_general(a, b, (((1,), (0,)), ((), ())), preferred_element_type=F32)


def nt(a, b):
    return lax.dot_general(a, b, (((1,), (1,)), ((), ())), preferred_element_type=F32)


def core_swap(x):
    n = lax.axis_size("dp")
    return lax.ppermute(x, "dp", [(i, i ^ 1) for i in range(n)])


def plane_swap(x, first):
    n = lax.axis_size("dp")
    hops = (2, 4) if first else (4, 2)
    return lax.ppermute(x, "dp", [(i, i ^ hops[i % 2]) for i in range(n)])


def column_shift(x, k):
    return lax.ppermute(x, "mp", [(i, (i + k) % MP) for i in range(MP)])


def pair_swap(x):
    return lax.ppermute(x, "mp", [(i, i ^ 1) for i in range(MP)])


def relayout(x):
    n = lax.axis_size("dp")
    pairs = []
    for d in range(n):
        for z in range(MP):
            if (d % 2) != (z // 2):
                pairs.append((d * MP + z, (d ^ 1) * MP + (z ^ 2)))
            else:
                pairs.append((d * MP + z, d * MP + z))
    return lax.ppermute(x, ("dp", "mp"), pairs)


def turn_columns(x, z):
    return jnp.stack([lax.dynamic_index_in_dim(x, (z - k) % MP, 0, False) for k in range(MP)])


def gather_small(x):
    return jnp.stack([x] + [column_shift(x, k) for k in range(1, MP)])


def gather_bundle(block):
    if lax.axis_size("dp") != 8:
        z = lax.axis_index("mp")
        whole = lax.all_gather(block, "dp", axis=0, tiled=True)
        whole = lax.all_gather(whole, "mp", axis=0, tiled=False)
        return [turn_columns(whole, z)]
    own = gather_small(block)
    one = plane_swap(own, True)
    two = plane_swap(own, False)
    three = plane_swap(one, False)
    mine = [own, one, two, three]
    return mine + [core_swap(m) for m in mine]


def row_offsets(g, c, rows):
    if lax.axis_size("dp") != 8:
        return [jnp.int32(0)]
    result = []
    for core in (c, 1 - c):
        first = jnp.where(core == 0, 1, 2)
        for hop in (0, first, 3 - first, 3):
            result.append(((g ^ hop) * 2 + core) * rows)
    return result


def send_columns(v):
    total = v[0].astype(F32)
    for k in range(1, MP):
        total = total + column_shift(v[k], -k).astype(F32)
    return total


def reduce_all(keep, away):
    if lax.axis_size("dp") != 8:
        z = lax.axis_index("mp")
        whole = turn_columns(keep[0], z).astype(F32)
        part = lax.psum_scatter(whole, "mp", scatter_dimension=0, tiled=False)
        return lax.psum_scatter(part, "dp", scatter_dimension=0, tiled=True)
    other = core_swap(away)

    def add(i):
        return keep[i].astype(F32) + other[i].astype(F32)

    got = plane_swap(jnp.stack([add(0), add(1)]).astype(BF16), True)
    got_two = plane_swap((add(2) + got[1].astype(F32)).astype(BF16), False)
    v = (add(3) + got[0].astype(F32) + got_two.astype(F32)).astype(BF16)
    return send_columns(v)


def reduce_heads(parts):
    c = lax.axis_index("dp") % 2
    n = lax.axis_size("dp")
    if n != 8:
        z = lax.axis_index("mp")
        wide = jnp.concatenate([parts[0], jnp.zeros_like(parts[0])], axis=0)
        wide = jnp.where(c == 0, wide, jnp.roll(wide, 2, axis=0))
        whole = turn_columns(wide, z).astype(F32)
        part = lax.psum_scatter(whole, "mp", scatter_dimension=0, tiled=False)
        return lax.psum_scatter(part, "dp", scatter_dimension=0, tiled=True)
    got = plane_swap(parts[0:2], True)
    got_two = plane_swap((parts[2].astype(F32) + got[1].astype(F32)).astype(BF16), False)
    v = (parts[3].astype(F32) + got[0].astype(F32) + got_two.astype(F32)).astype(BF16)

    total = column_turn(v[0], 0).astype(F32) + column_turn(v[1], 1).astype(F32)
    rows = total.shape[0] // 2
    kept = lax.dynamic_slice_in_dim(total, c * rows, rows, 0)
    sent = lax.dynamic_slice_in_dim(total, (1 - c) * rows, rows, 0).astype(BF16)
    return kept + core_swap(sent).astype(F32)


def sum_head_biases(v):
    c = lax.axis_index("dp") % 2
    n = lax.axis_size("dp")
    if n != 8:
        z = lax.axis_index("mp")
        zero = jnp.zeros_like(v)
        wide = jnp.where(c == 0, jnp.concatenate([v, zero]), jnp.concatenate([zero, v]))
        total = lax.psum(turn_columns(wide, z), ("dp", "mp"))
        return lax.dynamic_index_in_dim(total, z, 0, False)
    v = v + plane_swap(v, True)
    v = v + plane_swap(v, False)
    total = column_turn(v[0], 0) + column_turn(v[1], 1)
    return total + core_swap(total)


def column_turn(x, k):
    n = lax.axis_size("dp")
    pairs = []
    for d in range(n):
        for z in range(MP):
            pairs.append((d * MP + z, d * MP + (z - k - 2 * (d % 2)) % MP))
    return lax.ppermute(x, ("dp", "mp"), pairs)


def sum_vectors(vectors, columns):
    if lax.axis_size("dp") != 8:
        z = lax.axis_index("mp")
        vectors, columns = lax.psum((vectors, turn_columns(columns, z)), ("dp", "mp"))
        return vectors, lax.dynamic_index_in_dim(columns, z, 0, False)
    n = vectors.shape[0]
    m = columns.shape[1]
    both = jnp.concatenate([vectors, columns.reshape(MP * m, -1)])
    both = both + core_swap(both)
    both = both + plane_swap(both, True)
    both = both + plane_swap(both, False)
    total = both[: n + m]
    for k in range(1, MP):
        at = n + m * (MP - k)
        total = total + column_shift(jnp.concatenate([both[:n], both[at : at + m]]), k)
    return total[:n], total[n:]


def lane_index(shape):
    return lax.broadcasted_iota(jnp.int32, shape, len(shape) - 1)


def half_swap(x):
    lane = lane_index(x.shape)
    return jnp.where(
        lane % HD < HD // 2,
        pltpu.roll(x, LANES - HD // 2, x.ndim - 1),
        pltpu.roll(x, HD // 2, x.ndim - 1),
    )


def norm_parts(r):
    mean = jnp.mean(r, axis=-1, keepdims=True)
    centred = r - mean
    scale = lax.rsqrt(jnp.mean(centred * centred, axis=-1, keepdims=True) + EPSILON)
    return centred * scale, scale


def norm_back(dy, n, scale, gain):
    gdy = dy * gain
    mean_one = jnp.mean(gdy, axis=-1, keepdims=True)
    mean_two = jnp.mean(gdy * n, axis=-1, keepdims=True)
    return (gdy - mean_one - n * mean_two) * scale


def start_pieces(scal, pieces, sems, base, copies):
    started = []
    for i, piece in enumerate(pieces):
        offset = pl.multiple_of(scal[i], 32)
        source, target = copies(piece, offset)
        copy = pltpu.make_async_copy(source, target, sems.at[base + i])
        copy.start()
        started.append(copy)
    return started


def attend_kernel(n_pieces, rows, *refs):
    scal, x_ref, bias_ref, cos_ref, sin_ref, qcode_ref, kcode_ref = refs[:7]
    pieces = refs[7 : 7 + n_pieces]
    q_ref, k_ref, v_ref, own_ref, sib_ref, lse_ref = refs[7 + n_pieces : 13 + n_pieces]
    w_ref, lse_cols, sems = refs[13 + n_pieces :]
    first_z = scal[n_pieces]

    copies = start_pieces(
        scal,
        pieces,
        sems,
        0,
        lambda piece, offset: (
            piece.at[pl.ds(first_z, 2)],
            w_ref.at[:, pl.ds(offset, rows), :],
        ),
    )
    for copy in copies:
        copy.wait()
    keys = x_ref.shape[0]
    queries = keys // 2
    block = queries // 2

    for z in range(2):

        def project(i, _, z=z):
            at = pl.ds(pl.multiple_of(i * block, block), block)
            cos, sin = cos_ref[at, :], sin_ref[at, :]
            p = nn(x_ref[at, :], w_ref[z, :, LANES : 5 * LANES]) + bias_ref[z, :, LANES:]
            low_half = lane_index((block, LANES)) < HD
            mixed = p[:, 0:LANES]
            mixed = mixed * cos + half_swap(mixed) * sin
            pair = p[:, LANES : 2 * LANES]
            pair = pair * cos + half_swap(pair) * sin
            k_ref[z, 0, at, :] = pair.astype(BF16)
            k_ref[z, 1, at, :] = jnp.where(low_half, pltpu.roll(mixed, HD, 1), 0.0).astype(BF16)
            v_ref[z, 0, at, :] = p[:, 2 * LANES : 3 * LANES].astype(BF16)
            v_ref[z, 1, at, :] = jnp.where(low_half, p[:, 3 * LANES :], 0.0).astype(BF16)

            @pl.when(i < 2)
            def _():
                q = nn(x_ref[at, :], w_ref[z, :, 0:LANES]) + bias_ref[z, :, 0:LANES]
                q = q * cos + half_swap(q) * sin
                q_ref[z, 0, at, :] = q.astype(BF16) * BF16(HD**-0.5)
                q_ref[z, 1, at, :] = jnp.where(low_half, mixed, 0.0).astype(BF16) * BF16(HD**-0.5)

            return 0

        lax.fori_loop(0, 4, project, 0)

    lse_cols[...] = jnp.zeros_like(lse_cols)
    qblock = 256

    def one_block(i, _):
        at = pl.ds(pl.multiple_of(i * qblock, qblock), qblock)
        visible = qcode_ref[at, :] == kcode_ref[...]
        low_half = lane_index((qblock, LANES)) < HD
        lane = lane_index((qblock, LANES))
        for z in range(2):
            outs = []
            for h in range(3):
                tile = h // 2
                q = q_ref[z, tile, at, :]
                if h < 2:
                    q = jnp.where(low_half == (h == 0), q, BF16(0))
                s = nt(q, k_ref[z, tile])
                s = jnp.where(visible, s, NEGATIVE)
                m = jnp.max(s, axis=-1, keepdims=True)
                p = jnp.exp(s - m)
                l = jnp.sum(p, axis=-1, keepdims=True)
                o = nn(p.astype(BF16), v_ref[z, tile])
                outs.append(o / l)
                lse_cols[at, :] = jnp.where(lane == 3 * z + h, m + jnp.log(l), lse_cols[at, :])
            single = pltpu.roll(outs[2], HD, 1).astype(BF16)
            pair = jnp.where(low_half, outs[0], outs[1]).astype(BF16)
            mixed_ref[at, pl.ds(z * 256, LANES)] = single
            mixed_ref[at, pl.ds(z * 256 + LANES, LANES)] = pair
        return 0

    mixed_ref = own_ref
    lax.fori_loop(0, queries // qblock, one_block, 0)
    sib_ref[...] = own_ref[pl.ds(block, block), :]
    lse_ref[...] = jnp.transpose(lse_cols[...])[0:8, :]


def vmem():
    return pl.BlockSpec(memory_space=pltpu.VMEM)


def smem():
    return pl.BlockSpec(memory_space=pltpu.SMEM)


def anywhere():
    return pl.BlockSpec(memory_space=pl.ANY)


def params():
    return pltpu.CompilerParams(vmem_limit_bytes=VMEM_LIMIT)


def shape(dims, dtype):
    return jax.ShapeDtypeStruct(dims, dtype)


def piece_rows(pieces):
    return pieces[0].shape[1]


def attend(scal, x_full, bias, tables, pieces):
    cos, sin, qcode, kcode = tables[:4]
    keys, width = x_full.shape
    queries = keys // 2
    return pl.pallas_call(
        partial(attend_kernel, len(pieces), piece_rows(pieces)),
        out_shape=(
            shape((2, 2, queries, LANES), BF16),
            shape((2, 2, keys, LANES), BF16),
            shape((2, 2, keys, LANES), BF16),
            shape((queries, 512), BF16),
            shape((queries // 2, 512), BF16),
            shape((8, queries), F32),
        ),
        in_specs=[smem()] + [vmem()] * 6 + [anywhere()] * len(pieces),
        out_specs=(vmem(),) * 6,
        scratch_shapes=[
            pltpu.VMEM((2, width, 6 * LANES), BF16),
            pltpu.VMEM((queries, LANES), F32),
            pltpu.SemaphoreType.DMA((len(pieces),)),
        ],
        compiler_params=params(),
        cost_estimate=pl.CostEstimate(
            flops=16_000_000_000, bytes_accessed=16_000_000, transcendentals=8_000_000
        ),
        name="attend",
    )(scal, x_full, bias, cos, sin, qcode, kcode, *pieces)


def feed_kernel(n_pieces, rows, layer_last, *refs):
    scal, x_ref, own_ref, sib_ref, vec_ref, bin_ref = refs[:6]
    attn = refs[6 : 6 + n_pieces]
    feed = refs[6 + n_pieces : 6 + 2 * n_pieces]
    at = 6 + 2 * n_pieces
    next_ref, low_ref, r1_ref, r2_ref, e_ref, gp_ref = refs[at : at + 6]
    wo_ref, win_ref, wback_ref, sems = refs[at + 6 :]
    out_copies = start_pieces(
        scal,
        attn,
        sems,
        0,
        lambda piece, offset: (
            piece.at[:, :, pl.ds(4 * LANES, 2 * LANES)],
            wo_ref.at[:, pl.ds(offset, rows), :],
        ),
    )
    width = x_ref.shape[1]
    in_copies = start_pieces(
        scal,
        feed,
        sems,
        n_pieces,
        lambda piece, offset: (
            piece.at[:, :, pl.ds(0, width)],
            win_ref.at[:, pl.ds(offset, rows), :],
        ),
    )
    back_copies = start_pieces(
        scal,
        feed,
        sems,
        2 * n_pieces,
        lambda piece, offset: (
            piece.at[:, :, pl.ds(width, width)],
            wback_ref.at[:, pl.ds(offset, rows), :],
        ),
    )
    first_z = scal[n_pieces]
    for copy in out_copies:
        copy.wait()
    a = jnp.zeros(x_ref.shape, F32)
    for z in range(2):
        a = a + nt(own_ref[:, z * 256 : z * 256 + 256], wo_ref[first_z + z])
        a = a + nt(sib_ref[:, z * 256 : z * 256 + 256], wo_ref[2 - first_z + z])
    r1 = x_ref[...] + a + vec_ref[0:1, :]
    r1_ref[...] = r1
    n1, _ = norm_parts(r1)
    h = n1 * vec_ref[1:2, :] + vec_ref[2:3, :]
    low_ref[...] = h.astype(BF16)
    r2_ref[...] = h + vec_ref[3:4, :]
    for copy in in_copies:
        copy.wait()
    for copy in back_copies:
        copy.wait()

    def one(z, _):
        u = nn(low_ref[...], win_ref[z]) + bin_ref[z]
        cdf = 0.5 * (1.0 + lax.erf(u * (2.0**-0.5)))
        pdf = jnp.exp(u * u * -0.5) * 0.3989422804014327
        e = (u * cdf).astype(BF16)
        e_ref[z] = e
        gp_ref[z] = (cdf + u * pdf).astype(BF16)
        r2_ref[...] += nt(e, wback_ref[z])
        return 0

    lax.fori_loop(0, MP, one, 0)
    n2, _ = norm_parts(r2_ref[...])
    result = n2 * vec_ref[4:5, :] + vec_ref[5:6, :]
    next_ref[...] = result
    low_ref[...] = result.astype(BF16)


def feed_forward(scal, x, own, sib, vec, bias_in, attn, feed):
    rows, width = x.shape
    count = len(attn)
    return pl.pallas_call(
        partial(feed_kernel, count, piece_rows(attn), False),
        out_shape=(
            shape((rows, width), F32),
            shape((rows, width), BF16),
            shape((rows, width), F32),
            shape((rows, width), F32),
            shape((MP, rows, width), BF16),
            shape((MP, rows, width), BF16),
        ),
        in_specs=[smem()] + [vmem()] * 5 + [anywhere()] * (2 * count),
        out_specs=(vmem(),) * 6,
        scratch_shapes=[
            pltpu.VMEM((MP, width, 2 * LANES), BF16),
            pltpu.VMEM((MP, width, width), BF16),
            pltpu.VMEM((MP, width, width), BF16),
            pltpu.SemaphoreType.DMA((3 * count,)),
        ],
        compiler_params=params(),
        cost_estimate=pl.CostEstimate(
            flops=8_000_000_000, bytes_accessed=20_000_000, transcendentals=2_400_000
        ),
        name="feed",
    )(scal, x, own, sib, vec, bias_in, *attn, *feed)


def feed_back_kernel(n_pieces, rows, *refs):
    scal, dy_ref, r1_ref, r2_ref, e_ref, gp_ref, own_ref, sib_ref, vec_ref = refs[:9]
    attn = refs[9 : 9 + n_pieces]
    feed = refs[9 + n_pieces : 9 + 2 * n_pieces]
    at = 9 + 2 * n_pieces
    dr1_ref, dzown_ref, dzsib_ref, dvec_ref, dbin_ref = refs[at : at + 5]
    outs = 2 if n_pieces == 8 else 1
    grads = refs[at + 5 : at + 5 + outs]
    wo_ref, win_ref, wback_ref, df_ref, dft_ref, ht_ref, dw_ref, sems = refs[at + 5 + outs :]
    width = dy_ref.shape[1]
    back_copies = start_pieces(
        scal,
        feed,
        sems,
        2 * n_pieces,
        lambda piece, offset: (
            piece.at[:, :, pl.ds(width, width)],
            wback_ref.at[:, pl.ds(offset, rows), :],
        ),
    )
    in_copies = start_pieces(
        scal,
        feed,
        sems,
        n_pieces,
        lambda piece, offset: (
            piece.at[:, :, pl.ds(0, width)],
            win_ref.at[:, pl.ds(offset, rows), :],
        ),
    )
    out_copies = start_pieces(
        scal,
        attn,
        sems,
        0,
        lambda piece, offset: (
            piece.at[:, :, pl.ds(4 * LANES, 2 * LANES)],
            wo_ref.at[:, pl.ds(offset, rows), :],
        ),
    )
    first_z = scal[n_pieces]
    dy = dy_ref[...]
    n2, scale2 = norm_parts(r2_ref[...])
    dvec_ref[4:5, :] = jnp.sum(dy * n2, axis=0, keepdims=True)
    dvec_ref[5:6, :] = jnp.sum(dy, axis=0, keepdims=True)
    dr2 = norm_back(dy, n2, scale2, vec_ref[4:5, :])
    dvec_ref[3:4, :] = jnp.sum(dr2, axis=0, keepdims=True)
    dr1_ref[...] = dr2
    df = dr2.astype(BF16)
    df_ref[...] = df
    dft_ref[...] = jnp.transpose(df)
    n1, _ = norm_parts(r1_ref[...])
    h = (n1 * vec_ref[1:2, :] + vec_ref[2:3, :]).astype(BF16)
    ht_ref[...] = jnp.transpose(h)
    for copy in back_copies + in_copies:
        copy.wait()

    def one(z, _):
        de = nn(df_ref[...], wback_ref[z])
        du = de * gp_ref[z].astype(F32)
        dbin_ref[z] = jnp.sum(du, axis=0, keepdims=True)
        dub = du.astype(BF16)
        dr1_ref[...] += nt(dub, win_ref[z])
        dw_ref[z, :, 0:width] = nn(ht_ref[...], dub).astype(BF16)
        dw_ref[z, :, width : 2 * width] = nn(dft_ref[...], e_ref[z]).astype(BF16)
        return 0

    lax.fori_loop(0, MP, one, 0)
    dh = dr1_ref[...]
    n1, scale1 = norm_parts(r1_ref[...])
    dvec_ref[1:2, :] = jnp.sum(dh * n1, axis=0, keepdims=True)
    dvec_ref[2:3, :] = jnp.sum(dh, axis=0, keepdims=True)
    dr1 = norm_back(dh, n1, scale1, vec_ref[1:2, :])
    dvec_ref[0:1, :] = jnp.sum(dr1, axis=0, keepdims=True)
    dr1_ref[...] = dr1
    da = dr1.astype(BF16)
    dft_ref[...] = jnp.transpose(da)
    for copy in out_copies:
        copy.wait()
    used = lane_index((da.shape[0], 2 * LANES)) >= HD
    for z in range(2):
        for mixed_ref, dz_ref, z_at in (
            (own_ref, dzown_ref, first_z + z),
            (sib_ref, dzsib_ref, 2 - first_z + z),
        ):
            part = mixed_ref[:, z * 256 : z * 256 + 256]
            dw_ref[z_at, :, 2 * width :] = nn(dft_ref[...], part).astype(BF16)
            dz = nn(da, wo_ref[z_at])
            dz_ref[:, z * 256 : z * 256 + 256] = jnp.where(used, dz, 0.0).astype(BF16)
    flight = []
    for i in range(n_pieces):
        offset = pl.multiple_of(scal[i], 32)
        target = grads[i // 4].at[PIECE_ORDER[i % 4] if n_pieces == 8 else 0]
        copy = pltpu.make_async_copy(dw_ref.at[:, pl.ds(offset, rows), :], target, sems.at[i])
        copy.start()
        flight.append(copy)
    for copy in flight:
        copy.wait()


PIECE_ORDER = (3, 0, 2, 1)


def feed_back(scal, dy, r1, r2, e, gp, own, sib, vec, attn, feed):
    rows, width = dy.shape
    count = len(attn)
    prows = piece_rows(attn)
    lanes = 2 * width + 2 * LANES
    grads = (shape((4, MP, prows, lanes), BF16),) * 2
    if count != 8:
        grads = (shape((1, MP, prows, lanes), BF16),)
    return pl.pallas_call(
        partial(feed_back_kernel, count, prows),
        out_shape=(
            shape((rows, width), F32),
            shape((rows, 512), BF16),
            shape((rows, 512), BF16),
            shape((6, width), F32),
            shape((MP, 1, width), F32),
            *grads,
        ),
        in_specs=[smem()] + [vmem()] * 8 + [anywhere()] * (2 * count),
        out_specs=(vmem(),) * 5 + (anywhere(),) * len(grads),
        scratch_shapes=[
            pltpu.VMEM((MP, width, 2 * LANES), BF16),
            pltpu.VMEM((MP, width, width), BF16),
            pltpu.VMEM((MP, width, width), BF16),
            pltpu.VMEM((rows, width), BF16),
            pltpu.VMEM((width, rows), BF16),
            pltpu.VMEM((width, rows), BF16),
            pltpu.VMEM((MP, width, lanes), BF16),
            pltpu.SemaphoreType.DMA((3 * count,)),
        ],
        compiler_params=params(),
        cost_estimate=pl.CostEstimate(
            flops=16_000_000_000, bytes_accessed=40_000_000, transcendentals=0
        ),
        name="feed_back",
    )(scal, dy, r1, r2, e, gp, own, sib, vec, *attn, *feed)


def attend_back_kernel(n_pieces, rows, *refs):
    (
        scal,
        x_ref,
        cos_ref,
        sin_ref,
        qcode_ref,
        kcode_ref,
        q_ref,
        k_ref,
        v_ref,
        mixed_ref,
        dzown_ref,
        dzsib_ref,
        lse_ref,
    ) = refs[:13]
    pieces = refs[13 : 13 + n_pieces]
    dx_ref, dxs_ref, dbias_ref, parts_ref = refs[13 + n_pieces : 17 + n_pieces]
    (
        w_ref,
        xt_ref,
        dz_ref,
        delta_ref,
        dt_ref,
        dqt_ref,
        pair_ref,
        dw_ref,
        low_ref,
        sums_ref,
        sems,
    ) = refs[17 + n_pieces :]
    first_z = scal[n_pieces]
    copies = start_pieces(
        scal,
        pieces,
        sems,
        0,
        lambda piece, offset: (
            piece.at[pl.ds(first_z, 2)],
            w_ref.at[:, pl.ds(offset, rows), :],
        ),
    )
    keys, width = x_ref.shape
    queries = keys // 2
    block = queries // 2
    for z in range(2):
        for half, source in enumerate((dzown_ref, dzsib_ref)):
            at = pl.ds(half * block, block)
            dz_ref[z, 0, at, :] = source[:, z * 256 + LANES : z * 256 + 256]
            dz_ref[z, 1, at, :] = pltpu.roll(
                source[:, z * 256 : z * 256 + LANES].astype(F32), HD, 1
            ).astype(BF16)
        single = pltpu.roll(mixed_ref[:, z * 256 : z * 256 + LANES].astype(F32), HD, 1)
        pair = mixed_ref[:, z * 256 + LANES : z * 256 + 256].astype(F32)
        prod_one = jnp.transpose(pair * dz_ref[z, 0].astype(F32))
        prod_two = jnp.transpose(single * dz_ref[z, 1].astype(F32))
        delta_ref[3 * z : 3 * z + 1, :] = jnp.sum(prod_one[0:HD], axis=0, keepdims=True)
        delta_ref[3 * z + 1 : 3 * z + 2, :] = jnp.sum(prod_one[HD:], axis=0, keepdims=True)
        delta_ref[3 * z + 2 : 3 * z + 3, :] = jnp.sum(prod_two[0:HD], axis=0, keepdims=True)

    kblock = 256
    low_q = lane_index((queries, LANES)) < HD
    low_k = lane_index((kblock, LANES)) < HD
    for z in range(2):
        for h in range(3):
            tile = h // 2
            q = q_ref[z, tile]
            dz = dz_ref[z, tile]
            if h < 2:
                keep = low_q == (h == 0)
                q = jnp.where(keep, q, BF16(0))
                dz = jnp.where(keep, dz, BF16(0))
            pair_ref[0] = q
            pair_ref[1] = dz
            lse = lse_ref[3 * z + h : 3 * z + h + 1, :]
            delta = delta_ref[3 * z + h : 3 * z + h + 1, :]
            if h != 1:
                dqt_ref[...] = jnp.zeros_like(dqt_ref)

            def one_block(i, _, z=z, h=h, tile=tile, lse=lse, delta=delta):
                at = pl.ds(pl.multiple_of(i * kblock, kblock), kblock)
                kb = k_ref[z, tile, at, :]
                vb = v_ref[z, tile, at, :]
                if h < 2:
                    kb_own = jnp.where(low_k == (h == 0), kb, BF16(0))
                else:
                    kb_own = kb
                visible = kcode_ref[at, :] == qcode_ref[...]
                s = nt(kb, pair_ref[0])
                s = jnp.where(visible, s, NEGATIVE)
                p = jnp.exp(s - lse)
                dp = nt(vb, pair_ref[1])
                ds = (p * (dp - delta)).astype(BF16)
                dv = nn(p.astype(BF16), pair_ref[1])
                dk = nn(ds, pair_ref[0])
                dqt_ref[...] += nn(jnp.transpose(kb_own), ds)
                if h == 1:
                    dt_ref[2, at, :] += dk
                    dt_ref[3, at, :] += dv
                elif h == 0:
                    dt_ref[2, at, :] = dk
                    dt_ref[3, at, :] = dv
                else:
                    dt_ref[1, at, :] = pltpu.roll(dk, HD, 1)
                    dt_ref[4, at, :] = dv
                return 0

            lax.fori_loop(0, keys // kblock, one_block, 0)
            if h >= 1:
                dq = jnp.transpose(dqt_ref[...]) * HD**-0.5
                if h == 1:
                    dt_ref[0, 0:queries, :] = dq
                else:
                    dt_ref[1, 0:queries, :] += dq

        if z == 0:
            xt_ref[...] = jnp.transpose(x_ref[...])
            for copy in copies:
                copy.wait()
        for tile in range(5):
            count = queries if tile == 0 else keys
            t = dt_ref[tile, 0:count, :]
            if tile < 3:
                t = t * cos_ref[0:count, :] - half_swap(t) * sin_ref[0:count, :]
            dbias_ref[z, :, tile * LANES : (tile + 1) * LANES] = jnp.sum(t, axis=0, keepdims=True)
            low_ref[0:count, tile * LANES : (tile + 1) * LANES] = t.astype(BF16)
        dw_ref[z, :, 0:LANES] = nn(
            xt_ref[:, 0:queries], low_ref[0:queries, 0:LANES]
        ).astype(BF16)
        dw_ref[z, :, LANES:] = nn(xt_ref[...], low_ref[:, LANES:]).astype(BF16)
        for i in range(4):
            at = pl.ds(i * block, block)
            part = nt(low_ref[at, LANES:], w_ref[z, :, LANES : 5 * LANES])
            if i < 2:
                part = part + nt(low_ref[at, 0:LANES], w_ref[z, :, 0:LANES])
            if z == 0:
                sums_ref[i] = part
            else:
                target = dx_ref if i % 2 == 0 else dxs_ref
                target[i // 2] = (sums_ref[i] + part).astype(BF16)

    flight = []
    for i in range(min(n_pieces, 4)):
        offset = pl.multiple_of(scal[n_pieces + 1 + i], 32)
        copy = pltpu.make_async_copy(
            dw_ref.at[:, pl.ds(offset, parts_ref.shape[2]), :],
            parts_ref.at[PIECE_ORDER[i] if n_pieces == 8 else 0],
            sems.at[i],
        )
        copy.start()
        flight.append(copy)
    for copy in flight:
        copy.wait()


def attend_back(scal, x_full, tables, saved, mixed, dz_own, dz_sib, pieces):
    cos, sin, _, _, qcode, kcode = tables
    q, k, v, lse = saved
    keys, width = x_full.shape
    queries = keys // 2
    block = queries // 2
    count = len(pieces)
    parts = (4, 2, 2 * piece_rows(pieces), 5 * LANES)
    if count != 8:
        parts = (1, 2, piece_rows(pieces), 5 * LANES)
    return pl.pallas_call(
        partial(attend_back_kernel, count, piece_rows(pieces)),
        out_shape=(
            shape((2, block, width), BF16),
            shape((2, block, width), BF16),
            shape((2, 1, 5 * LANES), F32),
            shape(parts, BF16),
        ),
        in_specs=[smem()] + [vmem()] * 12 + [anywhere()] * count,
        out_specs=(vmem(),) * 3 + (anywhere(),),
        scratch_shapes=[
            pltpu.VMEM((2, width, 6 * LANES), BF16),
            pltpu.VMEM((width, keys), BF16),
            pltpu.VMEM((2, 2, queries, LANES), BF16),
            pltpu.VMEM((8, queries), F32),
            pltpu.VMEM((5, keys, LANES), F32),
            pltpu.VMEM((LANES, queries), F32),
            pltpu.VMEM((2, queries, LANES), BF16),
            pltpu.VMEM((2, width, 5 * LANES), BF16),
            pltpu.VMEM((keys, 5 * LANES), BF16),
            pltpu.VMEM((4, block, width), F32),
            pltpu.SemaphoreType.DMA((count,)),
        ],
        compiler_params=params(),
        cost_estimate=pl.CostEstimate(
            flops=40_000_000_000, bytes_accessed=20_000_000, transcendentals=8_000_000
        ),
        name="attend_back",
    )(scal, x_full, cos, sin, qcode, kcode, q, k, v, mixed, dz_own, dz_sib, lse, *pieces)


def head_tiles(q, k, v, o):
    return jnp.concatenate(
        [
            q[..., :LANES],
            q[..., LANES:],
            k[..., LANES:],
            k[..., :LANES],
            v[..., :LANES],
            v[..., LANES:],
            o[..., LANES:],
            o[..., :LANES],
        ],
        axis=-1,
    )


def head_columns(t):
    q = jnp.concatenate([t[..., 0:128], t[..., 128:192]], axis=-1)
    k = jnp.concatenate([t[..., 256:384], t[..., 192:256]], axis=-1)
    v = jnp.concatenate([t[..., 384:512], t[..., 512:576]], axis=-1)
    return q, k, v


def make_tables(positions, bucket, lengths):
    slot = LEN_MAX // (3 - bucket)
    sequence = positions // slot
    place = positions - sequence * slot
    limit = jnp.sum(
        jnp.where(sequence[:, None] == jnp.arange(3)[None, :], lengths[None, :], 0), axis=1
    )
    lane = jnp.arange(LANES) % HD
    frequency = 10000.0 ** (-2.0 * (lane % (HD // 2)).astype(F32) / HD)
    angles = place.astype(F32)[:, None] * frequency[None, :]
    sign = jnp.where(lane < HD // 2, -1.0, 1.0)
    cos = jnp.cos(angles)
    sin = jnp.sin(angles) * sign[None, :]
    kcode = jnp.where(place < limit, sequence, -1).astype(F32)
    qcode = sequence[: positions.shape[0] // 2].astype(F32)
    return cos, sin, qcode[:, None], kcode[None, :], qcode[None, :], kcode[:, None]


def per_device(
    tokens, w_qkv, b_qkv, w_out, vectors, w_in, b_in, w_back, cotangent, lengths, buckets
):
    layers = w_qkv.shape[0]
    rows, width = tokens.shape
    d = lax.axis_index("dp")
    z = lax.axis_index("mp")
    g, c = d // 2, d % 2

    gathered = []
    for layer_at in range(layers):
        low = w_qkv[layer_at].astype(BF16)
        attn = head_tiles(low[0], low[1], low[2], w_out[layer_at].astype(BF16).T)
        feed = jnp.concatenate(
            [w_in[layer_at].astype(BF16), w_back[layer_at].astype(BF16).T], axis=-1
        )
        gathered.append((gather_bundle(attn), gather_bundle(feed)))
    piece_height = w_qkv.shape[2]
    offsets = row_offsets(g, c, piece_height)
    first = jnp.where(c == 0, 1, 2)
    spans = [(g ^ hop) * 2 * piece_height for hop in (0, first, 3 - first, 3)]
    if len(offsets) == 1:
        spans = [jnp.int32(0)] * 4
    scal = jnp.stack(offsets + [2 * c] + spans).astype(jnp.int32)

    zero = jnp.zeros((layers, LANES // 2), F32)
    v_bias = b_qkv[:, 2]
    bias_tiles = jnp.concatenate(
        [
            b_qkv[:, 0],
            b_qkv[:, 1, LANES:],
            b_qkv[:, 1, :LANES],
            v_bias,
            zero,
        ],
        axis=-1,
    )
    small = gather_small(jnp.concatenate([bias_tiles, b_in], axis=-1))
    bias_all = small[:, :, : 5 * LANES]
    bias_in_all = small[:, :, 5 * LANES :]

    meta = jnp.concatenate([buckets, lengths[0]])
    other_meta = core_swap(meta)
    half = z // 2
    meta = jnp.where(half == c, meta, other_meta)
    place = z % 2
    quarters = [2 * c + place, 2 * (1 - c) + place, 2 * c + 1 - place, 2 * (1 - c) + 1 - place]
    positions = jnp.concatenate([q * rows + jnp.arange(rows, dtype=jnp.int32) for q in quarters])
    tables = make_tables(positions, meta[0], meta[1:])

    tokens = relayout(tokens)
    low = tokens
    stream = tokens.astype(F32)
    states = []
    for layer_at in range(layers):
        attn, feed = gathered[layer_at]
        two = jnp.stack([low, pair_swap(low)])
        others = core_swap(two)
        x_full = jnp.concatenate([two[0], others[0], two[1], others[1]], axis=0)
        bias = lax.dynamic_slice_in_dim(bias_all[:, layer_at], 2 * c, 2, 0)[:, None, :]
        q, k, v, mixed, mixed_sib, lse = attend(scal, x_full, bias, tables, attn)
        others_mixed = core_swap(mixed_sib)
        own_mixed = mixed[:rows]
        stream, low, r1, r2, e, gp = feed_forward(
            scal,
            stream,
            own_mixed,
            others_mixed,
            vectors[layer_at],
            bias_in_all[:, layer_at][:, None, :],
            attn,
            feed,
        )
        states.append((x_full, (q, k, v, lse), mixed, own_mixed, others_mixed, r1, r2, e, gp))
    result = relayout(low)

    gradient = relayout(cotangent).astype(F32)
    masters = []
    vector_grads = []
    in_biases = []
    head_biases = []
    for layer_at in reversed(range(layers)):
        attn, feed = gathered[layer_at]
        x_full, saved, mixed, own_mixed, others_mixed, r1, r2, e, gp = states[layer_at]
        back = feed_back(
            scal, gradient, r1, r2, e, gp, own_mixed, others_mixed, vectors[layer_at], attn, feed
        )
        dr1, dz_own, dz_sib, dvec, dbin = back[:5]
        dz_others = core_swap(dz_sib)
        feed_grad = reduce_all(back[5], back[-1])
        dx, dx_sib, dbias, parts = attend_back(
            scal, x_full, tables, saved, mixed, dz_own, dz_others, attn
        )
        got = dx.astype(F32) + core_swap(dx_sib).astype(F32)
        gradient = dr1 + got[0] + pair_swap(got[1].astype(BF16)).astype(F32)
        head_grad = reduce_heads(parts)
        masters.insert(0, (feed_grad, head_grad))
        vector_grads.insert(0, dvec)
        in_biases.insert(0, dbin[:, 0])
        head_biases.insert(0, sum_head_biases(dbias[:, 0]))
    grad_tokens = relayout(gradient.astype(BF16)).astype(F32)

    layers_of = jnp.stack(in_biases, axis=1)
    grad_vectors, grad_b_in = sum_vectors(jnp.concatenate(vector_grads), layers_of)
    grad_vectors = grad_vectors.reshape(vectors.shape)
    grad_b_qkv = jnp.stack([jnp.stack(head_columns(b)) for b in head_biases])

    grad_qkv = jnp.stack([jnp.stack(head_columns(m[1])) for m in masters])
    grad_in = jnp.stack([m[0][:, :width] for m in masters])
    grad_back = jnp.stack([m[0][:, width : 2 * width].T for m in masters])
    grad_out = jnp.stack(
        [
            jnp.concatenate(
                [m[0][:, 2 * width + LANES :], m[0][:, 2 * width + HD : 2 * width + LANES]], axis=-1
            ).T
            for m in masters
        ]
    )
    return (
        result,
        grad_tokens,
        grad_qkv,
        grad_b_qkv,
        grad_out,
        grad_vectors,
        grad_in,
        grad_b_in,
        grad_back,
    )


def solution(mesh):
    return jax.shard_map(
        per_device,
        mesh=mesh,
        in_specs=(
            P(("dp", "mp"), None),
            P(None, None, "dp", "mp"),
            P(None, None, "mp"),
            P(None, "mp", "dp"),
            P(),
            P(None, "dp", "mp"),
            P(None, "mp"),
            P(None, "mp", "dp"),
            P(("dp", "mp"), None),
            P("dp", None),
            P("dp"),
        ),
        out_specs=(
            P(("dp", "mp"), None),
            P(("dp", "mp"), None),
            P(None, None, "dp", "mp"),
            P(None, None, "mp"),
            P(None, "mp", "dp"),
            P(),
            P(None, "dp", "mp"),
            P(None, "mp"),
            P(None, "mp", "dp"),
        ),
        check_vma=False,
    )
```

```python
from functools import partial

import jax
import jax.numpy as jnp
from jax import lax
from jax.experimental import pallas as pl
from jax.experimental.pallas import tpu as pltpu
from jax.sharding import PartitionSpec as P

HD = 64
LEN_MAX = 1536
EPSILON = 1e-06
NEGATIVE = -1e30
F32 = jnp.float32
BF16 = jnp.bfloat16
LANES = 128
MP = 4
VMEM_LIMIT = 60 * 1024 * 1024


def nn(a, b):
    return lax.dot_general(a, b, (((1,), (0,)), ((), ())), preferred_element_type=F32)


def nt(a, b):
    return lax.dot_general(a, b, (((1,), (1,)), ((), ())), preferred_element_type=F32)


def core_swap(x):
    n = lax.axis_size("dp")
    return lax.ppermute(x, "dp", [(i, i ^ 1) for i in range(n)])


def plane_swap(x, first):
    n = lax.axis_size("dp")
    hops = (2, 4) if first else (4, 2)
    return lax.ppermute(x, "dp", [(i, i ^ hops[i % 2]) for i in range(n)])


def column_shift(x, k):
    return lax.ppermute(x, "mp", [(i, (i + k) % MP) for i in range(MP)])


def pair_swap(x):
    return lax.ppermute(x, "mp", [(i, i ^ 1) for i in range(MP)])


def relayout(x):
    n = lax.axis_size("dp")
    pairs = []
    for d in range(n):
        for z in range(MP):
            if (d % 2) != (z // 2):
                pairs.append((d * MP + z, (d ^ 1) * MP + (z ^ 2)))
            else:
                pairs.append((d * MP + z, d * MP + z))
    return lax.ppermute(x, ("dp", "mp"), pairs)


def turn_columns(x, z):
    return jnp.stack([lax.dynamic_index_in_dim(x, (z - k) % MP, 0, False) for k in range(MP)])


def row_offsets(g, c, rows):
    if lax.axis_size("dp") != 8:
        return [jnp.int32(0)]
    result = []
    for core in (c, 1 - c):
        first = jnp.where(core == 0, 1, 2)
        for hop in (0, first, 3 - first, 3):
            result.append(((g ^ hop) * 2 + core) * rows)
    return result


def send_columns(v):
    total = v[0].astype(F32)
    for k in range(1, MP):
        total = total + column_shift(v[k], -k).astype(F32)
    return total


def reduce_all(keep, away):
    if lax.axis_size("dp") != 8:
        z = lax.axis_index("mp")
        whole = turn_columns(keep[0], z).astype(F32)
        part = lax.psum_scatter(whole, "mp", scatter_dimension=0, tiled=False)
        return lax.psum_scatter(part, "dp", scatter_dimension=0, tiled=True)
    other = core_swap(away)

    def add(i):
        return keep[i].astype(F32) + other[i].astype(F32)

    got = plane_swap(jnp.stack([add(0), add(1)]).astype(BF16), True)
    got_two = plane_swap((add(2) + got[1].astype(F32)).astype(BF16), False)
    v = (add(3) + got[0].astype(F32) + got_two.astype(F32)).astype(BF16)
    return send_columns(v)


def reduce_heads(parts):
    c = lax.axis_index("dp") % 2
    n = lax.axis_size("dp")
    if n != 8:
        z = lax.axis_index("mp")
        wide = jnp.concatenate([parts[0], jnp.zeros_like(parts[0])], axis=0)
        wide = jnp.where(c == 0, wide, jnp.roll(wide, 2, axis=0))
        whole = turn_columns(wide, z).astype(F32)
        part = lax.psum_scatter(whole, "mp", scatter_dimension=0, tiled=False)
        return lax.psum_scatter(part, "dp", scatter_dimension=0, tiled=True)
    got = plane_swap(parts[0:2], True)
    got_two = plane_swap((parts[2].astype(F32) + got[1].astype(F32)).astype(BF16), False)
    v = (parts[3].astype(F32) + got[0].astype(F32) + got_two.astype(F32)).astype(BF16)

    total = column_turn(v[0], 0).astype(F32) + column_turn(v[1], 1).astype(F32)
    rows = total.shape[0] // 2
    kept = lax.dynamic_slice_in_dim(total, c * rows, rows, 0)
    sent = lax.dynamic_slice_in_dim(total, (1 - c) * rows, rows, 0).astype(BF16)
    return kept + core_swap(sent).astype(F32)


def sum_head_biases(v):
    c = lax.axis_index("dp") % 2
    n = lax.axis_size("dp")
    if n != 8:
        z = lax.axis_index("mp")
        zero = jnp.zeros_like(v)
        wide = jnp.where(c == 0, jnp.concatenate([v, zero]), jnp.concatenate([zero, v]))
        total = lax.psum(turn_columns(wide, z), ("dp", "mp"))
        return lax.dynamic_index_in_dim(total, z, 0, False)
    v = v + plane_swap(v, True)
    v = v + plane_swap(v, False)
    total = column_turn(v[0], 0) + column_turn(v[1], 1)
    return total + core_swap(total)


def column_turn(x, k):
    n = lax.axis_size("dp")
    pairs = []
    for d in range(n):
        for z in range(MP):
            pairs.append((d * MP + z, d * MP + (z - k - 2 * (d % 2)) % MP))
    return lax.ppermute(x, ("dp", "mp"), pairs)


def sum_vectors(vectors, columns):
    if lax.axis_size("dp") != 8:
        z = lax.axis_index("mp")
        vectors, columns = lax.psum((vectors, turn_columns(columns, z)), ("dp", "mp"))
        return vectors, lax.dynamic_index_in_dim(columns, z, 0, False)
    n = vectors.shape[0]
    m = columns.shape[1]
    both = jnp.concatenate([vectors, columns.reshape(MP * m, -1)])
    both = both + core_swap(both)
    both = both + plane_swap(both, True)
    both = both + plane_swap(both, False)
    total = both[: n + m]
    for k in range(1, MP):
        at = n + m * (MP - k)
        total = total + column_shift(jnp.concatenate([both[:n], both[at : at + m]]), k)
    return total[:n], total[n:]


def lane_index(shape):
    return lax.broadcasted_iota(jnp.int32, shape, len(shape) - 1)


def half_swap(x):
    lane = lane_index(x.shape)
    return jnp.where(
        lane % HD < HD // 2,
        pltpu.roll(x, LANES - HD // 2, x.ndim - 1),
        pltpu.roll(x, HD // 2, x.ndim - 1),
    )


def norm_parts(r):
    mean = jnp.mean(r, axis=-1, keepdims=True)
    centred = r - mean
    scale = lax.rsqrt(jnp.mean(centred * centred, axis=-1, keepdims=True) + EPSILON)
    return centred * scale, scale


def norm_back(dy, n, scale, gain):
    gdy = dy * gain
    mean_one = jnp.mean(gdy, axis=-1, keepdims=True)
    mean_two = jnp.mean(gdy * n, axis=-1, keepdims=True)
    return (gdy - mean_one - n * mean_two) * scale


def vmem():
    return pl.BlockSpec(memory_space=pltpu.VMEM)


def smem():
    return pl.BlockSpec(memory_space=pltpu.SMEM)


def anywhere():
    return pl.BlockSpec(memory_space=pl.ANY)


def params():
    return pltpu.CompilerParams(vmem_limit_bytes=VMEM_LIMIT)


def shape(dims, dtype):
    return jax.ShapeDtypeStruct(dims, dtype)


def project_rows(i, z, x, w_ref, bias, cos, sin, q_ref, k_ref, v_ref):
    block = x.shape[0]
    at = pl.ds(i * block, block)
    p = nn(x, w_ref[z, :, LANES : 5 * LANES]) + bias[:, LANES:]
    low_half = lane_index((block, LANES)) < HD
    mixed = p[:, 0:LANES]
    mixed = mixed * cos + half_swap(mixed) * sin
    pair = p[:, LANES : 2 * LANES]
    pair = pair * cos + half_swap(pair) * sin
    k_ref[z, 0, at, :] = pair.astype(BF16)
    k_ref[z, 1, at, :] = jnp.where(low_half, pltpu.roll(mixed, HD, 1), 0.0).astype(BF16)
    v_ref[z, 0, at, :] = p[:, 2 * LANES : 3 * LANES].astype(BF16)
    v_ref[z, 1, at, :] = jnp.where(low_half, p[:, 3 * LANES :], 0.0).astype(BF16)
    if i < 2:
        q = nn(x, w_ref[z, :, 0:LANES]) + bias[:, 0:LANES]
        q = q * cos + half_swap(q) * sin
        q_ref[z, 0, at, :] = q.astype(BF16) * BF16(HD**-0.5)
        q_ref[z, 1, at, :] = jnp.where(low_half, mixed, 0.0).astype(BF16) * BF16(HD**-0.5)


def attend_rows(i, qblock, qcode_ref, kcode_ref, q_ref, k_ref, v_ref, mixed_ref, lse_cols):
    at = pl.ds(pl.multiple_of(i * qblock, qblock), qblock)
    visible = qcode_ref[at, :] == kcode_ref[...]
    low_half = lane_index((qblock, LANES)) < HD
    lane = lane_index((qblock, LANES))
    for z in range(2):
        outs = []
        for h in range(3):
            tile = h // 2
            q = q_ref[z, tile, at, :]
            if h < 2:
                q = jnp.where(low_half == (h == 0), q, BF16(0))
            s = nt(q, k_ref[z, tile])
            s = jnp.where(visible, s, NEGATIVE)
            m = jnp.max(s, axis=-1, keepdims=True)
            p = jnp.exp(s - m)
            l = jnp.sum(p, axis=-1, keepdims=True)
            o = nn(p.astype(BF16), v_ref[z, tile])
            outs.append(o / l)
            lse_cols[at, :] = jnp.where(lane == 3 * z + h, m + jnp.log(l), lse_cols[at, :])
        mixed_ref[at, pl.ds(z * 256, LANES)] = pltpu.roll(outs[2], HD, 1).astype(BF16)
        mixed_ref[at, pl.ds(z * 256 + LANES, LANES)] = jnp.where(
            low_half, outs[0], outs[1]
        ).astype(BF16)


def forward_kernel(n_layers, *refs):
    n_in, per_layer = 7, 11
    blocks, tokens, cot, small, meta, frequency, vectors = refs[:n_in]
    w_all, dy_out, low_out, cos_out, sin_out, qrow_out, kcol_out = refs[n_in : n_in + 7]
    saved = [
        refs[n_in + 7 + l * per_layer : n_in + 7 + (l + 1) * per_layer] for l in range(n_layers)
    ]
    (
        xfull,
        mixed_in,
        small_all,
        meta_in,
        wa,
        wo,
        win,
        wback,
        cos_ref,
        sin_ref,
        qcode_ref,
        kcode_ref,
        qrow_ref,
        kcol_ref,
        q_ref,
        k_ref,
        v_ref,
        mixed_ref,
        lse_cols,
        lse_ref,
        stream,
        sum_ref,
        r1_ref,
        low_ref,
        e_ref,
        gp_ref,
        z_send,
        z_recv,
        p_send,
        p_recv,
        c_send,
        c_recv,
        x_send,
        x_recv,
        t_send,
        t_recv,
        l_sem,
        w_sem,
        s_sem,
    ) = refs[n_in + 7 + n_layers * per_layer :]
    rows = stream.shape[0]
    width = stream.shape[1]
    height = blocks.shape[1]
    chunks = blocks.shape[0]

    d = lax.axis_index("dp")
    z = lax.axis_index("mp")
    c = d % 2
    x = (d // 2) % 2
    y = d // 4
    flip_x, flip_y = 1 - 2 * x, 1 - 2 * y
    one_x, one_y = x + (1 - c) * flip_x, y + c * flip_y
    two_x, two_y = x + c * flip_x, y + (1 - c) * flip_y

    def device(yy, xx, cc, zz):
        return (yy * 4 + xx * 2 + cc, zz)

    def rows_of(yy, xx):
        return pl.ds(pl.multiple_of((yy * 4 + xx * 2 + c) * height, 32), height)

    sibling = device(y, x, 1 - c, z)
    first = device(one_y, one_x, c, z)
    second = device(two_y, two_x, c, z)
    pair_z = z + 1 - 2 * (z % 2)
    pair = device(y, x, c, pair_z)
    away = device(y, x, 1 - c, (z + 2) % MP)
    moved = c != z // 2
    columns = [device(y, x, c, (z + s) % MP) for s in range(1, MP)]
    own_rows = rows_of(y, x)
    first_rows = rows_of(one_y, one_x)
    second_rows = rows_of(two_y, two_x)
    third_rows = rows_of(1 - y, 1 - x)

    barrier = pltpu.get_barrier_semaphore()
    partners = columns + [first, second, sibling, away]
    for partner in partners:
        pl.semaphore_signal(
            barrier, inc=1, device_id=partner, device_id_type=pl.DeviceIdType.MESH
        )
    pl.semaphore_wait(barrier, len(partners))

    def remote(source, target, send, recv, to):
        return pltpu.make_async_remote_copy(
            src_ref=source,
            dst_ref=target,
            send_sem=send,
            recv_sem=recv,
            device_id=to,
            device_id_type=pl.DeviceIdType.MESH,
        )

    sent = []

    def go(make, *at):
        make(*at).start()
        sent.append((make, at))

    def local_copy(k):
        return pltpu.make_async_copy(blocks.at[k], w_all.at[k, z, own_rows], l_sem.at[k])

    def z_copy(k, s):
        return remote(
            blocks.at[k], w_all.at[k, z, own_rows], z_send.at[k, s], z_recv.at[k, s], columns[s]
        )

    def p_copy(k, n):
        source = w_all.at[k, :, first_rows if n == 2 else own_rows]
        return remote(
            source, source, p_send.at[k, n], p_recv.at[k, n], first if n == 0 else second
        )

    def c_copy(k, n):
        source = w_all.at[k, :, (own_rows, first_rows, second_rows, third_rows)[n]]
        return remote(source, source, c_send.at[k, n], c_recv.at[k, n], sibling)

    def step_send(k):
        local_copy(k).start()
        for s in range(MP - 1):
            go(z_copy, k, s)

    def step_plane(k):
        local_copy(k).wait()
        for s in range(MP - 1):
            z_copy(k, s).wait_recv()
        go(p_copy, k, 0)
        go(p_copy, k, 1)
        go(c_copy, k, 0)
        if k + 2 < chunks:
            step_send(k + 2)

    def step_forward(k):
        p_copy(k, 0).wait_recv()
        go(p_copy, k, 2)
        go(c_copy, k, 1)
        p_copy(k, 1).wait_recv()
        go(c_copy, k, 2)

    def step_last(k):
        p_copy(k, 2).wait_recv()
        go(c_copy, k, 3)

    def step_ready(k):
        for n in range(4):
            c_copy(k, n).wait_recv()

    plan = []
    for k in range(chunks):
        plan.append(partial(step_plane, k))
        plan.append(partial(step_forward, k))
        plan.append(partial(step_last, k))
    for k in range(chunks - 1):
        at = plan.index(plan[3 * k + 2])
        plan[at], plan[at + 1] = plan[at + 1], plan[at]
    position = [0]

    def take(until):
        steps = plan[position[0] : until]
        position[0] = max(position[0], until)
        return steps

    def run(steps):
        for step in steps:
            step()

    def meta_copy():
        return remote(meta, meta_in, t_send.at[0], t_recv.at[0], sibling)

    def small_copy(s):
        return remote(small, small_all.at[z], t_send.at[3 + s], t_recv.at[3 + s], columns[s])

    go(meta_copy)
    token_copy = remote(tokens, xfull.at[0, 0], t_send.at[1], t_recv.at[1], away)
    token_local = pltpu.make_async_copy(tokens, xfull.at[0, 0], l_sem.at[chunks])

    @pl.when(moved)
    def _():
        token_copy.start()

    @pl.when(jnp.logical_not(moved))
    def _():
        token_local.start()

    step_send(0)
    for s in range(MP - 1):
        go(small_copy, s)
    step_send(1)
    small_local = pltpu.make_async_copy(small, small_all.at[z], l_sem.at[chunks + 1])
    small_local.start()

    meta_copy().wait_recv()
    info = jnp.where(moved, meta_in[...], meta[...])
    slot = info[0:1, :]
    limits = [info[n : n + 1, :] for n in range(1, 4)]
    half = z % 2
    quarters = [2 * c + half, 2 * (1 - c) + half, 2 * c + 1 - half, 2 * (1 - c) + 1 - half]

    def codes(place_all, slot, limits):
        seq = jnp.where(place_all >= slot, 1.0, 0.0) + jnp.where(place_all >= 2.0 * slot, 1.0, 0.0)
        place = place_all - seq * slot
        limit = jnp.where(seq == 0.0, limits[0], jnp.where(seq == 1.0, limits[1], limits[2]))
        return seq, place, jnp.where(place < limit, seq, -1.0)

    sign = jnp.where(lane_index((1, LANES)) % HD < HD // 2, -1.0, 1.0)
    for i in range(4):
        at = pl.ds(i * rows, rows)
        base = quarters[i] * rows
        index = lax.broadcasted_iota(jnp.int32, (rows, LANES), 0) + base
        seq, place, kcode = codes(index.astype(F32), slot, limits)
        angle = place * frequency[...]
        cos_ref[at, :] = jnp.cos(angle)
        sin_ref[at, :] = jnp.sin(angle) * sign
        kcol_ref[at, :] = kcode[:, 0:1]
        if i < 2:
            qcode_ref[at, :] = seq[:, 0:1]
        index = lax.broadcasted_iota(jnp.int32, (1, rows), 1) + base
        seq, place, kcode = codes(
            index.astype(F32), slot[:, 0:1], [limit[:, 0:1] for limit in limits]
        )
        kcode_ref[:, pl.ds(i * rows, rows)] = kcode
        if i < 2:
            qrow_ref[:, pl.ds(i * rows, rows)] = seq

    @pl.when(moved)
    def _():
        token_copy.wait_recv()

    @pl.when(jnp.logical_not(moved))
    def _():
        token_local.wait()

    def x_copy(l, n):
        source = xfull.at[l, 2 if n == 2 else 0]
        target = xfull.at[l, (2, 1, 3)[n]]
        return remote(
            source, target, x_send.at[l, n], x_recv.at[l, n], pair if n == 0 else sibling
        )

    def m_copy(l):
        return remote(
            mixed_ref.at[pl.ds(rows, rows)],
            mixed_in.at[l],
            x_send.at[l, 3],
            x_recv.at[l, 3],
            sibling,
        )

    stores = {}

    def store(name, source, target):
        copy = pltpu.make_async_copy(source, target, s_sem.at[len(stores)])
        copy.start()
        stores[name] = copy

    waited = set()

    def stored(*names):
        for name in names:
            if name in stores and name not in waited:
                waited.add(name)
                stores[name].wait()

    stream[...] = xfull[0, 0].astype(F32)
    store("cos", cos_ref, cos_out)
    store("sin", sin_ref, sin_out)
    store("qrow", qrow_ref, qrow_out)
    store("kcol", kcol_ref, kcol_out)

    cot_copy = remote(cot, dy_out, t_send.at[2], t_recv.at[2], away)
    cot_local = pltpu.make_async_copy(cot, dy_out, l_sem.at[chunks + 2])

    def load(source, target, n):
        copy = pltpu.make_async_copy(source, target, w_sem.at[n])
        copy.start()
        return copy

    qblock = 256
    count = 2 * rows // qblock
    own_z = [(z - 2 * c - k + MP) % MP for k in range(2)]
    other_z = [(at + 2) % MP for at in own_z]
    for l in range(n_layers):
        xs, qs, ks, vs, ms, mis, ls, r1s, r2s, es, gps = saved[l]
        last = l - 1
        go(x_copy, l, 0)
        go(x_copy, l, 1)
        run(take(9 * l + 3))
        x_copy(l, 0).wait_recv()
        go(x_copy, l, 2)
        run(take(9 * l + 4))
        step_ready(3 * l)
        wa_loads = [
            load(w_all.at[3 * l, own_z[k], :, pl.ds(0, 5 * LANES)], wa.at[k], k) for k in range(2)
        ]
        wo_load = load(w_all.at[3 * l, :, :, pl.ds(4 * LANES, 2 * LANES)], wo, 2)
        if l == 0:

            @pl.when(moved)
            def _():
                cot_copy.start()

            @pl.when(jnp.logical_not(moved))
            def _():
                cot_local.start()

            for s in range(MP - 1):
                small_copy(s).wait_recv()
            small_local.wait()
        else:
            m_copy(last).wait_send()
        stored(("q", last), ("k", last), ("v", last), ("mixed", last), ("lse", last))
        lse_cols[...] = jnp.zeros_like(lse_cols)
        for copy in wa_loads:
            copy.wait()
        for i in range(4):
            if i == 1:
                x_copy(l, 1).wait_recv()
            if i == 3:
                run(take(9 * l + 6 - l))
                x_copy(l, 2).wait_recv()
            at = pl.ds(i * rows, rows)
            for k in range(2):
                bias = small_all[own_z[k], pl.ds(l, 1), pl.ds(0, 5 * LANES)]
                project_rows(
                    i, k, xfull[l, i], wa, bias, cos_ref[at, :], sin_ref[at, :], q_ref, k_ref, v_ref
                )
        store(("q", l), q_ref, qs)
        store(("k", l), k_ref, ks)
        store(("v", l), v_ref, vs)
        store(("x", l), xfull.at[l], xs)
        steps = [take(9 * l + 7), take(9 * l + 8 - l), take(9 * l + 9 - l)]

        def one_block(n, _, l=l, steps=steps):
            attend_rows(
                count - 1 - n, qblock, qcode_ref, kcode_ref, q_ref, k_ref, v_ref, mixed_ref, lse_cols
            )
            for j in range(count):

                @pl.when(n == j)
                def _(j=j):
                    if j == 1:
                        m_copy(l).start()
                    run(steps[j])

            return 0

        lax.fori_loop(0, count, one_block, 0)
        lse_ref[...] = jnp.transpose(lse_cols[...])[0:8, :]
        store(("mixed", l), mixed_ref, ms)
        store(("lse", l), lse_ref, ls)
        step_ready(3 * l + 1)
        win_load = load(w_all.at[3 * l + 1], win, 3)
        stored(("r1", last), ("r2", last), ("e", last), ("gp", last))
        wo_load.wait()
        m_copy(l).wait_recv()
        store(("mixed_in", l), mixed_in.at[l], mis)
        a = jnp.zeros((rows, width), F32)
        for k in range(2):
            a = a + nt(mixed_ref[0:rows, k * 256 : k * 256 + 256], wo[own_z[k]])
            a = a + nt(mixed_in[l, :, k * 256 : k * 256 + 256], wo[other_z[k]])
        vec = vectors[l]
        r1 = stream[...] + a + vec[0:1, :]
        r1_ref[...] = r1
        store(("r1", l), r1_ref, r1s)
        n1, _ = norm_parts(r1)
        h = n1 * vec[1:2, :] + vec[2:3, :]
        low_ref[...] = h.astype(BF16)
        sum_ref[...] = h + vec[3:4, :]
        win_load.wait()

        def inner(zz, _, l=l):
            u = nn(low_ref[...], win[zz]) + small_all[zz, pl.ds(l, 1), pl.ds(5 * LANES, width)]
            cdf = 0.5 * (1.0 + lax.erf(u * (2.0**-0.5)))
            pdf = jnp.exp(u * u * -0.5) * 0.3989422804014327
            e_ref[zz] = (u * cdf).astype(BF16)
            gp_ref[zz] = (cdf + u * pdf).astype(BF16)
            return 0

        lax.fori_loop(0, 2, inner, 0)
        run(take(9 * l + 10 - l))
        lax.fori_loop(2, MP, inner, 0)
        run(take(10 if l == 0 else 18))
        step_ready(3 * l + 2)
        wback_load = load(w_all.at[3 * l + 2], wback, 4)
        store(("e", l), e_ref, es)
        store(("gp", l), gp_ref, gps)
        wback_load.wait()

        def outer(zz, _):
            sum_ref[...] += nt(e_ref[zz], wback[zz])
            return 0

        lax.fori_loop(0, MP, outer, 0)
        store(("r2", l), sum_ref, r2s)
        n2, _ = norm_parts(sum_ref[...])
        result = n2 * vec[4:5, :] + vec[5:6, :]
        if l + 1 < n_layers:
            stream[...] = result
            xfull[l + 1, 0] = result.astype(BF16)
        else:
            low_ref[...] = result.astype(BF16)
            store("low", low_ref, low_out)

    m_copy(n_layers - 1).wait_send()
    for make, at in sent:
        make(*at).wait_send()
    @pl.when(moved)
    def _():
        token_copy.wait_send()
        cot_copy.wait_send()
        cot_copy.wait_recv()

    @pl.when(jnp.logical_not(moved))
    def _():
        cot_local.wait()

    stored(*stores)


def forward(blocks, tokens, cot, small, meta, frequency, vectors):
    n_layers = vectors.shape[0]
    chunks, height, width = blocks.shape
    rows = tokens.shape[0]
    queries, keys = 2 * rows, 4 * rows
    layer_out = (
        shape((4, rows, width), BF16),
        shape((2, 2, queries, LANES), BF16),
        shape((2, 2, keys, LANES), BF16),
        shape((2, 2, keys, LANES), BF16),
        shape((queries, 512), BF16),
        shape((rows, 512), BF16),
        shape((8, queries), F32),
        shape((rows, width), F32),
        shape((rows, width), F32),
        shape((MP, rows, width), BF16),
        shape((MP, rows, width), BF16),
    )
    outs = (
        shape((chunks, MP, 8 * height, width), BF16),
        shape((rows, width), BF16),
        shape((rows, width), BF16),
        shape((keys, LANES), F32),
        shape((keys, LANES), F32),
        shape((1, queries), F32),
        shape((keys, 1), F32),
    ) + layer_out * n_layers
    sem = pltpu.SemaphoreType.DMA
    results = pl.pallas_call(
        partial(forward_kernel, n_layers),
        out_shape=outs,
        in_specs=[anywhere()] * 3 + [vmem()] * 4,
        out_specs=(anywhere(),) * len(outs),
        scratch_shapes=[
            pltpu.VMEM((n_layers, 4, rows, width), BF16),
            pltpu.VMEM((n_layers, rows, 512), BF16),
            pltpu.VMEM((MP,) + small.shape, F32),
            pltpu.VMEM(meta.shape, F32),
            pltpu.VMEM((2, width, 5 * LANES), BF16),
            pltpu.VMEM((MP, width, 2 * LANES), BF16),
            pltpu.VMEM((MP, width, width), BF16),
            pltpu.VMEM((MP, width, width), BF16),
            pltpu.VMEM((keys, LANES), F32),
            pltpu.VMEM((keys, LANES), F32),
            pltpu.VMEM((queries, 1), F32),
            pltpu.VMEM((1, keys), F32),
            pltpu.VMEM((1, queries), F32),
            pltpu.VMEM((keys, 1), F32),
            pltpu.VMEM((2, 2, queries, LANES), BF16),
            pltpu.VMEM((2, 2, keys, LANES), BF16),
            pltpu.VMEM((2, 2, keys, LANES), BF16),
            pltpu.VMEM((queries, 512), BF16),
            pltpu.VMEM((queries, LANES), F32),
            pltpu.VMEM((8, queries), F32),
            pltpu.VMEM((rows, width), F32),
            pltpu.VMEM((rows, width), F32),
            pltpu.VMEM((rows, width), F32),
            pltpu.VMEM((rows, width), BF16),
            pltpu.VMEM((MP, rows, width), BF16),
            pltpu.VMEM((MP, rows, width), BF16),
            sem((chunks, 3)),
            sem((chunks, 3)),
            sem((chunks, 3)),
            sem((chunks, 3)),
            sem((chunks, 4)),
            sem((chunks, 4)),
            sem((n_layers, 4)),
            sem((n_layers, 4)),
            sem((6,)),
            sem((6,)),
            sem((chunks + 3,)),
            sem((5,)),
            sem((5 + 11 * n_layers,)),
        ],
        compiler_params=pltpu.CompilerParams(
            vmem_limit_bytes=VMEM_LIMIT, collective_id=0, has_side_effects=True
        ),
        cost_estimate=pl.CostEstimate(
            flops=100_000_000_000, bytes_accessed=100_000_000, transcendentals=20_000_000
        ),
        name="forward",
    )(blocks, tokens, cot, small, meta, frequency, vectors)
    head = results[:7]
    states = [results[7 + 11 * l : 18 + 11 * l] for l in range(n_layers)]
    return head, states


def attend_kernel(chunk, *refs):
    scal, x_ref, bias_ref, cos_ref, sin_ref, qcode_ref, kcode_ref, w_all = refs[:8]
    q_ref, k_ref, v_ref, mixed_ref, lse_ref, w_ref, lse_cols, sems = refs[8:]
    copies = [
        pltpu.make_async_copy(
            w_all.at[chunk, scal[k], :, pl.ds(0, 5 * LANES)], w_ref.at[k], sems.at[k]
        )
        for k in range(2)
    ]
    for copy in copies:
        copy.start()
    for copy in copies:
        copy.wait()
    rows = x_ref.shape[1]
    for i in range(4):
        at = pl.ds(i * rows, rows)
        for k in range(2):
            project_rows(
                i,
                k,
                x_ref[i],
                w_ref,
                bias_ref[k],
                cos_ref[at, :],
                sin_ref[at, :],
                q_ref,
                k_ref,
                v_ref,
            )
    lse_cols[...] = jnp.zeros_like(lse_cols)

    def one_block(i, _):
        attend_rows(i, 256, qcode_ref, kcode_ref, q_ref, k_ref, v_ref, mixed_ref, lse_cols)
        return 0

    lax.fori_loop(0, 2 * rows // 256, one_block, 0)
    lse_ref[...] = jnp.transpose(lse_cols[...])[0:8, :]


def attend(scal, x_full, bias, tables, qcode, kcode, w_all, chunk):
    cos, sin = tables[:2]
    _, rows, width = x_full.shape
    queries, keys = 2 * rows, 4 * rows
    return pl.pallas_call(
        partial(attend_kernel, chunk),
        out_shape=(
            shape((2, 2, queries, LANES), BF16),
            shape((2, 2, keys, LANES), BF16),
            shape((2, 2, keys, LANES), BF16),
            shape((queries, 512), BF16),
            shape((8, queries), F32),
        ),
        in_specs=[smem()] + [vmem()] * 6 + [anywhere()],
        out_specs=(vmem(),) * 5,
        scratch_shapes=[
            pltpu.VMEM((2, width, 5 * LANES), BF16),
            pltpu.VMEM((queries, LANES), F32),
            pltpu.SemaphoreType.DMA((2,)),
        ],
        compiler_params=params(),
        name="attend",
    )(scal, x_full, bias, cos, sin, qcode, kcode, w_all)


def feed_kernel(chunk, *refs):
    scal, x_ref, own_ref, sib_ref, vec_ref, bin_ref, w_all = refs[:7]
    next_ref, low_ref, r1_ref, r2_ref, e_ref, gp_ref, wo_ref, win_ref, wback_ref, sems = refs[7:]
    copies = [
        pltpu.make_async_copy(
            w_all.at[chunk, :, :, pl.ds(4 * LANES, 2 * LANES)], wo_ref, sems.at[0]
        ),
        pltpu.make_async_copy(w_all.at[chunk + 1], win_ref, sems.at[1]),
        pltpu.make_async_copy(w_all.at[chunk + 2], wback_ref, sems.at[2]),
    ]
    for copy in copies:
        copy.start()
    for copy in copies:
        copy.wait()
    a = jnp.zeros(x_ref.shape, F32)
    for k in range(2):
        a = a + nt(own_ref[:, k * 256 : k * 256 + 256], wo_ref[scal[k]])
        a = a + nt(sib_ref[:, k * 256 : k * 256 + 256], wo_ref[lax.rem(scal[k] + 2, MP)])
    r1 = x_ref[...] + a + vec_ref[0:1, :]
    r1_ref[...] = r1
    n1, _ = norm_parts(r1)
    h = n1 * vec_ref[1:2, :] + vec_ref[2:3, :]
    low_ref[...] = h.astype(BF16)
    r2_ref[...] = h + vec_ref[3:4, :]

    def one(z, _):
        u = nn(low_ref[...], win_ref[z]) + bin_ref[z]
        cdf = 0.5 * (1.0 + lax.erf(u * (2.0**-0.5)))
        pdf = jnp.exp(u * u * -0.5) * 0.3989422804014327
        e = (u * cdf).astype(BF16)
        e_ref[z] = e
        gp_ref[z] = (cdf + u * pdf).astype(BF16)
        r2_ref[...] += nt(e, wback_ref[z])
        return 0

    lax.fori_loop(0, MP, one, 0)
    n2, _ = norm_parts(r2_ref[...])
    result = n2 * vec_ref[4:5, :] + vec_ref[5:6, :]
    next_ref[...] = result
    low_ref[...] = result.astype(BF16)


def feed_forward(scal, x, own, sib, vec, bias_in, w_all, chunk):
    rows, width = x.shape
    return pl.pallas_call(
        partial(feed_kernel, chunk),
        out_shape=(
            shape((rows, width), F32),
            shape((rows, width), BF16),
            shape((rows, width), F32),
            shape((rows, width), F32),
            shape((MP, rows, width), BF16),
            shape((MP, rows, width), BF16),
        ),
        in_specs=[smem()] + [vmem()] * 5 + [anywhere()],
        out_specs=(vmem(),) * 6,
        scratch_shapes=[
            pltpu.VMEM((MP, width, 2 * LANES), BF16),
            pltpu.VMEM((MP, width, width), BF16),
            pltpu.VMEM((MP, width, width), BF16),
            pltpu.SemaphoreType.DMA((3,)),
        ],
        compiler_params=params(),
        name="feed",
    )(scal, x, own, sib, vec, bias_in, w_all)


def plain_forward(blocks, tokens, cot, small, meta, frequency, vectors):
    n_layers = vectors.shape[0]
    rows, width = tokens.shape
    c, z = lax.axis_index("dp") % 2, lax.axis_index("mp")
    w_all = lax.all_gather(blocks, "dp", axis=1, tiled=True)
    w_all = jnp.swapaxes(lax.all_gather(w_all, "mp", axis=0, tiled=False), 0, 1)
    small_all = lax.all_gather(small, "mp", axis=0, tiled=False)
    own_z = jnp.stack([(z - 2 * c - k) % MP for k in range(2)]).astype(jnp.int32)
    info = jnp.where(z // 2 == c, meta, core_swap(meta))
    place = z % 2
    quarters = [2 * c + place, 2 * (1 - c) + place, 2 * c + 1 - place, 2 * (1 - c) + 1 - place]
    positions = jnp.concatenate(
        [q * rows + jnp.arange(rows, dtype=jnp.int32) for q in quarters]
    ).astype(F32)
    slot = info[0, 0]
    seq = jnp.where(positions >= slot, 1.0, 0.0) + jnp.where(positions >= 2.0 * slot, 1.0, 0.0)
    place = positions - seq * slot
    limit = jnp.where(seq == 0.0, info[1, 0], jnp.where(seq == 1.0, info[2, 0], info[3, 0]))
    kcode = jnp.where(place < limit, seq, -1.0)
    qcode = seq[: 2 * rows]
    angles = place[:, None] * frequency
    sign = jnp.where(jnp.arange(LANES) % HD < HD // 2, -1.0, 1.0)
    cos, sin = jnp.cos(angles), jnp.sin(angles) * sign[None, :]
    low = relayout(tokens)
    stream = low.astype(F32)
    states = []
    for l in range(n_layers):
        two = jnp.stack([low, pair_swap(low)])
        others = core_swap(two)
        x_full = jnp.stack([two[0], others[0], two[1], others[1]])
        bias = jnp.stack(
            [
                lax.dynamic_index_in_dim(small_all, own_z[k], 0, False)[l : l + 1, : 5 * LANES]
                for k in range(2)
            ]
        )
        q, k, v, mixed, lse = attend(
            own_z, x_full, bias, (cos, sin), qcode[:, None], kcode[None, :], w_all, 3 * l
        )
        other = core_swap(mixed[rows:])
        stream, low, r1, r2, e, gp = feed_forward(
            own_z,
            stream,
            mixed[:rows],
            other,
            vectors[l],
            small_all[:, l : l + 1, 5 * LANES :],
            w_all,
            3 * l,
        )
        states.append((x_full, q, k, v, mixed, other, lse, r1, r2, e, gp))
    return (w_all, relayout(cot), low, cos, sin, qcode[None, :], kcode[:, None]), states


def feed_back_kernel(n_pieces, rows, chunk, *refs):
    scal, dy_ref, r1_ref, r2_ref, e_ref, gp_ref, own_ref, sib_ref, vec_ref, w_all = refs[:10]
    at = 10
    dr1_ref, dzown_ref, dzsib_ref, dvec_ref, dbin_ref = refs[at : at + 5]
    outs = 2 if n_pieces == 8 else 1
    grads = refs[at + 5 : at + 5 + outs]
    wo_ref, win_ref, wback_ref, df_ref, dft_ref, ht_ref, dw_ref, sems = refs[at + 5 + outs :]
    width = dy_ref.shape[1]
    columns = [scal[n_pieces + k] for k in range(MP)]
    first_z = scal[n_pieces + MP]

    def fetch(source, target, base):
        copies = [
            pltpu.make_async_copy(source(columns[k]), target.at[k], sems.at[base + k])
            for k in range(MP)
        ]
        for copy in copies:
            copy.start()
        return copies

    back_copies = fetch(lambda z: w_all.at[chunk + 2, z], wback_ref, 0)
    in_copies = fetch(lambda z: w_all.at[chunk + 1, z], win_ref, MP)
    out_copies = fetch(
        lambda z: w_all.at[chunk, z, :, pl.ds(4 * LANES, 2 * LANES)], wo_ref, 2 * MP
    )
    dy = dy_ref[...]
    n2, scale2 = norm_parts(r2_ref[...])
    dvec_ref[4:5, :] = jnp.sum(dy * n2, axis=0, keepdims=True)
    dvec_ref[5:6, :] = jnp.sum(dy, axis=0, keepdims=True)
    dr2 = norm_back(dy, n2, scale2, vec_ref[4:5, :])
    dvec_ref[3:4, :] = jnp.sum(dr2, axis=0, keepdims=True)
    dr1_ref[...] = dr2
    df = dr2.astype(BF16)
    df_ref[...] = df
    dft_ref[...] = jnp.transpose(df)
    n1, _ = norm_parts(r1_ref[...])
    h = (n1 * vec_ref[1:2, :] + vec_ref[2:3, :]).astype(BF16)
    ht_ref[...] = jnp.transpose(h)
    for copy in back_copies + in_copies:
        copy.wait()

    def one(z, _):
        de = nn(df_ref[...], wback_ref[z])
        at = scal[n_pieces + z]
        du = de * gp_ref[at].astype(F32)
        dbin_ref[z] = jnp.sum(du, axis=0, keepdims=True)
        dub = du.astype(BF16)
        dr1_ref[...] += nt(dub, win_ref[z])
        dw_ref[z, :, 0:width] = nn(ht_ref[...], dub).astype(BF16)
        dw_ref[z, :, width : 2 * width] = nn(dft_ref[...], e_ref[at]).astype(BF16)
        return 0

    lax.fori_loop(0, MP, one, 0)
    dh = dr1_ref[...]
    n1, scale1 = norm_parts(r1_ref[...])
    dvec_ref[1:2, :] = jnp.sum(dh * n1, axis=0, keepdims=True)
    dvec_ref[2:3, :] = jnp.sum(dh, axis=0, keepdims=True)
    dr1 = norm_back(dh, n1, scale1, vec_ref[1:2, :])
    dvec_ref[0:1, :] = jnp.sum(dr1, axis=0, keepdims=True)
    dr1_ref[...] = dr1
    da = dr1.astype(BF16)
    dft_ref[...] = jnp.transpose(da)
    for copy in out_copies:
        copy.wait()
    used = lane_index((da.shape[0], 2 * LANES)) >= HD
    for z in range(2):
        for mixed_ref, dz_ref, z_at in (
            (own_ref, dzown_ref, first_z + z),
            (sib_ref, dzsib_ref, 2 - first_z + z),
        ):
            part = mixed_ref[:, z * 256 : z * 256 + 256]
            dw_ref[z_at, :, 2 * width :] = nn(dft_ref[...], part).astype(BF16)
            dz = nn(da, wo_ref[z_at])
            dz_ref[:, z * 256 : z * 256 + 256] = jnp.where(used, dz, 0.0).astype(BF16)
    flight = []
    for i in range(n_pieces):
        offset = pl.multiple_of(scal[i], 32)
        target = grads[i // 4].at[PIECE_ORDER[i % 4] if n_pieces == 8 else 0]
        copy = pltpu.make_async_copy(dw_ref.at[:, pl.ds(offset, rows), :], target, sems.at[i])
        copy.start()
        flight.append(copy)
    for copy in flight:
        copy.wait()


PIECE_ORDER = (3, 0, 2, 1)


def feed_back(scal, prows, count, dy, r1, r2, e, gp, own, sib, vec, w_all, chunk):
    rows, width = dy.shape
    lanes = 2 * width + 2 * LANES
    grads = (shape((4, MP, prows, lanes), BF16),) * 2
    if count != 8:
        grads = (shape((1, MP, prows, lanes), BF16),)
    return pl.pallas_call(
        partial(feed_back_kernel, count, prows, chunk),
        out_shape=(
            shape((rows, width), F32),
            shape((rows, 512), BF16),
            shape((rows, 512), BF16),
            shape((6, width), F32),
            shape((MP, 1, width), F32),
            *grads,
        ),
        in_specs=[smem()] + [vmem()] * 8 + [anywhere()],
        out_specs=(vmem(),) * 5 + (anywhere(),) * len(grads),
        scratch_shapes=[
            pltpu.VMEM((MP, width, 2 * LANES), BF16),
            pltpu.VMEM((MP, width, width), BF16),
            pltpu.VMEM((MP, width, width), BF16),
            pltpu.VMEM((rows, width), BF16),
            pltpu.VMEM((width, rows), BF16),
            pltpu.VMEM((width, rows), BF16),
            pltpu.VMEM((MP, width, lanes), BF16),
            pltpu.SemaphoreType.DMA((3 * MP,)),
        ],
        compiler_params=params(),
        cost_estimate=pl.CostEstimate(
            flops=16_000_000_000, bytes_accessed=40_000_000, transcendentals=0
        ),
        name="feed_back",
    )(scal, dy, r1, r2, e, gp, own, sib, vec, w_all)


def attend_back_kernel(n_pieces, chunk, *refs):
    (
        scal,
        x_ref,
        cos_ref,
        sin_ref,
        qcode_ref,
        kcode_ref,
        q_ref,
        k_ref,
        v_ref,
        mixed_ref,
        dzown_ref,
        dzsib_ref,
        lse_ref,
        w_all,
    ) = refs[:14]
    dx_ref, dxs_ref, dbias_ref, parts_ref = refs[14:18]
    (
        w_ref,
        xt_ref,
        dz_ref,
        delta_ref,
        dt_ref,
        dqt_ref,
        pair_ref,
        dw_ref,
        low_ref,
        sums_ref,
        sems,
    ) = refs[18:]
    copies = [
        pltpu.make_async_copy(
            w_all.at[chunk, scal[n_pieces + 9 + k], :, pl.ds(0, 5 * LANES)],
            w_ref.at[k],
            sems.at[k],
        )
        for k in range(2)
    ]
    for copy in copies:
        copy.start()
    keys, width = x_ref.shape
    queries = keys // 2
    block = queries // 2
    for z in range(2):
        for half, source in enumerate((dzown_ref, dzsib_ref)):
            at = pl.ds(half * block, block)
            dz_ref[z, 0, at, :] = source[:, z * 256 + LANES : z * 256 + 256]
            dz_ref[z, 1, at, :] = pltpu.roll(
                source[:, z * 256 : z * 256 + LANES].astype(F32), HD, 1
            ).astype(BF16)
        single = pltpu.roll(mixed_ref[:, z * 256 : z * 256 + LANES].astype(F32), HD, 1)
        pair = mixed_ref[:, z * 256 + LANES : z * 256 + 256].astype(F32)
        prod_one = jnp.transpose(pair * dz_ref[z, 0].astype(F32))
        prod_two = jnp.transpose(single * dz_ref[z, 1].astype(F32))
        delta_ref[3 * z : 3 * z + 1, :] = jnp.sum(prod_one[0:HD], axis=0, keepdims=True)
        delta_ref[3 * z + 1 : 3 * z + 2, :] = jnp.sum(prod_one[HD:], axis=0, keepdims=True)
        delta_ref[3 * z + 2 : 3 * z + 3, :] = jnp.sum(prod_two[0:HD], axis=0, keepdims=True)

    kblock = 256
    low_q = lane_index((queries, LANES)) < HD
    low_k = lane_index((kblock, LANES)) < HD
    for z in range(2):
        for h in range(3):
            tile = h // 2
            q = q_ref[z, tile]
            dz = dz_ref[z, tile]
            if h < 2:
                keep = low_q == (h == 0)
                q = jnp.where(keep, q, BF16(0))
                dz = jnp.where(keep, dz, BF16(0))
            pair_ref[0] = q
            pair_ref[1] = dz
            lse = lse_ref[3 * z + h : 3 * z + h + 1, :]
            delta = delta_ref[3 * z + h : 3 * z + h + 1, :]
            if h != 1:
                dqt_ref[...] = jnp.zeros_like(dqt_ref)

            def one_block(i, _, z=z, h=h, tile=tile, lse=lse, delta=delta):
                at = pl.ds(pl.multiple_of(i * kblock, kblock), kblock)
                kb = k_ref[z, tile, at, :]
                vb = v_ref[z, tile, at, :]
                if h < 2:
                    kb_own = jnp.where(low_k == (h == 0), kb, BF16(0))
                else:
                    kb_own = kb
                visible = kcode_ref[at, :] == qcode_ref[...]
                s = nt(kb, pair_ref[0])
                s = jnp.where(visible, s, NEGATIVE)
                p = jnp.exp(s - lse)
                dp = nt(vb, pair_ref[1])
                ds = (p * (dp - delta)).astype(BF16)
                dv = nn(p.astype(BF16), pair_ref[1])
                dk = nn(ds, pair_ref[0])
                dqt_ref[...] += nn(jnp.transpose(kb_own), ds)
                if h == 1:
                    dt_ref[2, at, :] += dk
                    dt_ref[3, at, :] += dv
                elif h == 0:
                    dt_ref[2, at, :] = dk
                    dt_ref[3, at, :] = dv
                else:
                    dt_ref[1, at, :] = pltpu.roll(dk, HD, 1)
                    dt_ref[4, at, :] = dv
                return 0

            lax.fori_loop(0, keys // kblock, one_block, 0)
            if h >= 1:
                dq = jnp.transpose(dqt_ref[...]) * HD**-0.5
                if h == 1:
                    dt_ref[0, 0:queries, :] = dq
                else:
                    dt_ref[1, 0:queries, :] += dq

        if z == 0:
            xt_ref[...] = jnp.transpose(x_ref[...])
            for copy in copies:
                copy.wait()
        for tile in range(5):
            count = queries if tile == 0 else keys
            t = dt_ref[tile, 0:count, :]
            if tile < 3:
                t = t * cos_ref[0:count, :] - half_swap(t) * sin_ref[0:count, :]
            dbias_ref[z, :, tile * LANES : (tile + 1) * LANES] = jnp.sum(t, axis=0, keepdims=True)
            low_ref[0:count, tile * LANES : (tile + 1) * LANES] = t.astype(BF16)
        dw_ref[z, :, 0:LANES] = nn(
            xt_ref[:, 0:queries], low_ref[0:queries, 0:LANES]
        ).astype(BF16)
        dw_ref[z, :, LANES:] = nn(xt_ref[...], low_ref[:, LANES:]).astype(BF16)
        for i in range(4):
            at = pl.ds(i * block, block)
            part = nt(low_ref[at, LANES:], w_ref[z, :, LANES : 5 * LANES])
            if i < 2:
                part = part + nt(low_ref[at, 0:LANES], w_ref[z, :, 0:LANES])
            if z == 0:
                sums_ref[i] = part
            else:
                target = dx_ref if i % 2 == 0 else dxs_ref
                target[i // 2] = (sums_ref[i] + part).astype(BF16)

    flight = []
    for i in range(min(n_pieces, 4)):
        offset = pl.multiple_of(scal[n_pieces + 5 + i], 32)
        copy = pltpu.make_async_copy(
            dw_ref.at[:, pl.ds(offset, parts_ref.shape[2]), :],
            parts_ref.at[PIECE_ORDER[i] if n_pieces == 8 else 0],
            sems.at[i],
        )
        copy.start()
        flight.append(copy)
    for copy in flight:
        copy.wait()


def attend_back(scal, prows, count, x_full, tables, saved, mixed, dz_own, dz_sib, w_all, chunk):
    cos, sin, qcode, kcode = tables
    q, k, v, lse = saved
    keys, width = x_full.shape
    queries = keys // 2
    block = queries // 2
    parts = (4, 2, 2 * prows, 5 * LANES)
    if count != 8:
        parts = (1, 2, prows, 5 * LANES)
    return pl.pallas_call(
        partial(attend_back_kernel, count, chunk),
        out_shape=(
            shape((2, block, width), BF16),
            shape((2, block, width), BF16),
            shape((2, 1, 5 * LANES), F32),
            shape(parts, BF16),
        ),
        in_specs=[smem()] + [vmem()] * 12 + [anywhere()],
        out_specs=(vmem(),) * 3 + (anywhere(),),
        scratch_shapes=[
            pltpu.VMEM((2, width, 5 * LANES), BF16),
            pltpu.VMEM((width, keys), BF16),
            pltpu.VMEM((2, 2, queries, LANES), BF16),
            pltpu.VMEM((8, queries), F32),
            pltpu.VMEM((5, keys, LANES), F32),
            pltpu.VMEM((LANES, queries), F32),
            pltpu.VMEM((2, queries, LANES), BF16),
            pltpu.VMEM((2, width, 5 * LANES), BF16),
            pltpu.VMEM((keys, 5 * LANES), BF16),
            pltpu.VMEM((4, block, width), F32),
            pltpu.SemaphoreType.DMA((4,)),
        ],
        compiler_params=params(),
        cost_estimate=pl.CostEstimate(
            flops=40_000_000_000, bytes_accessed=20_000_000, transcendentals=8_000_000
        ),
        name="attend_back",
    )(scal, x_full, cos, sin, qcode, kcode, q, k, v, mixed, dz_own, dz_sib, lse, w_all)


def head_tiles(q, k, v, o):
    return jnp.concatenate(
        [
            q[..., :LANES],
            q[..., LANES:],
            k[..., LANES:],
            k[..., :LANES],
            v[..., :LANES],
            v[..., LANES:],
            o[..., LANES:],
            o[..., :LANES],
        ],
        axis=-1,
    )


def head_columns(t):
    q = jnp.concatenate([t[..., 0:128], t[..., 128:192]], axis=-1)
    k = jnp.concatenate([t[..., 256:384], t[..., 192:256]], axis=-1)
    v = jnp.concatenate([t[..., 384:512], t[..., 512:576]], axis=-1)
    return q, k, v


def per_device(
    tokens, w_qkv, b_qkv, w_out, vectors, w_in, b_in, w_back, cotangent, lengths, buckets
):
    layers = w_qkv.shape[0]
    rows, width = tokens.shape
    d = lax.axis_index("dp")
    z = lax.axis_index("mp")
    g, c = d // 2, d % 2

    blocks = []
    for l in range(layers):
        low = w_qkv[l].astype(BF16)
        blocks.append(head_tiles(low[0], low[1], low[2], w_out[l].astype(BF16).T))
        blocks.append(w_in[l].astype(BF16))
        blocks.append(w_back[l].astype(BF16).T)
    blocks = jnp.stack(blocks)
    height = w_qkv.shape[2]
    pieces = 8 if lax.axis_size("dp") == 8 else 1
    piece_rows = height if pieces == 8 else width

    small = jnp.concatenate(
        [
            b_qkv[:, 0],
            b_qkv[:, 1, LANES:],
            b_qkv[:, 1, :LANES],
            b_qkv[:, 2],
            jnp.zeros((layers, HD), F32),
            b_in,
        ],
        axis=-1,
    )
    small = jnp.pad(small, ((0, 8 - layers), (0, 0)))
    slot = LEN_MAX // (3 - buckets)
    meta = jnp.concatenate([slot, lengths[0]]).astype(F32)
    meta = jnp.broadcast_to(jnp.pad(meta, (0, 4))[:, None], (8, LANES))
    exponents = jnp.arange(LANES, dtype=jnp.int32) % (HD // 2)
    frequency = 10000.0 ** (-2.0 * exponents.astype(F32) / HD)[None, :]

    run = forward if pieces == 8 else plain_forward
    head, states = run(blocks, tokens, cotangent, small, meta, frequency, vectors)
    w_all, gradient, low, cos, sin, qcode, kcode = head
    result = relayout(low)
    gradient = gradient.astype(F32)

    first = jnp.where(c == 0, 1, 2)
    spans = [(g ^ hop) * 2 * height for hop in (0, first, 3 - first, 3)]
    if pieces == 1:
        spans = [jnp.int32(0)] * 4
    column_of = [(z - k) % MP for k in range(MP)]
    own_z = [(z - 2 * c - k) % MP for k in range(2)]
    scal = jnp.stack(row_offsets(g, c, height) + column_of + [2 * c] + spans + own_z)
    scal = scal.astype(jnp.int32)

    masters = []
    vector_grads = []
    in_biases = []
    head_biases = []
    for layer_at in reversed(range(layers)):
        x_full, q, k, v, mixed, mixed_in, lse, r1, r2, e, gp = states[layer_at]
        back = feed_back(
            scal,
            piece_rows,
            pieces,
            gradient,
            r1,
            r2,
            e,
            gp,
            mixed[:rows],
            mixed_in,
            vectors[layer_at],
            w_all,
            3 * layer_at,
        )
        dr1, dz_own, dz_sib, dvec, dbin = back[:5]
        dz_others = core_swap(dz_sib)
        feed_grad = reduce_all(back[5], back[-1])
        dx, dx_sib, dbias, parts = attend_back(
            scal,
            piece_rows,
            pieces,
            x_full.reshape(4 * rows, width),
            (cos, sin, qcode, kcode),
            (q, k, v, lse),
            mixed,
            dz_own,
            dz_others,
            w_all,
            3 * layer_at,
        )
        got = dx.astype(F32) + core_swap(dx_sib).astype(F32)
        gradient = dr1 + got[0] + pair_swap(got[1].astype(BF16)).astype(F32)
        head_grad = reduce_heads(parts)
        masters.insert(0, (feed_grad, head_grad))
        vector_grads.insert(0, dvec)
        in_biases.insert(0, dbin[:, 0])
        head_biases.insert(0, sum_head_biases(dbias[:, 0]))
    grad_tokens = relayout(gradient.astype(BF16)).astype(F32)

    layers_of = jnp.stack(in_biases, axis=1)
    grad_vectors, grad_b_in = sum_vectors(jnp.concatenate(vector_grads), layers_of)
    grad_vectors = grad_vectors.reshape(vectors.shape)
    grad_b_qkv = jnp.stack([jnp.stack(head_columns(b)) for b in head_biases])

    grad_qkv = jnp.stack([jnp.stack(head_columns(m[1])) for m in masters])
    grad_in = jnp.stack([m[0][:, :width] for m in masters])
    grad_back = jnp.stack([m[0][:, width : 2 * width].T for m in masters])
    grad_out = jnp.stack(
        [
            jnp.concatenate(
                [m[0][:, 2 * width + LANES :], m[0][:, 2 * width + HD : 2 * width + LANES]], axis=-1
            ).T
            for m in masters
        ]
    )
    return (
        result,
        grad_tokens,
        grad_qkv,
        grad_b_qkv,
        grad_out,
        grad_vectors,
        grad_in,
        grad_b_in,
        grad_back,
    )


def solution(mesh):
    return jax.shard_map(
        per_device,
        mesh=mesh,
        in_specs=(
            P(("dp", "mp"), None),
            P(None, None, "dp", "mp"),
            P(None, None, "mp"),
            P(None, "mp", "dp"),
            P(),
            P(None, "dp", "mp"),
            P(None, "mp"),
            P(None, "mp", "dp"),
            P(("dp", "mp"), None),
            P("dp", None),
            P("dp"),
        ),
        out_specs=(
            P(("dp", "mp"), None),
            P(("dp", "mp"), None),
            P(None, None, "dp", "mp"),
            P(None, None, "mp"),
            P(None, "mp", "dp"),
            P(),
            P(None, "dp", "mp"),
            P(None, "mp"),
            P(None, "mp", "dp"),
        ),
        check_vma=False,
    )
```

```python
from functools import partial

import jax
import jax.numpy as jnp
from jax import lax
from jax.experimental import pallas as pl
from jax.experimental.pallas import tpu as pltpu
from jax.sharding import PartitionSpec as P

HD = 64
LEN_MAX = 1536
EPSILON = 1e-06
NEGATIVE = -1e30
F32 = jnp.float32
BF16 = jnp.bfloat16
LANES = 128
MP = 4
VMEM_LIMIT = 60 * 1024 * 1024
BACK_LIMIT = 63 * 1024 * 1024


def nn(a, b):
    return lax.dot_general(a, b, (((1,), (0,)), ((), ())), preferred_element_type=F32)


def nt(a, b):
    return lax.dot_general(a, b, (((1,), (1,)), ((), ())), preferred_element_type=F32)


def core_swap(x):
    n = lax.axis_size("dp")
    return lax.ppermute(x, "dp", [(i, i ^ 1) for i in range(n)])


def plane_swap(x, first):
    n = lax.axis_size("dp")
    hops = (2, 4) if first else (4, 2)
    return lax.ppermute(x, "dp", [(i, i ^ hops[i % 2]) for i in range(n)])


def column_shift(x, k):
    return lax.ppermute(x, "mp", [(i, (i + k) % MP) for i in range(MP)])


def pair_swap(x):
    return lax.ppermute(x, "mp", [(i, i ^ 1) for i in range(MP)])


def relayout(x):
    n = lax.axis_size("dp")
    pairs = []
    for d in range(n):
        for z in range(MP):
            if (d % 2) != (z // 2):
                pairs.append((d * MP + z, (d ^ 1) * MP + (z ^ 2)))
            else:
                pairs.append((d * MP + z, d * MP + z))
    return lax.ppermute(x, ("dp", "mp"), pairs)


def turn_columns(x, z):
    return jnp.stack([lax.dynamic_index_in_dim(x, (z - k) % MP, 0, False) for k in range(MP)])


def row_offsets(g, c, rows):
    if lax.axis_size("dp") != 8:
        return [jnp.int32(0)]
    result = []
    for core in (c, 1 - c):
        first = jnp.where(core == 0, 1, 2)
        for hop in (0, first, 3 - first, 3):
            result.append(((g ^ hop) * 2 + core) * rows)
    return result


def send_columns(v):
    total = v[0].astype(F32)
    for k in range(1, MP):
        total = total + column_shift(v[k], -k).astype(F32)
    return total


def reduce_all(keep, away):
    if lax.axis_size("dp") != 8:
        z = lax.axis_index("mp")
        whole = turn_columns(keep[0], z).astype(F32)
        part = lax.psum_scatter(whole, "mp", scatter_dimension=0, tiled=False)
        return lax.psum_scatter(part, "dp", scatter_dimension=0, tiled=True)
    other = core_swap(away)

    def add(i):
        return keep[i].astype(F32) + other[i].astype(F32)

    got = plane_swap(jnp.stack([add(0), add(1)]).astype(BF16), True)
    got_two = plane_swap((add(2) + got[1].astype(F32)).astype(BF16), False)
    v = (add(3) + got[0].astype(F32) + got_two.astype(F32)).astype(BF16)
    return send_columns(v)


def reduce_heads(parts):
    c = lax.axis_index("dp") % 2
    n = lax.axis_size("dp")
    if n != 8:
        z = lax.axis_index("mp")
        wide = jnp.concatenate([parts[0], jnp.zeros_like(parts[0])], axis=0)
        wide = jnp.where(c == 0, wide, jnp.roll(wide, 2, axis=0))
        whole = turn_columns(wide, z).astype(F32)
        part = lax.psum_scatter(whole, "mp", scatter_dimension=0, tiled=False)
        return lax.psum_scatter(part, "dp", scatter_dimension=0, tiled=True)
    got = plane_swap(parts[0:2], True)
    got_two = plane_swap((parts[2].astype(F32) + got[1].astype(F32)).astype(BF16), False)
    v = (parts[3].astype(F32) + got[0].astype(F32) + got_two.astype(F32)).astype(BF16)

    total = column_turn(v[0], 0).astype(F32) + column_turn(v[1], 1).astype(F32)
    rows = total.shape[0] // 2
    kept = lax.dynamic_slice_in_dim(total, c * rows, rows, 0)
    sent = lax.dynamic_slice_in_dim(total, (1 - c) * rows, rows, 0).astype(BF16)
    return kept + core_swap(sent).astype(F32)


def sum_head_biases(v):
    c = lax.axis_index("dp") % 2
    n = lax.axis_size("dp")
    if n != 8:
        z = lax.axis_index("mp")
        zero = jnp.zeros_like(v)
        wide = jnp.where(c == 0, jnp.concatenate([v, zero]), jnp.concatenate([zero, v]))
        total = lax.psum(turn_columns(wide, z), ("dp", "mp"))
        return lax.dynamic_index_in_dim(total, z, 0, False)
    v = v + plane_swap(v, True)
    v = v + plane_swap(v, False)
    total = column_turn(v[0], 0) + column_turn(v[1], 1)
    return total + core_swap(total)


def column_turn(x, k):
    n = lax.axis_size("dp")
    pairs = []
    for d in range(n):
        for z in range(MP):
            pairs.append((d * MP + z, d * MP + (z - k - 2 * (d % 2)) % MP))
    return lax.ppermute(x, ("dp", "mp"), pairs)


def sum_vectors(vectors, columns):
    if lax.axis_size("dp") != 8:
        z = lax.axis_index("mp")
        vectors, columns = lax.psum((vectors, turn_columns(columns, z)), ("dp", "mp"))
        return vectors, lax.dynamic_index_in_dim(columns, z, 0, False)
    n = vectors.shape[0]
    m = columns.shape[1]
    both = jnp.concatenate([vectors, columns.reshape(MP * m, -1)])
    both = both + core_swap(both)
    both = both + plane_swap(both, True)
    both = both + plane_swap(both, False)
    total = both[: n + m]
    for k in range(1, MP):
        at = n + m * (MP - k)
        total = total + column_shift(jnp.concatenate([both[:n], both[at : at + m]]), k)
    return total[:n], total[n:]


def lane_index(shape):
    return lax.broadcasted_iota(jnp.int32, shape, len(shape) - 1)


def half_swap(x):
    lane = lane_index(x.shape)
    return jnp.where(
        lane % HD < HD // 2,
        pltpu.roll(x, LANES - HD // 2, x.ndim - 1),
        pltpu.roll(x, HD // 2, x.ndim - 1),
    )


def norm_parts(r):
    mean = jnp.mean(r, axis=-1, keepdims=True)
    centred = r - mean
    scale = lax.rsqrt(jnp.mean(centred * centred, axis=-1, keepdims=True) + EPSILON)
    return centred * scale, scale


def norm_back(dy, n, scale, gain):
    gdy = dy * gain
    mean_one = jnp.mean(gdy, axis=-1, keepdims=True)
    mean_two = jnp.mean(gdy * n, axis=-1, keepdims=True)
    return (gdy - mean_one - n * mean_two) * scale


def vmem():
    return pl.BlockSpec(memory_space=pltpu.VMEM)


def smem():
    return pl.BlockSpec(memory_space=pltpu.SMEM)


def anywhere():
    return pl.BlockSpec(memory_space=pl.ANY)


def params():
    return pltpu.CompilerParams(vmem_limit_bytes=VMEM_LIMIT)


def shape(dims, dtype):
    return jax.ShapeDtypeStruct(dims, dtype)


def project_rows(i, z, x, w_ref, bias, cos, sin, q_ref, k_ref, v_ref):
    block = x.shape[0]
    at = pl.ds(i * block, block)
    p = nn(x, w_ref[z, :, LANES : 5 * LANES]) + bias[:, LANES:]
    low_half = lane_index((block, LANES)) < HD
    mixed = p[:, 0:LANES]
    mixed = mixed * cos + half_swap(mixed) * sin
    pair = p[:, LANES : 2 * LANES]
    pair = pair * cos + half_swap(pair) * sin
    k_ref[z, 0, at, :] = pair.astype(BF16)
    k_ref[z, 1, at, :] = jnp.where(low_half, pltpu.roll(mixed, HD, 1), 0.0).astype(BF16)
    v_ref[z, 0, at, :] = p[:, 2 * LANES : 3 * LANES].astype(BF16)
    v_ref[z, 1, at, :] = jnp.where(low_half, p[:, 3 * LANES :], 0.0).astype(BF16)
    if i < 2:
        q = nn(x, w_ref[z, :, 0:LANES]) + bias[:, 0:LANES]
        q = q * cos + half_swap(q) * sin
        q_ref[z, 0, at, :] = q.astype(BF16) * BF16(HD**-0.5)
        q_ref[z, 1, at, :] = jnp.where(low_half, mixed, 0.0).astype(BF16) * BF16(HD**-0.5)


def attend_rows(i, qblock, qcode_ref, kcode_ref, q_ref, k_ref, v_ref, mixed_ref, lse_cols):
    at = pl.ds(pl.multiple_of(i * qblock, qblock), qblock)
    visible = qcode_ref[at, :] == kcode_ref[...]
    low_half = lane_index((qblock, LANES)) < HD
    lane = lane_index((qblock, LANES))
    for z in range(2):
        outs = []
        for h in range(3):
            tile = h // 2
            q = q_ref[z, tile, at, :]
            if h < 2:
                q = jnp.where(low_half == (h == 0), q, BF16(0))
            s = nt(q, k_ref[z, tile])
            s = jnp.where(visible, s, NEGATIVE)
            m = jnp.max(s, axis=-1, keepdims=True)
            p = jnp.exp(s - m)
            l = jnp.sum(p, axis=-1, keepdims=True)
            o = nn(p.astype(BF16), v_ref[z, tile])
            outs.append(o / l)
            lse_cols[at, :] = jnp.where(lane == 3 * z + h, m + jnp.log(l), lse_cols[at, :])
        mixed_ref[at, pl.ds(z * 256, LANES)] = pltpu.roll(outs[2], HD, 1).astype(BF16)
        mixed_ref[at, pl.ds(z * 256 + LANES, LANES)] = jnp.where(
            low_half, outs[0], outs[1]
        ).astype(BF16)


def forward_kernel(n_layers, *refs):
    n_in, per_layer = 7, 11
    blocks, tokens, cot, small, meta, frequency, vectors = refs[:n_in]
    w_all, dy_out, low_out, cos_out, sin_out, qrow_out, kcol_out = refs[n_in : n_in + 7]
    saved = [
        refs[n_in + 7 + l * per_layer : n_in + 7 + (l + 1) * per_layer] for l in range(n_layers)
    ]
    (
        xfull,
        mixed_in,
        small_all,
        meta_in,
        wa,
        wo,
        win,
        wback,
        cos_ref,
        sin_ref,
        qcode_ref,
        kcode_ref,
        qrow_ref,
        kcol_ref,
        q_ref,
        k_ref,
        v_ref,
        mixed_ref,
        lse_cols,
        lse_ref,
        stream,
        sum_ref,
        r1_ref,
        low_ref,
        e_ref,
        gp_ref,
        z_send,
        z_recv,
        p_send,
        p_recv,
        c_send,
        c_recv,
        x_send,
        x_recv,
        t_send,
        t_recv,
        l_sem,
        w_sem,
        s_sem,
    ) = refs[n_in + 7 + n_layers * per_layer :]
    rows = stream.shape[0]
    width = stream.shape[1]
    height = blocks.shape[1]
    chunks = blocks.shape[0]

    d = lax.axis_index("dp")
    z = lax.axis_index("mp")
    c = d % 2
    x = (d // 2) % 2
    y = d // 4
    flip_x, flip_y = 1 - 2 * x, 1 - 2 * y
    one_x, one_y = x + (1 - c) * flip_x, y + c * flip_y
    two_x, two_y = x + c * flip_x, y + (1 - c) * flip_y

    def device(yy, xx, cc, zz):
        return (yy * 4 + xx * 2 + cc, zz)

    def rows_of(yy, xx):
        return pl.ds(pl.multiple_of((yy * 4 + xx * 2 + c) * height, 32), height)

    sibling = device(y, x, 1 - c, z)
    first = device(one_y, one_x, c, z)
    second = device(two_y, two_x, c, z)
    pair_z = z + 1 - 2 * (z % 2)
    pair = device(y, x, c, pair_z)
    away = device(y, x, 1 - c, (z + 2) % MP)
    moved = c != z // 2
    columns = [device(y, x, c, (z + s) % MP) for s in range(1, MP)]
    own_rows = rows_of(y, x)
    first_rows = rows_of(one_y, one_x)
    second_rows = rows_of(two_y, two_x)
    third_rows = rows_of(1 - y, 1 - x)

    barrier = pltpu.get_barrier_semaphore()
    partners = columns + [first, second, sibling, away]
    for partner in partners:
        pl.semaphore_signal(
            barrier, inc=1, device_id=partner, device_id_type=pl.DeviceIdType.MESH
        )
    pl.semaphore_wait(barrier, len(partners))

    def remote(source, target, send, recv, to):
        return pltpu.make_async_remote_copy(
            src_ref=source,
            dst_ref=target,
            send_sem=send,
            recv_sem=recv,
            device_id=to,
            device_id_type=pl.DeviceIdType.MESH,
        )

    sent = []

    def go(make, *at):
        make(*at).start()
        sent.append((make, at))

    def local_copy(k):
        return pltpu.make_async_copy(blocks.at[k], w_all.at[k, z, own_rows], l_sem.at[k])

    def z_copy(k, s):
        return remote(
            blocks.at[k], w_all.at[k, z, own_rows], z_send.at[k, s], z_recv.at[k, s], columns[s]
        )

    def p_copy(k, n):
        source = w_all.at[k, :, first_rows if n == 2 else own_rows]
        return remote(
            source, source, p_send.at[k, n], p_recv.at[k, n], first if n == 0 else second
        )

    def c_copy(k, n):
        source = w_all.at[k, :, (own_rows, first_rows, second_rows, third_rows)[n]]
        return remote(source, source, c_send.at[k, n], c_recv.at[k, n], sibling)

    def step_send(k):
        local_copy(k).start()
        for s in range(MP - 1):
            go(z_copy, k, s)

    def step_plane(k):
        local_copy(k).wait()
        for s in range(MP - 1):
            z_copy(k, s).wait_recv()
        go(p_copy, k, 0)
        go(p_copy, k, 1)
        go(c_copy, k, 0)
        if k + 2 < chunks:
            step_send(k + 2)

    def step_forward(k):
        p_copy(k, 0).wait_recv()
        go(p_copy, k, 2)
        go(c_copy, k, 1)
        p_copy(k, 1).wait_recv()
        go(c_copy, k, 2)

    def step_last(k):
        p_copy(k, 2).wait_recv()
        go(c_copy, k, 3)

    def step_ready(k):
        for n in range(4):
            c_copy(k, n).wait_recv()

    plan = []
    for k in range(chunks):
        plan.append(partial(step_plane, k))
        plan.append(partial(step_forward, k))
        plan.append(partial(step_last, k))
    for k in range(chunks - 1):
        at = plan.index(plan[3 * k + 2])
        plan[at], plan[at + 1] = plan[at + 1], plan[at]
    position = [0]

    def take(until):
        steps = plan[position[0] : until]
        position[0] = max(position[0], until)
        return steps

    def run(steps):
        for step in steps:
            step()

    def meta_copy():
        return remote(meta, meta_in, t_send.at[0], t_recv.at[0], sibling)

    def small_copy(s):
        return remote(small, small_all.at[z], t_send.at[3 + s], t_recv.at[3 + s], columns[s])

    go(meta_copy)
    token_copy = remote(tokens, xfull.at[0, 0], t_send.at[1], t_recv.at[1], away)
    token_local = pltpu.make_async_copy(tokens, xfull.at[0, 0], l_sem.at[chunks])

    @pl.when(moved)
    def _():
        token_copy.start()

    @pl.when(jnp.logical_not(moved))
    def _():
        token_local.start()

    step_send(0)
    for s in range(MP - 1):
        go(small_copy, s)
    step_send(1)
    small_local = pltpu.make_async_copy(small, small_all.at[z], l_sem.at[chunks + 1])
    small_local.start()

    meta_copy().wait_recv()
    info = jnp.where(moved, meta_in[...], meta[...])
    slot = info[0:1, :]
    limits = [info[n : n + 1, :] for n in range(1, 4)]
    half = z % 2
    quarters = [2 * c + half, 2 * (1 - c) + half, 2 * c + 1 - half, 2 * (1 - c) + 1 - half]

    def codes(place_all, slot, limits):
        seq = jnp.where(place_all >= slot, 1.0, 0.0) + jnp.where(place_all >= 2.0 * slot, 1.0, 0.0)
        place = place_all - seq * slot
        limit = jnp.where(seq == 0.0, limits[0], jnp.where(seq == 1.0, limits[1], limits[2]))
        return seq, place, jnp.where(place < limit, seq, -1.0)

    sign = jnp.where(lane_index((1, LANES)) % HD < HD // 2, -1.0, 1.0)
    for i in range(4):
        at = pl.ds(i * rows, rows)
        base = quarters[i] * rows
        index = lax.broadcasted_iota(jnp.int32, (rows, LANES), 0) + base
        seq, place, kcode = codes(index.astype(F32), slot, limits)
        angle = place * frequency[...]
        cos_ref[at, :] = jnp.cos(angle)
        sin_ref[at, :] = jnp.sin(angle) * sign
        kcol_ref[at, :] = kcode[:, 0:1]
        if i < 2:
            qcode_ref[at, :] = seq[:, 0:1]
        index = lax.broadcasted_iota(jnp.int32, (1, rows), 1) + base
        seq, place, kcode = codes(
            index.astype(F32), slot[:, 0:1], [limit[:, 0:1] for limit in limits]
        )
        kcode_ref[:, pl.ds(i * rows, rows)] = kcode
        if i < 2:
            qrow_ref[:, pl.ds(i * rows, rows)] = seq

    @pl.when(moved)
    def _():
        token_copy.wait_recv()

    @pl.when(jnp.logical_not(moved))
    def _():
        token_local.wait()

    def x_copy(l, n):
        source = xfull.at[l, 2 if n == 2 else 0]
        target = xfull.at[l, (2, 1, 3)[n]]
        return remote(
            source, target, x_send.at[l, n], x_recv.at[l, n], pair if n == 0 else sibling
        )

    def m_copy(l):
        return remote(
            mixed_ref.at[pl.ds(rows, rows)],
            mixed_in.at[l],
            x_send.at[l, 3],
            x_recv.at[l, 3],
            sibling,
        )

    def h_copy(l):
        return remote(low_ref, saved[l][10].at[1], x_send.at[l, 4], x_recv.at[l, 4], sibling)

    def e_copy(l):
        return remote(
            e_ref,
            saved[l][8].at[:, pl.ds(rows, rows), :],
            x_send.at[l, 5],
            x_recv.at[l, 5],
            sibling,
        )

    stores = {}

    def store(name, source, target):
        copy = pltpu.make_async_copy(source, target, s_sem.at[len(stores)])
        copy.start()
        stores[name] = copy

    waited = set()

    def stored(*names):
        for name in names:
            if name in stores and name not in waited:
                waited.add(name)
                stores[name].wait()

    stream[...] = xfull[0, 0].astype(F32)
    store("cos", cos_ref, cos_out)
    store("sin", sin_ref, sin_out)
    store("qrow", qrow_ref, qrow_out)
    store("kcol", kcol_ref, kcol_out)

    cot_copy = remote(cot, dy_out, t_send.at[2], t_recv.at[2], away)
    cot_local = pltpu.make_async_copy(cot, dy_out, l_sem.at[chunks + 2])

    def load(source, target, n):
        copy = pltpu.make_async_copy(source, target, w_sem.at[n])
        copy.start()
        return copy

    qblock = 256
    count = 2 * rows // qblock
    own_z = [(z - 2 * c - k + MP) % MP for k in range(2)]
    other_z = [(at + 2) % MP for at in own_z]
    for l in range(n_layers):
        xs, qs, ks, vs, ms, ls, r1s, r2s, es, gps, hs = saved[l]
        last = l - 1
        go(x_copy, l, 0)
        go(x_copy, l, 1)
        run(take(9 * l + 3))
        x_copy(l, 0).wait_recv()
        go(x_copy, l, 2)
        run(take(9 * l + 4))
        step_ready(3 * l)
        wa_loads = [
            load(w_all.at[3 * l, own_z[k], :, pl.ds(0, 5 * LANES)], wa.at[k], k) for k in range(2)
        ]
        wo_load = load(w_all.at[3 * l, :, :, pl.ds(4 * LANES, 2 * LANES)], wo, 2)
        if l == 0:

            @pl.when(moved)
            def _():
                cot_copy.start()

            @pl.when(jnp.logical_not(moved))
            def _():
                cot_local.start()

            for s in range(MP - 1):
                small_copy(s).wait_recv()
            small_local.wait()
        else:
            m_copy(last).wait_send()
        stored(("q", last), ("k", last), ("v", last), ("mixed", last), ("lse", last))
        lse_cols[...] = jnp.zeros_like(lse_cols)
        for copy in wa_loads:
            copy.wait()
        for i in range(4):
            if i == 1:
                x_copy(l, 1).wait_recv()
            if i == 3:
                run(take(9 * l + 6 - l))
                x_copy(l, 2).wait_recv()
            at = pl.ds(i * rows, rows)
            for k in range(2):
                bias = small_all[own_z[k], pl.ds(l, 1), pl.ds(0, 5 * LANES)]
                project_rows(
                    i, k, xfull[l, i], wa, bias, cos_ref[at, :], sin_ref[at, :], q_ref, k_ref, v_ref
                )
        store(("q", l), q_ref, qs)
        store(("k", l), k_ref, ks)
        store(("v", l), v_ref, vs)
        store(("x", l), xfull.at[l], xs)
        steps = [take(9 * l + 7), take(9 * l + 8 - l), take(9 * l + 9 - l)]

        def one_block(n, _, l=l, steps=steps):
            attend_rows(
                count - 1 - n, qblock, qcode_ref, kcode_ref, q_ref, k_ref, v_ref, mixed_ref, lse_cols
            )
            for j in range(count):

                @pl.when(n == j)
                def _(j=j):
                    if j == 1:
                        m_copy(l).start()
                    run(steps[j])

            return 0

        lax.fori_loop(0, count, one_block, 0)
        lse_ref[...] = jnp.transpose(lse_cols[...])[0:8, :]
        store(("mixed", l), mixed_ref, ms)
        store(("lse", l), lse_ref, ls)
        step_ready(3 * l + 1)
        win_load = load(w_all.at[3 * l + 1], win, 3)
        stored(("r1", last), ("r2", last), ("e", last), ("gp", last), ("h", last))
        if l > 0:
            h_copy(last).wait_send()
            e_copy(last).wait_send()
        wo_load.wait()
        m_copy(l).wait_recv()
        a = jnp.zeros((rows, width), F32)
        for k in range(2):
            a = a + nt(mixed_ref[0:rows, k * 256 : k * 256 + 256], wo[own_z[k]])
            a = a + nt(mixed_in[l, :, k * 256 : k * 256 + 256], wo[other_z[k]])
        vec = vectors[l]
        r1 = stream[...] + a + vec[0:1, :]
        r1_ref[...] = r1
        store(("r1", l), r1_ref, r1s)
        n1, _ = norm_parts(r1)
        h = n1 * vec[1:2, :] + vec[2:3, :]
        low_ref[...] = h.astype(BF16)
        store(("h", l), low_ref, hs.at[0])
        h_copy(l).start()
        sum_ref[...] = h + vec[3:4, :]
        win_load.wait()

        def inner(zz, _, l=l):
            u = nn(low_ref[...], win[zz]) + small_all[zz, pl.ds(l, 1), pl.ds(5 * LANES, width)]
            cdf = 0.5 * (1.0 + lax.erf(u * (2.0**-0.5)))
            pdf = jnp.exp(u * u * -0.5) * 0.3989422804014327
            e_ref[zz] = (u * cdf).astype(BF16)
            gp_ref[zz] = (cdf + u * pdf).astype(BF16)
            return 0

        lax.fori_loop(0, 2, inner, 0)
        run(take(9 * l + 10 - l))
        lax.fori_loop(2, MP, inner, 0)
        run(take(10 if l == 0 else 18))
        step_ready(3 * l + 2)
        wback_load = load(w_all.at[3 * l + 2], wback, 4)
        store(("e", l), e_ref, es.at[:, pl.ds(0, rows), :])
        e_copy(l).start()
        store(("gp", l), gp_ref, gps)
        wback_load.wait()

        def outer(zz, _):
            sum_ref[...] += nt(e_ref[zz], wback[zz])
            return 0

        lax.fori_loop(0, MP, outer, 0)
        store(("r2", l), sum_ref, r2s)
        n2, _ = norm_parts(sum_ref[...])
        result = n2 * vec[4:5, :] + vec[5:6, :]
        if l + 1 < n_layers:
            stream[...] = result
            xfull[l + 1, 0] = result.astype(BF16)
        else:
            h_copy(l).wait_send()
            stored(("h", l))
            low_ref[...] = result.astype(BF16)
            store("low", low_ref, low_out)

    m_copy(n_layers - 1).wait_send()
    e_copy(n_layers - 1).wait_send()
    for l in range(n_layers):
        h_copy(l).wait_recv()
        e_copy(l).wait_recv()
    for make, at in sent:
        make(*at).wait_send()
    @pl.when(moved)
    def _():
        token_copy.wait_send()
        cot_copy.wait_send()
        cot_copy.wait_recv()

    @pl.when(jnp.logical_not(moved))
    def _():
        cot_local.wait()

    stored(*stores)


def forward(blocks, tokens, cot, small, meta, frequency, vectors):
    n_layers = vectors.shape[0]
    chunks, height, width = blocks.shape
    rows = tokens.shape[0]
    queries, keys = 2 * rows, 4 * rows
    layer_out = (
        shape((4, rows, width), BF16),
        shape((2, 2, queries, LANES), BF16),
        shape((2, 2, keys, LANES), BF16),
        shape((2, 2, keys, LANES), BF16),
        shape((queries, 512), BF16),
        shape((8, queries), F32),
        shape((rows, width), F32),
        shape((rows, width), F32),
        shape((MP, 2 * rows, width), BF16),
        shape((MP, rows, width), BF16),
        shape((2, rows, width), BF16),
    )
    outs = (
        shape((chunks, MP, 8 * height, width), BF16),
        shape((rows, width), BF16),
        shape((rows, width), BF16),
        shape((keys, LANES), F32),
        shape((keys, LANES), F32),
        shape((1, queries), F32),
        shape((keys, 1), F32),
    ) + layer_out * n_layers
    sem = pltpu.SemaphoreType.DMA
    results = pl.pallas_call(
        partial(forward_kernel, n_layers),
        out_shape=outs,
        in_specs=[anywhere()] * 3 + [vmem()] * 4,
        out_specs=(anywhere(),) * len(outs),
        scratch_shapes=[
            pltpu.VMEM((n_layers, 4, rows, width), BF16),
            pltpu.VMEM((n_layers, rows, 512), BF16),
            pltpu.VMEM((MP,) + small.shape, F32),
            pltpu.VMEM(meta.shape, F32),
            pltpu.VMEM((2, width, 5 * LANES), BF16),
            pltpu.VMEM((MP, width, 2 * LANES), BF16),
            pltpu.VMEM((MP, width, width), BF16),
            pltpu.VMEM((MP, width, width), BF16),
            pltpu.VMEM((keys, LANES), F32),
            pltpu.VMEM((keys, LANES), F32),
            pltpu.VMEM((queries, 1), F32),
            pltpu.VMEM((1, keys), F32),
            pltpu.VMEM((1, queries), F32),
            pltpu.VMEM((keys, 1), F32),
            pltpu.VMEM((2, 2, queries, LANES), BF16),
            pltpu.VMEM((2, 2, keys, LANES), BF16),
            pltpu.VMEM((2, 2, keys, LANES), BF16),
            pltpu.VMEM((queries, 512), BF16),
            pltpu.VMEM((queries, LANES), F32),
            pltpu.VMEM((8, queries), F32),
            pltpu.VMEM((rows, width), F32),
            pltpu.VMEM((rows, width), F32),
            pltpu.VMEM((rows, width), F32),
            pltpu.VMEM((rows, width), BF16),
            pltpu.VMEM((MP, rows, width), BF16),
            pltpu.VMEM((MP, rows, width), BF16),
            sem((chunks, 3)),
            sem((chunks, 3)),
            sem((chunks, 3)),
            sem((chunks, 3)),
            sem((chunks, 4)),
            sem((chunks, 4)),
            sem((n_layers, 6)),
            sem((n_layers, 6)),
            sem((6,)),
            sem((6,)),
            sem((chunks + 3,)),
            sem((5,)),
            sem((5 + 11 * n_layers,)),
        ],
        compiler_params=pltpu.CompilerParams(
            vmem_limit_bytes=VMEM_LIMIT, collective_id=0, has_side_effects=True
        ),
        cost_estimate=pl.CostEstimate(
            flops=100_000_000_000, bytes_accessed=100_000_000, transcendentals=20_000_000
        ),
        name="forward",
    )(blocks, tokens, cot, small, meta, frequency, vectors)
    head = results[:7]
    states = [results[7 + 11 * l : 18 + 11 * l] for l in range(n_layers)]
    return head, states


def place_of(d, z):
    c = d % 2
    x = (d // 2) % 2
    y = d // 4
    flip_x, flip_y = 1 - 2 * x, 1 - 2 * y
    planes = (
        (y, x),
        (y + c * flip_y, x + (1 - c) * flip_x),
        (y + (1 - c) * flip_y, x + c * flip_x),
        (1 - y, 1 - x),
    )
    groups = [2 * yy + xx for yy, xx in planes]

    def device(group, cc, zz):
        return (group * 2 + cc, zz)

    return c, groups, device


def head_back(
    i,
    h,
    kblock,
    q_ref,
    k_ref,
    v_ref,
    dz_ref,
    lse_ref,
    delta_ref,
    qrow_ref,
    kcol_ref,
    pair_ref,
    dqt_ref,
    dt_ref,
):
    tile = h // 2
    keys, queries = k_ref.shape[2], q_ref.shape[2]
    low_q = lane_index((queries, LANES)) < HD
    low_k = lane_index((kblock, LANES)) < HD
    q = q_ref[i, tile]
    dz = dz_ref[i, tile]
    if h < 2:
        keep = low_q == (h == 0)
        q = jnp.where(keep, q, BF16(0))
        dz = jnp.where(keep, dz, BF16(0))
    pair_ref[0] = q
    pair_ref[1] = dz
    lse = lse_ref[3 * i + h : 3 * i + h + 1, :]
    delta = delta_ref[3 * i + h : 3 * i + h + 1, :]
    if h != 1:
        dqt_ref[...] = jnp.zeros_like(dqt_ref)

    def one_block(n, _):
        at = pl.ds(pl.multiple_of(n * kblock, kblock), kblock)
        kb = k_ref[i, tile, at, :]
        vb = v_ref[i, tile, at, :]
        kb_own = jnp.where(low_k == (h == 0), kb, BF16(0)) if h < 2 else kb
        visible = kcol_ref[at, :] == qrow_ref[...]
        s = nt(kb, pair_ref[0])
        s = jnp.where(visible, s, NEGATIVE)
        p = jnp.exp(s - lse)
        dp = nt(vb, pair_ref[1])
        ds = (p * (dp - delta)).astype(BF16)
        dv = nn(p.astype(BF16), pair_ref[1])
        dk = nn(ds, pair_ref[0])
        dqt_ref[...] += nn(jnp.transpose(kb_own), ds)
        if h == 1:
            dt_ref[2, at, :] += dk
            dt_ref[3, at, :] += dv
        elif h == 0:
            dt_ref[2, at, :] = dk
            dt_ref[3, at, :] = dv
        else:
            dt_ref[1, at, :] = pltpu.roll(dk, HD, 1)
            dt_ref[4, at, :] = dv
        return 0

    lax.fori_loop(0, keys // kblock, one_block, 0)
    if h >= 1:
        dq = jnp.transpose(dqt_ref[...]) * HD**-0.5
        if h == 1:
            dt_ref[0, 0:queries, :] = dq
        else:
            dt_ref[1, 0:queries, :] += dq


def head_deltas(i, mixed_ref, dz_ref, delta_ref):
    single = pltpu.roll(mixed_ref[:, i * 256 : i * 256 + LANES].astype(F32), HD, 1)
    pair = mixed_ref[:, i * 256 + LANES : i * 256 + 256].astype(F32)
    prod_one = jnp.transpose(pair * dz_ref[i, 0].astype(F32))
    prod_two = jnp.transpose(single * dz_ref[i, 1].astype(F32))
    delta_ref[3 * i : 3 * i + 1, :] = jnp.sum(prod_one[0:HD], axis=0, keepdims=True)
    delta_ref[3 * i + 1 : 3 * i + 2, :] = jnp.sum(prod_one[HD:], axis=0, keepdims=True)
    delta_ref[3 * i + 2 : 3 * i + 3, :] = jnp.sum(prod_two[0:HD], axis=0, keepdims=True)


def norm_back_rows(acc_ref, r_ref, low_ref, gain):
    rows, width = acc_ref.shape
    step = 32

    def body(i, sums):
        at = pl.ds(pl.multiple_of(i * step, step), step)
        dy = acc_ref[at, :]
        n, scale = norm_parts(r_ref[at, :])
        dr = norm_back(dy, n, scale, gain)
        acc_ref[at, :] = dr
        low_ref[at, :] = dr.astype(BF16)
        return (
            sums[0] + jnp.sum(dy * n, axis=0, keepdims=True),
            sums[1] + jnp.sum(dy, axis=0, keepdims=True),
            sums[2] + jnp.sum(dr, axis=0, keepdims=True),
        )

    zero = jnp.zeros((1, width), F32)
    return lax.fori_loop(0, rows // step, body, (zero, zero, zero))


def backward_kernel(n_layers, *refs):
    n_in, per_layer = 7, 11
    w_all, dy_in, cos_in, sin_in, qrow_ref, kcol_ref, vectors = refs[:n_in]
    saved = [refs[n_in + l * per_layer : n_in + (l + 1) * per_layer] for l in range(n_layers)]
    at = n_in + n_layers * per_layer
    tokens_out, feed_out, attn_out, small_out = refs[at : at + 4]
    (
        pool,
        gp_ref,
        r1_ref,
        r2_ref,
        acc_ref,
        df_ref,
        dfin_ref,
        da_ref,
        dain_ref,
        h_ref,
        turn_ref,
        ht_ref,
        dft_ref,
        du_ref,
        t_ref,
        one_in,
        two_in,
        z_in,
        dwo_ref,
        ta_ref,
        a_one_in,
        a_two_in,
        a_z_in,
        a_c_in,
        a_sum_ref,
        a_out_ref,
        wa,
        q_ref,
        k_ref,
        v_ref,
        mixed_ref,
        lse_ref,
        delta_ref,
        dz_ref,
        dt_ref,
        dqt_ref,
        pair_ref,
        cos_ref,
        sin_ref,
        dxc_in,
        dxp_in,
        back_in,
        v_stage,
        v_in,
        dbin_ref,
        c_send,
        c_recv,
        one_send,
        one_recv,
        two_send,
        two_recv,
        z_send,
        z_recv,
        a_send,
        a_recv,
        v_send,
        v_recv,
        t_send,
        t_recv,
        w_sem,
        s_sem,
        o_sem,
    ) = refs[at + 4 :]
    part_ref, dxs_ref, dxp_ref = r2_ref, h_ref, df_ref
    rows, width = acc_ref.shape
    height = t_ref.shape[2]
    queries = 2 * rows

    d = lax.axis_index("dp")
    z = lax.axis_index("mp")
    c, groups, device = place_of(d, z)
    sibling = device(groups[0], 1 - c, z)
    first = device(groups[1], c, z)
    second = device(groups[2], c, z)
    away = device(groups[0], 1 - c, (z + 2) % MP)
    pair = device(groups[0], c, z + 1 - 2 * (z % 2))
    columns = [device(groups[0], c, (z + s) % MP) for s in range(1, MP)]
    moved = c != z // 2

    barrier = pltpu.get_barrier_semaphore()
    partners = columns + [first, second, sibling, away]
    for partner in partners:
        pl.semaphore_signal(
            barrier, inc=1, device_id=partner, device_id_type=pl.DeviceIdType.MESH
        )

    def remote(source, target, send, recv, to):
        return pltpu.make_async_remote_copy(
            src_ref=source,
            dst_ref=target,
            send_sem=send,
            recv_sem=recv,
            device_id=to,
            device_id_type=pl.DeviceIdType.MESH,
        )

    def column(k):
        return (z - k + MP) % MP

    own_z = [(z - 2 * c - i + MP) % MP for i in range(2)]

    def load(source, target, sem):
        return pltpu.make_async_copy(source, target, sem)

    def early_loads(l):
        _, _, _, _, _, _, r1s, r2s, _, _, hs = saved[l]
        return [
            load(r2s, r2_ref, s_sem.at[0]),
            load(r1s, r1_ref, s_sem.at[1]),
            load(hs, h_ref, s_sem.at[2]),
        ]

    def weight_loads(l, k):
        slot = k % 2
        gps = saved[l][9]
        return [
            load(w_all.at[3 * l + 2, column(k)], pool.at[2 + slot], w_sem.at[slot, 0]),
            load(w_all.at[3 * l + 1, column(k)], pool.at[slot], w_sem.at[slot, 1]),
            load(gps.at[column(k)], gp_ref.at[slot], w_sem.at[slot, 2]),
        ]

    def e_load(l, k):
        slot = k % 2
        es = saved[l][8]
        return load(es.at[column(k)], pool.at[4 + slot], w_sem.at[slot, 3])

    def late_loads(l):
        _, qs, ks, vs, ms, ls = saved[l][:6]
        return [
            load(qs, q_ref, s_sem.at[3]),
            load(ks, k_ref, s_sem.at[4]),
            load(vs, v_ref, s_sem.at[5]),
            load(ms, mixed_ref, s_sem.at[6]),
            load(ls, lse_ref, s_sem.at[7]),
            load(w_all.at[3 * l, own_z[0]], wa.at[0], s_sem.at[8]),
            load(w_all.at[3 * l, own_z[1]], wa.at[1], s_sem.at[9]),
        ]

    def x_loads(l):
        xs = saved[l][0]
        return [
            load(xs.at[n], pool.at[2 + n // 2, pl.ds(n % 2 * rows, rows)], s_sem.at[14 + n])
            for n in range(4)
        ]

    dy_load = load(dy_in, df_ref, s_sem.at[11])
    table_loads = [load(cos_in, cos_ref, s_sem.at[12]), load(sin_in, sin_ref, s_sem.at[13])]
    dy_load.start()
    for copy in early_loads(n_layers - 1) + weight_loads(n_layers - 1, 0):
        copy.start()
    for copy in table_loads + late_loads(n_layers - 1):
        copy.start()

    def df_copy(l):
        return remote(df_ref, dfin_ref, c_send.at[l, 0], c_recv.at[l, 0], sibling)

    def da_copy(l):
        return remote(da_ref, dain_ref, c_send.at[l, 1], c_recv.at[l, 1], sibling)

    def du_copy(l, k):
        return remote(
            du_ref.at[k, pl.ds(0, rows)],
            du_ref.at[k, pl.ds(rows, rows)],
            c_send.at[l, 2 + k],
            c_recv.at[l, 2 + k],
            sibling,
        )

    def dxs_copy(l):
        return remote(dxs_ref, dxc_in, c_send.at[l, 6], c_recv.at[l, 6], sibling)

    def dxp_copy(l):
        return remote(dxp_ref, dxp_in.at[l], a_send.at[l, 5], a_recv.at[l, 5], pair)

    def one_copy(l, k, n):
        return remote(
            t_ref.at[k, groups[1 if n == 0 else 3]],
            one_in.at[k, n],
            one_send.at[l, k, n],
            one_recv.at[l, k, n],
            first,
        )

    def two_copy(l, k):
        return remote(
            t_ref.at[k, groups[2]], two_in.at[k], two_send.at[l, k], two_recv.at[l, k], second
        )

    def z_copy(l, k):
        return remote(
            t_ref.at[k, groups[0]],
            z_in.at[l, k - 1],
            z_send.at[l, k],
            z_recv.at[l, k],
            device(groups[0], c, column(k)),
        )

    def span(group):
        return pl.ds(pl.multiple_of(group * 2 * height, 32), 2 * height)

    def a_one_copy(l, n):
        return remote(
            ta_ref.at[:, span(groups[1 if n == 0 else 3]), :],
            a_one_in.at[n],
            a_send.at[l, n],
            a_recv.at[l, n],
            first,
        )

    def a_two_copy(l):
        return remote(
            ta_ref.at[:, span(groups[2]), :],
            a_two_in,
            a_send.at[l, 2],
            a_recv.at[l, 2],
            second,
        )

    def a_z_copy(l, i):
        return remote(
            ta_ref.at[i, span(groups[0]), :],
            a_z_in.at[i],
            a_send.at[l, 3 + i],
            a_recv.at[l, 3 + i],
            device(groups[0], c, own_z[i]),
        )

    def a_c_copy(l):
        return remote(
            a_out_ref, a_c_in.at[l], c_send.at[l, 7], c_recv.at[l, 7], sibling
        )

    def v_copy(l, n):
        to = (sibling, first, second, columns[0], columns[1], columns[2])[n]
        return remote(
            v_stage.at[l, min(n, 3)], v_in.at[l, n], v_send.at[l, n], v_recv.at[l, n], to
        )

    def step_one(l, k):
        for n in range(2):
            one_copy(l, k, n).wait_recv()
        g = groups[2]
        t_ref[k, g] = (t_ref[k, g].astype(F32) + one_in[k, 1].astype(F32)).astype(BF16)
        two_copy(l, k).start()

    def step_two(l, k):
        two_copy(l, k).wait_recv()
        g = groups[0]
        t_ref[k, g] = (
            t_ref[k, g].astype(F32) + one_in[k, 0].astype(F32) + two_in[k].astype(F32)
        ).astype(BF16)
        if k > 0:
            z_copy(l, k).start()

    def step_feed_end(l):
        total = t_ref[0, groups[0]].astype(F32)
        for k in range(1, MP):
            z_copy(l, k).wait_recv()
            total = total + z_in[l, k - 1].astype(F32)
        feed_out[l] = total

    def step_a_one(l):
        for n in range(2):
            a_one_copy(l, n).wait_recv()
        for i in range(2):
            at = span(groups[2])
            ta_ref[i, at, :] = (
                ta_ref[i, at, :].astype(F32) + a_one_in[1, i].astype(F32)
            ).astype(BF16)
        a_two_copy(l).start()

    def step_a_two(l):
        a_two_copy(l).wait_recv()
        for i in range(2):
            at = span(groups[0])
            ta_ref[i, at, :] = (
                ta_ref[i, at, :].astype(F32)
                + a_one_in[0, i].astype(F32)
                + a_two_in[i].astype(F32)
            ).astype(BF16)

        @pl.when(c == 1)
        def _():
            a_z_copy(l, 0).start()

        a_z_copy(l, 1).start()

    def step_a_z(l):
        a_z_copy(l, 1).wait_recv()

        @pl.when(c == 0)
        def _():
            a_sum_ref[...] = ta_ref[0, span(groups[0]), :].astype(F32) + a_z_in[1].astype(F32)

        @pl.when(c == 1)
        def _():
            a_z_copy(l, 0).wait_recv()
            a_sum_ref[...] = a_z_in[0].astype(F32) + a_z_in[1].astype(F32)

        other = pl.ds(pl.multiple_of((1 - c) * height, 32), height)
        a_out_ref[...] = a_sum_ref[other, :].astype(BF16)
        a_c_copy(l).start()

    def step_a_end(l):
        a_c_copy(l).wait_recv()
        own = pl.ds(pl.multiple_of(c * height, 32), height)
        attn_out[l] = a_sum_ref[own, :] + a_c_in[l].astype(F32)

    def step_v(l, n):
        v_copy(l, n - 1).wait_recv()
        v_stage[l, n] = v_stage[l, n - 1] + v_in[l, n - 1]
        if n < 3:
            v_copy(l, n).start()
        else:
            for s in range(3, 6):
                v_copy(l, s).start()

    def step_v_end(l):
        total = v_stage[l, 3, 0:6, :]
        one = v_stage[l, 3, 6:7, :]
        two = v_stage[l, 3, 10:11, :]
        for s in range(1, MP):
            v_copy(l, 2 + s).wait_recv()
            got = v_in[l, 2 + s]
            total = total + got[0:6, :]
            one = one + got[6 + MP - s : 7 + MP - s, :]
            two = two + got[10 + MP - s : 11 + MP - s, :]
        small_out[l, 0:6, :] = total
        small_out[l, 6:7, :] = one
        small_out[l, 7:8, :] = two

    kblock = 256
    for l in reversed(range(n_layers)):
        top = l == n_layers - 1
        vec = vectors[l]
        copies = early_loads(l)
        if top:
            dy_load.wait()
            acc_ref[...] = df_ref[...].astype(F32)
        else:
            dxp_copy(l + 1).wait_send()
            step_a_one(l + 1)
        for copy in copies:
            copy.wait()
        v_stage[l, 0] = jnp.zeros((16, width), F32)
        sums = norm_back_rows(acc_ref, r2_ref, df_ref, vec[4:5, :])
        v_stage[l, 0, 4:5, :], v_stage[l, 0, 5:6, :], v_stage[l, 0, 3:4, :] = sums
        if top:
            pl.semaphore_wait(barrier, len(partners))
        df_copy(l).start()
        if not top:
            for k in range(MP):
                du_copy(l + 1, k).wait_send()

        def inner(k, _, l=l):
            for copy in weight_loads(l, k):
                copy.wait()

            @pl.when(k + 1 < MP)
            def _():
                for copy in weight_loads(l, k + 1):
                    copy.start()

            slot = k % 2
            de = nn(df_ref[...], pool[2 + slot])
            du = de * gp_ref[slot].astype(F32)
            dbin_ref[k] = jnp.sum(du, axis=0, keepdims=True)
            dub = du.astype(BF16)
            du_ref[k, pl.ds(0, rows), :] = dub
            du_copy(l, k).start()
            acc_ref[...] += nt(dub, pool[slot])
            return 0

        lax.fori_loop(0, MP, inner, 0)
        for copy in x_loads(l):
            copy.start()
        e_load(l, 0).start()
        for k in range(MP):
            v_stage[l, 0, 6 + k : 7 + k, :] = dbin_ref[k]
        if not top:
            step_a_two(l + 1)
            da_copy(l + 1).wait_send()
        sums = norm_back_rows(acc_ref, r1_ref, da_ref, vec[1:2, :])
        v_stage[l, 0, 1:2, :], v_stage[l, 0, 2:3, :], v_stage[l, 0, 0:1, :] = sums
        da_copy(l).start()

        def turned(source, target, half):
            turn_ref[...] = jnp.transpose(source)
            for g in range(4):
                at = pl.ds(pl.multiple_of((2 * g + c) * height, 32), height)
                target[pl.ds(g * height, height), pl.ds(half * rows, rows)] = turn_ref[at, :]

        turned(h_ref[0], ht_ref, 0)
        turned(h_ref[1], ht_ref, 1)
        turned(df_ref[...], dft_ref, 0)
        df_copy(l).wait_recv()
        turned(dfin_ref[...], dft_ref, 1)
        if not top:
            for k in range(MP):
                for n in range(2):
                    one_copy(l + 1, k, n).wait_send()
                two_copy(l + 1, k).wait_send()
                if k > 0:
                    z_copy(l + 1, k).wait_send()

        def outer(k, _, l=l):
            e_load(l, k).wait()

            @pl.when(k + 1 < MP)
            def _():
                e_load(l, k + 1).start()

            back = nn(dft_ref[...], pool[4 + k % 2]).astype(BF16)
            t_ref[k, :, :, pl.ds(width, width)] = back.reshape(4, height, width)
            du_copy(l, k).wait_recv()
            into = nn(ht_ref[...], du_ref[k]).astype(BF16)
            t_ref[k, :, :, pl.ds(0, width)] = into.reshape(4, height, width)
            for n in range(2):
                one_copy(l, k, n).start()
            return 0

        lax.fori_loop(0, MP, outer, 0)
        if not top:
            step_a_z(l + 1)
        for copy in late_loads(l):
            copy.wait()
        da_copy(l).wait_recv()
        low_half = lane_index((rows, LANES)) < HD
        for half, source in enumerate((da_ref, dain_ref)):
            at = pl.ds(half * rows, rows)
            for i in range(2):
                dz = nn(source[...], wa[i, :, 4 * LANES :])
                dz_ref[i, 0, at, :] = dz[:, LANES:].astype(BF16)
                dz_ref[i, 1, at, :] = jnp.where(
                    low_half, pltpu.roll(dz[:, :LANES], HD, 1), 0.0
                ).astype(BF16)
            pool[6, :, pl.ds(half * rows, rows)] = jnp.transpose(source[...])
        for i in range(2):
            dwo_ref[i] = nn(pool[6], mixed_ref[:, i * 256 : i * 256 + 256]).astype(BF16)
            head_deltas(i, mixed_ref, dz_ref, delta_ref)
        for copy in x_loads(l):
            copy.wait()
        for half in range(2):
            pool[half] = jnp.transpose(pool[2 + half])
        if top:
            for copy in table_loads:
                copy.wait()
        if not top:
            step_a_end(l + 1)

        steps = [[] for _ in range(6)]
        for k in range(MP):
            steps[k].append(partial(step_one, l, k))
            steps[k + 1].append(partial(step_two, l, k))
        steps[5].append(partial(step_feed_end, l))
        if not top:
            for n in range(1, 4):
                steps[n - 1].append(partial(step_v, l + 1, n))
            steps[3].append(partial(step_v_end, l + 1))
        for i in range(2):
            for h in range(3):
                head_back(
                    i,
                    h,
                    kblock,
                    q_ref,
                    k_ref,
                    v_ref,
                    dz_ref,
                    lse_ref,
                    delta_ref,
                    qrow_ref,
                    kcol_ref,
                    pair_ref,
                    dqt_ref,
                    dt_ref,
                )
                for step in steps[3 * i + h]:
                    step()
            for tile in range(5):
                total = jnp.zeros((1, LANES), F32)
                for half in range(1 if tile == 0 else 2):
                    at = pl.ds(half * queries, queries)
                    t = dt_ref[tile, at, :]
                    if tile < 3:
                        t = t * cos_ref[at, :] - half_swap(t) * sin_ref[at, :]
                    total = total + jnp.sum(t, axis=0, keepdims=True)
                    pool[2 + 2 * i + half, :, tile * LANES : (tile + 1) * LANES] = t.astype(BF16)
                for core in range(2):
                    v_stage[
                        l, 0, 10 + 2 * core + i : 11 + 2 * core + i, tile * LANES : (tile + 1) * LANES
                    ] = jnp.where(c == core, total, 0.0)
        v_copy(l, 0).start()

        def spread(n):
            half, at = n // 2, pl.ds((n % 2) * rows, rows)
            total = jnp.zeros((rows, width), F32)
            for i in range(2):
                low = pool.at[2 + 2 * i + half]
                total = total + nt(low[at, LANES : 5 * LANES], wa[i, :, LANES : 5 * LANES])
                if half == 0:
                    total = total + nt(low[at, 0:LANES], wa[i, :, 0:LANES])
            return total

        df_copy(l).wait_send()
        dxs_ref[1] = spread(3).astype(BF16)
        dxs_ref[0] = spread(1).astype(BF16)
        dxs_copy(l).start()
        part_ref[...] = spread(2)
        dxs_copy(l).wait_recv()
        dxp_ref[...] = (part_ref[...] + dxc_in[1].astype(F32)).astype(BF16)
        dxp_copy(l).start()
        acc_ref[...] += spread(0) + dxc_in[0].astype(F32)
        if not top:
            for n in range(2):
                a_one_copy(l + 1, n).wait_send()
            a_two_copy(l + 1).wait_send()
            a_z_copy(l + 1, 1).wait_send()

            @pl.when(c == 1)
            def _(l=l):
                a_z_copy(l + 1, 0).wait_send()

            a_c_copy(l + 1).wait_send()
        for i in range(2):
            low = [pool.at[2 + 2 * i + half] for half in range(2)]
            ta_ref[i, :, 0:LANES] = nn(pool[0], low[0][:, 0:LANES]).astype(BF16)
            more = nn(pool[0], low[0][:, LANES : 5 * LANES]) + nn(
                pool[1], low[1][:, LANES : 5 * LANES]
            )
            ta_ref[i, :, LANES : 4 * LANES] = more[:, : 3 * LANES].astype(BF16)
            ta_ref[i, :, 4 * LANES : 5 * LANES] = (
                more[:, 3 * LANES :] + dwo_ref[i, :, 0:LANES].astype(F32)
            ).astype(BF16)
            ta_ref[i, :, 5 * LANES :] = dwo_ref[i, :, LANES:]
        for n in range(2):
            a_one_copy(l, n).start()
        if l > 0:
            dxs_copy(l).wait_send()
            for copy in early_loads(l - 1) + weight_loads(l - 1, 0) + late_loads(l - 1):
                copy.start()
        dxp_copy(l).wait_recv()
        acc_ref[...] += dxp_in[l].astype(F32)

    dxp_copy(0).wait_send()
    df_ref[...] = acc_ref[...].astype(BF16)
    back_copy = remote(df_ref, back_in, t_send.at[0], t_recv.at[0], away)

    @pl.when(moved)
    def _():
        back_copy.start()

    step_v(0, 1)
    step_a_one(0)
    step_v(0, 2)
    step_a_two(0)
    step_v(0, 3)
    step_v_end(0)

    @pl.when(moved)
    def _():
        back_copy.wait_recv()
        acc_ref[...] = back_in[...].astype(F32)

    out_copy = pltpu.make_async_copy(acc_ref, tokens_out, o_sem.at[0])
    out_copy.start()
    step_a_z(0)
    step_a_end(0)
    out_copy.wait()

    @pl.when(moved)
    def _():
        back_copy.wait_send()

    da_copy(0).wait_send()
    dxs_copy(0).wait_send()
    for k in range(MP):
        du_copy(0, k).wait_send()
        for n in range(2):
            one_copy(0, k, n).wait_send()
        two_copy(0, k).wait_send()
        if k > 0:
            z_copy(0, k).wait_send()
    for n in range(2):
        a_one_copy(0, n).wait_send()
    a_two_copy(0).wait_send()
    a_z_copy(0, 1).wait_send()

    @pl.when(c == 1)
    def _():
        a_z_copy(0, 0).wait_send()

    a_c_copy(0).wait_send()
    for l in range(n_layers):
        for n in range(6):
            v_copy(l, n).wait_send()


def backward(w_all, dy, cos, sin, qrow, kcol, vectors, states):
    n_layers, _, width = vectors.shape
    rows = dy.shape[0]
    height = width // 8
    queries, keys = 2 * rows, 4 * rows
    sem = pltpu.SemaphoreType.DMA
    flat = [array for state in states for array in state]
    return pl.pallas_call(
        partial(backward_kernel, n_layers),
        out_shape=(
            shape((rows, width), F32),
            shape((n_layers, height, 2 * width), F32),
            shape((n_layers, height, width), F32),
            shape((n_layers, 8, width), F32),
        ),
        in_specs=[anywhere()] * 4 + [vmem()] * 3 + [anywhere()] * len(flat),
        out_specs=(anywhere(), vmem(), vmem(), vmem()),
        scratch_shapes=[
            pltpu.VMEM((7, width, width), BF16),
            pltpu.VMEM((2, rows, width), BF16),
            pltpu.VMEM((rows, width), F32),
            pltpu.VMEM((rows, width), F32),
            pltpu.VMEM((rows, width), F32),
            pltpu.VMEM((rows, width), BF16),
            pltpu.VMEM((rows, width), BF16),
            pltpu.VMEM((rows, width), BF16),
            pltpu.VMEM((rows, width), BF16),
            pltpu.VMEM((2, rows, width), BF16),
            pltpu.VMEM((width, rows), BF16),
            pltpu.VMEM((4 * height, 2 * rows), BF16),
            pltpu.VMEM((4 * height, 2 * rows), BF16),
            pltpu.VMEM((MP, 2 * rows, width), BF16),
            pltpu.VMEM((MP, 4, height, 2 * width), BF16),
            pltpu.VMEM((MP, 2, height, 2 * width), BF16),
            pltpu.VMEM((MP, height, 2 * width), BF16),
            pltpu.VMEM((n_layers, MP - 1, height, 2 * width), BF16),
            pltpu.VMEM((2, width, 2 * LANES), BF16),
            pltpu.VMEM((2, width, width), BF16),
            pltpu.VMEM((2, 2, 2 * height, width), BF16),
            pltpu.VMEM((2, 2 * height, width), BF16),
            pltpu.VMEM((2, 2 * height, width), BF16),
            pltpu.VMEM((n_layers, height, width), BF16),
            pltpu.VMEM((2 * height, width), F32),
            pltpu.VMEM((height, width), BF16),
            pltpu.VMEM((2, width, width), BF16),
            pltpu.VMEM((2, 2, queries, LANES), BF16),
            pltpu.VMEM((2, 2, keys, LANES), BF16),
            pltpu.VMEM((2, 2, keys, LANES), BF16),
            pltpu.VMEM((queries, 512), BF16),
            pltpu.VMEM((8, queries), F32),
            pltpu.VMEM((8, queries), F32),
            pltpu.VMEM((2, 2, queries, LANES), BF16),
            pltpu.VMEM((5, keys, LANES), F32),
            pltpu.VMEM((LANES, queries), F32),
            pltpu.VMEM((2, queries, LANES), BF16),
            pltpu.VMEM((keys, LANES), F32),
            pltpu.VMEM((keys, LANES), F32),
            pltpu.VMEM((2, rows, width), BF16),
            pltpu.VMEM((n_layers, rows, width), BF16),
            pltpu.VMEM((rows, width), BF16),
            pltpu.VMEM((n_layers, 4, 16, width), F32),
            pltpu.VMEM((n_layers, 6, 16, width), F32),
            pltpu.VMEM((MP, 1, width), F32),
            sem((n_layers, 8)),
            sem((n_layers, 8)),
            sem((n_layers, MP, 2)),
            sem((n_layers, MP, 2)),
            sem((n_layers, MP)),
            sem((n_layers, MP)),
            sem((n_layers, MP)),
            sem((n_layers, MP)),
            sem((n_layers, 6)),
            sem((n_layers, 6)),
            sem((n_layers, 6)),
            sem((n_layers, 6)),
            sem((1,)),
            sem((1,)),
            sem((2, 4)),
            sem((18,)),
            sem((1,)),
        ],
        compiler_params=pltpu.CompilerParams(
            vmem_limit_bytes=BACK_LIMIT, collective_id=1, has_side_effects=True
        ),
        cost_estimate=pl.CostEstimate(
            flops=200_000_000_000, bytes_accessed=100_000_000, transcendentals=20_000_000
        ),
        name="backward",
    )(w_all, dy, cos, sin, qrow, kcol, vectors, *flat)


def attend_kernel(chunk, *refs):
    scal, x_ref, bias_ref, cos_ref, sin_ref, qcode_ref, kcode_ref, w_all = refs[:8]
    q_ref, k_ref, v_ref, mixed_ref, lse_ref, w_ref, lse_cols, sems = refs[8:]
    copies = [
        pltpu.make_async_copy(
            w_all.at[chunk, scal[k], :, pl.ds(0, 5 * LANES)], w_ref.at[k], sems.at[k]
        )
        for k in range(2)
    ]
    for copy in copies:
        copy.start()
    for copy in copies:
        copy.wait()
    rows = x_ref.shape[1]
    for i in range(4):
        at = pl.ds(i * rows, rows)
        for k in range(2):
            project_rows(
                i,
                k,
                x_ref[i],
                w_ref,
                bias_ref[k],
                cos_ref[at, :],
                sin_ref[at, :],
                q_ref,
                k_ref,
                v_ref,
            )
    lse_cols[...] = jnp.zeros_like(lse_cols)

    def one_block(i, _):
        attend_rows(i, 256, qcode_ref, kcode_ref, q_ref, k_ref, v_ref, mixed_ref, lse_cols)
        return 0

    lax.fori_loop(0, 2 * rows // 256, one_block, 0)
    lse_ref[...] = jnp.transpose(lse_cols[...])[0:8, :]


def attend(scal, x_full, bias, tables, qcode, kcode, w_all, chunk):
    cos, sin = tables[:2]
    _, rows, width = x_full.shape
    queries, keys = 2 * rows, 4 * rows
    return pl.pallas_call(
        partial(attend_kernel, chunk),
        out_shape=(
            shape((2, 2, queries, LANES), BF16),
            shape((2, 2, keys, LANES), BF16),
            shape((2, 2, keys, LANES), BF16),
            shape((queries, 512), BF16),
            shape((8, queries), F32),
        ),
        in_specs=[smem()] + [vmem()] * 6 + [anywhere()],
        out_specs=(vmem(),) * 5,
        scratch_shapes=[
            pltpu.VMEM((2, width, 5 * LANES), BF16),
            pltpu.VMEM((queries, LANES), F32),
            pltpu.SemaphoreType.DMA((2,)),
        ],
        compiler_params=params(),
        name="attend",
    )(scal, x_full, bias, cos, sin, qcode, kcode, w_all)


def feed_kernel(chunk, *refs):
    scal, x_ref, own_ref, sib_ref, vec_ref, bin_ref, w_all = refs[:7]
    next_ref, low_ref, r1_ref, r2_ref, e_ref, gp_ref, wo_ref, win_ref, wback_ref, sems = refs[7:]
    copies = [
        pltpu.make_async_copy(
            w_all.at[chunk, :, :, pl.ds(4 * LANES, 2 * LANES)], wo_ref, sems.at[0]
        ),
        pltpu.make_async_copy(w_all.at[chunk + 1], win_ref, sems.at[1]),
        pltpu.make_async_copy(w_all.at[chunk + 2], wback_ref, sems.at[2]),
    ]
    for copy in copies:
        copy.start()
    for copy in copies:
        copy.wait()
    a = jnp.zeros(x_ref.shape, F32)
    for k in range(2):
        a = a + nt(own_ref[:, k * 256 : k * 256 + 256], wo_ref[scal[k]])
        a = a + nt(sib_ref[:, k * 256 : k * 256 + 256], wo_ref[lax.rem(scal[k] + 2, MP)])
    r1 = x_ref[...] + a + vec_ref[0:1, :]
    r1_ref[...] = r1
    n1, _ = norm_parts(r1)
    h = n1 * vec_ref[1:2, :] + vec_ref[2:3, :]
    low_ref[...] = h.astype(BF16)
    r2_ref[...] = h + vec_ref[3:4, :]

    def one(z, _):
        u = nn(low_ref[...], win_ref[z]) + bin_ref[z]
        cdf = 0.5 * (1.0 + lax.erf(u * (2.0**-0.5)))
        pdf = jnp.exp(u * u * -0.5) * 0.3989422804014327
        e = (u * cdf).astype(BF16)
        e_ref[z] = e
        gp_ref[z] = (cdf + u * pdf).astype(BF16)
        r2_ref[...] += nt(e, wback_ref[z])
        return 0

    lax.fori_loop(0, MP, one, 0)
    n2, _ = norm_parts(r2_ref[...])
    result = n2 * vec_ref[4:5, :] + vec_ref[5:6, :]
    next_ref[...] = result
    low_ref[...] = result.astype(BF16)


def feed_forward(scal, x, own, sib, vec, bias_in, w_all, chunk):
    rows, width = x.shape
    return pl.pallas_call(
        partial(feed_kernel, chunk),
        out_shape=(
            shape((rows, width), F32),
            shape((rows, width), BF16),
            shape((rows, width), F32),
            shape((rows, width), F32),
            shape((MP, rows, width), BF16),
            shape((MP, rows, width), BF16),
        ),
        in_specs=[smem()] + [vmem()] * 5 + [anywhere()],
        out_specs=(vmem(),) * 6,
        scratch_shapes=[
            pltpu.VMEM((MP, width, 2 * LANES), BF16),
            pltpu.VMEM((MP, width, width), BF16),
            pltpu.VMEM((MP, width, width), BF16),
            pltpu.SemaphoreType.DMA((3,)),
        ],
        compiler_params=params(),
        name="feed",
    )(scal, x, own, sib, vec, bias_in, w_all)


def plain_forward(blocks, tokens, cot, small, meta, frequency, vectors):
    n_layers = vectors.shape[0]
    rows, width = tokens.shape
    c, z = lax.axis_index("dp") % 2, lax.axis_index("mp")
    w_all = lax.all_gather(blocks, "dp", axis=1, tiled=True)
    w_all = jnp.swapaxes(lax.all_gather(w_all, "mp", axis=0, tiled=False), 0, 1)
    small_all = lax.all_gather(small, "mp", axis=0, tiled=False)
    own_z = jnp.stack([(z - 2 * c - k) % MP for k in range(2)]).astype(jnp.int32)
    info = jnp.where(z // 2 == c, meta, core_swap(meta))
    place = z % 2
    quarters = [2 * c + place, 2 * (1 - c) + place, 2 * c + 1 - place, 2 * (1 - c) + 1 - place]
    positions = jnp.concatenate(
        [q * rows + jnp.arange(rows, dtype=jnp.int32) for q in quarters]
    ).astype(F32)
    slot = info[0, 0]
    seq = jnp.where(positions >= slot, 1.0, 0.0) + jnp.where(positions >= 2.0 * slot, 1.0, 0.0)
    place = positions - seq * slot
    limit = jnp.where(seq == 0.0, info[1, 0], jnp.where(seq == 1.0, info[2, 0], info[3, 0]))
    kcode = jnp.where(place < limit, seq, -1.0)
    qcode = seq[: 2 * rows]
    angles = place[:, None] * frequency
    sign = jnp.where(jnp.arange(LANES) % HD < HD // 2, -1.0, 1.0)
    cos, sin = jnp.cos(angles), jnp.sin(angles) * sign[None, :]
    low = relayout(tokens)
    stream = low.astype(F32)
    states = []
    for l in range(n_layers):
        two = jnp.stack([low, pair_swap(low)])
        others = core_swap(two)
        x_full = jnp.stack([two[0], others[0], two[1], others[1]])
        bias = jnp.stack(
            [
                lax.dynamic_index_in_dim(small_all, own_z[k], 0, False)[l : l + 1, : 5 * LANES]
                for k in range(2)
            ]
        )
        q, k, v, mixed, lse = attend(
            own_z, x_full, bias, (cos, sin), qcode[:, None], kcode[None, :], w_all, 3 * l
        )
        other = core_swap(mixed[rows:])
        stream, low, r1, r2, e, gp = feed_forward(
            own_z,
            stream,
            mixed[:rows],
            other,
            vectors[l],
            small_all[:, l : l + 1, 5 * LANES :],
            w_all,
            3 * l,
        )
        states.append((x_full, q, k, v, mixed, other, lse, r1, r2, e, gp))
    return (w_all, relayout(cot), low, cos, sin, qcode[None, :], kcode[:, None]), states


def feed_back_kernel(n_pieces, rows, chunk, *refs):
    scal, dy_ref, r1_ref, r2_ref, e_ref, gp_ref, own_ref, sib_ref, vec_ref, w_all = refs[:10]
    at = 10
    dr1_ref, dzown_ref, dzsib_ref, dvec_ref, dbin_ref = refs[at : at + 5]
    outs = 2 if n_pieces == 8 else 1
    grads = refs[at + 5 : at + 5 + outs]
    wo_ref, win_ref, wback_ref, df_ref, dft_ref, ht_ref, dw_ref, sems = refs[at + 5 + outs :]
    width = dy_ref.shape[1]
    columns = [scal[n_pieces + k] for k in range(MP)]
    first_z = scal[n_pieces + MP]

    def fetch(source, target, base):
        copies = [
            pltpu.make_async_copy(source(columns[k]), target.at[k], sems.at[base + k])
            for k in range(MP)
        ]
        for copy in copies:
            copy.start()
        return copies

    back_copies = fetch(lambda z: w_all.at[chunk + 2, z], wback_ref, 0)
    in_copies = fetch(lambda z: w_all.at[chunk + 1, z], win_ref, MP)
    out_copies = fetch(
        lambda z: w_all.at[chunk, z, :, pl.ds(4 * LANES, 2 * LANES)], wo_ref, 2 * MP
    )
    dy = dy_ref[...]
    n2, scale2 = norm_parts(r2_ref[...])
    dvec_ref[4:5, :] = jnp.sum(dy * n2, axis=0, keepdims=True)
    dvec_ref[5:6, :] = jnp.sum(dy, axis=0, keepdims=True)
    dr2 = norm_back(dy, n2, scale2, vec_ref[4:5, :])
    dvec_ref[3:4, :] = jnp.sum(dr2, axis=0, keepdims=True)
    dr1_ref[...] = dr2
    df = dr2.astype(BF16)
    df_ref[...] = df
    dft_ref[...] = jnp.transpose(df)
    n1, _ = norm_parts(r1_ref[...])
    h = (n1 * vec_ref[1:2, :] + vec_ref[2:3, :]).astype(BF16)
    ht_ref[...] = jnp.transpose(h)
    for copy in back_copies + in_copies:
        copy.wait()

    def one(z, _):
        de = nn(df_ref[...], wback_ref[z])
        at = scal[n_pieces + z]
        du = de * gp_ref[at].astype(F32)
        dbin_ref[z] = jnp.sum(du, axis=0, keepdims=True)
        dub = du.astype(BF16)
        dr1_ref[...] += nt(dub, win_ref[z])
        dw_ref[z, :, 0:width] = nn(ht_ref[...], dub).astype(BF16)
        dw_ref[z, :, width : 2 * width] = nn(dft_ref[...], e_ref[at]).astype(BF16)
        return 0

    lax.fori_loop(0, MP, one, 0)
    dh = dr1_ref[...]
    n1, scale1 = norm_parts(r1_ref[...])
    dvec_ref[1:2, :] = jnp.sum(dh * n1, axis=0, keepdims=True)
    dvec_ref[2:3, :] = jnp.sum(dh, axis=0, keepdims=True)
    dr1 = norm_back(dh, n1, scale1, vec_ref[1:2, :])
    dvec_ref[0:1, :] = jnp.sum(dr1, axis=0, keepdims=True)
    dr1_ref[...] = dr1
    da = dr1.astype(BF16)
    dft_ref[...] = jnp.transpose(da)
    for copy in out_copies:
        copy.wait()
    used = lane_index((da.shape[0], 2 * LANES)) >= HD
    for z in range(2):
        for mixed_ref, dz_ref, z_at in (
            (own_ref, dzown_ref, first_z + z),
            (sib_ref, dzsib_ref, 2 - first_z + z),
        ):
            part = mixed_ref[:, z * 256 : z * 256 + 256]
            dw_ref[z_at, :, 2 * width :] = nn(dft_ref[...], part).astype(BF16)
            dz = nn(da, wo_ref[z_at])
            dz_ref[:, z * 256 : z * 256 + 256] = jnp.where(used, dz, 0.0).astype(BF16)
    flight = []
    for i in range(n_pieces):
        offset = pl.multiple_of(scal[i], 32)
        target = grads[i // 4].at[PIECE_ORDER[i % 4] if n_pieces == 8 else 0]
        copy = pltpu.make_async_copy(dw_ref.at[:, pl.ds(offset, rows), :], target, sems.at[i])
        copy.start()
        flight.append(copy)
    for copy in flight:
        copy.wait()


PIECE_ORDER = (3, 0, 2, 1)


def feed_back(scal, prows, count, dy, r1, r2, e, gp, own, sib, vec, w_all, chunk):
    rows, width = dy.shape
    lanes = 2 * width + 2 * LANES
    grads = (shape((4, MP, prows, lanes), BF16),) * 2
    if count != 8:
        grads = (shape((1, MP, prows, lanes), BF16),)
    return pl.pallas_call(
        partial(feed_back_kernel, count, prows, chunk),
        out_shape=(
            shape((rows, width), F32),
            shape((rows, 512), BF16),
            shape((rows, 512), BF16),
            shape((6, width), F32),
            shape((MP, 1, width), F32),
            *grads,
        ),
        in_specs=[smem()] + [vmem()] * 8 + [anywhere()],
        out_specs=(vmem(),) * 5 + (anywhere(),) * len(grads),
        scratch_shapes=[
            pltpu.VMEM((MP, width, 2 * LANES), BF16),
            pltpu.VMEM((MP, width, width), BF16),
            pltpu.VMEM((MP, width, width), BF16),
            pltpu.VMEM((rows, width), BF16),
            pltpu.VMEM((width, rows), BF16),
            pltpu.VMEM((width, rows), BF16),
            pltpu.VMEM((MP, width, lanes), BF16),
            pltpu.SemaphoreType.DMA((3 * MP,)),
        ],
        compiler_params=params(),
        cost_estimate=pl.CostEstimate(
            flops=16_000_000_000, bytes_accessed=40_000_000, transcendentals=0
        ),
        name="feed_back",
    )(scal, dy, r1, r2, e, gp, own, sib, vec, w_all)


def attend_back_kernel(n_pieces, chunk, *refs):
    (
        scal,
        x_ref,
        cos_ref,
        sin_ref,
        qcode_ref,
        kcode_ref,
        q_ref,
        k_ref,
        v_ref,
        mixed_ref,
        dzown_ref,
        dzsib_ref,
        lse_ref,
        w_all,
    ) = refs[:14]
    dx_ref, dxs_ref, dbias_ref, parts_ref = refs[14:18]
    (
        w_ref,
        xt_ref,
        dz_ref,
        delta_ref,
        dt_ref,
        dqt_ref,
        pair_ref,
        dw_ref,
        low_ref,
        sums_ref,
        sems,
    ) = refs[18:]
    copies = [
        pltpu.make_async_copy(
            w_all.at[chunk, scal[n_pieces + 9 + k], :, pl.ds(0, 5 * LANES)],
            w_ref.at[k],
            sems.at[k],
        )
        for k in range(2)
    ]
    for copy in copies:
        copy.start()
    keys, width = x_ref.shape
    queries = keys // 2
    block = queries // 2
    for z in range(2):
        for half, source in enumerate((dzown_ref, dzsib_ref)):
            at = pl.ds(half * block, block)
            dz_ref[z, 0, at, :] = source[:, z * 256 + LANES : z * 256 + 256]
            dz_ref[z, 1, at, :] = pltpu.roll(
                source[:, z * 256 : z * 256 + LANES].astype(F32), HD, 1
            ).astype(BF16)
        single = pltpu.roll(mixed_ref[:, z * 256 : z * 256 + LANES].astype(F32), HD, 1)
        pair = mixed_ref[:, z * 256 + LANES : z * 256 + 256].astype(F32)
        prod_one = jnp.transpose(pair * dz_ref[z, 0].astype(F32))
        prod_two = jnp.transpose(single * dz_ref[z, 1].astype(F32))
        delta_ref[3 * z : 3 * z + 1, :] = jnp.sum(prod_one[0:HD], axis=0, keepdims=True)
        delta_ref[3 * z + 1 : 3 * z + 2, :] = jnp.sum(prod_one[HD:], axis=0, keepdims=True)
        delta_ref[3 * z + 2 : 3 * z + 3, :] = jnp.sum(prod_two[0:HD], axis=0, keepdims=True)

    kblock = 256
    low_q = lane_index((queries, LANES)) < HD
    low_k = lane_index((kblock, LANES)) < HD
    for z in range(2):
        for h in range(3):
            tile = h // 2
            q = q_ref[z, tile]
            dz = dz_ref[z, tile]
            if h < 2:
                keep = low_q == (h == 0)
                q = jnp.where(keep, q, BF16(0))
                dz = jnp.where(keep, dz, BF16(0))
            pair_ref[0] = q
            pair_ref[1] = dz
            lse = lse_ref[3 * z + h : 3 * z + h + 1, :]
            delta = delta_ref[3 * z + h : 3 * z + h + 1, :]
            if h != 1:
                dqt_ref[...] = jnp.zeros_like(dqt_ref)

            def one_block(i, _, z=z, h=h, tile=tile, lse=lse, delta=delta):
                at = pl.ds(pl.multiple_of(i * kblock, kblock), kblock)
                kb = k_ref[z, tile, at, :]
                vb = v_ref[z, tile, at, :]
                if h < 2:
                    kb_own = jnp.where(low_k == (h == 0), kb, BF16(0))
                else:
                    kb_own = kb
                visible = kcode_ref[at, :] == qcode_ref[...]
                s = nt(kb, pair_ref[0])
                s = jnp.where(visible, s, NEGATIVE)
                p = jnp.exp(s - lse)
                dp = nt(vb, pair_ref[1])
                ds = (p * (dp - delta)).astype(BF16)
                dv = nn(p.astype(BF16), pair_ref[1])
                dk = nn(ds, pair_ref[0])
                dqt_ref[...] += nn(jnp.transpose(kb_own), ds)
                if h == 1:
                    dt_ref[2, at, :] += dk
                    dt_ref[3, at, :] += dv
                elif h == 0:
                    dt_ref[2, at, :] = dk
                    dt_ref[3, at, :] = dv
                else:
                    dt_ref[1, at, :] = pltpu.roll(dk, HD, 1)
                    dt_ref[4, at, :] = dv
                return 0

            lax.fori_loop(0, keys // kblock, one_block, 0)
            if h >= 1:
                dq = jnp.transpose(dqt_ref[...]) * HD**-0.5
                if h == 1:
                    dt_ref[0, 0:queries, :] = dq
                else:
                    dt_ref[1, 0:queries, :] += dq

        if z == 0:
            xt_ref[...] = jnp.transpose(x_ref[...])
            for copy in copies:
                copy.wait()
        for tile in range(5):
            count = queries if tile == 0 else keys
            t = dt_ref[tile, 0:count, :]
            if tile < 3:
                t = t * cos_ref[0:count, :] - half_swap(t) * sin_ref[0:count, :]
            dbias_ref[z, :, tile * LANES : (tile + 1) * LANES] = jnp.sum(t, axis=0, keepdims=True)
            low_ref[0:count, tile * LANES : (tile + 1) * LANES] = t.astype(BF16)
        dw_ref[z, :, 0:LANES] = nn(
            xt_ref[:, 0:queries], low_ref[0:queries, 0:LANES]
        ).astype(BF16)
        dw_ref[z, :, LANES:] = nn(xt_ref[...], low_ref[:, LANES:]).astype(BF16)
        for i in range(4):
            at = pl.ds(i * block, block)
            part = nt(low_ref[at, LANES:], w_ref[z, :, LANES : 5 * LANES])
            if i < 2:
                part = part + nt(low_ref[at, 0:LANES], w_ref[z, :, 0:LANES])
            if z == 0:
                sums_ref[i] = part
            else:
                target = dx_ref if i % 2 == 0 else dxs_ref
                target[i // 2] = (sums_ref[i] + part).astype(BF16)

    flight = []
    for i in range(min(n_pieces, 4)):
        offset = pl.multiple_of(scal[n_pieces + 5 + i], 32)
        copy = pltpu.make_async_copy(
            dw_ref.at[:, pl.ds(offset, parts_ref.shape[2]), :],
            parts_ref.at[PIECE_ORDER[i] if n_pieces == 8 else 0],
            sems.at[i],
        )
        copy.start()
        flight.append(copy)
    for copy in flight:
        copy.wait()


def attend_back(scal, prows, count, x_full, tables, saved, mixed, dz_own, dz_sib, w_all, chunk):
    cos, sin, qcode, kcode = tables
    q, k, v, lse = saved
    keys, width = x_full.shape
    queries = keys // 2
    block = queries // 2
    parts = (4, 2, 2 * prows, 5 * LANES)
    if count != 8:
        parts = (1, 2, prows, 5 * LANES)
    return pl.pallas_call(
        partial(attend_back_kernel, count, chunk),
        out_shape=(
            shape((2, block, width), BF16),
            shape((2, block, width), BF16),
            shape((2, 1, 5 * LANES), F32),
            shape(parts, BF16),
        ),
        in_specs=[smem()] + [vmem()] * 12 + [anywhere()],
        out_specs=(vmem(),) * 3 + (anywhere(),),
        scratch_shapes=[
            pltpu.VMEM((2, width, 5 * LANES), BF16),
            pltpu.VMEM((width, keys), BF16),
            pltpu.VMEM((2, 2, queries, LANES), BF16),
            pltpu.VMEM((8, queries), F32),
            pltpu.VMEM((5, keys, LANES), F32),
            pltpu.VMEM((LANES, queries), F32),
            pltpu.VMEM((2, queries, LANES), BF16),
            pltpu.VMEM((2, width, 5 * LANES), BF16),
            pltpu.VMEM((keys, 5 * LANES), BF16),
            pltpu.VMEM((4, block, width), F32),
            pltpu.SemaphoreType.DMA((4,)),
        ],
        compiler_params=params(),
        cost_estimate=pl.CostEstimate(
            flops=40_000_000_000, bytes_accessed=20_000_000, transcendentals=8_000_000
        ),
        name="attend_back",
    )(scal, x_full, cos, sin, qcode, kcode, q, k, v, mixed, dz_own, dz_sib, lse, w_all)


def head_tiles(q, k, v, o):
    return jnp.concatenate(
        [
            q[..., :LANES],
            q[..., LANES:],
            k[..., LANES:],
            k[..., :LANES],
            v[..., :LANES],
            v[..., LANES:],
            o[..., LANES:],
            o[..., :LANES],
        ],
        axis=-1,
    )


def head_columns(t):
    q = jnp.concatenate([t[..., 0:128], t[..., 128:192]], axis=-1)
    k = jnp.concatenate([t[..., 256:384], t[..., 192:256]], axis=-1)
    v = jnp.concatenate([t[..., 384:512], t[..., 512:576]], axis=-1)
    return q, k, v


def per_device(
    tokens, w_qkv, b_qkv, w_out, vectors, w_in, b_in, w_back, cotangent, lengths, buckets
):
    layers = w_qkv.shape[0]
    rows, width = tokens.shape
    d = lax.axis_index("dp")
    z = lax.axis_index("mp")
    g, c = d // 2, d % 2

    blocks = []
    for l in range(layers):
        low = w_qkv[l].astype(BF16)
        blocks.append(head_tiles(low[0], low[1], low[2], w_out[l].astype(BF16).T))
        blocks.append(w_in[l].astype(BF16))
        blocks.append(w_back[l].astype(BF16).T)
    blocks = jnp.stack(blocks)
    height = w_qkv.shape[2]
    pieces = 8 if lax.axis_size("dp") == 8 else 1
    piece_rows = height if pieces == 8 else width

    small = jnp.concatenate(
        [
            b_qkv[:, 0],
            b_qkv[:, 1, LANES:],
            b_qkv[:, 1, :LANES],
            b_qkv[:, 2],
            jnp.zeros((layers, HD), F32),
            b_in,
        ],
        axis=-1,
    )
    small = jnp.pad(small, ((0, 8 - layers), (0, 0)))
    slot = LEN_MAX // (3 - buckets)
    meta = jnp.concatenate([slot, lengths[0]]).astype(F32)
    meta = jnp.broadcast_to(jnp.pad(meta, (0, 4))[:, None], (8, LANES))
    exponents = jnp.arange(LANES, dtype=jnp.int32) % (HD // 2)
    frequency = 10000.0 ** (-2.0 * exponents.astype(F32) / HD)[None, :]

    if pieces == 8:
        head, states = forward(blocks, tokens, cotangent, small, meta, frequency, vectors)
        w_all, dy, low, cos, sin, qrow, kcol = head
        result = relayout(low)
        grad_tokens, feed_grads, attn_grads, small_grads = backward(
            w_all, dy, cos, sin, qrow, kcol, vectors, states
        )
        grad_qkv = jnp.stack(head_columns(attn_grads), axis=1)
        grad_in = feed_grads[:, :, :width]
        grad_back = jnp.swapaxes(feed_grads[:, :, width:], 1, 2)
        grad_out = jnp.concatenate(
            [attn_grads[:, :, 5 * LANES :], attn_grads[:, :, 4 * LANES + HD : 5 * LANES]], axis=-1
        )
        grad_out = jnp.swapaxes(grad_out, 1, 2)
        grad_b_qkv = jnp.stack(head_columns(small_grads[:, 7, :]), axis=1)
        return (
            result,
            grad_tokens,
            grad_qkv,
            grad_b_qkv,
            grad_out,
            small_grads[:, :6],
            grad_in,
            small_grads[:, 6],
            grad_back,
        )

    head, states = plain_forward(blocks, tokens, cotangent, small, meta, frequency, vectors)
    w_all, gradient, low, cos, sin, qcode, kcode = head
    result = relayout(low)
    gradient = gradient.astype(F32)

    first = jnp.where(c == 0, 1, 2)
    spans = [(g ^ hop) * 2 * height for hop in (0, first, 3 - first, 3)]
    if pieces == 1:
        spans = [jnp.int32(0)] * 4
    column_of = [(z - k) % MP for k in range(MP)]
    own_z = [(z - 2 * c - k) % MP for k in range(2)]
    scal = jnp.stack(row_offsets(g, c, height) + column_of + [2 * c] + spans + own_z)
    scal = scal.astype(jnp.int32)

    masters = []
    vector_grads = []
    in_biases = []
    head_biases = []
    for layer_at in reversed(range(layers)):
        x_full, q, k, v, mixed, mixed_in, lse, r1, r2, e, gp = states[layer_at]
        back = feed_back(
            scal,
            piece_rows,
            pieces,
            gradient,
            r1,
            r2,
            e,
            gp,
            mixed[:rows],
            mixed_in,
            vectors[layer_at],
            w_all,
            3 * layer_at,
        )
        dr1, dz_own, dz_sib, dvec, dbin = back[:5]
        dz_others = core_swap(dz_sib)
        feed_grad = reduce_all(back[5], back[-1])
        dx, dx_sib, dbias, parts = attend_back(
            scal,
            piece_rows,
            pieces,
            x_full.reshape(4 * rows, width),
            (cos, sin, qcode, kcode),
            (q, k, v, lse),
            mixed,
            dz_own,
            dz_others,
            w_all,
            3 * layer_at,
        )
        got = dx.astype(F32) + core_swap(dx_sib).astype(F32)
        gradient = dr1 + got[0] + pair_swap(got[1].astype(BF16)).astype(F32)
        head_grad = reduce_heads(parts)
        masters.insert(0, (feed_grad, head_grad))
        vector_grads.insert(0, dvec)
        in_biases.insert(0, dbin[:, 0])
        head_biases.insert(0, sum_head_biases(dbias[:, 0]))
    grad_tokens = relayout(gradient.astype(BF16)).astype(F32)

    layers_of = jnp.stack(in_biases, axis=1)
    grad_vectors, grad_b_in = sum_vectors(jnp.concatenate(vector_grads), layers_of)
    grad_vectors = grad_vectors.reshape(vectors.shape)
    grad_b_qkv = jnp.stack([jnp.stack(head_columns(b)) for b in head_biases])

    grad_qkv = jnp.stack([jnp.stack(head_columns(m[1])) for m in masters])
    grad_in = jnp.stack([m[0][:, :width] for m in masters])
    grad_back = jnp.stack([m[0][:, width : 2 * width].T for m in masters])
    grad_out = jnp.stack(
        [
            jnp.concatenate(
                [m[0][:, 2 * width + LANES :], m[0][:, 2 * width + HD : 2 * width + LANES]], axis=-1
            ).T
            for m in masters
        ]
    )
    return (
        result,
        grad_tokens,
        grad_qkv,
        grad_b_qkv,
        grad_out,
        grad_vectors,
        grad_in,
        grad_b_in,
        grad_back,
    )


def solution(mesh):
    return jax.shard_map(
        per_device,
        mesh=mesh,
        in_specs=(
            P(("dp", "mp"), None),
            P(None, None, "dp", "mp"),
            P(None, None, "mp"),
            P(None, "mp", "dp"),
            P(),
            P(None, "dp", "mp"),
            P(None, "mp"),
            P(None, "mp", "dp"),
            P(("dp", "mp"), None),
            P("dp", None),
            P("dp"),
        ),
        out_specs=(
            P(("dp", "mp"), None),
            P(("dp", "mp"), None),
            P(None, None, "dp", "mp"),
            P(None, None, "mp"),
            P(None, "mp", "dp"),
            P(),
            P(None, "dp", "mp"),
            P(None, "mp"),
            P(None, "mp", "dp"),
        ),
        check_vma=False,
    )
```

```python
from functools import partial

import jax
import jax.numpy as jnp
from jax import lax
from jax.experimental import pallas as pl
from jax.experimental.pallas import tpu as pltpu
from jax.sharding import PartitionSpec as P

HD = 64
LEN_MAX = 1536
EPSILON = 1e-06
NEGATIVE = -1e30
F32 = jnp.float32
BF16 = jnp.bfloat16
LANES = 128
MP = 4
SPLIT = 2
VMEM_LIMIT = 60 * 1024 * 1024
BACK_LIMIT = 63 * 1024 * 1024


def nn(a, b):
    return lax.dot_general(a, b, (((1,), (0,)), ((), ())), preferred_element_type=F32)


def nt(a, b):
    return lax.dot_general(a, b, (((1,), (1,)), ((), ())), preferred_element_type=F32)


def core_swap(x):
    n = lax.axis_size("dp")
    return lax.ppermute(x, "dp", [(i, i ^ 1) for i in range(n)])


def plane_swap(x, first):
    n = lax.axis_size("dp")
    hops = (2, 4) if first else (4, 2)
    return lax.ppermute(x, "dp", [(i, i ^ hops[i % 2]) for i in range(n)])


def column_shift(x, k):
    return lax.ppermute(x, "mp", [(i, (i + k) % MP) for i in range(MP)])


def pair_swap(x):
    return lax.ppermute(x, "mp", [(i, i ^ 1) for i in range(MP)])


def relayout(x):
    n = lax.axis_size("dp")
    pairs = []
    for d in range(n):
        for z in range(MP):
            if (d % 2) != (z // 2):
                pairs.append((d * MP + z, (d ^ 1) * MP + (z ^ 2)))
            else:
                pairs.append((d * MP + z, d * MP + z))
    return lax.ppermute(x, ("dp", "mp"), pairs)


def turn_columns(x, z):
    return jnp.stack([lax.dynamic_index_in_dim(x, (z - k) % MP, 0, False) for k in range(MP)])


def row_offsets(g, c, rows):
    if lax.axis_size("dp") != 8:
        return [jnp.int32(0)]
    result = []
    for core in (c, 1 - c):
        first = jnp.where(core == 0, 1, 2)
        for hop in (0, first, 3 - first, 3):
            result.append(((g ^ hop) * 2 + core) * rows)
    return result


def send_columns(v):
    total = v[0].astype(F32)
    for k in range(1, MP):
        total = total + column_shift(v[k], -k).astype(F32)
    return total


def reduce_all(keep, away):
    if lax.axis_size("dp") != 8:
        z = lax.axis_index("mp")
        whole = turn_columns(keep[0], z).astype(F32)
        part = lax.psum_scatter(whole, "mp", scatter_dimension=0, tiled=False)
        return lax.psum_scatter(part, "dp", scatter_dimension=0, tiled=True)
    other = core_swap(away)

    def add(i):
        return keep[i].astype(F32) + other[i].astype(F32)

    got = plane_swap(jnp.stack([add(0), add(1)]).astype(BF16), True)
    got_two = plane_swap((add(2) + got[1].astype(F32)).astype(BF16), False)
    v = (add(3) + got[0].astype(F32) + got_two.astype(F32)).astype(BF16)
    return send_columns(v)


def reduce_heads(parts):
    c = lax.axis_index("dp") % 2
    n = lax.axis_size("dp")
    if n != 8:
        z = lax.axis_index("mp")
        wide = jnp.concatenate([parts[0], jnp.zeros_like(parts[0])], axis=0)
        wide = jnp.where(c == 0, wide, jnp.roll(wide, 2, axis=0))
        whole = turn_columns(wide, z).astype(F32)
        part = lax.psum_scatter(whole, "mp", scatter_dimension=0, tiled=False)
        return lax.psum_scatter(part, "dp", scatter_dimension=0, tiled=True)
    got = plane_swap(parts[0:2], True)
    got_two = plane_swap((parts[2].astype(F32) + got[1].astype(F32)).astype(BF16), False)
    v = (parts[3].astype(F32) + got[0].astype(F32) + got_two.astype(F32)).astype(BF16)

    total = column_turn(v[0], 0).astype(F32) + column_turn(v[1], 1).astype(F32)
    rows = total.shape[0] // 2
    kept = lax.dynamic_slice_in_dim(total, c * rows, rows, 0)
    sent = lax.dynamic_slice_in_dim(total, (1 - c) * rows, rows, 0).astype(BF16)
    return kept + core_swap(sent).astype(F32)


def sum_head_biases(v):
    c = lax.axis_index("dp") % 2
    n = lax.axis_size("dp")
    if n != 8:
        z = lax.axis_index("mp")
        zero = jnp.zeros_like(v)
        wide = jnp.where(c == 0, jnp.concatenate([v, zero]), jnp.concatenate([zero, v]))
        total = lax.psum(turn_columns(wide, z), ("dp", "mp"))
        return lax.dynamic_index_in_dim(total, z, 0, False)
    v = v + plane_swap(v, True)
    v = v + plane_swap(v, False)
    total = column_turn(v[0], 0) + column_turn(v[1], 1)
    return total + core_swap(total)


def column_turn(x, k):
    n = lax.axis_size("dp")
    pairs = []
    for d in range(n):
        for z in range(MP):
            pairs.append((d * MP + z, d * MP + (z - k - 2 * (d % 2)) % MP))
    return lax.ppermute(x, ("dp", "mp"), pairs)


def sum_vectors(vectors, columns):
    if lax.axis_size("dp") != 8:
        z = lax.axis_index("mp")
        vectors, columns = lax.psum((vectors, turn_columns(columns, z)), ("dp", "mp"))
        return vectors, lax.dynamic_index_in_dim(columns, z, 0, False)
    n = vectors.shape[0]
    m = columns.shape[1]
    both = jnp.concatenate([vectors, columns.reshape(MP * m, -1)])
    both = both + core_swap(both)
    both = both + plane_swap(both, True)
    both = both + plane_swap(both, False)
    total = both[: n + m]
    for k in range(1, MP):
        at = n + m * (MP - k)
        total = total + column_shift(jnp.concatenate([both[:n], both[at : at + m]]), k)
    return total[:n], total[n:]


def lane_index(shape):
    return lax.broadcasted_iota(jnp.int32, shape, len(shape) - 1)


def half_swap(x):
    lane = lane_index(x.shape)
    return jnp.where(
        lane % HD < HD // 2,
        pltpu.roll(x, LANES - HD // 2, x.ndim - 1),
        pltpu.roll(x, HD // 2, x.ndim - 1),
    )


def norm_parts(r):
    mean = jnp.mean(r, axis=-1, keepdims=True)
    centred = r - mean
    scale = lax.rsqrt(jnp.mean(centred * centred, axis=-1, keepdims=True) + EPSILON)
    return centred * scale, scale


def norm_back(dy, n, scale, gain):
    gdy = dy * gain
    mean_one = jnp.mean(gdy, axis=-1, keepdims=True)
    mean_two = jnp.mean(gdy * n, axis=-1, keepdims=True)
    return (gdy - mean_one - n * mean_two) * scale


def vmem():
    return pl.BlockSpec(memory_space=pltpu.VMEM)


def smem():
    return pl.BlockSpec(memory_space=pltpu.SMEM)


def anywhere():
    return pl.BlockSpec(memory_space=pl.ANY)


def params():
    return pltpu.CompilerParams(vmem_limit_bytes=VMEM_LIMIT)


def shape(dims, dtype):
    return jax.ShapeDtypeStruct(dims, dtype)


def project_rows(i, z, x, w_ref, bias, cos, sin, q_ref, k_ref, v_ref):
    block = x.shape[0]
    at = pl.ds(i * block, block)
    p = nn(x, w_ref[z, :, LANES : 5 * LANES]) + bias[:, LANES:]
    low_half = lane_index((block, LANES)) < HD
    mixed = p[:, 0:LANES]
    mixed = mixed * cos + half_swap(mixed) * sin
    pair = p[:, LANES : 2 * LANES]
    pair = pair * cos + half_swap(pair) * sin
    k_ref[z, 0, at, :] = pair.astype(BF16)
    k_ref[z, 1, at, :] = jnp.where(low_half, pltpu.roll(mixed, HD, 1), 0.0).astype(BF16)
    v_ref[z, 0, at, :] = p[:, 2 * LANES : 3 * LANES].astype(BF16)
    v_ref[z, 1, at, :] = jnp.where(low_half, p[:, 3 * LANES :], 0.0).astype(BF16)
    if i < 2:
        q = nn(x, w_ref[z, :, 0:LANES]) + bias[:, 0:LANES]
        q = q * cos + half_swap(q) * sin
        q_ref[z, 0, at, :] = q.astype(BF16) * BF16(HD**-0.5)
        q_ref[z, 1, at, :] = jnp.where(low_half, mixed, 0.0).astype(BF16) * BF16(HD**-0.5)


def attend_rows(
    i, qblock, qcode_ref, kcode_ref, q_ref, k_ref, v_ref, mixed_ref, lse_cols, between=None
):
    at = pl.ds(pl.multiple_of(i * qblock, qblock), qblock)
    visible = qcode_ref[at, :] == kcode_ref[...]
    low_half = lane_index((qblock, LANES)) < HD
    lane = lane_index((qblock, LANES))
    for z in range(2):
        outs = []
        for h in range(3):
            tile = h // 2
            q = q_ref[z, tile, at, :]
            if h < 2:
                q = jnp.where(low_half == (h == 0), q, BF16(0))
            s = nt(q, k_ref[z, tile])
            s = jnp.where(visible, s, NEGATIVE)
            m = jnp.max(s, axis=-1, keepdims=True)
            p = jnp.exp(s - m)
            l = jnp.sum(p, axis=-1, keepdims=True)
            o = nn(p.astype(BF16), v_ref[z, tile])
            outs.append(o / l)
            lse_cols[at, :] = jnp.where(lane == 3 * z + h, m + jnp.log(l), lse_cols[at, :])
        mixed_ref[at, pl.ds(z * 256, LANES)] = pltpu.roll(outs[2], HD, 1).astype(BF16)
        mixed_ref[at, pl.ds(z * 256 + LANES, LANES)] = jnp.where(
            low_half, outs[0], outs[1]
        ).astype(BF16)
        if between is not None:
            between(z)


def mirrored(z):
    return [z, z + 1 - 2 * (z % 2), (z + 2) % MP, MP - 1 - z]


def head_columns_of(z, c):
    base = (z + 2 * c) % MP
    return [base, base + 1 - 2 * (base % 2)]


def forward_kernel(n_layers, *refs):
    n_in, per_layer = 7, 11
    blocks, tokens, cot, small, meta, frequency, vectors = refs[:n_in]
    w_all, dy_out, low_out, cos_out, sin_out, qrow_out, kcol_out = refs[n_in : n_in + 7]
    saved = [
        refs[n_in + 7 + l * per_layer : n_in + 7 + (l + 1) * per_layer] for l in range(n_layers)
    ]
    (
        xfull,
        mixed_in,
        small_all,
        meta_in,
        wa,
        wo,
        win,
        wback,
        cos_ref,
        sin_ref,
        qcode_ref,
        kcode_ref,
        qrow_ref,
        kcol_ref,
        q_ref,
        k_ref,
        v_ref,
        mixed_ref,
        lse_cols,
        lse_ref,
        stream,
        sum_ref,
        r1_ref,
        low_ref,
        e_ref,
        gp_ref,
        z_send,
        z_recv,
        p_send,
        p_recv,
        c_send,
        c_recv,
        x_send,
        x_recv,
        t_send,
        t_recv,
        l_sem,
        w_sem,
        s_sem,
    ) = refs[n_in + 7 + n_layers * per_layer :]
    rows = stream.shape[0]
    width = stream.shape[1]
    height = blocks.shape[1]
    parts = blocks.shape[0] * SPLIT

    d = lax.axis_index("dp")
    z = lax.axis_index("mp")
    c = d % 2
    x = (d // 2) % 2
    y = d // 4
    flip_x, flip_y = 1 - 2 * x, 1 - 2 * y
    one_x, one_y = x + (1 - c) * flip_x, y + c * flip_y
    two_x, two_y = x + c * flip_x, y + (1 - c) * flip_y

    def device(yy, xx, cc, zz):
        return (yy * 4 + xx * 2 + cc, zz)

    part_rows = height // SPLIT
    planes = ((y, x), (one_y, one_x), (two_y, two_x), (1 - y, 1 - x))

    def rows_of(k, n):
        yy, xx = planes[n]
        start = (yy * 4 + xx * 2 + c) * height + k % SPLIT * part_rows
        return pl.ds(pl.multiple_of(start, 16), part_rows)

    sibling = device(y, x, 1 - c, z)
    first = device(one_y, one_x, c, z)
    second = device(two_y, two_x, c, z)
    pair = device(y, x, c, z + 1 - 2 * (z % 2))
    away = device(y, x, 1 - c, (z + 2) % MP)
    moved = c != z // 2
    mirror = mirrored(z)
    columns = [device(y, x, c, mirror[m]) for m in range(1, MP)]
    barrier = pltpu.get_barrier_semaphore()
    partners = columns + [first, second, sibling, away]
    for partner in partners:
        pl.semaphore_signal(
            barrier, inc=1, device_id=partner, device_id_type=pl.DeviceIdType.MESH
        )
    pl.semaphore_wait(barrier, len(partners))

    def remote(source, target, send, recv, to):
        return pltpu.make_async_remote_copy(
            src_ref=source,
            dst_ref=target,
            send_sem=send,
            recv_sem=recv,
            device_id=to,
            device_id_type=pl.DeviceIdType.MESH,
        )

    sent = []

    def go(make, *at):
        make(*at).start()
        sent.append((make, at))

    def block(k):
        return blocks.at[k // SPLIT, pl.ds(k % SPLIT * part_rows, part_rows)]

    def local_copy(k):
        return pltpu.make_async_copy(block(k), w_all.at[k // SPLIT, z, rows_of(k, 0)], l_sem.at[k])

    def z_copy(k, n):
        if n == 2:
            source = target = w_all.at[k // SPLIT, mirror[2], rows_of(k, 0)]
        else:
            source, target = block(k), w_all.at[k // SPLIT, z, rows_of(k, 0)]
        return remote(
            source, target, z_send.at[k, n], z_recv.at[k, n], columns[1 if n == 1 else 0]
        )

    def p_copy(k, n):
        source = w_all.at[k // SPLIT, :, rows_of(k, 1 if n == 2 else 0)]
        return remote(
            source, source, p_send.at[k, n], p_recv.at[k, n], first if n == 0 else second
        )

    def c_copy(k, n):
        source = w_all.at[k // SPLIT, :, rows_of(k, n)]
        return remote(source, source, c_send.at[k, n], c_recv.at[k, n], sibling)

    def step_send(k):
        local_copy(k).start()
        go(z_copy, k, 1)
        go(z_copy, k, 0)

    def step_across(k):
        z_copy(k, 1).wait_recv()
        go(z_copy, k, 2)

    def step_plane(k):
        local_copy(k).wait()
        z_copy(k, 0).wait_recv()
        z_copy(k, 2).wait_recv()
        go(p_copy, k, 0)
        go(p_copy, k, 1)
        go(c_copy, k, 0)
        if k + 1 < parts:
            step_across(k + 1)
        if k + 2 < parts:
            step_send(k + 2)

    def step_forward(k):
        p_copy(k, 0).wait_recv()
        go(p_copy, k, 2)
        go(c_copy, k, 1)
        p_copy(k, 1).wait_recv()
        go(c_copy, k, 2)

    def step_last(k):
        p_copy(k, 2).wait_recv()
        go(c_copy, k, 3)

    def step_ready(chunk):
        for k in range(chunk * SPLIT, (chunk + 1) * SPLIT):
            for n in range(4):
                c_copy(k, n).wait_recv()

    turns = parts + 2
    position = [0]

    def take(until):
        steps = []
        for n in range(position[0], until):
            if n < parts:
                steps.append(partial(step_plane, n))
            if 0 <= n - 2:
                steps.append(partial(step_last, n - 2))
            if 0 <= n - 1 < parts:
                steps.append(partial(step_forward, n - 1))
        position[0] = max(position[0], until)
        return steps

    def run(steps):
        for step in steps:
            step()

    def meta_copy():
        return remote(meta, meta_in, t_send.at[0], t_recv.at[0], sibling)

    def small_copy(s):
        return remote(small, small_all.at[z], t_send.at[3 + s], t_recv.at[3 + s], columns[s])

    step_send(0)
    go(meta_copy)
    for n in range(MP - 1):
        go(small_copy, n)
    token_copy = remote(tokens, xfull.at[0, 0], t_send.at[1], t_recv.at[1], away)
    token_local = pltpu.make_async_copy(tokens, xfull.at[0, 0], l_sem.at[parts])
    step_across(0)

    @pl.when(moved)
    def _():
        token_copy.start()

    @pl.when(jnp.logical_not(moved))
    def _():
        token_local.start()

    step_send(1)
    small_local = pltpu.make_async_copy(small, small_all.at[z], l_sem.at[parts + 1])
    small_local.start()

    meta_copy().wait_recv()
    info = jnp.where(moved, meta_in[...], meta[...])
    slot = info[0:1, :]
    limits = [info[n : n + 1, :] for n in range(1, 4)]
    half = z % 2
    quarters = [2 * c + half, 2 * (1 - c) + half, 2 * c + 1 - half, 2 * (1 - c) + 1 - half]

    def codes(place_all, slot, limits):
        seq = jnp.where(place_all >= slot, 1.0, 0.0) + jnp.where(place_all >= 2.0 * slot, 1.0, 0.0)
        place = place_all - seq * slot
        limit = jnp.where(seq == 0.0, limits[0], jnp.where(seq == 1.0, limits[1], limits[2]))
        return seq, place, jnp.where(place < limit, seq, -1.0)

    sign = jnp.where(lane_index((1, LANES)) % HD < HD // 2, -1.0, 1.0)
    for i in range(4):
        at = pl.ds(i * rows, rows)
        base = quarters[i] * rows
        index = lax.broadcasted_iota(jnp.int32, (rows, LANES), 0) + base
        seq, place, kcode = codes(index.astype(F32), slot, limits)
        angle = place * frequency[...]
        cos_ref[at, :] = jnp.cos(angle)
        sin_ref[at, :] = jnp.sin(angle) * sign
        kcol_ref[at, :] = kcode[:, 0:1]
        if i < 2:
            qcode_ref[at, :] = seq[:, 0:1]
        index = lax.broadcasted_iota(jnp.int32, (1, rows), 1) + base
        seq, place, kcode = codes(
            index.astype(F32), slot[:, 0:1], [limit[:, 0:1] for limit in limits]
        )
        kcode_ref[:, pl.ds(i * rows, rows)] = kcode
        if i < 2:
            qrow_ref[:, pl.ds(i * rows, rows)] = seq

    run(take(1))

    @pl.when(moved)
    def _():
        token_copy.wait_recv()

    @pl.when(jnp.logical_not(moved))
    def _():
        token_local.wait()

    def x_copy(l, n):
        source = xfull.at[l, 2 if n == 2 else 0]
        target = xfull.at[l, (2, 1, 3)[n]]
        return remote(
            source, target, x_send.at[l, n], x_recv.at[l, n], pair if n == 0 else sibling
        )

    def m_copy(l):
        return remote(
            mixed_ref.at[pl.ds(rows, rows)],
            mixed_in.at[l],
            x_send.at[l, 3],
            x_recv.at[l, 3],
            sibling,
        )

    def h_copy(l):
        return remote(low_ref, saved[l][10].at[1], x_send.at[l, 4], x_recv.at[l, 4], sibling)

    def e_copy(l):
        return remote(
            e_ref,
            saved[l][8].at[:, pl.ds(rows, rows), :],
            x_send.at[l, 5],
            x_recv.at[l, 5],
            sibling,
        )

    stores = {}

    def store(name, source, target):
        copy = pltpu.make_async_copy(source, target, s_sem.at[len(stores)])
        copy.start()
        stores[name] = copy

    waited = set()

    def stored(*names):
        for name in names:
            if name in stores and name not in waited:
                waited.add(name)
                stores[name].wait()

    stream[...] = xfull[0, 0].astype(F32)
    store("cos", cos_ref, cos_out)
    store("sin", sin_ref, sin_out)
    store("qrow", qrow_ref, qrow_out)
    store("kcol", kcol_ref, kcol_out)

    cot_copy = remote(cot, dy_out, t_send.at[2], t_recv.at[2], away)
    cot_local = pltpu.make_async_copy(cot, dy_out, l_sem.at[parts + 2])

    def load(source, target, n):
        copy = pltpu.make_async_copy(source, target, w_sem.at[n])
        copy.start()
        return copy

    qblock = 256
    count = 2 * rows // qblock
    own_z = head_columns_of(z, c)
    other_z = [(at + 2) % MP for at in own_z]
    for l in range(n_layers):
        xs, qs, ks, vs, ms, ls, r1s, r2s, es, gps, hs = saved[l]
        last = l - 1
        go(x_copy, l, 0)
        go(x_copy, l, 1)
        run(take(2 if l == 0 else 9))
        x_copy(l, 0).wait_recv()
        go(x_copy, l, 2)
        run(take(4 if l == 0 else 10))
        step_ready(3 * l)
        wa_loads = [
            load(w_all.at[3 * l, own_z[k], :, pl.ds(0, 5 * LANES)], wa.at[k], k) for k in range(2)
        ]
        wo_load = load(w_all.at[3 * l, :, :, pl.ds(4 * LANES, 2 * LANES)], wo, 2)
        if l == 0:

            @pl.when(moved)
            def _():
                cot_copy.start()

            @pl.when(jnp.logical_not(moved))
            def _():
                cot_local.start()

            for s in range(MP - 1):
                small_copy(s).wait_recv()
            small_local.wait()
        else:
            m_copy(last).wait_send()
        stored(("q", last), ("k", last), ("v", last), ("mixed", last), ("lse", last))
        lse_cols[...] = jnp.zeros_like(lse_cols)
        for copy in wa_loads:
            copy.wait()
        for i in range(4):
            if i == 1:
                x_copy(l, 1).wait_recv()
            if i == 3:
                run(take(5 if l == 0 else 10))
                x_copy(l, 2).wait_recv()
            at = pl.ds(i * rows, rows)
            for k in range(2):
                bias = small_all[own_z[k], pl.ds(l, 1), pl.ds(0, 5 * LANES)]
                project_rows(
                    i, k, xfull[l, i], wa, bias, cos_ref[at, :], sin_ref[at, :], q_ref, k_ref, v_ref
                )
        store(("q", l), q_ref, qs)
        store(("k", l), k_ref, ks)
        store(("v", l), v_ref, vs)
        store(("x", l), xfull.at[l], xs)
        ends = (5, 5, 6, 6, 6, 7) if l == 0 else (11, 11, 11, 12, 12, 13)
        steps = [take(end) for end in ends]

        def one_block(n, _, l=l, steps=steps):
            def between(k):
                for j in range(count):
                    if steps[2 * j + k] or (j, k) == (1, 1):

                        @pl.when(n == j)
                        def _(j=j):
                            if (j, k) == (1, 1):
                                m_copy(l).start()
                            run(steps[2 * j + k])

            attend_rows(
                count - 1 - n,
                qblock,
                qcode_ref,
                kcode_ref,
                q_ref,
                k_ref,
                v_ref,
                mixed_ref,
                lse_cols,
                between,
            )
            return 0

        lax.fori_loop(0, count, one_block, 0)
        lse_ref[...] = jnp.transpose(lse_cols[...])[0:8, :]
        store(("mixed", l), mixed_ref, ms)
        store(("lse", l), lse_ref, ls)
        step_ready(3 * l + 1)
        win_load = load(w_all.at[3 * l + 1], win, 3)
        stored(("r1", last), ("r2", last), ("e", last), ("gp", last), ("h", last))
        if l > 0:
            h_copy(last).wait_send()
            e_copy(last).wait_send()
        wo_load.wait()
        m_copy(l).wait_recv()
        a = jnp.zeros((rows, width), F32)
        for k in range(2):
            a = a + nt(mixed_ref[0:rows, k * 256 : k * 256 + 256], wo[own_z[k]])
            a = a + nt(mixed_in[l, :, k * 256 : k * 256 + 256], wo[other_z[k]])
        vec = vectors[l]
        r1 = stream[...] + a + vec[0:1, :]
        r1_ref[...] = r1
        store(("r1", l), r1_ref, r1s)
        n1, _ = norm_parts(r1)
        h = n1 * vec[1:2, :] + vec[2:3, :]
        low_ref[...] = h.astype(BF16)
        store(("h", l), low_ref, hs.at[0])
        h_copy(l).start()
        sum_ref[...] = h + vec[3:4, :]
        win_load.wait()

        def inner(zz, _, l=l):
            u = nn(low_ref[...], win[zz]) + small_all[zz, pl.ds(l, 1), pl.ds(5 * LANES, width)]
            cdf = 0.5 * (1.0 + lax.erf(u * (2.0**-0.5)))
            pdf = jnp.exp(u * u * -0.5) * 0.3989422804014327
            e_ref[zz] = (u * cdf).astype(BF16)
            gp_ref[zz] = (cdf + u * pdf).astype(BF16)
            return 0

        lax.fori_loop(0, 2, inner, 0)
        run(take(7 if l == 0 else 13))
        lax.fori_loop(2, MP, inner, 0)
        run(take(8 if l == 0 else turns))
        step_ready(3 * l + 2)
        wback_load = load(w_all.at[3 * l + 2], wback, 4)
        store(("e", l), e_ref, es.at[:, pl.ds(0, rows), :])
        e_copy(l).start()
        store(("gp", l), gp_ref, gps)
        wback_load.wait()

        def outer(zz, _):
            sum_ref[...] += nt(e_ref[zz], wback[zz])
            return 0

        lax.fori_loop(0, MP, outer, 0)
        store(("r2", l), sum_ref, r2s)
        n2, _ = norm_parts(sum_ref[...])
        result = n2 * vec[4:5, :] + vec[5:6, :]
        if l + 1 < n_layers:
            stream[...] = result
            xfull[l + 1, 0] = result.astype(BF16)
        else:
            h_copy(l).wait_send()
            stored(("h", l))
            low_ref[...] = result.astype(BF16)
            store("low", low_ref, low_out)

    m_copy(n_layers - 1).wait_send()
    e_copy(n_layers - 1).wait_send()
    for l in range(n_layers):
        h_copy(l).wait_recv()
        e_copy(l).wait_recv()
    for make, at in sent:
        make(*at).wait_send()
    @pl.when(moved)
    def _():
        token_copy.wait_send()
        cot_copy.wait_send()
        cot_copy.wait_recv()

    @pl.when(jnp.logical_not(moved))
    def _():
        cot_local.wait()

    stored(*stores)


def forward(blocks, tokens, cot, small, meta, frequency, vectors):
    n_layers = vectors.shape[0]
    chunks, height, width = blocks.shape
    rows = tokens.shape[0]
    queries, keys = 2 * rows, 4 * rows
    layer_out = (
        shape((4, rows, width), BF16),
        shape((2, 2, queries, LANES), BF16),
        shape((2, 2, keys, LANES), BF16),
        shape((2, 2, keys, LANES), BF16),
        shape((queries, 512), BF16),
        shape((8, queries), F32),
        shape((rows, width), F32),
        shape((rows, width), F32),
        shape((MP, 2 * rows, width), BF16),
        shape((MP, rows, width), BF16),
        shape((2, rows, width), BF16),
    )
    outs = (
        shape((chunks, MP, 8 * height, width), BF16),
        shape((rows, width), BF16),
        shape((rows, width), BF16),
        shape((keys, LANES), F32),
        shape((keys, LANES), F32),
        shape((1, queries), F32),
        shape((keys, 1), F32),
    ) + layer_out * n_layers
    sem = pltpu.SemaphoreType.DMA
    results = pl.pallas_call(
        partial(forward_kernel, n_layers),
        out_shape=outs,
        in_specs=[anywhere()] * 3 + [vmem()] * 4,
        out_specs=(anywhere(),) * len(outs),
        scratch_shapes=[
            pltpu.VMEM((n_layers, 4, rows, width), BF16),
            pltpu.VMEM((n_layers, rows, 512), BF16),
            pltpu.VMEM((MP,) + small.shape, F32),
            pltpu.VMEM(meta.shape, F32),
            pltpu.VMEM((2, width, 5 * LANES), BF16),
            pltpu.VMEM((MP, width, 2 * LANES), BF16),
            pltpu.VMEM((MP, width, width), BF16),
            pltpu.VMEM((MP, width, width), BF16),
            pltpu.VMEM((keys, LANES), F32),
            pltpu.VMEM((keys, LANES), F32),
            pltpu.VMEM((queries, 1), F32),
            pltpu.VMEM((1, keys), F32),
            pltpu.VMEM((1, queries), F32),
            pltpu.VMEM((keys, 1), F32),
            pltpu.VMEM((2, 2, queries, LANES), BF16),
            pltpu.VMEM((2, 2, keys, LANES), BF16),
            pltpu.VMEM((2, 2, keys, LANES), BF16),
            pltpu.VMEM((queries, 512), BF16),
            pltpu.VMEM((queries, LANES), F32),
            pltpu.VMEM((8, queries), F32),
            pltpu.VMEM((rows, width), F32),
            pltpu.VMEM((rows, width), F32),
            pltpu.VMEM((rows, width), F32),
            pltpu.VMEM((rows, width), BF16),
            pltpu.VMEM((MP, rows, width), BF16),
            pltpu.VMEM((MP, rows, width), BF16),
            sem((chunks * SPLIT, 3)),
            sem((chunks * SPLIT, 3)),
            sem((chunks * SPLIT, 3)),
            sem((chunks * SPLIT, 3)),
            sem((chunks * SPLIT, 4)),
            sem((chunks * SPLIT, 4)),
            sem((n_layers, 6)),
            sem((n_layers, 6)),
            sem((6,)),
            sem((6,)),
            sem((chunks * SPLIT + 3,)),
            sem((5,)),
            sem((5 + 11 * n_layers,)),
        ],
        compiler_params=pltpu.CompilerParams(
            vmem_limit_bytes=VMEM_LIMIT, collective_id=0, has_side_effects=True
        ),
        cost_estimate=pl.CostEstimate(
            flops=100_000_000_000, bytes_accessed=100_000_000, transcendentals=20_000_000
        ),
        name="forward",
    )(blocks, tokens, cot, small, meta, frequency, vectors)
    head = results[:7]
    states = [results[7 + 11 * l : 18 + 11 * l] for l in range(n_layers)]
    return head, states


def place_of(d, z):
    c = d % 2
    x = (d // 2) % 2
    y = d // 4
    flip_x, flip_y = 1 - 2 * x, 1 - 2 * y
    planes = (
        (y, x),
        (y + c * flip_y, x + (1 - c) * flip_x),
        (y + (1 - c) * flip_y, x + c * flip_x),
        (1 - y, 1 - x),
    )
    groups = [2 * yy + xx for yy, xx in planes]

    def device(group, cc, zz):
        return (group * 2 + cc, zz)

    return c, groups, device


def head_back(
    i,
    h,
    kblock,
    q_ref,
    k_ref,
    v_ref,
    dz_ref,
    lse_ref,
    delta_ref,
    qrow_ref,
    kcol_ref,
    pair_ref,
    dqt_ref,
    dt_ref,
):
    tile = h // 2
    keys, queries = k_ref.shape[2], q_ref.shape[2]
    low_q = lane_index((queries, LANES)) < HD
    low_k = lane_index((kblock, LANES)) < HD
    q = q_ref[i, tile]
    dz = dz_ref[i, tile]
    if h < 2:
        keep = low_q == (h == 0)
        q = jnp.where(keep, q, BF16(0))
        dz = jnp.where(keep, dz, BF16(0))
    pair_ref[0] = q
    pair_ref[1] = dz
    lse = lse_ref[3 * i + h : 3 * i + h + 1, :]
    delta = delta_ref[3 * i + h : 3 * i + h + 1, :]
    if h != 1:
        dqt_ref[...] = jnp.zeros_like(dqt_ref)

    def one_block(n, _):
        at = pl.ds(pl.multiple_of(n * kblock, kblock), kblock)
        kb = k_ref[i, tile, at, :]
        vb = v_ref[i, tile, at, :]
        kb_own = jnp.where(low_k == (h == 0), kb, BF16(0)) if h < 2 else kb
        visible = kcol_ref[at, :] == qrow_ref[...]
        s = nt(kb, pair_ref[0])
        s = jnp.where(visible, s, NEGATIVE)
        p = jnp.exp(s - lse)
        dp = nt(vb, pair_ref[1])
        ds = (p * (dp - delta)).astype(BF16)
        dv = nn(p.astype(BF16), pair_ref[1])
        dk = nn(ds, pair_ref[0])
        dqt_ref[...] += nn(jnp.transpose(kb_own), ds)
        if h == 1:
            dt_ref[2, at, :] += dk
            dt_ref[3, at, :] += dv
        elif h == 0:
            dt_ref[2, at, :] = dk
            dt_ref[3, at, :] = dv
        else:
            dt_ref[1, at, :] = pltpu.roll(dk, HD, 1)
            dt_ref[4, at, :] = dv
        return 0

    lax.fori_loop(0, keys // kblock, one_block, 0)
    if h >= 1:
        dq = jnp.transpose(dqt_ref[...]) * HD**-0.5
        if h == 1:
            dt_ref[0, 0:queries, :] = dq
        else:
            dt_ref[1, 0:queries, :] += dq


def head_deltas(i, mixed_ref, dz_ref, delta_ref):
    single = pltpu.roll(mixed_ref[:, i * 256 : i * 256 + LANES].astype(F32), HD, 1)
    pair = mixed_ref[:, i * 256 + LANES : i * 256 + 256].astype(F32)
    prod_one = jnp.transpose(pair * dz_ref[i, 0].astype(F32))
    prod_two = jnp.transpose(single * dz_ref[i, 1].astype(F32))
    delta_ref[3 * i : 3 * i + 1, :] = jnp.sum(prod_one[0:HD], axis=0, keepdims=True)
    delta_ref[3 * i + 1 : 3 * i + 2, :] = jnp.sum(prod_one[HD:], axis=0, keepdims=True)
    delta_ref[3 * i + 2 : 3 * i + 3, :] = jnp.sum(prod_two[0:HD], axis=0, keepdims=True)


def norm_back_rows(acc_ref, r_ref, low_ref, gain):
    rows, width = acc_ref.shape
    step = 32

    def body(i, sums):
        at = pl.ds(pl.multiple_of(i * step, step), step)
        dy = acc_ref[at, :]
        n, scale = norm_parts(r_ref[at, :])
        dr = norm_back(dy, n, scale, gain)
        acc_ref[at, :] = dr
        low_ref[at, :] = dr.astype(BF16)
        return (
            sums[0] + jnp.sum(dy * n, axis=0, keepdims=True),
            sums[1] + jnp.sum(dy, axis=0, keepdims=True),
            sums[2] + jnp.sum(dr, axis=0, keepdims=True),
        )

    zero = jnp.zeros((1, width), F32)
    return lax.fori_loop(0, rows // step, body, (zero, zero, zero))


def backward_kernel(n_layers, *refs):
    n_in, per_layer = 8, 11
    w_all, dy_in, cos_in, sin_in, low_in, qrow_ref, kcol_ref, vectors = refs[:n_in]
    saved = [refs[n_in + l * per_layer : n_in + (l + 1) * per_layer] for l in range(n_layers)]
    at = n_in + n_layers * per_layer
    (
        tokens_out,
        result_out,
        qkv_out,
        bqkv_out,
        outw_out,
        vec_out,
        in_out,
        bin_out,
        back_out,
    ) = refs[at : at + 9]
    (
        pool,
        gp_ref,
        r1_ref,
        r2_ref,
        acc_ref,
        df_ref,
        dfin_ref,
        da_ref,
        dain_ref,
        h_ref,
        turn_ref,
        ht_ref,
        dft_ref,
        du_ref,
        t_ref,
        one_in,
        two_in,
        z_in,
        dwo_ref,
        ta_ref,
        a_one_in,
        a_two_in,
        a_z_in,
        a_c_in,
        a_sum_ref,
        a_out_ref,
        wa,
        q_ref,
        k_ref,
        v_ref,
        mixed_ref,
        lse_ref,
        delta_ref,
        dz_ref,
        dt_ref,
        dqt_ref,
        pair_ref,
        cos_ref,
        sin_ref,
        dxc_in,
        dxp_in,
        back_in,
        v_stage,
        v_in,
        dbin_ref,
        across_ref,
        feed_sum,
        c_send,
        c_recv,
        one_send,
        one_recv,
        two_send,
        two_recv,
        z_send,
        z_recv,
        a_send,
        a_recv,
        x_send,
        x_recv,
        v_send,
        v_recv,
        t_send,
        t_recv,
        w_sem,
        s_sem,
        o_sem,
    ) = refs[at + 9 :]
    part_ref, dxs_ref, dxp_ref = r2_ref, h_ref, df_ref
    rows, width = acc_ref.shape
    height = t_ref.shape[3]
    queries = 2 * rows

    d = lax.axis_index("dp")
    z = lax.axis_index("mp")
    c, groups, device = place_of(d, z)
    sibling = device(groups[0], 1 - c, z)
    first = device(groups[1], c, z)
    second = device(groups[2], c, z)
    away = device(groups[0], 1 - c, (z + 2) % MP)
    pair = device(groups[0], c, z + 1 - 2 * (z % 2))
    mirror = mirrored(z)
    columns = [device(groups[0], c, mirror[m]) for m in range(1, MP)]
    across = columns[1]
    moved = c != z // 2

    barrier = pltpu.get_barrier_semaphore()
    partners = columns + [first, second, sibling, away]
    for partner in partners:
        pl.semaphore_signal(
            barrier, inc=1, device_id=partner, device_id_type=pl.DeviceIdType.MESH
        )

    def remote(source, target, send, recv, to):
        return pltpu.make_async_remote_copy(
            src_ref=source,
            dst_ref=target,
            send_sem=send,
            recv_sem=recv,
            device_id=to,
            device_id_type=pl.DeviceIdType.MESH,
        )

    def column(k):
        base = (z + 2 * (k // 2)) % MP
        return base + (k % 2) * (1 - 2 * (base % 2))

    own_z = head_columns_of(z, c)

    def load(source, target, sem):
        return pltpu.make_async_copy(source, target, sem)

    def early_loads(l):
        _, _, _, _, _, _, r1s, r2s, _, _, hs = saved[l]
        return [
            load(r2s, r2_ref, s_sem.at[0]),
            load(r1s, r1_ref, s_sem.at[1]),
            load(hs, h_ref, s_sem.at[2]),
        ]

    def weight_loads(l, k):
        slot = k % 2
        gps = saved[l][9]
        return [
            load(w_all.at[3 * l + 2, column(k)], pool.at[2 + slot], w_sem.at[slot, 0]),
            load(w_all.at[3 * l + 1, column(k)], pool.at[slot], w_sem.at[slot, 1]),
            load(gps.at[column(k)], gp_ref.at[slot], w_sem.at[slot, 2]),
        ]

    def e_load(l, n):
        slot = n % 2
        es = saved[l][8]
        return load(es.at[column(MP - 1 - n)], pool.at[4 + slot], w_sem.at[slot, 3])

    def late_loads(l):
        _, qs, ks, vs, ms, ls = saved[l][:6]
        return [
            load(qs, q_ref, s_sem.at[3]),
            load(ks, k_ref, s_sem.at[4]),
            load(vs, v_ref, s_sem.at[5]),
            load(ms, mixed_ref, s_sem.at[6]),
            load(ls, lse_ref, s_sem.at[7]),
            load(w_all.at[3 * l, own_z[0]], wa.at[0], s_sem.at[8]),
            load(w_all.at[3 * l, own_z[1]], wa.at[1], s_sem.at[9]),
        ]

    def x_loads(l):
        xs = saved[l][0]
        return [
            load(xs.at[n], pool.at[2 + n // 2, pl.ds(n % 2 * rows, rows)], s_sem.at[14 + n])
            for n in range(4)
        ]

    dy_load = load(dy_in, df_ref, s_sem.at[11])
    table_loads = [load(cos_in, cos_ref, s_sem.at[12]), load(sin_in, sin_ref, s_sem.at[13])]
    dy_load.start()
    for copy in early_loads(n_layers - 1) + [e_load(n_layers - 1, 0)]:
        copy.start()
    for copy in weight_loads(n_layers - 1, 0):
        copy.start()
    for copy in table_loads + late_loads(n_layers - 1):
        copy.start()

    def df_copy(l):
        return remote(df_ref, dfin_ref, c_send.at[l, 0], c_recv.at[l, 0], sibling)

    def da_copy(l):
        return remote(da_ref, dain_ref, c_send.at[l, 1], c_recv.at[l, 1], sibling)

    def du_copy(l, k):
        return remote(
            du_ref.at[k, pl.ds(0, rows)],
            du_ref.at[k, pl.ds(rows, rows)],
            c_send.at[l, 2 + k],
            c_recv.at[l, 2 + k],
            sibling,
        )

    def dxs_copy(l, n):
        return remote(
            dxs_ref.at[n], dxc_in.at[n], c_send.at[l, 6 + n], c_recv.at[l, 6 + n], sibling
        )

    def dxp_copy(l):
        return remote(dxp_ref, dxp_in.at[l], x_send.at[l], x_recv.at[l], pair)

    def one_copy(l, h, k, n):
        return remote(
            t_ref.at[h, k, groups[1 if n == 0 else 3]],
            one_in.at[h, k, n],
            one_send.at[l, h, k, n],
            one_recv.at[l, h, k, n],
            first,
        )

    def two_copy(l, h, k):
        return remote(
            t_ref.at[h, k, groups[2]],
            two_in.at[h, k],
            two_send.at[l, h, k],
            two_recv.at[l, h, k],
            second,
        )

    def z_copy(l, h, k):
        return remote(
            across_ref.at[h] if k == 2 else t_ref.at[h, k, groups[0]],
            z_in.at[l, h, k - 1],
            z_send.at[l, h, k],
            z_recv.at[l, h, k],
            across if k == 2 else pair,
        )

    def span(group):
        return pl.ds(pl.multiple_of(group * 2 * height, 32), 2 * height)

    def a_one_copy(l, i, n):
        return remote(
            ta_ref.at[i, span(groups[1 if n == 0 else 3]), :],
            a_one_in.at[i, n],
            a_send.at[l, i, n],
            a_recv.at[l, i, n],
            first,
        )

    def a_two_copy(l, i):
        return remote(
            ta_ref.at[i, span(groups[2]), :],
            a_two_in.at[i],
            a_send.at[l, i, 2],
            a_recv.at[l, i, 2],
            second,
        )

    def a_z_copy(l, i):
        return remote(
            ta_ref.at[i, span(groups[0]), :],
            a_z_in.at[i],
            a_send.at[l, i, 3],
            a_recv.at[l, i, 3],
            pair if i == 1 else across,
        )

    def a_c_copy(l):
        return remote(a_out_ref, a_c_in.at[l], c_send.at[l, 8], c_recv.at[l, 8], sibling)

    def v_copy(l, n):
        to = (sibling, first, second, columns[0], columns[1], columns[2])[n]
        return remote(
            v_stage.at[l, min(n, 3)], v_in.at[l, n], v_send.at[l, n], v_recv.at[l, n], to
        )

    def step_one(l, h, k):
        for n in range(2):
            one_copy(l, h, k, n).wait_recv()
        g = groups[2]
        t_ref[h, k, g] = (t_ref[h, k, g].astype(F32) + one_in[h, k, 1].astype(F32)).astype(BF16)
        two_copy(l, h, k).start()

    def step_two(l, h, k):
        two_copy(l, h, k).wait_recv()
        g = groups[0]
        total = (
            t_ref[h, k, g].astype(F32) + one_in[h, k, 0].astype(F32) + two_in[h, k].astype(F32)
        )
        if k == 0:
            feed_sum[h] = total
            return
        if k == 2:
            z_copy(l, h, 3).wait_recv()
            if l + 1 < n_layers:
                z_copy(l + 1, h, 2).wait_send()
            across_ref[h] = (total + z_in[l, h, 2].astype(F32)).astype(BF16)
        else:
            t_ref[h, k, g] = total.astype(BF16)
        z_copy(l, h, k).start()

    def step_feed_end(l, h):
        total = feed_sum[h]
        for k in range(1, MP - 1):
            z_copy(l, h, k).wait_recv()
            total = total + z_in[l, h, k - 1].astype(F32)
        if h == 1:
            in_out[l] = total
        else:
            back_out[l] = jnp.transpose(total)

    def feed_sent(l, h):
        for k in range(MP):
            for n in range(2):
                one_copy(l, h, k, n).wait_send()
            two_copy(l, h, k).wait_send()
            if k in (1, 3):
                z_copy(l, h, k).wait_send()

    def step_a_one(l, i):
        for n in range(2):
            a_one_copy(l, i, n).wait_recv()
        at = span(groups[2])
        ta_ref[i, at, :] = (ta_ref[i, at, :].astype(F32) + a_one_in[i, 1].astype(F32)).astype(BF16)
        a_two_copy(l, i).start()

    def step_a_two(l, i):
        a_two_copy(l, i).wait_recv()
        at = span(groups[0])
        total = (
            ta_ref[i, at, :].astype(F32)
            + a_one_in[i, 0].astype(F32)
            + a_two_in[i].astype(F32)
        )
        if i == 1:
            ta_ref[i, at, :] = total.astype(BF16)
            a_z_copy(l, 1).start()
        else:
            a_z_copy(l, 1).wait_recv()
            total = total + a_z_in[1].astype(F32)
            a_sum_ref[...] = total

            @pl.when(c == 1)
            def _():
                ta_ref[i, at, :] = total.astype(BF16)
                a_z_copy(l, 0).start()

    def step_a_z(l):
        @pl.when(c == 1)
        def _():
            a_z_copy(l, 0).wait_recv()
            a_sum_ref[...] = a_z_in[0].astype(F32)

        other = pl.ds(pl.multiple_of((1 - c) * height, 32), height)
        a_out_ref[...] = a_sum_ref[other, :].astype(BF16)
        a_c_copy(l).start()

    def step_a_end(l):
        a_c_copy(l).wait_recv()
        own = pl.ds(pl.multiple_of(c * height, 32), height)
        total = a_sum_ref[own, :] + a_c_in[l].astype(F32)
        tile = [total[:, n * LANES : (n + 1) * LANES] for n in range(6)]
        turned_one = pltpu.roll(tile[1], HD, 1)
        turned_four = pltpu.roll(tile[4], HD, 1)
        for n, (two, one) in enumerate(
            ((tile[0], tile[1]), (tile[2], turned_one), (tile[3], tile[4]))
        ):
            qkv_out[l, n, :, 0:LANES] = two
            qkv_out[l, n, :, LANES:] = one[:, :HD]
        outw_out[l, 0:LANES, :] = jnp.transpose(tile[5])
        outw_out[l, LANES:, :] = jnp.transpose(turned_four)[:HD]

    def a_sent(l, i):
        for n in range(2):
            a_one_copy(l, i, n).wait_send()
        a_two_copy(l, i).wait_send()
        if i == 1:
            a_z_copy(l, 1).wait_send()
        else:

            @pl.when(c == 1)
            def _():
                a_z_copy(l, 0).wait_send()

    def step_v(l, n):
        v_copy(l, n - 1).wait_recv()
        v_stage[l, n] = v_stage[l, n - 1] + v_in[l, n - 1]
        if n < 3:
            v_copy(l, n).start()
        else:
            for s in range(3, 6):
                v_copy(l, s).start()

    def step_v_end(l):
        total = v_stage[l, 3, 0:6, :]
        one = v_stage[l, 3, 6:7, :]
        two = v_stage[l, 3, 10:11, :]
        for s in range(1, MP):
            v_copy(l, 2 + s).wait_recv()
            got = v_in[l, 2 + s]
            total = total + got[0:6, :]
            one = one + got[6 + s : 7 + s, :]
            two = two + got[10 + s : 11 + s, :]
        vec_out[l] = total
        bin_out[l] = one
        turned_one = pltpu.roll(two[:, LANES : 2 * LANES], HD, 1)
        for n, at in enumerate((0, 2, 3)):
            bqkv_out[l, n : n + 1, 0:LANES] = two[:, at * LANES : (at + 1) * LANES]
        bqkv_out[l, 0:1, LANES:] = two[:, LANES : LANES + HD]
        bqkv_out[l, 1:2, LANES:] = turned_one[:, :HD]
        bqkv_out[l, 2:3, LANES:] = two[:, 4 * LANES : 4 * LANES + HD]

    result_copy = remote(low_in, result_out, t_send.at[1], t_recv.at[1], away)
    result_local = pltpu.make_async_copy(low_in, result_out, o_sem.at[1])
    kblock = 256
    for l in reversed(range(n_layers)):
        top = l == n_layers - 1
        vec = vectors[l]
        copies = early_loads(l)
        if top:
            dy_load.wait()
            acc_ref[...] = df_ref[...].astype(F32)
        else:
            dxp_copy(l + 1).wait_send()
        for copy in copies:
            copy.wait()
        v_stage[l, 0] = jnp.zeros((16, width), F32)
        sums = norm_back_rows(acc_ref, r2_ref, df_ref, vec[4:5, :])
        v_stage[l, 0, 4:5, :], v_stage[l, 0, 5:6, :], v_stage[l, 0, 3:4, :] = sums
        if top:
            pl.semaphore_wait(barrier, len(partners))
        df_copy(l).start()
        if top:

            @pl.when(moved)
            def _():
                result_copy.start()

            @pl.when(jnp.logical_not(moved))
            def _():
                result_local.start()

        def turned(source, target, half):
            turn_ref[...] = jnp.transpose(source)
            for g in range(4):
                at = pl.ds(pl.multiple_of((2 * g + c) * height, 32), height)
                target[pl.ds(g * height, height), pl.ds(half * rows, rows)] = turn_ref[at, :]

        turned(df_ref[...], dft_ref, 0)
        turned(h_ref[0], ht_ref, 0)
        turned(h_ref[1], ht_ref, 1)
        if not top:
            feed_sent(l + 1, 0)
            step_v(l + 1, 1)
        df_copy(l).wait_recv()
        turned(dfin_ref[...], dft_ref, 1)

        def back_grads(n, _, l=l):
            e_load(l, n).wait()

            @pl.when(n + 1 < MP)
            def _():
                e_load(l, n + 1).start()

            k = MP - 1 - n
            grad = nn(dft_ref[...], pool[4 + n % 2]).astype(BF16)
            t_ref[0, k] = grad.reshape(4, height, width)
            for to in range(2):
                one_copy(l, 0, k, to).start()
            return 0

        lax.fori_loop(0, MP, back_grads, 0)
        if not top:
            for k in range(MP):
                du_copy(l + 1, k).wait_send()

        def inner(k, _, l=l):
            for copy in weight_loads(l, k):
                copy.wait()

            @pl.when(k + 1 < MP)
            def _():
                for copy in weight_loads(l, k + 1):
                    copy.start()

            slot = k % 2
            de = nn(df_ref[...], pool[2 + slot])
            du = de * gp_ref[slot].astype(F32)
            dbin_ref[k] = jnp.sum(du, axis=0, keepdims=True)
            dub = du.astype(BF16)
            du_ref[k, pl.ds(0, rows), :] = dub
            du_copy(l, k).start()
            acc_ref[...] += nt(dub, pool[slot])
            return 0

        lax.fori_loop(0, MP, inner, 0)
        for copy in x_loads(l):
            copy.start()
        for k in range(MP):
            v_stage[l, 0, 6 + k : 7 + k, :] = dbin_ref[k]
        if not top:
            step_a_one(l + 1, 0)
            for h in range(2):
                step_feed_end(l + 1, h)
            step_v(l + 1, 2)
            da_copy(l + 1).wait_send()
        for k in (3, 2, 1, 0):
            step_one(l, 0, k)
        sums = norm_back_rows(acc_ref, r1_ref, da_ref, vec[1:2, :])
        v_stage[l, 0, 1:2, :], v_stage[l, 0, 2:3, :], v_stage[l, 0, 0:1, :] = sums
        da_copy(l).start()
        if not top:
            feed_sent(l + 1, 1)

        def in_grads(n, _, l=l):
            k = MP - 1 - n
            du_copy(l, k).wait_recv()
            grad = nn(ht_ref[...], du_ref[k]).astype(BF16)
            t_ref[1, k] = grad.reshape(4, height, width)
            for to in range(2):
                one_copy(l, 1, k, to).start()
            return 0

        lax.fori_loop(0, MP, in_grads, 0)
        if not top:
            step_a_two(l + 1, 0)
            step_v(l + 1, 3)
        for k in (3, 1, 0):
            step_two(l, 0, k)
        for copy in late_loads(l):
            copy.wait()
        da_copy(l).wait_recv()
        low_half = lane_index((rows, LANES)) < HD
        for half, source in enumerate((da_ref, dain_ref)):
            at = pl.ds(half * rows, rows)
            for i in range(2):
                dz = nn(source[...], wa[i, :, 4 * LANES :])
                dz_ref[i, 0, at, :] = dz[:, LANES:].astype(BF16)
                dz_ref[i, 1, at, :] = jnp.where(
                    low_half, pltpu.roll(dz[:, :LANES], HD, 1), 0.0
                ).astype(BF16)
            pool[6, :, pl.ds(half * rows, rows)] = jnp.transpose(source[...])
        for i in range(2):
            dwo_ref[i] = nn(pool[6], mixed_ref[:, i * 256 : i * 256 + 256]).astype(BF16)
            head_deltas(i, mixed_ref, dz_ref, delta_ref)
        for copy in x_loads(l):
            copy.wait()
        for half in range(2):
            pool[half] = jnp.transpose(pool[2 + half])
        if top:
            for copy in table_loads:
                copy.wait()
        steps = [[] for _ in range(6)]
        if not top:
            steps[0] = [partial(step_v_end, l + 1), partial(step_a_z, l + 1)]
            steps[1] = [partial(step_a_end, l + 1)]
        steps[1].append(partial(step_two, l, 0, 2))
        steps[1] += [partial(step_one, l, 1, k) for k in (3, 2, 1, 0)]
        steps[3] = [partial(step_two, l, 1, k) for k in (3, 1, 0)]
        steps[4] = [partial(step_two, l, 1, 2), partial(step_a_one, l, 1)]
        steps[5] = [partial(step_a_two, l, 1)]

        def weight_grads(i, l=l, top=top):
            if not top:
                a_sent(l + 1, i)
                if i == 0:
                    a_c_copy(l + 1).wait_send()
            low = [pool.at[2 + 2 * i + half] for half in range(2)]
            ta_ref[i, :, 0:LANES] = nn(pool[0], low[0][:, 0:LANES]).astype(BF16)
            more = nn(pool[0], low[0][:, LANES : 5 * LANES]) + nn(
                pool[1], low[1][:, LANES : 5 * LANES]
            )
            ta_ref[i, :, LANES : 4 * LANES] = more[:, : 3 * LANES].astype(BF16)
            ta_ref[i, :, 4 * LANES : 5 * LANES] = (
                more[:, 3 * LANES :] + dwo_ref[i, :, 0:LANES].astype(F32)
            ).astype(BF16)
            ta_ref[i, :, 5 * LANES :] = dwo_ref[i, :, LANES:]
            for n in range(2):
                a_one_copy(l, i, n).start()

        for turn, i in enumerate((1, 0)):
            for h in range(3):
                head_back(
                    i,
                    h,
                    kblock,
                    q_ref,
                    k_ref,
                    v_ref,
                    dz_ref,
                    lse_ref,
                    delta_ref,
                    qrow_ref,
                    kcol_ref,
                    pair_ref,
                    dqt_ref,
                    dt_ref,
                )
                for step in steps[3 * turn + h]:
                    step()
            for tile in range(5):
                total = jnp.zeros((1, LANES), F32)
                for half in range(1 if tile == 0 else 2):
                    at = pl.ds(half * queries, queries)
                    t = dt_ref[tile, at, :]
                    if tile < 3:
                        t = t * cos_ref[at, :] - half_swap(t) * sin_ref[at, :]
                    total = total + jnp.sum(t, axis=0, keepdims=True)
                    pool[2 + 2 * i + half, :, tile * LANES : (tile + 1) * LANES] = t.astype(BF16)
                for core in range(2):
                    v_stage[
                        l, 0, 10 + 2 * core + i : 11 + 2 * core + i, tile * LANES : (tile + 1) * LANES
                    ] = jnp.where(c == core, total, 0.0)
            if i == 1:
                weight_grads(1)
        v_copy(l, 0).start()

        def spread(n):
            half, at = n // 2, pl.ds((n % 2) * rows, rows)
            total = jnp.zeros((rows, width), F32)
            for i in range(2):
                low = pool.at[2 + 2 * i + half]
                total = total + nt(low[at, LANES : 5 * LANES], wa[i, :, LANES : 5 * LANES])
                if half == 0:
                    total = total + nt(low[at, 0:LANES], wa[i, :, 0:LANES])
            return total

        df_copy(l).wait_send()
        dxs_ref[1] = spread(3).astype(BF16)
        dxs_copy(l, 1).start()
        part_ref[...] = spread(2)
        dxs_copy(l, 1).wait_recv()
        dxp_ref[...] = (part_ref[...] + dxc_in[1].astype(F32)).astype(BF16)
        dxp_copy(l).start()
        dxs_ref[0] = spread(1).astype(BF16)
        dxs_copy(l, 0).start()
        acc_ref[...] += spread(0)
        weight_grads(0)
        dxs_copy(l, 0).wait_recv()
        acc_ref[...] += dxc_in[0].astype(F32)
        if l > 0:
            for n in range(2):
                dxs_copy(l, n).wait_send()
            first_loads = early_loads(l - 1) + [e_load(l - 1, 0)] + weight_loads(l - 1, 0)
            for copy in first_loads + late_loads(l - 1):
                copy.start()
        dxp_copy(l).wait_recv()
        acc_ref[...] += dxp_in[l].astype(F32)

    dxp_copy(0).wait_send()
    df_ref[...] = acc_ref[...].astype(BF16)
    back_copy = remote(df_ref, back_in, t_send.at[0], t_recv.at[0], away)

    @pl.when(moved)
    def _():
        back_copy.start()

    step_v(0, 1)
    for h in range(2):
        step_feed_end(0, h)
    step_a_one(0, 0)
    step_v(0, 2)
    step_a_two(0, 0)
    step_v(0, 3)
    step_v_end(0)

    @pl.when(moved)
    def _():
        back_copy.wait_recv()
        acc_ref[...] = back_in[...].astype(F32)

    out_copy = pltpu.make_async_copy(acc_ref, tokens_out, o_sem.at[0])
    out_copy.start()
    step_a_z(0)
    step_a_end(0)
    out_copy.wait()

    @pl.when(moved)
    def _():
        back_copy.wait_send()
        result_copy.wait_send()
        result_copy.wait_recv()

    @pl.when(jnp.logical_not(moved))
    def _():
        result_local.wait()

    da_copy(0).wait_send()
    for n in range(2):
        dxs_copy(0, n).wait_send()
    for k in range(MP):
        du_copy(0, k).wait_send()
    for h in range(2):
        feed_sent(0, h)
        z_copy(0, h, 2).wait_send()
    for i in range(2):
        a_sent(0, i)
    a_c_copy(0).wait_send()
    for l in range(n_layers):
        for n in range(6):
            v_copy(l, n).wait_send()


def backward(w_all, dy, cos, sin, low, qrow, kcol, vectors, states):
    n_layers, _, width = vectors.shape
    rows = dy.shape[0]
    height = width // 8
    queries, keys = 2 * rows, 4 * rows
    sem = pltpu.SemaphoreType.DMA
    flat = [array for state in states for array in state]
    return pl.pallas_call(
        partial(backward_kernel, n_layers),
        out_shape=(
            shape((rows, width), F32),
            shape((rows, width), BF16),
            shape((n_layers, 3, height, 3 * HD), F32),
            shape((n_layers, 3, 3 * HD), F32),
            shape((n_layers, 3 * HD, height), F32),
            shape((n_layers, 6, width), F32),
            shape((n_layers, height, width), F32),
            shape((n_layers, 1, width), F32),
            shape((n_layers, width, height), F32),
        ),
        in_specs=[anywhere()] * 5 + [vmem()] * 3 + [anywhere()] * len(flat),
        out_specs=(anywhere(), anywhere()) + (vmem(),) * 7,
        scratch_shapes=[
            pltpu.VMEM((7, width, width), BF16),
            pltpu.VMEM((2, rows, width), BF16),
            pltpu.VMEM((rows, width), F32),
            pltpu.VMEM((rows, width), F32),
            pltpu.VMEM((rows, width), F32),
            pltpu.VMEM((rows, width), BF16),
            pltpu.VMEM((rows, width), BF16),
            pltpu.VMEM((rows, width), BF16),
            pltpu.VMEM((rows, width), BF16),
            pltpu.VMEM((2, rows, width), BF16),
            pltpu.VMEM((width, rows), BF16),
            pltpu.VMEM((4 * height, 2 * rows), BF16),
            pltpu.VMEM((4 * height, 2 * rows), BF16),
            pltpu.VMEM((MP, 2 * rows, width), BF16),
            pltpu.VMEM((2, MP, 4, height, width), BF16),
            pltpu.VMEM((2, MP, 2, height, width), BF16),
            pltpu.VMEM((2, MP, height, width), BF16),
            pltpu.VMEM((n_layers, 2, MP - 1, height, width), BF16),
            pltpu.VMEM((2, width, 2 * LANES), BF16),
            pltpu.VMEM((2, width, width), BF16),
            pltpu.VMEM((2, 2, 2 * height, width), BF16),
            pltpu.VMEM((2, 2 * height, width), BF16),
            pltpu.VMEM((2, 2 * height, width), BF16),
            pltpu.VMEM((n_layers, height, width), BF16),
            pltpu.VMEM((2 * height, width), F32),
            pltpu.VMEM((height, width), BF16),
            pltpu.VMEM((2, width, width), BF16),
            pltpu.VMEM((2, 2, queries, LANES), BF16),
            pltpu.VMEM((2, 2, keys, LANES), BF16),
            pltpu.VMEM((2, 2, keys, LANES), BF16),
            pltpu.VMEM((queries, 512), BF16),
            pltpu.VMEM((8, queries), F32),
            pltpu.VMEM((8, queries), F32),
            pltpu.VMEM((2, 2, queries, LANES), BF16),
            pltpu.VMEM((5, keys, LANES), F32),
            pltpu.VMEM((LANES, queries), F32),
            pltpu.VMEM((2, queries, LANES), BF16),
            pltpu.VMEM((keys, LANES), F32),
            pltpu.VMEM((keys, LANES), F32),
            pltpu.VMEM((2, rows, width), BF16),
            pltpu.VMEM((n_layers, rows, width), BF16),
            pltpu.VMEM((rows, width), BF16),
            pltpu.VMEM((n_layers, 4, 16, width), F32),
            pltpu.VMEM((n_layers, 6, 16, width), F32),
            pltpu.VMEM((MP, 1, width), F32),
            pltpu.VMEM((2, height, width), BF16),
            pltpu.VMEM((2, height, width), F32),
            sem((n_layers, 9)),
            sem((n_layers, 9)),
            sem((n_layers, 2, MP, 2)),
            sem((n_layers, 2, MP, 2)),
            sem((n_layers, 2, MP)),
            sem((n_layers, 2, MP)),
            sem((n_layers, 2, MP)),
            sem((n_layers, 2, MP)),
            sem((n_layers, 2, 4)),
            sem((n_layers, 2, 4)),
            sem((n_layers,)),
            sem((n_layers,)),
            sem((n_layers, 6)),
            sem((n_layers, 6)),
            sem((2,)),
            sem((2,)),
            sem((2, 4)),
            sem((18,)),
            sem((2,)),
        ],
        compiler_params=pltpu.CompilerParams(
            vmem_limit_bytes=BACK_LIMIT, collective_id=1, has_side_effects=True
        ),
        cost_estimate=pl.CostEstimate(
            flops=200_000_000_000, bytes_accessed=100_000_000, transcendentals=20_000_000
        ),
        name="backward",
    )(w_all, dy, cos, sin, low, qrow, kcol, vectors, *flat)


def attend_kernel(chunk, *refs):
    scal, x_ref, bias_ref, cos_ref, sin_ref, qcode_ref, kcode_ref, w_all = refs[:8]
    q_ref, k_ref, v_ref, mixed_ref, lse_ref, w_ref, lse_cols, sems = refs[8:]
    copies = [
        pltpu.make_async_copy(
            w_all.at[chunk, scal[k], :, pl.ds(0, 5 * LANES)], w_ref.at[k], sems.at[k]
        )
        for k in range(2)
    ]
    for copy in copies:
        copy.start()
    for copy in copies:
        copy.wait()
    rows = x_ref.shape[1]
    for i in range(4):
        at = pl.ds(i * rows, rows)
        for k in range(2):
            project_rows(
                i,
                k,
                x_ref[i],
                w_ref,
                bias_ref[k],
                cos_ref[at, :],
                sin_ref[at, :],
                q_ref,
                k_ref,
                v_ref,
            )
    lse_cols[...] = jnp.zeros_like(lse_cols)

    def one_block(i, _):
        attend_rows(i, 256, qcode_ref, kcode_ref, q_ref, k_ref, v_ref, mixed_ref, lse_cols)
        return 0

    lax.fori_loop(0, 2 * rows // 256, one_block, 0)
    lse_ref[...] = jnp.transpose(lse_cols[...])[0:8, :]


def attend(scal, x_full, bias, tables, qcode, kcode, w_all, chunk):
    cos, sin = tables[:2]
    _, rows, width = x_full.shape
    queries, keys = 2 * rows, 4 * rows
    return pl.pallas_call(
        partial(attend_kernel, chunk),
        out_shape=(
            shape((2, 2, queries, LANES), BF16),
            shape((2, 2, keys, LANES), BF16),
            shape((2, 2, keys, LANES), BF16),
            shape((queries, 512), BF16),
            shape((8, queries), F32),
        ),
        in_specs=[smem()] + [vmem()] * 6 + [anywhere()],
        out_specs=(vmem(),) * 5,
        scratch_shapes=[
            pltpu.VMEM((2, width, 5 * LANES), BF16),
            pltpu.VMEM((queries, LANES), F32),
            pltpu.SemaphoreType.DMA((2,)),
        ],
        compiler_params=params(),
        name="attend",
    )(scal, x_full, bias, cos, sin, qcode, kcode, w_all)


def feed_kernel(chunk, *refs):
    scal, x_ref, own_ref, sib_ref, vec_ref, bin_ref, w_all = refs[:7]
    next_ref, low_ref, r1_ref, r2_ref, e_ref, gp_ref, wo_ref, win_ref, wback_ref, sems = refs[7:]
    copies = [
        pltpu.make_async_copy(
            w_all.at[chunk, :, :, pl.ds(4 * LANES, 2 * LANES)], wo_ref, sems.at[0]
        ),
        pltpu.make_async_copy(w_all.at[chunk + 1], win_ref, sems.at[1]),
        pltpu.make_async_copy(w_all.at[chunk + 2], wback_ref, sems.at[2]),
    ]
    for copy in copies:
        copy.start()
    for copy in copies:
        copy.wait()
    a = jnp.zeros(x_ref.shape, F32)
    for k in range(2):
        a = a + nt(own_ref[:, k * 256 : k * 256 + 256], wo_ref[scal[k]])
        a = a + nt(sib_ref[:, k * 256 : k * 256 + 256], wo_ref[lax.rem(scal[k] + 2, MP)])
    r1 = x_ref[...] + a + vec_ref[0:1, :]
    r1_ref[...] = r1
    n1, _ = norm_parts(r1)
    h = n1 * vec_ref[1:2, :] + vec_ref[2:3, :]
    low_ref[...] = h.astype(BF16)
    r2_ref[...] = h + vec_ref[3:4, :]

    def one(z, _):
        u = nn(low_ref[...], win_ref[z]) + bin_ref[z]
        cdf = 0.5 * (1.0 + lax.erf(u * (2.0**-0.5)))
        pdf = jnp.exp(u * u * -0.5) * 0.3989422804014327
        e = (u * cdf).astype(BF16)
        e_ref[z] = e
        gp_ref[z] = (cdf + u * pdf).astype(BF16)
        r2_ref[...] += nt(e, wback_ref[z])
        return 0

    lax.fori_loop(0, MP, one, 0)
    n2, _ = norm_parts(r2_ref[...])
    result = n2 * vec_ref[4:5, :] + vec_ref[5:6, :]
    next_ref[...] = result
    low_ref[...] = result.astype(BF16)


def feed_forward(scal, x, own, sib, vec, bias_in, w_all, chunk):
    rows, width = x.shape
    return pl.pallas_call(
        partial(feed_kernel, chunk),
        out_shape=(
            shape((rows, width), F32),
            shape((rows, width), BF16),
            shape((rows, width), F32),
            shape((rows, width), F32),
            shape((MP, rows, width), BF16),
            shape((MP, rows, width), BF16),
        ),
        in_specs=[smem()] + [vmem()] * 5 + [anywhere()],
        out_specs=(vmem(),) * 6,
        scratch_shapes=[
            pltpu.VMEM((MP, width, 2 * LANES), BF16),
            pltpu.VMEM((MP, width, width), BF16),
            pltpu.VMEM((MP, width, width), BF16),
            pltpu.SemaphoreType.DMA((3,)),
        ],
        compiler_params=params(),
        name="feed",
    )(scal, x, own, sib, vec, bias_in, w_all)


def plain_forward(blocks, tokens, cot, small, meta, frequency, vectors):
    n_layers = vectors.shape[0]
    rows, width = tokens.shape
    c, z = lax.axis_index("dp") % 2, lax.axis_index("mp")
    w_all = lax.all_gather(blocks, "dp", axis=1, tiled=True)
    w_all = jnp.swapaxes(lax.all_gather(w_all, "mp", axis=0, tiled=False), 0, 1)
    small_all = lax.all_gather(small, "mp", axis=0, tiled=False)
    own_z = jnp.stack([(z - 2 * c - k) % MP for k in range(2)]).astype(jnp.int32)
    info = jnp.where(z // 2 == c, meta, core_swap(meta))
    place = z % 2
    quarters = [2 * c + place, 2 * (1 - c) + place, 2 * c + 1 - place, 2 * (1 - c) + 1 - place]
    positions = jnp.concatenate(
        [q * rows + jnp.arange(rows, dtype=jnp.int32) for q in quarters]
    ).astype(F32)
    slot = info[0, 0]
    seq = jnp.where(positions >= slot, 1.0, 0.0) + jnp.where(positions >= 2.0 * slot, 1.0, 0.0)
    place = positions - seq * slot
    limit = jnp.where(seq == 0.0, info[1, 0], jnp.where(seq == 1.0, info[2, 0], info[3, 0]))
    kcode = jnp.where(place < limit, seq, -1.0)
    qcode = seq[: 2 * rows]
    angles = place[:, None] * frequency
    sign = jnp.where(jnp.arange(LANES) % HD < HD // 2, -1.0, 1.0)
    cos, sin = jnp.cos(angles), jnp.sin(angles) * sign[None, :]
    low = relayout(tokens)
    stream = low.astype(F32)
    states = []
    for l in range(n_layers):
        two = jnp.stack([low, pair_swap(low)])
        others = core_swap(two)
        x_full = jnp.stack([two[0], others[0], two[1], others[1]])
        bias = jnp.stack(
            [
                lax.dynamic_index_in_dim(small_all, own_z[k], 0, False)[l : l + 1, : 5 * LANES]
                for k in range(2)
            ]
        )
        q, k, v, mixed, lse = attend(
            own_z, x_full, bias, (cos, sin), qcode[:, None], kcode[None, :], w_all, 3 * l
        )
        other = core_swap(mixed[rows:])
        stream, low, r1, r2, e, gp = feed_forward(
            own_z,
            stream,
            mixed[:rows],
            other,
            vectors[l],
            small_all[:, l : l + 1, 5 * LANES :],
            w_all,
            3 * l,
        )
        states.append((x_full, q, k, v, mixed, other, lse, r1, r2, e, gp))
    return (w_all, relayout(cot), low, cos, sin, qcode[None, :], kcode[:, None]), states


def feed_back_kernel(n_pieces, rows, chunk, *refs):
    scal, dy_ref, r1_ref, r2_ref, e_ref, gp_ref, own_ref, sib_ref, vec_ref, w_all = refs[:10]
    at = 10
    dr1_ref, dzown_ref, dzsib_ref, dvec_ref, dbin_ref = refs[at : at + 5]
    outs = 2 if n_pieces == 8 else 1
    grads = refs[at + 5 : at + 5 + outs]
    wo_ref, win_ref, wback_ref, df_ref, dft_ref, ht_ref, dw_ref, sems = refs[at + 5 + outs :]
    width = dy_ref.shape[1]
    columns = [scal[n_pieces + k] for k in range(MP)]
    first_z = scal[n_pieces + MP]

    def fetch(source, target, base):
        copies = [
            pltpu.make_async_copy(source(columns[k]), target.at[k], sems.at[base + k])
            for k in range(MP)
        ]
        for copy in copies:
            copy.start()
        return copies

    back_copies = fetch(lambda z: w_all.at[chunk + 2, z], wback_ref, 0)
    in_copies = fetch(lambda z: w_all.at[chunk + 1, z], win_ref, MP)
    out_copies = fetch(
        lambda z: w_all.at[chunk, z, :, pl.ds(4 * LANES, 2 * LANES)], wo_ref, 2 * MP
    )
    dy = dy_ref[...]
    n2, scale2 = norm_parts(r2_ref[...])
    dvec_ref[4:5, :] = jnp.sum(dy * n2, axis=0, keepdims=True)
    dvec_ref[5:6, :] = jnp.sum(dy, axis=0, keepdims=True)
    dr2 = norm_back(dy, n2, scale2, vec_ref[4:5, :])
    dvec_ref[3:4, :] = jnp.sum(dr2, axis=0, keepdims=True)
    dr1_ref[...] = dr2
    df = dr2.astype(BF16)
    df_ref[...] = df
    dft_ref[...] = jnp.transpose(df)
    n1, _ = norm_parts(r1_ref[...])
    h = (n1 * vec_ref[1:2, :] + vec_ref[2:3, :]).astype(BF16)
    ht_ref[...] = jnp.transpose(h)
    for copy in back_copies + in_copies:
        copy.wait()

    def one(z, _):
        de = nn(df_ref[...], wback_ref[z])
        at = scal[n_pieces + z]
        du = de * gp_ref[at].astype(F32)
        dbin_ref[z] = jnp.sum(du, axis=0, keepdims=True)
        dub = du.astype(BF16)
        dr1_ref[...] += nt(dub, win_ref[z])
        dw_ref[z, :, 0:width] = nn(ht_ref[...], dub).astype(BF16)
        dw_ref[z, :, width : 2 * width] = nn(dft_ref[...], e_ref[at]).astype(BF16)
        return 0

    lax.fori_loop(0, MP, one, 0)
    dh = dr1_ref[...]
    n1, scale1 = norm_parts(r1_ref[...])
    dvec_ref[1:2, :] = jnp.sum(dh * n1, axis=0, keepdims=True)
    dvec_ref[2:3, :] = jnp.sum(dh, axis=0, keepdims=True)
    dr1 = norm_back(dh, n1, scale1, vec_ref[1:2, :])
    dvec_ref[0:1, :] = jnp.sum(dr1, axis=0, keepdims=True)
    dr1_ref[...] = dr1
    da = dr1.astype(BF16)
    dft_ref[...] = jnp.transpose(da)
    for copy in out_copies:
        copy.wait()
    used = lane_index((da.shape[0], 2 * LANES)) >= HD
    for z in range(2):
        for mixed_ref, dz_ref, z_at in (
            (own_ref, dzown_ref, first_z + z),
            (sib_ref, dzsib_ref, 2 - first_z + z),
        ):
            part = mixed_ref[:, z * 256 : z * 256 + 256]
            dw_ref[z_at, :, 2 * width :] = nn(dft_ref[...], part).astype(BF16)
            dz = nn(da, wo_ref[z_at])
            dz_ref[:, z * 256 : z * 256 + 256] = jnp.where(used, dz, 0.0).astype(BF16)
    flight = []
    for i in range(n_pieces):
        offset = pl.multiple_of(scal[i], 32)
        target = grads[i // 4].at[PIECE_ORDER[i % 4] if n_pieces == 8 else 0]
        copy = pltpu.make_async_copy(dw_ref.at[:, pl.ds(offset, rows), :], target, sems.at[i])
        copy.start()
        flight.append(copy)
    for copy in flight:
        copy.wait()


PIECE_ORDER = (3, 0, 2, 1)


def feed_back(scal, prows, count, dy, r1, r2, e, gp, own, sib, vec, w_all, chunk):
    rows, width = dy.shape
    lanes = 2 * width + 2 * LANES
    grads = (shape((4, MP, prows, lanes), BF16),) * 2
    if count != 8:
        grads = (shape((1, MP, prows, lanes), BF16),)
    return pl.pallas_call(
        partial(feed_back_kernel, count, prows, chunk),
        out_shape=(
            shape((rows, width), F32),
            shape((rows, 512), BF16),
            shape((rows, 512), BF16),
            shape((6, width), F32),
            shape((MP, 1, width), F32),
            *grads,
        ),
        in_specs=[smem()] + [vmem()] * 8 + [anywhere()],
        out_specs=(vmem(),) * 5 + (anywhere(),) * len(grads),
        scratch_shapes=[
            pltpu.VMEM((MP, width, 2 * LANES), BF16),
            pltpu.VMEM((MP, width, width), BF16),
            pltpu.VMEM((MP, width, width), BF16),
            pltpu.VMEM((rows, width), BF16),
            pltpu.VMEM((width, rows), BF16),
            pltpu.VMEM((width, rows), BF16),
            pltpu.VMEM((MP, width, lanes), BF16),
            pltpu.SemaphoreType.DMA((3 * MP,)),
        ],
        compiler_params=params(),
        cost_estimate=pl.CostEstimate(
            flops=16_000_000_000, bytes_accessed=40_000_000, transcendentals=0
        ),
        name="feed_back",
    )(scal, dy, r1, r2, e, gp, own, sib, vec, w_all)


def attend_back_kernel(n_pieces, chunk, *refs):
    (
        scal,
        x_ref,
        cos_ref,
        sin_ref,
        qcode_ref,
        kcode_ref,
        q_ref,
        k_ref,
        v_ref,
        mixed_ref,
        dzown_ref,
        dzsib_ref,
        lse_ref,
        w_all,
    ) = refs[:14]
    dx_ref, dxs_ref, dbias_ref, parts_ref = refs[14:18]
    (
        w_ref,
        xt_ref,
        dz_ref,
        delta_ref,
        dt_ref,
        dqt_ref,
        pair_ref,
        dw_ref,
        low_ref,
        sums_ref,
        sems,
    ) = refs[18:]
    copies = [
        pltpu.make_async_copy(
            w_all.at[chunk, scal[n_pieces + 9 + k], :, pl.ds(0, 5 * LANES)],
            w_ref.at[k],
            sems.at[k],
        )
        for k in range(2)
    ]
    for copy in copies:
        copy.start()
    keys, width = x_ref.shape
    queries = keys // 2
    block = queries // 2
    for z in range(2):
        for half, source in enumerate((dzown_ref, dzsib_ref)):
            at = pl.ds(half * block, block)
            dz_ref[z, 0, at, :] = source[:, z * 256 + LANES : z * 256 + 256]
            dz_ref[z, 1, at, :] = pltpu.roll(
                source[:, z * 256 : z * 256 + LANES].astype(F32), HD, 1
            ).astype(BF16)
        single = pltpu.roll(mixed_ref[:, z * 256 : z * 256 + LANES].astype(F32), HD, 1)
        pair = mixed_ref[:, z * 256 + LANES : z * 256 + 256].astype(F32)
        prod_one = jnp.transpose(pair * dz_ref[z, 0].astype(F32))
        prod_two = jnp.transpose(single * dz_ref[z, 1].astype(F32))
        delta_ref[3 * z : 3 * z + 1, :] = jnp.sum(prod_one[0:HD], axis=0, keepdims=True)
        delta_ref[3 * z + 1 : 3 * z + 2, :] = jnp.sum(prod_one[HD:], axis=0, keepdims=True)
        delta_ref[3 * z + 2 : 3 * z + 3, :] = jnp.sum(prod_two[0:HD], axis=0, keepdims=True)

    kblock = 256
    low_q = lane_index((queries, LANES)) < HD
    low_k = lane_index((kblock, LANES)) < HD
    for z in range(2):
        for h in range(3):
            tile = h // 2
            q = q_ref[z, tile]
            dz = dz_ref[z, tile]
            if h < 2:
                keep = low_q == (h == 0)
                q = jnp.where(keep, q, BF16(0))
                dz = jnp.where(keep, dz, BF16(0))
            pair_ref[0] = q
            pair_ref[1] = dz
            lse = lse_ref[3 * z + h : 3 * z + h + 1, :]
            delta = delta_ref[3 * z + h : 3 * z + h + 1, :]
            if h != 1:
                dqt_ref[...] = jnp.zeros_like(dqt_ref)

            def one_block(i, _, z=z, h=h, tile=tile, lse=lse, delta=delta):
                at = pl.ds(pl.multiple_of(i * kblock, kblock), kblock)
                kb = k_ref[z, tile, at, :]
                vb = v_ref[z, tile, at, :]
                if h < 2:
                    kb_own = jnp.where(low_k == (h == 0), kb, BF16(0))
                else:
                    kb_own = kb
                visible = kcode_ref[at, :] == qcode_ref[...]
                s = nt(kb, pair_ref[0])
                s = jnp.where(visible, s, NEGATIVE)
                p = jnp.exp(s - lse)
                dp = nt(vb, pair_ref[1])
                ds = (p * (dp - delta)).astype(BF16)
                dv = nn(p.astype(BF16), pair_ref[1])
                dk = nn(ds, pair_ref[0])
                dqt_ref[...] += nn(jnp.transpose(kb_own), ds)
                if h == 1:
                    dt_ref[2, at, :] += dk
                    dt_ref[3, at, :] += dv
                elif h == 0:
                    dt_ref[2, at, :] = dk
                    dt_ref[3, at, :] = dv
                else:
                    dt_ref[1, at, :] = pltpu.roll(dk, HD, 1)
                    dt_ref[4, at, :] = dv
                return 0

            lax.fori_loop(0, keys // kblock, one_block, 0)
            if h >= 1:
                dq = jnp.transpose(dqt_ref[...]) * HD**-0.5
                if h == 1:
                    dt_ref[0, 0:queries, :] = dq
                else:
                    dt_ref[1, 0:queries, :] += dq

        if z == 0:
            xt_ref[...] = jnp.transpose(x_ref[...])
            for copy in copies:
                copy.wait()
        for tile in range(5):
            count = queries if tile == 0 else keys
            t = dt_ref[tile, 0:count, :]
            if tile < 3:
                t = t * cos_ref[0:count, :] - half_swap(t) * sin_ref[0:count, :]
            dbias_ref[z, :, tile * LANES : (tile + 1) * LANES] = jnp.sum(t, axis=0, keepdims=True)
            low_ref[0:count, tile * LANES : (tile + 1) * LANES] = t.astype(BF16)
        dw_ref[z, :, 0:LANES] = nn(
            xt_ref[:, 0:queries], low_ref[0:queries, 0:LANES]
        ).astype(BF16)
        dw_ref[z, :, LANES:] = nn(xt_ref[...], low_ref[:, LANES:]).astype(BF16)
        for i in range(4):
            at = pl.ds(i * block, block)
            part = nt(low_ref[at, LANES:], w_ref[z, :, LANES : 5 * LANES])
            if i < 2:
                part = part + nt(low_ref[at, 0:LANES], w_ref[z, :, 0:LANES])
            if z == 0:
                sums_ref[i] = part
            else:
                target = dx_ref if i % 2 == 0 else dxs_ref
                target[i // 2] = (sums_ref[i] + part).astype(BF16)

    flight = []
    for i in range(min(n_pieces, 4)):
        offset = pl.multiple_of(scal[n_pieces + 5 + i], 32)
        copy = pltpu.make_async_copy(
            dw_ref.at[:, pl.ds(offset, parts_ref.shape[2]), :],
            parts_ref.at[PIECE_ORDER[i] if n_pieces == 8 else 0],
            sems.at[i],
        )
        copy.start()
        flight.append(copy)
    for copy in flight:
        copy.wait()


def attend_back(scal, prows, count, x_full, tables, saved, mixed, dz_own, dz_sib, w_all, chunk):
    cos, sin, qcode, kcode = tables
    q, k, v, lse = saved
    keys, width = x_full.shape
    queries = keys // 2
    block = queries // 2
    parts = (4, 2, 2 * prows, 5 * LANES)
    if count != 8:
        parts = (1, 2, prows, 5 * LANES)
    return pl.pallas_call(
        partial(attend_back_kernel, count, chunk),
        out_shape=(
            shape((2, block, width), BF16),
            shape((2, block, width), BF16),
            shape((2, 1, 5 * LANES), F32),
            shape(parts, BF16),
        ),
        in_specs=[smem()] + [vmem()] * 12 + [anywhere()],
        out_specs=(vmem(),) * 3 + (anywhere(),),
        scratch_shapes=[
            pltpu.VMEM((2, width, 5 * LANES), BF16),
            pltpu.VMEM((width, keys), BF16),
            pltpu.VMEM((2, 2, queries, LANES), BF16),
            pltpu.VMEM((8, queries), F32),
            pltpu.VMEM((5, keys, LANES), F32),
            pltpu.VMEM((LANES, queries), F32),
            pltpu.VMEM((2, queries, LANES), BF16),
            pltpu.VMEM((2, width, 5 * LANES), BF16),
            pltpu.VMEM((keys, 5 * LANES), BF16),
            pltpu.VMEM((4, block, width), F32),
            pltpu.SemaphoreType.DMA((4,)),
        ],
        compiler_params=params(),
        cost_estimate=pl.CostEstimate(
            flops=40_000_000_000, bytes_accessed=20_000_000, transcendentals=8_000_000
        ),
        name="attend_back",
    )(scal, x_full, cos, sin, qcode, kcode, q, k, v, mixed, dz_own, dz_sib, lse, w_all)


def head_tiles(q, k, v, o):
    return jnp.concatenate(
        [
            q[..., :LANES],
            q[..., LANES:],
            k[..., LANES:],
            k[..., :LANES],
            v[..., :LANES],
            v[..., LANES:],
            o[..., LANES:],
            o[..., :LANES],
        ],
        axis=-1,
    )


def head_columns(t):
    q = jnp.concatenate([t[..., 0:128], t[..., 128:192]], axis=-1)
    k = jnp.concatenate([t[..., 256:384], t[..., 192:256]], axis=-1)
    v = jnp.concatenate([t[..., 384:512], t[..., 512:576]], axis=-1)
    return q, k, v


def per_device(
    tokens, w_qkv, b_qkv, w_out, vectors, w_in, b_in, w_back, cotangent, lengths, buckets
):
    layers = w_qkv.shape[0]
    rows, width = tokens.shape
    d = lax.axis_index("dp")
    z = lax.axis_index("mp")
    g, c = d // 2, d % 2

    blocks = []
    for l in range(layers):
        low = w_qkv[l].astype(BF16)
        blocks.append(head_tiles(low[0], low[1], low[2], w_out[l].astype(BF16).T))
        blocks.append(w_in[l].astype(BF16))
        blocks.append(w_back[l].astype(BF16).T)
    blocks = jnp.stack(blocks)
    height = w_qkv.shape[2]
    pieces = 8 if lax.axis_size("dp") == 8 else 1
    piece_rows = height if pieces == 8 else width

    small = jnp.concatenate(
        [
            b_qkv[:, 0],
            b_qkv[:, 1, LANES:],
            b_qkv[:, 1, :LANES],
            b_qkv[:, 2],
            jnp.zeros((layers, HD), F32),
            b_in,
        ],
        axis=-1,
    )
    small = jnp.pad(small, ((0, 8 - layers), (0, 0)))
    slot = LEN_MAX // (3 - buckets)
    meta = jnp.concatenate([slot, lengths[0]]).astype(F32)
    meta = jnp.broadcast_to(jnp.pad(meta, (0, 4))[:, None], (8, LANES))
    exponents = jnp.arange(LANES, dtype=jnp.int32) % (HD // 2)
    frequency = 10000.0 ** (-2.0 * exponents.astype(F32) / HD)[None, :]

    if pieces == 8:
        head, states = forward(blocks, tokens, cotangent, small, meta, frequency, vectors)
        w_all, dy, low, cos, sin, qrow, kcol = head
        grads = backward(w_all, dy, cos, sin, low, qrow, kcol, vectors, states)
        grad_tokens, result, grad_qkv, grad_b_qkv, grad_out, grad_vec, grad_in = grads[:7]
        return (
            result,
            grad_tokens,
            grad_qkv,
            grad_b_qkv,
            grad_out,
            grad_vec,
            grad_in,
            grads[7].reshape(layers, width),
            grads[8],
        )

    head, states = plain_forward(blocks, tokens, cotangent, small, meta, frequency, vectors)
    w_all, gradient, low, cos, sin, qcode, kcode = head
    result = relayout(low)
    gradient = gradient.astype(F32)

    first = jnp.where(c == 0, 1, 2)
    spans = [(g ^ hop) * 2 * height for hop in (0, first, 3 - first, 3)]
    if pieces == 1:
        spans = [jnp.int32(0)] * 4
    column_of = [(z - k) % MP for k in range(MP)]
    own_z = [(z - 2 * c - k) % MP for k in range(2)]
    scal = jnp.stack(row_offsets(g, c, height) + column_of + [2 * c] + spans + own_z)
    scal = scal.astype(jnp.int32)

    masters = []
    vector_grads = []
    in_biases = []
    head_biases = []
    for layer_at in reversed(range(layers)):
        x_full, q, k, v, mixed, mixed_in, lse, r1, r2, e, gp = states[layer_at]
        back = feed_back(
            scal,
            piece_rows,
            pieces,
            gradient,
            r1,
            r2,
            e,
            gp,
            mixed[:rows],
            mixed_in,
            vectors[layer_at],
            w_all,
            3 * layer_at,
        )
        dr1, dz_own, dz_sib, dvec, dbin = back[:5]
        dz_others = core_swap(dz_sib)
        feed_grad = reduce_all(back[5], back[-1])
        dx, dx_sib, dbias, parts = attend_back(
            scal,
            piece_rows,
            pieces,
            x_full.reshape(4 * rows, width),
            (cos, sin, qcode, kcode),
            (q, k, v, lse),
            mixed,
            dz_own,
            dz_others,
            w_all,
            3 * layer_at,
        )
        got = dx.astype(F32) + core_swap(dx_sib).astype(F32)
        gradient = dr1 + got[0] + pair_swap(got[1].astype(BF16)).astype(F32)
        head_grad = reduce_heads(parts)
        masters.insert(0, (feed_grad, head_grad))
        vector_grads.insert(0, dvec)
        in_biases.insert(0, dbin[:, 0])
        head_biases.insert(0, sum_head_biases(dbias[:, 0]))
    grad_tokens = relayout(gradient.astype(BF16)).astype(F32)

    layers_of = jnp.stack(in_biases, axis=1)
    grad_vectors, grad_b_in = sum_vectors(jnp.concatenate(vector_grads), layers_of)
    grad_vectors = grad_vectors.reshape(vectors.shape)
    grad_b_qkv = jnp.stack([jnp.stack(head_columns(b)) for b in head_biases])

    grad_qkv = jnp.stack([jnp.stack(head_columns(m[1])) for m in masters])
    grad_in = jnp.stack([m[0][:, :width] for m in masters])
    grad_back = jnp.stack([m[0][:, width : 2 * width].T for m in masters])
    grad_out = jnp.stack(
        [
            jnp.concatenate(
                [m[0][:, 2 * width + LANES :], m[0][:, 2 * width + HD : 2 * width + LANES]], axis=-1
            ).T
            for m in masters
        ]
    )
    return (
        result,
        grad_tokens,
        grad_qkv,
        grad_b_qkv,
        grad_out,
        grad_vectors,
        grad_in,
        grad_b_in,
        grad_back,
    )


def solution(mesh):
    return jax.shard_map(
        per_device,
        mesh=mesh,
        in_specs=(
            P(("dp", "mp"), None),
            P(None, None, "dp", "mp"),
            P(None, None, "mp"),
            P(None, "mp", "dp"),
            P(),
            P(None, "dp", "mp"),
            P(None, "mp"),
            P(None, "mp", "dp"),
            P(("dp", "mp"), None),
            P("dp", None),
            P("dp"),
        ),
        out_specs=(
            P(("dp", "mp"), None),
            P(("dp", "mp"), None),
            P(None, None, "dp", "mp"),
            P(None, None, "mp"),
            P(None, "mp", "dp"),
            P(),
            P(None, "dp", "mp"),
            P(None, "mp"),
            P(None, "mp", "dp"),
        ),
        check_vma=False,
    )
```

```python
from functools import partial

import jax
import jax.numpy as jnp
from jax import lax
from jax.experimental import pallas as pl
from jax.experimental.pallas import tpu as pltpu
from jax.sharding import PartitionSpec as P

HD = 64
LEN_MAX = 1536
EPSILON = 1e-06
NEGATIVE = -1e30
F32 = jnp.float32
BF16 = jnp.bfloat16
LANES = 128
MP = 4
SPLIT = 2
VMEM_LIMIT = 60 * 1024 * 1024
BACK_LIMIT = 63 * 1024 * 1024


def nn(a, b):
    return lax.dot_general(a, b, (((1,), (0,)), ((), ())), preferred_element_type=F32)


def nt(a, b):
    return lax.dot_general(a, b, (((1,), (1,)), ((), ())), preferred_element_type=F32)


def core_swap(x):
    n = lax.axis_size("dp")
    return lax.ppermute(x, "dp", [(i, i ^ 1) for i in range(n)])


def plane_swap(x, first):
    n = lax.axis_size("dp")
    hops = (2, 4) if first else (4, 2)
    return lax.ppermute(x, "dp", [(i, i ^ hops[i % 2]) for i in range(n)])


def column_shift(x, k):
    return lax.ppermute(x, "mp", [(i, (i + k) % MP) for i in range(MP)])


def pair_swap(x):
    return lax.ppermute(x, "mp", [(i, i ^ 1) for i in range(MP)])


def relayout(x):
    n = lax.axis_size("dp")
    pairs = []
    for d in range(n):
        for z in range(MP):
            if (d % 2) != (z // 2):
                pairs.append((d * MP + z, (d ^ 1) * MP + (z ^ 2)))
            else:
                pairs.append((d * MP + z, d * MP + z))
    return lax.ppermute(x, ("dp", "mp"), pairs)


def turn_columns(x, z):
    return jnp.stack([lax.dynamic_index_in_dim(x, (z - k) % MP, 0, False) for k in range(MP)])


def row_offsets(g, c, rows):
    if lax.axis_size("dp") != 8:
        return [jnp.int32(0)]
    result = []
    for core in (c, 1 - c):
        first = jnp.where(core == 0, 1, 2)
        for hop in (0, first, 3 - first, 3):
            result.append(((g ^ hop) * 2 + core) * rows)
    return result


def send_columns(v):
    total = v[0].astype(F32)
    for k in range(1, MP):
        total = total + column_shift(v[k], -k).astype(F32)
    return total


def reduce_all(keep, away):
    if lax.axis_size("dp") != 8:
        z = lax.axis_index("mp")
        whole = turn_columns(keep[0], z).astype(F32)
        part = lax.psum_scatter(whole, "mp", scatter_dimension=0, tiled=False)
        return lax.psum_scatter(part, "dp", scatter_dimension=0, tiled=True)
    other = core_swap(away)

    def add(i):
        return keep[i].astype(F32) + other[i].astype(F32)

    got = plane_swap(jnp.stack([add(0), add(1)]).astype(BF16), True)
    got_two = plane_swap((add(2) + got[1].astype(F32)).astype(BF16), False)
    v = (add(3) + got[0].astype(F32) + got_two.astype(F32)).astype(BF16)
    return send_columns(v)


def reduce_heads(parts):
    c = lax.axis_index("dp") % 2
    n = lax.axis_size("dp")
    if n != 8:
        z = lax.axis_index("mp")
        wide = jnp.concatenate([parts[0], jnp.zeros_like(parts[0])], axis=0)
        wide = jnp.where(c == 0, wide, jnp.roll(wide, 2, axis=0))
        whole = turn_columns(wide, z).astype(F32)
        part = lax.psum_scatter(whole, "mp", scatter_dimension=0, tiled=False)
        return lax.psum_scatter(part, "dp", scatter_dimension=0, tiled=True)
    got = plane_swap(parts[0:2], True)
    got_two = plane_swap((parts[2].astype(F32) + got[1].astype(F32)).astype(BF16), False)
    v = (parts[3].astype(F32) + got[0].astype(F32) + got_two.astype(F32)).astype(BF16)

    total = column_turn(v[0], 0).astype(F32) + column_turn(v[1], 1).astype(F32)
    rows = total.shape[0] // 2
    kept = lax.dynamic_slice_in_dim(total, c * rows, rows, 0)
    sent = lax.dynamic_slice_in_dim(total, (1 - c) * rows, rows, 0).astype(BF16)
    return kept + core_swap(sent).astype(F32)


def sum_head_biases(v):
    c = lax.axis_index("dp") % 2
    n = lax.axis_size("dp")
    if n != 8:
        z = lax.axis_index("mp")
        zero = jnp.zeros_like(v)
        wide = jnp.where(c == 0, jnp.concatenate([v, zero]), jnp.concatenate([zero, v]))
        total = lax.psum(turn_columns(wide, z), ("dp", "mp"))
        return lax.dynamic_index_in_dim(total, z, 0, False)
    v = v + plane_swap(v, True)
    v = v + plane_swap(v, False)
    total = column_turn(v[0], 0) + column_turn(v[1], 1)
    return total + core_swap(total)


def column_turn(x, k):
    n = lax.axis_size("dp")
    pairs = []
    for d in range(n):
        for z in range(MP):
            pairs.append((d * MP + z, d * MP + (z - k - 2 * (d % 2)) % MP))
    return lax.ppermute(x, ("dp", "mp"), pairs)


def sum_vectors(vectors, columns):
    if lax.axis_size("dp") != 8:
        z = lax.axis_index("mp")
        vectors, columns = lax.psum((vectors, turn_columns(columns, z)), ("dp", "mp"))
        return vectors, lax.dynamic_index_in_dim(columns, z, 0, False)
    n = vectors.shape[0]
    m = columns.shape[1]
    both = jnp.concatenate([vectors, columns.reshape(MP * m, -1)])
    both = both + core_swap(both)
    both = both + plane_swap(both, True)
    both = both + plane_swap(both, False)
    total = both[: n + m]
    for k in range(1, MP):
        at = n + m * (MP - k)
        total = total + column_shift(jnp.concatenate([both[:n], both[at : at + m]]), k)
    return total[:n], total[n:]


def lane_index(shape):
    return lax.broadcasted_iota(jnp.int32, shape, len(shape) - 1)


def half_swap(x):
    lane = lane_index(x.shape)
    return jnp.where(
        lane % HD < HD // 2,
        pltpu.roll(x, LANES - HD // 2, x.ndim - 1),
        pltpu.roll(x, HD // 2, x.ndim - 1),
    )


def norm_parts(r):
    mean = jnp.mean(r, axis=-1, keepdims=True)
    centred = r - mean
    scale = lax.rsqrt(jnp.mean(centred * centred, axis=-1, keepdims=True) + EPSILON)
    return centred * scale, scale


def norm_back(dy, n, scale, gain):
    gdy = dy * gain
    mean_one = jnp.mean(gdy, axis=-1, keepdims=True)
    mean_two = jnp.mean(gdy * n, axis=-1, keepdims=True)
    return (gdy - mean_one - n * mean_two) * scale


def vmem():
    return pl.BlockSpec(memory_space=pltpu.VMEM)


def smem():
    return pl.BlockSpec(memory_space=pltpu.SMEM)


def anywhere():
    return pl.BlockSpec(memory_space=pl.ANY)


def params():
    return pltpu.CompilerParams(vmem_limit_bytes=VMEM_LIMIT)


def shape(dims, dtype):
    return jax.ShapeDtypeStruct(dims, dtype)


def project_rows(i, z, x, w_ref, bias, cos, sin, q_ref, k_ref, v_ref):
    block = x.shape[0]
    at = pl.ds(i * block, block)
    p = nn(x, w_ref[z, :, LANES : 5 * LANES]) + bias[:, LANES:]
    low_half = lane_index((block, LANES)) < HD
    mixed = p[:, 0:LANES]
    mixed = mixed * cos + half_swap(mixed) * sin
    pair = p[:, LANES : 2 * LANES]
    pair = pair * cos + half_swap(pair) * sin
    k_ref[z, 0, at, :] = pair.astype(BF16)
    k_ref[z, 1, at, :] = jnp.where(low_half, pltpu.roll(mixed, HD, 1), 0.0).astype(BF16)
    v_ref[z, 0, at, :] = p[:, 2 * LANES : 3 * LANES].astype(BF16)
    v_ref[z, 1, at, :] = jnp.where(low_half, p[:, 3 * LANES :], 0.0).astype(BF16)
    if i < 2:
        q = nn(x, w_ref[z, :, 0:LANES]) + bias[:, 0:LANES]
        q = q * cos + half_swap(q) * sin
        q_ref[z, 0, at, :] = q.astype(BF16) * BF16(HD**-0.5)
        q_ref[z, 1, at, :] = jnp.where(low_half, mixed, 0.0).astype(BF16) * BF16(HD**-0.5)


def attend_rows(
    i, qblock, qcode_ref, kcode_ref, q_ref, k_ref, v_ref, mixed_ref, lse_cols, between=None
):
    at = pl.ds(pl.multiple_of(i * qblock, qblock), qblock)
    visible = qcode_ref[at, :] == kcode_ref[...]
    low_half = lane_index((qblock, LANES)) < HD
    lane = lane_index((qblock, LANES))
    for z in range(2):
        outs = []
        for h in range(3):
            tile = h // 2
            q = q_ref[z, tile, at, :]
            if h < 2:
                q = jnp.where(low_half == (h == 0), q, BF16(0))
            s = nt(q, k_ref[z, tile])
            s = jnp.where(visible, s, NEGATIVE)
            m = jnp.max(s, axis=-1, keepdims=True)
            p = jnp.exp(s - m)
            l = jnp.sum(p, axis=-1, keepdims=True)
            o = nn(p.astype(BF16), v_ref[z, tile])
            outs.append(o / l)
            lse_cols[at, :] = jnp.where(lane == 3 * z + h, m + jnp.log(l), lse_cols[at, :])
        mixed_ref[at, pl.ds(z * 256, LANES)] = pltpu.roll(outs[2], HD, 1).astype(BF16)
        mixed_ref[at, pl.ds(z * 256 + LANES, LANES)] = jnp.where(
            low_half, outs[0], outs[1]
        ).astype(BF16)
        if between is not None:
            between(z)


def mirrored(z):
    return [z, z + 1 - 2 * (z % 2), (z + 2) % MP, MP - 1 - z]


def head_columns_of(z, c):
    base = (z + 2 * c) % MP
    return [base, base + 1 - 2 * (base % 2)]


def forward_kernel(n_layers, *refs):
    n_in, per_layer = 7, 11
    blocks, tokens, cot, small, meta, frequency, vectors = refs[:n_in]
    w_all, dy_out, low_out, cos_out, sin_out, qrow_out, kcol_out = refs[n_in : n_in + 7]
    saved = [
        refs[n_in + 7 + l * per_layer : n_in + 7 + (l + 1) * per_layer] for l in range(n_layers)
    ]
    (
        xfull,
        mixed_in,
        small_all,
        meta_in,
        wa,
        wo,
        win,
        wback,
        cos_ref,
        sin_ref,
        qcode_ref,
        kcode_ref,
        qrow_ref,
        kcol_ref,
        q_ref,
        k_ref,
        v_ref,
        mixed_ref,
        lse_cols,
        lse_ref,
        stream,
        sum_ref,
        r1_ref,
        low_ref,
        e_ref,
        gp_ref,
        z_send,
        z_recv,
        p_send,
        p_recv,
        c_send,
        c_recv,
        x_send,
        x_recv,
        t_send,
        t_recv,
        l_sem,
        w_sem,
        s_sem,
    ) = refs[n_in + 7 + n_layers * per_layer :]
    rows = stream.shape[0]
    width = stream.shape[1]
    height = blocks.shape[1]
    parts = blocks.shape[0] * SPLIT

    d = lax.axis_index("dp")
    z = lax.axis_index("mp")
    c = d % 2
    x = (d // 2) % 2
    y = d // 4
    flip_x, flip_y = 1 - 2 * x, 1 - 2 * y
    one_x, one_y = x + (1 - c) * flip_x, y + c * flip_y
    two_x, two_y = x + c * flip_x, y + (1 - c) * flip_y

    def device(yy, xx, cc, zz):
        return (yy * 4 + xx * 2 + cc, zz)

    part_rows = height // SPLIT
    planes = ((y, x), (one_y, one_x), (two_y, two_x), (1 - y, 1 - x))

    def rows_of(k, n):
        yy, xx = planes[n]
        start = (yy * 4 + xx * 2 + c) * height + k % SPLIT * part_rows
        return pl.ds(pl.multiple_of(start, 16), part_rows)

    sibling = device(y, x, 1 - c, z)
    first = device(one_y, one_x, c, z)
    second = device(two_y, two_x, c, z)
    pair = device(y, x, c, z + 1 - 2 * (z % 2))
    away = device(y, x, 1 - c, (z + 2) % MP)
    moved = c != z // 2
    mirror = mirrored(z)
    columns = [device(y, x, c, mirror[m]) for m in range(1, MP)]
    barrier = pltpu.get_barrier_semaphore()
    partners = columns + [first, second, sibling, away]
    for partner in partners:
        pl.semaphore_signal(
            barrier, inc=1, device_id=partner, device_id_type=pl.DeviceIdType.MESH
        )
    pl.semaphore_wait(barrier, len(partners))

    def remote(source, target, send, recv, to):
        return pltpu.make_async_remote_copy(
            src_ref=source,
            dst_ref=target,
            send_sem=send,
            recv_sem=recv,
            device_id=to,
            device_id_type=pl.DeviceIdType.MESH,
        )

    sent = []

    def go(make, *at):
        make(*at).start()
        sent.append((make, at))

    def block(k):
        return blocks.at[k // SPLIT, pl.ds(k % SPLIT * part_rows, part_rows)]

    def local_copy(k):
        return pltpu.make_async_copy(block(k), w_all.at[k // SPLIT, z, rows_of(k, 0)], l_sem.at[k])

    def z_copy(k, n):
        if n == 2:
            source = target = w_all.at[k // SPLIT, mirror[2], rows_of(k, 0)]
        else:
            source, target = block(k), w_all.at[k // SPLIT, z, rows_of(k, 0)]
        return remote(
            source, target, z_send.at[k, n], z_recv.at[k, n], columns[1 if n == 1 else 0]
        )

    def p_copy(k, n):
        source = w_all.at[k // SPLIT, :, rows_of(k, 1 if n == 2 else 0)]
        return remote(
            source, source, p_send.at[k, n], p_recv.at[k, n], first if n == 0 else second
        )

    def c_copy(k, n):
        source = w_all.at[k // SPLIT, :, rows_of(k, n)]
        return remote(source, source, c_send.at[k, n], c_recv.at[k, n], sibling)

    def step_send(k):
        local_copy(k).start()
        go(z_copy, k, 1)
        go(z_copy, k, 0)

    def step_across(k):
        z_copy(k, 1).wait_recv()
        go(z_copy, k, 2)

    def step_plane(k):
        local_copy(k).wait()
        z_copy(k, 0).wait_recv()
        z_copy(k, 2).wait_recv()
        go(p_copy, k, 0)
        go(p_copy, k, 1)
        go(c_copy, k, 0)
        if k + 1 < parts:
            step_across(k + 1)
        if k + 2 < parts:
            step_send(k + 2)

    def step_forward(k):
        p_copy(k, 0).wait_recv()
        go(p_copy, k, 2)
        go(c_copy, k, 1)
        p_copy(k, 1).wait_recv()
        go(c_copy, k, 2)

    def step_last(k):
        p_copy(k, 2).wait_recv()
        go(c_copy, k, 3)

    def step_ready(chunk):
        for k in range(chunk * SPLIT, (chunk + 1) * SPLIT):
            for n in range(4):
                c_copy(k, n).wait_recv()

    turns = parts + 2
    position = [0]

    def take(until):
        steps = []
        for n in range(position[0], until):
            if n < 2:
                steps.append(partial(step_plane, n))
            if 0 <= n - 2:
                steps.append(partial(step_last, n - 2))
            if 0 <= n - 1 < parts:
                steps.append(partial(step_forward, n - 1))
            if n == 2:
                steps.append(partial(step_plane, 2))
            if 2 <= n < parts - 1:
                steps.append(partial(step_plane, n + 1))
        position[0] = max(position[0], until)
        return steps

    def run(steps):
        for step in steps:
            step()

    def meta_copy():
        return remote(meta, meta_in, t_send.at[0], t_recv.at[0], sibling)

    def small_copy(s):
        return remote(small, small_all.at[z], t_send.at[3 + s], t_recv.at[3 + s], columns[s])

    step_send(0)
    go(meta_copy)
    for n in range(MP - 1):
        go(small_copy, n)
    token_copy = remote(tokens, xfull.at[0, 0], t_send.at[1], t_recv.at[1], away)
    token_local = pltpu.make_async_copy(tokens, xfull.at[0, 0], l_sem.at[parts])
    step_across(0)

    @pl.when(moved)
    def _():
        token_copy.start()

    @pl.when(jnp.logical_not(moved))
    def _():
        token_local.start()

    step_send(1)
    small_local = pltpu.make_async_copy(small, small_all.at[z], l_sem.at[parts + 1])
    small_local.start()

    meta_copy().wait_recv()
    info = jnp.where(moved, meta_in[...], meta[...])
    slot = info[0:1, :]
    limits = [info[n : n + 1, :] for n in range(1, 4)]
    half = z % 2
    quarters = [2 * c + half, 2 * (1 - c) + half, 2 * c + 1 - half, 2 * (1 - c) + 1 - half]

    def codes(place_all, slot, limits):
        seq = jnp.where(place_all >= slot, 1.0, 0.0) + jnp.where(place_all >= 2.0 * slot, 1.0, 0.0)
        place = place_all - seq * slot
        limit = jnp.where(seq == 0.0, limits[0], jnp.where(seq == 1.0, limits[1], limits[2]))
        return seq, place, jnp.where(place < limit, seq, -1.0)

    sign = jnp.where(lane_index((1, LANES)) % HD < HD // 2, -1.0, 1.0)
    for i in range(4):
        at = pl.ds(i * rows, rows)
        base = quarters[i] * rows
        index = lax.broadcasted_iota(jnp.int32, (rows, LANES), 0) + base
        seq, place, kcode = codes(index.astype(F32), slot, limits)
        angle = place * frequency[...]
        cos_ref[at, :] = jnp.cos(angle)
        sin_ref[at, :] = jnp.sin(angle) * sign
        kcol_ref[at, :] = kcode[:, 0:1]
        if i < 2:
            qcode_ref[at, :] = seq[:, 0:1]
        index = lax.broadcasted_iota(jnp.int32, (1, rows), 1) + base
        seq, place, kcode = codes(
            index.astype(F32), slot[:, 0:1], [limit[:, 0:1] for limit in limits]
        )
        kcode_ref[:, pl.ds(i * rows, rows)] = kcode
        if i < 2:
            qrow_ref[:, pl.ds(i * rows, rows)] = seq

    run(take(1))

    @pl.when(moved)
    def _():
        token_copy.wait_recv()

    @pl.when(jnp.logical_not(moved))
    def _():
        token_local.wait()

    def x_copy(l, n):
        source = xfull.at[l, 2 if n == 2 else 0]
        target = xfull.at[l, (2, 1, 3)[n]]
        return remote(
            source, target, x_send.at[l, n], x_recv.at[l, n], pair if n == 0 else sibling
        )

    def m_copy(l):
        return remote(
            mixed_ref.at[pl.ds(rows, rows)],
            mixed_in.at[l],
            x_send.at[l, 3],
            x_recv.at[l, 3],
            sibling,
        )

    def h_copy(l):
        return remote(low_ref, saved[l][10].at[1], x_send.at[l, 4], x_recv.at[l, 4], sibling)

    def e_copy(l):
        return remote(
            e_ref,
            saved[l][8].at[:, pl.ds(rows, rows), :],
            x_send.at[l, 5],
            x_recv.at[l, 5],
            sibling,
        )

    stores = {}

    def store(name, source, target):
        copy = pltpu.make_async_copy(source, target, s_sem.at[len(stores)])
        copy.start()
        stores[name] = copy

    waited = set()

    def stored(*names):
        for name in names:
            if name in stores and name not in waited:
                waited.add(name)
                stores[name].wait()

    stream[...] = xfull[0, 0].astype(F32)
    store("cos", cos_ref, cos_out)
    store("sin", sin_ref, sin_out)
    store("qrow", qrow_ref, qrow_out)
    store("kcol", kcol_ref, kcol_out)

    cot_copy = remote(cot, dy_out, t_send.at[2], t_recv.at[2], away)
    cot_local = pltpu.make_async_copy(cot, dy_out, l_sem.at[parts + 2])

    def load(source, target, n):
        copy = pltpu.make_async_copy(source, target, w_sem.at[n])
        copy.start()
        return copy

    qblock = 256
    count = 2 * rows // qblock
    own_z = head_columns_of(z, c)
    other_z = [(at + 2) % MP for at in own_z]
    for l in range(n_layers):
        xs, qs, ks, vs, ms, ls, r1s, r2s, es, gps, hs = saved[l]
        last = l - 1
        go(x_copy, l, 0)
        go(x_copy, l, 1)
        if l == 0:
            run(take(2))
            x_copy(l, 0).wait_recv()
            go(x_copy, l, 2)
            run(take(4))
        else:
            run(take(10))
        step_ready(3 * l)
        wa_loads = [
            load(w_all.at[3 * l, own_z[k], :, pl.ds(0, 5 * LANES)], wa.at[k], k) for k in range(2)
        ]
        wo_load = load(w_all.at[3 * l, :, :, pl.ds(4 * LANES, 2 * LANES)], wo, 2)
        if l == 0:

            @pl.when(moved)
            def _():
                cot_copy.start()

            @pl.when(jnp.logical_not(moved))
            def _():
                cot_local.start()

            for s in range(MP - 1):
                small_copy(s).wait_recv()
            small_local.wait()
        else:
            m_copy(last).wait_send()
        stored(("q", last), ("k", last), ("v", last), ("mixed", last), ("lse", last))
        lse_cols[...] = jnp.zeros_like(lse_cols)
        for copy in wa_loads:
            copy.wait()
        for i in range(4):
            if i == 1:
                x_copy(l, 1).wait_recv()
            if i == 2 and l > 0:
                x_copy(l, 0).wait_recv()
                go(x_copy, l, 2)
            if i == 3:
                run(take(5 if l == 0 else 11))
                x_copy(l, 2).wait_recv()
            at = pl.ds(i * rows, rows)
            for k in range(2):
                bias = small_all[own_z[k], pl.ds(l, 1), pl.ds(0, 5 * LANES)]
                project_rows(
                    i, k, xfull[l, i], wa, bias, cos_ref[at, :], sin_ref[at, :], q_ref, k_ref, v_ref
                )
        store(("q", l), q_ref, qs)
        store(("k", l), k_ref, ks)
        store(("v", l), v_ref, vs)
        store(("x", l), xfull.at[l], xs)
        ends = (5, 5, 6, 6, 6, 7) if l == 0 else (11, 12, 12, 12, 13, 13)
        steps = [take(end) for end in ends]

        def one_block(n, _, l=l, steps=steps):
            def between(k):
                for j in range(count):
                    if steps[2 * j + k] or (j, k) in ((1, 1), (2, 0)):

                        @pl.when(n == j)
                        def _(j=j):
                            if (j, k) == (1, 1):
                                m_copy(l).start()
                            run(steps[2 * j + k])
                            if (j, k) == (2, 0):
                                step_ready(3 * l + 1)
                                load(w_all.at[3 * l + 1], win, 3)

            attend_rows(
                count - 1 - n,
                qblock,
                qcode_ref,
                kcode_ref,
                q_ref,
                k_ref,
                v_ref,
                mixed_ref,
                lse_cols,
                between,
            )
            return 0

        lax.fori_loop(0, count, one_block, 0)
        lse_ref[...] = jnp.transpose(lse_cols[...])[0:8, :]
        store(("mixed", l), mixed_ref, ms)
        store(("lse", l), lse_ref, ls)
        win_load = pltpu.make_async_copy(w_all.at[3 * l + 1], win, w_sem.at[3])
        stored(("r1", last), ("r2", last), ("e", last), ("gp", last), ("h", last))
        if l > 0:
            h_copy(last).wait_send()
            e_copy(last).wait_send()
        wo_load.wait()
        m_copy(l).wait_recv()
        a = jnp.zeros((rows, width), F32)
        for k in range(2):
            a = a + nt(mixed_ref[0:rows, k * 256 : k * 256 + 256], wo[own_z[k]])
            a = a + nt(mixed_in[l, :, k * 256 : k * 256 + 256], wo[other_z[k]])
        vec = vectors[l]
        r1 = stream[...] + a + vec[0:1, :]
        r1_ref[...] = r1
        store(("r1", l), r1_ref, r1s)
        n1, _ = norm_parts(r1)
        h = n1 * vec[1:2, :] + vec[2:3, :]
        low_ref[...] = h.astype(BF16)
        store(("h", l), low_ref, hs.at[0])
        h_copy(l).start()
        sum_ref[...] = h + vec[3:4, :]
        win_load.wait()

        def inner(zz, _, l=l):
            u = nn(low_ref[...], win[zz]) + small_all[zz, pl.ds(l, 1), pl.ds(5 * LANES, width)]
            cdf = 0.5 * (1.0 + lax.erf(u * (2.0**-0.5)))
            pdf = jnp.exp(u * u * -0.5) * 0.3989422804014327
            e_ref[zz] = (u * cdf).astype(BF16)
            gp_ref[zz] = (cdf + u * pdf).astype(BF16)
            return 0

        lax.fori_loop(0, 2, inner, 0)
        run(take(8 if l == 0 else turns))
        lax.fori_loop(2, MP - 1, inner, 0)
        step_ready(3 * l + 2)
        wback_load = load(w_all.at[3 * l + 2], wback, 4)
        lax.fori_loop(MP - 1, MP, inner, 0)
        store(("e", l), e_ref, es.at[:, pl.ds(0, rows), :])
        e_copy(l).start()
        store(("gp", l), gp_ref, gps)
        wback_load.wait()

        def outer(zz, _):
            sum_ref[...] += nt(e_ref[zz], wback[zz])
            return 0

        lax.fori_loop(0, MP, outer, 0)
        store(("r2", l), sum_ref, r2s)
        n2, _ = norm_parts(sum_ref[...])
        result = n2 * vec[4:5, :] + vec[5:6, :]
        if l + 1 < n_layers:
            stream[...] = result
            xfull[l + 1, 0] = result.astype(BF16)
        else:
            h_copy(l).wait_send()
            stored(("h", l))
            low_ref[...] = result.astype(BF16)
            store("low", low_ref, low_out)

    m_copy(n_layers - 1).wait_send()
    e_copy(n_layers - 1).wait_send()
    for l in range(n_layers):
        h_copy(l).wait_recv()
        e_copy(l).wait_recv()
    for make, at in sent:
        make(*at).wait_send()
    @pl.when(moved)
    def _():
        token_copy.wait_send()
        cot_copy.wait_send()
        cot_copy.wait_recv()

    @pl.when(jnp.logical_not(moved))
    def _():
        cot_local.wait()

    stored(*stores)


def forward(blocks, tokens, cot, small, meta, frequency, vectors):
    n_layers = vectors.shape[0]
    chunks, height, width = blocks.shape
    rows = tokens.shape[0]
    queries, keys = 2 * rows, 4 * rows
    layer_out = (
        shape((4, rows, width), BF16),
        shape((2, 2, queries, LANES), BF16),
        shape((2, 2, keys, LANES), BF16),
        shape((2, 2, keys, LANES), BF16),
        shape((queries, 512), BF16),
        shape((8, queries), F32),
        shape((rows, width), F32),
        shape((rows, width), F32),
        shape((MP, 2 * rows, width), BF16),
        shape((MP, rows, width), BF16),
        shape((2, rows, width), BF16),
    )
    outs = (
        shape((chunks, MP, 8 * height, width), BF16),
        shape((rows, width), BF16),
        shape((rows, width), BF16),
        shape((keys, LANES), F32),
        shape((keys, LANES), F32),
        shape((1, queries), F32),
        shape((keys, 1), F32),
    ) + layer_out * n_layers
    sem = pltpu.SemaphoreType.DMA
    results = pl.pallas_call(
        partial(forward_kernel, n_layers),
        out_shape=outs,
        in_specs=[anywhere()] * 3 + [vmem()] * 4,
        out_specs=(anywhere(),) * len(outs),
        scratch_shapes=[
            pltpu.VMEM((n_layers, 4, rows, width), BF16),
            pltpu.VMEM((n_layers, rows, 512), BF16),
            pltpu.VMEM((MP,) + small.shape, F32),
            pltpu.VMEM(meta.shape, F32),
            pltpu.VMEM((2, width, 5 * LANES), BF16),
            pltpu.VMEM((MP, width, 2 * LANES), BF16),
            pltpu.VMEM((MP, width, width), BF16),
            pltpu.VMEM((MP, width, width), BF16),
            pltpu.VMEM((keys, LANES), F32),
            pltpu.VMEM((keys, LANES), F32),
            pltpu.VMEM((queries, 1), F32),
            pltpu.VMEM((1, keys), F32),
            pltpu.VMEM((1, queries), F32),
            pltpu.VMEM((keys, 1), F32),
            pltpu.VMEM((2, 2, queries, LANES), BF16),
            pltpu.VMEM((2, 2, keys, LANES), BF16),
            pltpu.VMEM((2, 2, keys, LANES), BF16),
            pltpu.VMEM((queries, 512), BF16),
            pltpu.VMEM((queries, LANES), F32),
            pltpu.VMEM((8, queries), F32),
            pltpu.VMEM((rows, width), F32),
            pltpu.VMEM((rows, width), F32),
            pltpu.VMEM((rows, width), F32),
            pltpu.VMEM((rows, width), BF16),
            pltpu.VMEM((MP, rows, width), BF16),
            pltpu.VMEM((MP, rows, width), BF16),
            sem((chunks * SPLIT, 3)),
            sem((chunks * SPLIT, 3)),
            sem((chunks * SPLIT, 3)),
            sem((chunks * SPLIT, 3)),
            sem((chunks * SPLIT, 4)),
            sem((chunks * SPLIT, 4)),
            sem((n_layers, 6)),
            sem((n_layers, 6)),
            sem((6,)),
            sem((6,)),
            sem((chunks * SPLIT + 3,)),
            sem((5,)),
            sem((5 + 11 * n_layers,)),
        ],
        compiler_params=pltpu.CompilerParams(
            vmem_limit_bytes=VMEM_LIMIT, collective_id=0, has_side_effects=True
        ),
        cost_estimate=pl.CostEstimate(
            flops=100_000_000_000, bytes_accessed=100_000_000, transcendentals=20_000_000
        ),
        name="forward",
    )(blocks, tokens, cot, small, meta, frequency, vectors)
    head = results[:7]
    states = [results[7 + 11 * l : 18 + 11 * l] for l in range(n_layers)]
    return head, states


def place_of(d, z):
    c = d % 2
    x = (d // 2) % 2
    y = d // 4
    flip_x, flip_y = 1 - 2 * x, 1 - 2 * y
    planes = (
        (y, x),
        (y + c * flip_y, x + (1 - c) * flip_x),
        (y + (1 - c) * flip_y, x + c * flip_x),
        (1 - y, 1 - x),
    )
    groups = [2 * yy + xx for yy, xx in planes]

    def device(group, cc, zz):
        return (group * 2 + cc, zz)

    return c, groups, device


def head_back(
    i,
    h,
    kblock,
    q_ref,
    k_ref,
    v_ref,
    dz_ref,
    lse_ref,
    delta_ref,
    qrow_ref,
    kcol_ref,
    pair_ref,
    dqt_ref,
    dt_ref,
):
    tile = h // 2
    keys, queries = k_ref.shape[2], q_ref.shape[2]
    low_q = lane_index((queries, LANES)) < HD
    low_k = lane_index((kblock, LANES)) < HD
    q = q_ref[i, tile]
    dz = dz_ref[i, tile]
    if h < 2:
        keep = low_q == (h == 0)
        q = jnp.where(keep, q, BF16(0))
        dz = jnp.where(keep, dz, BF16(0))
    pair_ref[0] = q
    pair_ref[1] = dz
    lse = lse_ref[3 * i + h : 3 * i + h + 1, :]
    delta = delta_ref[3 * i + h : 3 * i + h + 1, :]
    if h != 1:
        dqt_ref[...] = jnp.zeros_like(dqt_ref)

    def one_block(n, _):
        at = pl.ds(pl.multiple_of(n * kblock, kblock), kblock)
        kb = k_ref[i, tile, at, :]
        vb = v_ref[i, tile, at, :]
        kb_own = jnp.where(low_k == (h == 0), kb, BF16(0)) if h < 2 else kb
        visible = kcol_ref[at, :] == qrow_ref[...]
        s = nt(kb, pair_ref[0])
        s = jnp.where(visible, s, NEGATIVE)
        p = jnp.exp(s - lse)
        dp = nt(vb, pair_ref[1])
        ds = (p * (dp - delta)).astype(BF16)
        dv = nn(p.astype(BF16), pair_ref[1])
        dk = nn(ds, pair_ref[0])
        dqt_ref[...] += nn(jnp.transpose(kb_own), ds)
        if h == 1:
            dt_ref[2, at, :] += dk
            dt_ref[3, at, :] += dv
        elif h == 0:
            dt_ref[2, at, :] = dk
            dt_ref[3, at, :] = dv
        else:
            dt_ref[1, at, :] = pltpu.roll(dk, HD, 1)
            dt_ref[4, at, :] = dv
        return 0

    lax.fori_loop(0, keys // kblock, one_block, 0)
    if h >= 1:
        dq = jnp.transpose(dqt_ref[...]) * HD**-0.5
        if h == 1:
            dt_ref[0, 0:queries, :] = dq
        else:
            dt_ref[1, 0:queries, :] += dq


def head_deltas(i, mixed_ref, dz_ref, delta_ref):
    single = pltpu.roll(mixed_ref[:, i * 256 : i * 256 + LANES].astype(F32), HD, 1)
    pair = mixed_ref[:, i * 256 + LANES : i * 256 + 256].astype(F32)
    prod_one = jnp.transpose(pair * dz_ref[i, 0].astype(F32))
    prod_two = jnp.transpose(single * dz_ref[i, 1].astype(F32))
    delta_ref[3 * i : 3 * i + 1, :] = jnp.sum(prod_one[0:HD], axis=0, keepdims=True)
    delta_ref[3 * i + 1 : 3 * i + 2, :] = jnp.sum(prod_one[HD:], axis=0, keepdims=True)
    delta_ref[3 * i + 2 : 3 * i + 3, :] = jnp.sum(prod_two[0:HD], axis=0, keepdims=True)


def norm_back_rows(acc_ref, r_ref, low_ref, gain):
    rows, width = acc_ref.shape
    step = 32

    def body(i, sums):
        at = pl.ds(pl.multiple_of(i * step, step), step)
        dy = acc_ref[at, :]
        n, scale = norm_parts(r_ref[at, :])
        dr = norm_back(dy, n, scale, gain)
        acc_ref[at, :] = dr
        low_ref[at, :] = dr.astype(BF16)
        return (
            sums[0] + jnp.sum(dy * n, axis=0, keepdims=True),
            sums[1] + jnp.sum(dy, axis=0, keepdims=True),
            sums[2] + jnp.sum(dr, axis=0, keepdims=True),
        )

    zero = jnp.zeros((1, width), F32)
    return lax.fori_loop(0, rows // step, body, (zero, zero, zero))


def backward_kernel(n_layers, *refs):
    n_in, per_layer = 8, 11
    w_all, dy_in, cos_in, sin_in, low_in, qrow_ref, kcol_ref, vectors = refs[:n_in]
    saved = [refs[n_in + l * per_layer : n_in + (l + 1) * per_layer] for l in range(n_layers)]
    at = n_in + n_layers * per_layer
    (
        tokens_out,
        result_out,
        qkv_out,
        bqkv_out,
        outw_out,
        vec_out,
        in_out,
        bin_out,
        back_out,
    ) = refs[at : at + 9]
    (
        pool,
        gp_ref,
        r1_ref,
        r2_ref,
        acc_ref,
        df_ref,
        dfin_ref,
        da_ref,
        dain_ref,
        h_ref,
        turn_ref,
        ht_ref,
        dft_ref,
        du_ref,
        t_ref,
        one_in,
        two_in,
        z_in,
        dwo_ref,
        ta_ref,
        a_one_in,
        a_two_in,
        a_z_in,
        a_c_in,
        a_sum_ref,
        a_out_ref,
        wa,
        q_ref,
        k_ref,
        v_ref,
        mixed_ref,
        lse_ref,
        delta_ref,
        dz_ref,
        dt_ref,
        dqt_ref,
        pair_ref,
        cos_ref,
        sin_ref,
        dxc_in,
        dxp_in,
        back_in,
        v_stage,
        v_in,
        dbin_ref,
        across_ref,
        feed_sum,
        c_send,
        c_recv,
        one_send,
        one_recv,
        two_send,
        two_recv,
        z_send,
        z_recv,
        a_send,
        a_recv,
        x_send,
        x_recv,
        v_send,
        v_recv,
        t_send,
        t_recv,
        w_sem,
        s_sem,
        o_sem,
    ) = refs[at + 9 :]
    part_ref, dxs_ref, dxp_ref = r2_ref, h_ref, df_ref
    rows, width = acc_ref.shape
    height = t_ref.shape[3]
    queries = 2 * rows

    d = lax.axis_index("dp")
    z = lax.axis_index("mp")
    c, groups, device = place_of(d, z)
    sibling = device(groups[0], 1 - c, z)
    first = device(groups[1], c, z)
    second = device(groups[2], c, z)
    away = device(groups[0], 1 - c, (z + 2) % MP)
    pair = device(groups[0], c, z + 1 - 2 * (z % 2))
    mirror = mirrored(z)
    columns = [device(groups[0], c, mirror[m]) for m in range(1, MP)]
    across = columns[1]
    moved = c != z // 2

    barrier = pltpu.get_barrier_semaphore()
    partners = columns + [first, second, sibling, away]
    for partner in partners:
        pl.semaphore_signal(
            barrier, inc=1, device_id=partner, device_id_type=pl.DeviceIdType.MESH
        )

    def remote(source, target, send, recv, to):
        return pltpu.make_async_remote_copy(
            src_ref=source,
            dst_ref=target,
            send_sem=send,
            recv_sem=recv,
            device_id=to,
            device_id_type=pl.DeviceIdType.MESH,
        )

    def column(k):
        base = (z + 2 * (k // 2)) % MP
        return base + (k % 2) * (1 - 2 * (base % 2))

    own_z = head_columns_of(z, c)

    def load(source, target, sem):
        return pltpu.make_async_copy(source, target, sem)

    def early_loads(l):
        _, _, _, _, _, _, r1s, r2s, _, _, hs = saved[l]
        return [
            load(r2s, r2_ref, s_sem.at[0]),
            load(r1s, r1_ref, s_sem.at[1]),
            load(hs, h_ref, s_sem.at[2]),
        ]

    def weight_loads(l, k):
        slot = k % 2
        gps = saved[l][9]
        return [
            load(w_all.at[3 * l + 2, column(k)], pool.at[2 + slot], w_sem.at[slot, 0]),
            load(w_all.at[3 * l + 1, column(k)], pool.at[slot], w_sem.at[slot, 1]),
            load(gps.at[column(k)], gp_ref.at[slot], w_sem.at[slot, 2]),
        ]

    def e_load(l, n):
        slot = n % 2
        es = saved[l][8]
        return load(es.at[column(MP - 1 - n)], pool.at[4 + slot], w_sem.at[slot, 3])

    def late_loads(l):
        _, qs, ks, vs, ms, ls = saved[l][:6]
        return [
            load(qs, q_ref, s_sem.at[3]),
            load(ks, k_ref, s_sem.at[4]),
            load(vs, v_ref, s_sem.at[5]),
            load(ms, mixed_ref, s_sem.at[6]),
            load(ls, lse_ref, s_sem.at[7]),
            load(w_all.at[3 * l, own_z[0]], wa.at[0], s_sem.at[8]),
            load(w_all.at[3 * l, own_z[1]], wa.at[1], s_sem.at[9]),
        ]

    def x_loads(l):
        xs = saved[l][0]
        return [
            load(xs.at[n], pool.at[2 + n // 2, pl.ds(n % 2 * rows, rows)], s_sem.at[14 + n])
            for n in range(4)
        ]

    dy_load = load(dy_in, df_ref, s_sem.at[11])
    table_loads = [load(cos_in, cos_ref, s_sem.at[12]), load(sin_in, sin_ref, s_sem.at[13])]
    dy_load.start()
    for copy in early_loads(n_layers - 1) + [e_load(n_layers - 1, 0)]:
        copy.start()
    for copy in weight_loads(n_layers - 1, 0):
        copy.start()
    for copy in table_loads + late_loads(n_layers - 1):
        copy.start()

    def df_copy(l):
        return remote(df_ref, dfin_ref, c_send.at[l, 0], c_recv.at[l, 0], sibling)

    def da_copy(l):
        return remote(da_ref, dain_ref, c_send.at[l, 1], c_recv.at[l, 1], sibling)

    def du_copy(l, k):
        return remote(
            du_ref.at[k, pl.ds(0, rows)],
            du_ref.at[k, pl.ds(rows, rows)],
            c_send.at[l, 2 + k],
            c_recv.at[l, 2 + k],
            sibling,
        )

    def dxs_copy(l, n):
        return remote(
            dxs_ref.at[n], dxc_in.at[n], c_send.at[l, 6 + n], c_recv.at[l, 6 + n], sibling
        )

    halves = [pl.ds(n * (rows // 2), rows // 2) for n in range(2)]

    def dxp_copy(l, n):
        return remote(
            dxp_ref.at[halves[n]],
            dxp_in.at[l, halves[n]],
            x_send.at[l, n],
            x_recv.at[l, n],
            pair,
        )

    def back_copy(n):
        return remote(
            df_ref.at[halves[n]], back_in.at[halves[n]], t_send.at[2 * n], t_recv.at[2 * n], away
        )

    def one_copy(l, h, k, n):
        return remote(
            t_ref.at[h, k, groups[1 if n == 0 else 3]],
            one_in.at[h, k, n],
            one_send.at[l, h, k, n],
            one_recv.at[l, h, k, n],
            first,
        )

    def two_copy(l, h, k):
        return remote(
            t_ref.at[h, k, groups[2]],
            two_in.at[h, k],
            two_send.at[l, h, k],
            two_recv.at[l, h, k],
            second,
        )

    def z_copy(l, h, k):
        return remote(
            across_ref.at[h] if k == 2 else t_ref.at[h, k, groups[0]],
            z_in.at[l, h, k - 1],
            z_send.at[l, h, k],
            z_recv.at[l, h, k],
            across if k == 2 else pair,
        )

    def span(group):
        return pl.ds(pl.multiple_of(group * 2 * height, 32), 2 * height)

    def a_one_copy(l, i, n):
        return remote(
            ta_ref.at[i, span(groups[1 if n == 0 else 3]), :],
            a_one_in.at[i, n],
            a_send.at[l, i, n],
            a_recv.at[l, i, n],
            first,
        )

    def a_two_copy(l, i):
        return remote(
            ta_ref.at[i, span(groups[2]), :],
            a_two_in.at[i],
            a_send.at[l, i, 2],
            a_recv.at[l, i, 2],
            second,
        )

    def a_z_copy(l, i):
        return remote(
            ta_ref.at[i, span(groups[0]), :],
            a_z_in.at[i],
            a_send.at[l, i, 3],
            a_recv.at[l, i, 3],
            pair if i == 1 else across,
        )

    def a_c_copy(l):
        return remote(a_out_ref, a_c_in.at[l], c_send.at[l, 8], c_recv.at[l, 8], sibling)

    def v_copy(l, n):
        to = (sibling, first, second, columns[0], columns[1], columns[2])[n]
        return remote(
            v_stage.at[l, min(n, 3)], v_in.at[l, n], v_send.at[l, n], v_recv.at[l, n], to
        )

    def step_one(l, h, k):
        for n in range(2):
            one_copy(l, h, k, n).wait_recv()
        g = groups[2]
        t_ref[h, k, g] = (t_ref[h, k, g].astype(F32) + one_in[h, k, 1].astype(F32)).astype(BF16)
        two_copy(l, h, k).start()

    def step_two(l, h, k):
        two_copy(l, h, k).wait_recv()
        g = groups[0]
        total = (
            t_ref[h, k, g].astype(F32) + one_in[h, k, 0].astype(F32) + two_in[h, k].astype(F32)
        )
        if k == 0:
            feed_sum[h] = total
            return
        if k == 2:
            z_copy(l, h, 3).wait_recv()
            if l + 1 < n_layers:
                z_copy(l + 1, h, 2).wait_send()
            across_ref[h] = (total + z_in[l, h, 2].astype(F32)).astype(BF16)
        else:
            t_ref[h, k, g] = total.astype(BF16)
        z_copy(l, h, k).start()

    def step_feed_end(l, h):
        total = feed_sum[h]
        for k in range(1, MP - 1):
            z_copy(l, h, k).wait_recv()
            total = total + z_in[l, h, k - 1].astype(F32)
        if h == 1:
            in_out[l] = total
        else:
            back_out[l] = jnp.transpose(total)

    def feed_sent(l, h):
        for k in range(MP):
            for n in range(2):
                one_copy(l, h, k, n).wait_send()
            two_copy(l, h, k).wait_send()
            if k in (1, 3):
                z_copy(l, h, k).wait_send()

    def step_a_one(l, i):
        for n in range(2):
            a_one_copy(l, i, n).wait_recv()
        at = span(groups[2])
        ta_ref[i, at, :] = (ta_ref[i, at, :].astype(F32) + a_one_in[i, 1].astype(F32)).astype(BF16)
        a_two_copy(l, i).start()

    def step_a_two(l, i):
        a_two_copy(l, i).wait_recv()
        at = span(groups[0])
        total = (
            ta_ref[i, at, :].astype(F32)
            + a_one_in[i, 0].astype(F32)
            + a_two_in[i].astype(F32)
        )
        if i == 1:
            ta_ref[i, at, :] = total.astype(BF16)
            a_z_copy(l, 1).start()
        else:
            a_z_copy(l, 1).wait_recv()
            total = total + a_z_in[1].astype(F32)
            a_sum_ref[...] = total

            @pl.when(c == 1)
            def _():
                ta_ref[i, at, :] = total.astype(BF16)
                a_z_copy(l, 0).start()

    def step_a_z(l):
        @pl.when(c == 1)
        def _():
            a_z_copy(l, 0).wait_recv()
            a_sum_ref[...] = a_z_in[0].astype(F32)

        other = pl.ds(pl.multiple_of((1 - c) * height, 32), height)
        a_out_ref[...] = a_sum_ref[other, :].astype(BF16)
        a_c_copy(l).start()

    def step_a_end(l):
        a_c_copy(l).wait_recv()
        own = pl.ds(pl.multiple_of(c * height, 32), height)
        total = a_sum_ref[own, :] + a_c_in[l].astype(F32)
        tile = [total[:, n * LANES : (n + 1) * LANES] for n in range(6)]
        turned_one = pltpu.roll(tile[1], HD, 1)
        turned_four = pltpu.roll(tile[4], HD, 1)
        for n, (two, one) in enumerate(
            ((tile[0], tile[1]), (tile[2], turned_one), (tile[3], tile[4]))
        ):
            qkv_out[l, n, :, 0:LANES] = two
            qkv_out[l, n, :, LANES:] = one[:, :HD]
        outw_out[l, 0:LANES, :] = jnp.transpose(tile[5])
        outw_out[l, LANES:, :] = jnp.transpose(turned_four)[:HD]

    def a_sent(l, i):
        for n in range(2):
            a_one_copy(l, i, n).wait_send()
        a_two_copy(l, i).wait_send()
        if i == 1:
            a_z_copy(l, 1).wait_send()
        else:

            @pl.when(c == 1)
            def _():
                a_z_copy(l, 0).wait_send()

    def step_v(l, n):
        v_copy(l, n - 1).wait_recv()
        v_stage[l, n] = v_stage[l, n - 1] + v_in[l, n - 1]
        if n < 3:
            v_copy(l, n).start()
        else:
            for s in range(3, 6):
                v_copy(l, s).start()

    def step_v_end(l):
        total = v_stage[l, 3, 0:6, :]
        one = v_stage[l, 3, 6:7, :]
        two = v_stage[l, 3, 10:11, :]
        for s in range(1, MP):
            v_copy(l, 2 + s).wait_recv()
            got = v_in[l, 2 + s]
            total = total + got[0:6, :]
            one = one + got[6 + s : 7 + s, :]
            two = two + got[10 + s : 11 + s, :]
        vec_out[l] = total
        bin_out[l] = one
        turned_one = pltpu.roll(two[:, LANES : 2 * LANES], HD, 1)
        for n, at in enumerate((0, 2, 3)):
            bqkv_out[l, n : n + 1, 0:LANES] = two[:, at * LANES : (at + 1) * LANES]
        bqkv_out[l, 0:1, LANES:] = two[:, LANES : LANES + HD]
        bqkv_out[l, 1:2, LANES:] = turned_one[:, :HD]
        bqkv_out[l, 2:3, LANES:] = two[:, 4 * LANES : 4 * LANES + HD]

    result_copy = remote(low_in, result_out, t_send.at[1], t_recv.at[1], away)
    result_local = pltpu.make_async_copy(low_in, result_out, o_sem.at[1])
    kblock = 256
    for l in reversed(range(n_layers)):
        top = l == n_layers - 1
        vec = vectors[l]
        copies = early_loads(l)
        if top:
            dy_load.wait()
            acc_ref[...] = df_ref[...].astype(F32)
        else:
            for n in range(2):
                dxp_copy(l + 1, n).wait_send()
        for copy in copies:
            copy.wait()
        v_stage[l, 0] = jnp.zeros((16, width), F32)
        sums = norm_back_rows(acc_ref, r2_ref, df_ref, vec[4:5, :])
        v_stage[l, 0, 4:5, :], v_stage[l, 0, 5:6, :], v_stage[l, 0, 3:4, :] = sums
        if top:
            pl.semaphore_wait(barrier, len(partners))
        df_copy(l).start()
        if top:

            @pl.when(moved)
            def _():
                result_copy.start()

            @pl.when(jnp.logical_not(moved))
            def _():
                result_local.start()

        def turned(source, target, half):
            turn_ref[...] = jnp.transpose(source)
            for g in range(4):
                at = pl.ds(pl.multiple_of((2 * g + c) * height, 32), height)
                target[pl.ds(g * height, height), pl.ds(half * rows, rows)] = turn_ref[at, :]

        turned(df_ref[...], dft_ref, 0)
        turned(h_ref[0], ht_ref, 0)
        turned(h_ref[1], ht_ref, 1)
        if not top:
            feed_sent(l + 1, 0)
            step_v(l + 1, 1)
        df_copy(l).wait_recv()
        turned(dfin_ref[...], dft_ref, 1)

        def back_grads(n, _, l=l):
            e_load(l, n).wait()

            @pl.when(n + 1 < MP)
            def _():
                e_load(l, n + 1).start()

            k = MP - 1 - n
            grad = nn(dft_ref[...], pool[4 + n % 2]).astype(BF16)
            t_ref[0, k] = grad.reshape(4, height, width)
            for to in range(2):
                one_copy(l, 0, k, to).start()
            return 0

        lax.fori_loop(0, MP, back_grads, 0)
        if not top:
            for k in range(MP):
                du_copy(l + 1, k).wait_send()

        def inner(k, _, l=l):
            for copy in weight_loads(l, k):
                copy.wait()

            @pl.when(k + 1 < MP)
            def _():
                for copy in weight_loads(l, k + 1):
                    copy.start()

            slot = k % 2
            de = nn(df_ref[...], pool[2 + slot])
            du = de * gp_ref[slot].astype(F32)
            dbin_ref[k] = jnp.sum(du, axis=0, keepdims=True)
            dub = du.astype(BF16)
            du_ref[k, pl.ds(0, rows), :] = dub
            du_copy(l, k).start()
            acc_ref[...] += nt(dub, pool[slot])
            return 0

        lax.fori_loop(0, MP, inner, 0)
        for copy in x_loads(l):
            copy.start()
        for k in range(MP):
            v_stage[l, 0, 6 + k : 7 + k, :] = dbin_ref[k]
        if not top:
            step_a_two(l + 1, 1)
            step_a_one(l + 1, 0)
            for h in range(2):
                step_feed_end(l + 1, h)
            step_v(l + 1, 2)
            da_copy(l + 1).wait_send()
        sums = norm_back_rows(acc_ref, r1_ref, da_ref, vec[1:2, :])
        v_stage[l, 0, 1:2, :], v_stage[l, 0, 2:3, :], v_stage[l, 0, 0:1, :] = sums
        da_copy(l).start()
        for k in (3, 2, 1, 0):
            step_one(l, 0, k)
        if not top:
            feed_sent(l + 1, 1)

        def in_grads(n, _, l=l):
            k = MP - 1 - n
            du_copy(l, k).wait_recv()
            grad = nn(ht_ref[...], du_ref[k]).astype(BF16)
            t_ref[1, k] = grad.reshape(4, height, width)
            for to in range(2):
                one_copy(l, 1, k, to).start()
            return 0

        lax.fori_loop(0, MP, in_grads, 0)
        if not top:
            step_a_two(l + 1, 0)
            step_v(l + 1, 3)
        for copy in late_loads(l):
            copy.wait()
        da_copy(l).wait_recv()
        low_half = lane_index((rows, LANES)) < HD
        for half, source in enumerate((da_ref, dain_ref)):
            at = pl.ds(half * rows, rows)
            for i in range(2):
                dz = nn(source[...], wa[i, :, 4 * LANES :])
                dz_ref[i, 0, at, :] = dz[:, LANES:].astype(BF16)
                dz_ref[i, 1, at, :] = jnp.where(
                    low_half, pltpu.roll(dz[:, :LANES], HD, 1), 0.0
                ).astype(BF16)
            pool[6, :, pl.ds(half * rows, rows)] = jnp.transpose(source[...])
        for i in range(2):
            dwo_ref[i] = nn(pool[6], mixed_ref[:, i * 256 : i * 256 + 256]).astype(BF16)
            head_deltas(i, mixed_ref, dz_ref, delta_ref)
        for copy in x_loads(l):
            copy.wait()
        for half in range(2):
            pool[half] = jnp.transpose(pool[2 + half])
        if top:
            for copy in table_loads:
                copy.wait()
        steps = [[] for _ in range(6)]
        if not top:
            steps[0] = [partial(step_v_end, l + 1), partial(step_a_z, l + 1)]
            steps[1] = [partial(step_a_end, l + 1)]
        steps[0] += [partial(step_two, l, 0, k) for k in (3, 1, 0)]
        steps[1] += [partial(step_one, l, 1, k) for k in (3, 2, 1, 0)]
        steps[2].append(partial(step_two, l, 0, 2))
        steps[3] = [partial(step_two, l, 1, k) for k in (3, 1, 0)]
        steps[5] = [partial(step_two, l, 1, 2), partial(step_a_one, l, 1)]

        def weight_grads(i, l=l, top=top):
            if not top:
                a_sent(l + 1, i)
                if i == 0:
                    a_c_copy(l + 1).wait_send()
            low = [pool.at[2 + 2 * i + half] for half in range(2)]
            ta_ref[i, :, 0:LANES] = nn(pool[0], low[0][:, 0:LANES]).astype(BF16)
            more = nn(pool[0], low[0][:, LANES : 5 * LANES]) + nn(
                pool[1], low[1][:, LANES : 5 * LANES]
            )
            ta_ref[i, :, LANES : 4 * LANES] = more[:, : 3 * LANES].astype(BF16)
            ta_ref[i, :, 4 * LANES : 5 * LANES] = (
                more[:, 3 * LANES :] + dwo_ref[i, :, 0:LANES].astype(F32)
            ).astype(BF16)
            ta_ref[i, :, 5 * LANES :] = dwo_ref[i, :, LANES:]
            for n in range(2):
                a_one_copy(l, i, n).start()

        for turn, i in enumerate((1, 0)):
            for h in range(3):
                head_back(
                    i,
                    h,
                    kblock,
                    q_ref,
                    k_ref,
                    v_ref,
                    dz_ref,
                    lse_ref,
                    delta_ref,
                    qrow_ref,
                    kcol_ref,
                    pair_ref,
                    dqt_ref,
                    dt_ref,
                )
                for step in steps[3 * turn + h]:
                    step()
            for tile in range(5):
                total = jnp.zeros((1, LANES), F32)
                for half in range(1 if tile == 0 else 2):
                    at = pl.ds(half * queries, queries)
                    t = dt_ref[tile, at, :]
                    if tile < 3:
                        t = t * cos_ref[at, :] - half_swap(t) * sin_ref[at, :]
                    total = total + jnp.sum(t, axis=0, keepdims=True)
                    pool[2 + 2 * i + half, :, tile * LANES : (tile + 1) * LANES] = t.astype(BF16)
                for core in range(2):
                    v_stage[
                        l, 0, 10 + 2 * core + i : 11 + 2 * core + i, tile * LANES : (tile + 1) * LANES
                    ] = jnp.where(c == core, total, 0.0)
            if i == 1:
                weight_grads(1)
        v_copy(l, 0).start()

        def spread(n):
            half, at = n // 2, pl.ds((n % 2) * rows, rows)
            total = jnp.zeros((rows, width), F32)
            for i in range(2):
                low = pool.at[2 + 2 * i + half]
                total = total + nt(low[at, LANES : 5 * LANES], wa[i, :, LANES : 5 * LANES])
                if half == 0:
                    total = total + nt(low[at, 0:LANES], wa[i, :, 0:LANES])
            return total

        df_copy(l).wait_send()
        dxs_ref[1] = spread(3).astype(BF16)
        dxs_copy(l, 1).start()
        part_ref[...] = spread(2)
        dxs_copy(l, 1).wait_recv()
        dxp_ref[...] = (part_ref[...] + dxc_in[1].astype(F32)).astype(BF16)
        for n in range(2):
            dxp_copy(l, n).start()
        dxs_ref[0] = spread(1).astype(BF16)
        dxs_copy(l, 0).start()
        acc_ref[...] += spread(0)
        weight_grads(0)
        dxs_copy(l, 0).wait_recv()
        acc_ref[...] += dxc_in[0].astype(F32)
        if l > 0:
            for n in range(2):
                dxs_copy(l, n).wait_send()
            first_loads = early_loads(l - 1) + [e_load(l - 1, 0)] + weight_loads(l - 1, 0)
            for copy in first_loads + late_loads(l - 1):
                copy.start()
        for n in range(2):
            dxp_copy(l, n).wait_recv()
            acc_ref[halves[n], :] += dxp_in[l, halves[n], :].astype(F32)
            if l == 0:
                dxp_copy(0, n).wait_send()
                df_ref[halves[n], :] = acc_ref[halves[n], :].astype(BF16)

                @pl.when(moved)
                def _(n=n):
                    back_copy(n).start()

    step_v(0, 1)
    step_a_two(0, 1)
    for h in range(2):
        step_feed_end(0, h)
    step_a_one(0, 0)
    step_v(0, 2)
    step_a_two(0, 0)
    step_v(0, 3)
    step_v_end(0)

    @pl.when(moved)
    def _():
        for n in range(2):
            back_copy(n).wait_recv()
        acc_ref[...] = back_in[...].astype(F32)

    out_copy = pltpu.make_async_copy(acc_ref, tokens_out, o_sem.at[0])
    out_copy.start()
    step_a_z(0)
    step_a_end(0)
    out_copy.wait()

    @pl.when(moved)
    def _():
        for n in range(2):
            back_copy(n).wait_send()
        result_copy.wait_send()
        result_copy.wait_recv()

    @pl.when(jnp.logical_not(moved))
    def _():
        result_local.wait()

    da_copy(0).wait_send()
    for n in range(2):
        dxs_copy(0, n).wait_send()
    for k in range(MP):
        du_copy(0, k).wait_send()
    for h in range(2):
        feed_sent(0, h)
        z_copy(0, h, 2).wait_send()
    for i in range(2):
        a_sent(0, i)
    a_c_copy(0).wait_send()
    for l in range(n_layers):
        for n in range(6):
            v_copy(l, n).wait_send()


def backward(w_all, dy, cos, sin, low, qrow, kcol, vectors, states):
    n_layers, _, width = vectors.shape
    rows = dy.shape[0]
    height = width // 8
    queries, keys = 2 * rows, 4 * rows
    sem = pltpu.SemaphoreType.DMA
    flat = [array for state in states for array in state]
    return pl.pallas_call(
        partial(backward_kernel, n_layers),
        out_shape=(
            shape((rows, width), F32),
            shape((rows, width), BF16),
            shape((n_layers, 3, height, 3 * HD), F32),
            shape((n_layers, 3, 3 * HD), F32),
            shape((n_layers, 3 * HD, height), F32),
            shape((n_layers, 6, width), F32),
            shape((n_layers, height, width), F32),
            shape((n_layers, 1, width), F32),
            shape((n_layers, width, height), F32),
        ),
        in_specs=[anywhere()] * 5 + [vmem()] * 3 + [anywhere()] * len(flat),
        out_specs=(anywhere(), anywhere()) + (vmem(),) * 7,
        scratch_shapes=[
            pltpu.VMEM((7, width, width), BF16),
            pltpu.VMEM((2, rows, width), BF16),
            pltpu.VMEM((rows, width), F32),
            pltpu.VMEM((rows, width), F32),
            pltpu.VMEM((rows, width), F32),
            pltpu.VMEM((rows, width), BF16),
            pltpu.VMEM((rows, width), BF16),
            pltpu.VMEM((rows, width), BF16),
            pltpu.VMEM((rows, width), BF16),
            pltpu.VMEM((2, rows, width), BF16),
            pltpu.VMEM((width, rows), BF16),
            pltpu.VMEM((4 * height, 2 * rows), BF16),
            pltpu.VMEM((4 * height, 2 * rows), BF16),
            pltpu.VMEM((MP, 2 * rows, width), BF16),
            pltpu.VMEM((2, MP, 4, height, width), BF16),
            pltpu.VMEM((2, MP, 2, height, width), BF16),
            pltpu.VMEM((2, MP, height, width), BF16),
            pltpu.VMEM((n_layers, 2, MP - 1, height, width), BF16),
            pltpu.VMEM((2, width, 2 * LANES), BF16),
            pltpu.VMEM((2, width, width), BF16),
            pltpu.VMEM((2, 2, 2 * height, width), BF16),
            pltpu.VMEM((2, 2 * height, width), BF16),
            pltpu.VMEM((2, 2 * height, width), BF16),
            pltpu.VMEM((n_layers, height, width), BF16),
            pltpu.VMEM((2 * height, width), F32),
            pltpu.VMEM((height, width), BF16),
            pltpu.VMEM((2, width, width), BF16),
            pltpu.VMEM((2, 2, queries, LANES), BF16),
            pltpu.VMEM((2, 2, keys, LANES), BF16),
            pltpu.VMEM((2, 2, keys, LANES), BF16),
            pltpu.VMEM((queries, 512), BF16),
            pltpu.VMEM((8, queries), F32),
            pltpu.VMEM((8, queries), F32),
            pltpu.VMEM((2, 2, queries, LANES), BF16),
            pltpu.VMEM((5, keys, LANES), F32),
            pltpu.VMEM((LANES, queries), F32),
            pltpu.VMEM((2, queries, LANES), BF16),
            pltpu.VMEM((keys, LANES), F32),
            pltpu.VMEM((keys, LANES), F32),
            pltpu.VMEM((2, rows, width), BF16),
            pltpu.VMEM((n_layers, rows, width), BF16),
            pltpu.VMEM((rows, width), BF16),
            pltpu.VMEM((n_layers, 4, 16, width), F32),
            pltpu.VMEM((n_layers, 6, 16, width), F32),
            pltpu.VMEM((MP, 1, width), F32),
            pltpu.VMEM((2, height, width), BF16),
            pltpu.VMEM((2, height, width), F32),
            sem((n_layers, 9)),
            sem((n_layers, 9)),
            sem((n_layers, 2, MP, 2)),
            sem((n_layers, 2, MP, 2)),
            sem((n_layers, 2, MP)),
            sem((n_layers, 2, MP)),
            sem((n_layers, 2, MP)),
            sem((n_layers, 2, MP)),
            sem((n_layers, 2, 4)),
            sem((n_layers, 2, 4)),
            sem((n_layers, 2)),
            sem((n_layers, 2)),
            sem((n_layers, 6)),
            sem((n_layers, 6)),
            sem((3,)),
            sem((3,)),
            sem((2, 4)),
            sem((18,)),
            sem((2,)),
        ],
        compiler_params=pltpu.CompilerParams(
            vmem_limit_bytes=BACK_LIMIT, collective_id=1, has_side_effects=True
        ),
        cost_estimate=pl.CostEstimate(
            flops=200_000_000_000, bytes_accessed=100_000_000, transcendentals=20_000_000
        ),
        name="backward",
    )(w_all, dy, cos, sin, low, qrow, kcol, vectors, *flat)


def attend_kernel(chunk, *refs):
    scal, x_ref, bias_ref, cos_ref, sin_ref, qcode_ref, kcode_ref, w_all = refs[:8]
    q_ref, k_ref, v_ref, mixed_ref, lse_ref, w_ref, lse_cols, sems = refs[8:]
    copies = [
        pltpu.make_async_copy(
            w_all.at[chunk, scal[k], :, pl.ds(0, 5 * LANES)], w_ref.at[k], sems.at[k]
        )
        for k in range(2)
    ]
    for copy in copies:
        copy.start()
    for copy in copies:
        copy.wait()
    rows = x_ref.shape[1]
    for i in range(4):
        at = pl.ds(i * rows, rows)
        for k in range(2):
            project_rows(
                i,
                k,
                x_ref[i],
                w_ref,
                bias_ref[k],
                cos_ref[at, :],
                sin_ref[at, :],
                q_ref,
                k_ref,
                v_ref,
            )
    lse_cols[...] = jnp.zeros_like(lse_cols)

    def one_block(i, _):
        attend_rows(i, 256, qcode_ref, kcode_ref, q_ref, k_ref, v_ref, mixed_ref, lse_cols)
        return 0

    lax.fori_loop(0, 2 * rows // 256, one_block, 0)
    lse_ref[...] = jnp.transpose(lse_cols[...])[0:8, :]


def attend(scal, x_full, bias, tables, qcode, kcode, w_all, chunk):
    cos, sin = tables[:2]
    _, rows, width = x_full.shape
    queries, keys = 2 * rows, 4 * rows
    return pl.pallas_call(
        partial(attend_kernel, chunk),
        out_shape=(
            shape((2, 2, queries, LANES), BF16),
            shape((2, 2, keys, LANES), BF16),
            shape((2, 2, keys, LANES), BF16),
            shape((queries, 512), BF16),
            shape((8, queries), F32),
        ),
        in_specs=[smem()] + [vmem()] * 6 + [anywhere()],
        out_specs=(vmem(),) * 5,
        scratch_shapes=[
            pltpu.VMEM((2, width, 5 * LANES), BF16),
            pltpu.VMEM((queries, LANES), F32),
            pltpu.SemaphoreType.DMA((2,)),
        ],
        compiler_params=params(),
        name="attend",
    )(scal, x_full, bias, cos, sin, qcode, kcode, w_all)


def feed_kernel(chunk, *refs):
    scal, x_ref, own_ref, sib_ref, vec_ref, bin_ref, w_all = refs[:7]
    next_ref, low_ref, r1_ref, r2_ref, e_ref, gp_ref, wo_ref, win_ref, wback_ref, sems = refs[7:]
    copies = [
        pltpu.make_async_copy(
            w_all.at[chunk, :, :, pl.ds(4 * LANES, 2 * LANES)], wo_ref, sems.at[0]
        ),
        pltpu.make_async_copy(w_all.at[chunk + 1], win_ref, sems.at[1]),
        pltpu.make_async_copy(w_all.at[chunk + 2], wback_ref, sems.at[2]),
    ]
    for copy in copies:
        copy.start()
    for copy in copies:
        copy.wait()
    a = jnp.zeros(x_ref.shape, F32)
    for k in range(2):
        a = a + nt(own_ref[:, k * 256 : k * 256 + 256], wo_ref[scal[k]])
        a = a + nt(sib_ref[:, k * 256 : k * 256 + 256], wo_ref[lax.rem(scal[k] + 2, MP)])
    r1 = x_ref[...] + a + vec_ref[0:1, :]
    r1_ref[...] = r1
    n1, _ = norm_parts(r1)
    h = n1 * vec_ref[1:2, :] + vec_ref[2:3, :]
    low_ref[...] = h.astype(BF16)
    r2_ref[...] = h + vec_ref[3:4, :]

    def one(z, _):
        u = nn(low_ref[...], win_ref[z]) + bin_ref[z]
        cdf = 0.5 * (1.0 + lax.erf(u * (2.0**-0.5)))
        pdf = jnp.exp(u * u * -0.5) * 0.3989422804014327
        e = (u * cdf).astype(BF16)
        e_ref[z] = e
        gp_ref[z] = (cdf + u * pdf).astype(BF16)
        r2_ref[...] += nt(e, wback_ref[z])
        return 0

    lax.fori_loop(0, MP, one, 0)
    n2, _ = norm_parts(r2_ref[...])
    result = n2 * vec_ref[4:5, :] + vec_ref[5:6, :]
    next_ref[...] = result
    low_ref[...] = result.astype(BF16)


def feed_forward(scal, x, own, sib, vec, bias_in, w_all, chunk):
    rows, width = x.shape
    return pl.pallas_call(
        partial(feed_kernel, chunk),
        out_shape=(
            shape((rows, width), F32),
            shape((rows, width), BF16),
            shape((rows, width), F32),
            shape((rows, width), F32),
            shape((MP, rows, width), BF16),
            shape((MP, rows, width), BF16),
        ),
        in_specs=[smem()] + [vmem()] * 5 + [anywhere()],
        out_specs=(vmem(),) * 6,
        scratch_shapes=[
            pltpu.VMEM((MP, width, 2 * LANES), BF16),
            pltpu.VMEM((MP, width, width), BF16),
            pltpu.VMEM((MP, width, width), BF16),
            pltpu.SemaphoreType.DMA((3,)),
        ],
        compiler_params=params(),
        name="feed",
    )(scal, x, own, sib, vec, bias_in, w_all)


def plain_forward(blocks, tokens, cot, small, meta, frequency, vectors):
    n_layers = vectors.shape[0]
    rows, width = tokens.shape
    c, z = lax.axis_index("dp") % 2, lax.axis_index("mp")
    w_all = lax.all_gather(blocks, "dp", axis=1, tiled=True)
    w_all = jnp.swapaxes(lax.all_gather(w_all, "mp", axis=0, tiled=False), 0, 1)
    small_all = lax.all_gather(small, "mp", axis=0, tiled=False)
    own_z = jnp.stack([(z - 2 * c - k) % MP for k in range(2)]).astype(jnp.int32)
    info = jnp.where(z // 2 == c, meta, core_swap(meta))
    place = z % 2
    quarters = [2 * c + place, 2 * (1 - c) + place, 2 * c + 1 - place, 2 * (1 - c) + 1 - place]
    positions = jnp.concatenate(
        [q * rows + jnp.arange(rows, dtype=jnp.int32) for q in quarters]
    ).astype(F32)
    slot = info[0, 0]
    seq = jnp.where(positions >= slot, 1.0, 0.0) + jnp.where(positions >= 2.0 * slot, 1.0, 0.0)
    place = positions - seq * slot
    limit = jnp.where(seq == 0.0, info[1, 0], jnp.where(seq == 1.0, info[2, 0], info[3, 0]))
    kcode = jnp.where(place < limit, seq, -1.0)
    qcode = seq[: 2 * rows]
    angles = place[:, None] * frequency
    sign = jnp.where(jnp.arange(LANES) % HD < HD // 2, -1.0, 1.0)
    cos, sin = jnp.cos(angles), jnp.sin(angles) * sign[None, :]
    low = relayout(tokens)
    stream = low.astype(F32)
    states = []
    for l in range(n_layers):
        two = jnp.stack([low, pair_swap(low)])
        others = core_swap(two)
        x_full = jnp.stack([two[0], others[0], two[1], others[1]])
        bias = jnp.stack(
            [
                lax.dynamic_index_in_dim(small_all, own_z[k], 0, False)[l : l + 1, : 5 * LANES]
                for k in range(2)
            ]
        )
        q, k, v, mixed, lse = attend(
            own_z, x_full, bias, (cos, sin), qcode[:, None], kcode[None, :], w_all, 3 * l
        )
        other = core_swap(mixed[rows:])
        stream, low, r1, r2, e, gp = feed_forward(
            own_z,
            stream,
            mixed[:rows],
            other,
            vectors[l],
            small_all[:, l : l + 1, 5 * LANES :],
            w_all,
            3 * l,
        )
        states.append((x_full, q, k, v, mixed, other, lse, r1, r2, e, gp))
    return (w_all, relayout(cot), low, cos, sin, qcode[None, :], kcode[:, None]), states


def feed_back_kernel(n_pieces, rows, chunk, *refs):
    scal, dy_ref, r1_ref, r2_ref, e_ref, gp_ref, own_ref, sib_ref, vec_ref, w_all = refs[:10]
    at = 10
    dr1_ref, dzown_ref, dzsib_ref, dvec_ref, dbin_ref = refs[at : at + 5]
    outs = 2 if n_pieces == 8 else 1
    grads = refs[at + 5 : at + 5 + outs]
    wo_ref, win_ref, wback_ref, df_ref, dft_ref, ht_ref, dw_ref, sems = refs[at + 5 + outs :]
    width = dy_ref.shape[1]
    columns = [scal[n_pieces + k] for k in range(MP)]
    first_z = scal[n_pieces + MP]

    def fetch(source, target, base):
        copies = [
            pltpu.make_async_copy(source(columns[k]), target.at[k], sems.at[base + k])
            for k in range(MP)
        ]
        for copy in copies:
            copy.start()
        return copies

    back_copies = fetch(lambda z: w_all.at[chunk + 2, z], wback_ref, 0)
    in_copies = fetch(lambda z: w_all.at[chunk + 1, z], win_ref, MP)
    out_copies = fetch(
        lambda z: w_all.at[chunk, z, :, pl.ds(4 * LANES, 2 * LANES)], wo_ref, 2 * MP
    )
    dy = dy_ref[...]
    n2, scale2 = norm_parts(r2_ref[...])
    dvec_ref[4:5, :] = jnp.sum(dy * n2, axis=0, keepdims=True)
    dvec_ref[5:6, :] = jnp.sum(dy, axis=0, keepdims=True)
    dr2 = norm_back(dy, n2, scale2, vec_ref[4:5, :])
    dvec_ref[3:4, :] = jnp.sum(dr2, axis=0, keepdims=True)
    dr1_ref[...] = dr2
    df = dr2.astype(BF16)
    df_ref[...] = df
    dft_ref[...] = jnp.transpose(df)
    n1, _ = norm_parts(r1_ref[...])
    h = (n1 * vec_ref[1:2, :] + vec_ref[2:3, :]).astype(BF16)
    ht_ref[...] = jnp.transpose(h)
    for copy in back_copies + in_copies:
        copy.wait()

    def one(z, _):
        de = nn(df_ref[...], wback_ref[z])
        at = scal[n_pieces + z]
        du = de * gp_ref[at].astype(F32)
        dbin_ref[z] = jnp.sum(du, axis=0, keepdims=True)
        dub = du.astype(BF16)
        dr1_ref[...] += nt(dub, win_ref[z])
        dw_ref[z, :, 0:width] = nn(ht_ref[...], dub).astype(BF16)
        dw_ref[z, :, width : 2 * width] = nn(dft_ref[...], e_ref[at]).astype(BF16)
        return 0

    lax.fori_loop(0, MP, one, 0)
    dh = dr1_ref[...]
    n1, scale1 = norm_parts(r1_ref[...])
    dvec_ref[1:2, :] = jnp.sum(dh * n1, axis=0, keepdims=True)
    dvec_ref[2:3, :] = jnp.sum(dh, axis=0, keepdims=True)
    dr1 = norm_back(dh, n1, scale1, vec_ref[1:2, :])
    dvec_ref[0:1, :] = jnp.sum(dr1, axis=0, keepdims=True)
    dr1_ref[...] = dr1
    da = dr1.astype(BF16)
    dft_ref[...] = jnp.transpose(da)
    for copy in out_copies:
        copy.wait()
    used = lane_index((da.shape[0], 2 * LANES)) >= HD
    for z in range(2):
        for mixed_ref, dz_ref, z_at in (
            (own_ref, dzown_ref, first_z + z),
            (sib_ref, dzsib_ref, 2 - first_z + z),
        ):
            part = mixed_ref[:, z * 256 : z * 256 + 256]
            dw_ref[z_at, :, 2 * width :] = nn(dft_ref[...], part).astype(BF16)
            dz = nn(da, wo_ref[z_at])
            dz_ref[:, z * 256 : z * 256 + 256] = jnp.where(used, dz, 0.0).astype(BF16)
    flight = []
    for i in range(n_pieces):
        offset = pl.multiple_of(scal[i], 32)
        target = grads[i // 4].at[PIECE_ORDER[i % 4] if n_pieces == 8 else 0]
        copy = pltpu.make_async_copy(dw_ref.at[:, pl.ds(offset, rows), :], target, sems.at[i])
        copy.start()
        flight.append(copy)
    for copy in flight:
        copy.wait()


PIECE_ORDER = (3, 0, 2, 1)


def feed_back(scal, prows, count, dy, r1, r2, e, gp, own, sib, vec, w_all, chunk):
    rows, width = dy.shape
    lanes = 2 * width + 2 * LANES
    grads = (shape((4, MP, prows, lanes), BF16),) * 2
    if count != 8:
        grads = (shape((1, MP, prows, lanes), BF16),)
    return pl.pallas_call(
        partial(feed_back_kernel, count, prows, chunk),
        out_shape=(
            shape((rows, width), F32),
            shape((rows, 512), BF16),
            shape((rows, 512), BF16),
            shape((6, width), F32),
            shape((MP, 1, width), F32),
            *grads,
        ),
        in_specs=[smem()] + [vmem()] * 8 + [anywhere()],
        out_specs=(vmem(),) * 5 + (anywhere(),) * len(grads),
        scratch_shapes=[
            pltpu.VMEM((MP, width, 2 * LANES), BF16),
            pltpu.VMEM((MP, width, width), BF16),
            pltpu.VMEM((MP, width, width), BF16),
            pltpu.VMEM((rows, width), BF16),
            pltpu.VMEM((width, rows), BF16),
            pltpu.VMEM((width, rows), BF16),
            pltpu.VMEM((MP, width, lanes), BF16),
            pltpu.SemaphoreType.DMA((3 * MP,)),
        ],
        compiler_params=params(),
        cost_estimate=pl.CostEstimate(
            flops=16_000_000_000, bytes_accessed=40_000_000, transcendentals=0
        ),
        name="feed_back",
    )(scal, dy, r1, r2, e, gp, own, sib, vec, w_all)


def attend_back_kernel(n_pieces, chunk, *refs):
    (
        scal,
        x_ref,
        cos_ref,
        sin_ref,
        qcode_ref,
        kcode_ref,
        q_ref,
        k_ref,
        v_ref,
        mixed_ref,
        dzown_ref,
        dzsib_ref,
        lse_ref,
        w_all,
    ) = refs[:14]
    dx_ref, dxs_ref, dbias_ref, parts_ref = refs[14:18]
    (
        w_ref,
        xt_ref,
        dz_ref,
        delta_ref,
        dt_ref,
        dqt_ref,
        pair_ref,
        dw_ref,
        low_ref,
        sums_ref,
        sems,
    ) = refs[18:]
    copies = [
        pltpu.make_async_copy(
            w_all.at[chunk, scal[n_pieces + 9 + k], :, pl.ds(0, 5 * LANES)],
            w_ref.at[k],
            sems.at[k],
        )
        for k in range(2)
    ]
    for copy in copies:
        copy.start()
    keys, width = x_ref.shape
    queries = keys // 2
    block = queries // 2
    for z in range(2):
        for half, source in enumerate((dzown_ref, dzsib_ref)):
            at = pl.ds(half * block, block)
            dz_ref[z, 0, at, :] = source[:, z * 256 + LANES : z * 256 + 256]
            dz_ref[z, 1, at, :] = pltpu.roll(
                source[:, z * 256 : z * 256 + LANES].astype(F32), HD, 1
            ).astype(BF16)
        single = pltpu.roll(mixed_ref[:, z * 256 : z * 256 + LANES].astype(F32), HD, 1)
        pair = mixed_ref[:, z * 256 + LANES : z * 256 + 256].astype(F32)
        prod_one = jnp.transpose(pair * dz_ref[z, 0].astype(F32))
        prod_two = jnp.transpose(single * dz_ref[z, 1].astype(F32))
        delta_ref[3 * z : 3 * z + 1, :] = jnp.sum(prod_one[0:HD], axis=0, keepdims=True)
        delta_ref[3 * z + 1 : 3 * z + 2, :] = jnp.sum(prod_one[HD:], axis=0, keepdims=True)
        delta_ref[3 * z + 2 : 3 * z + 3, :] = jnp.sum(prod_two[0:HD], axis=0, keepdims=True)

    kblock = 256
    low_q = lane_index((queries, LANES)) < HD
    low_k = lane_index((kblock, LANES)) < HD
    for z in range(2):
        for h in range(3):
            tile = h // 2
            q = q_ref[z, tile]
            dz = dz_ref[z, tile]
            if h < 2:
                keep = low_q == (h == 0)
                q = jnp.where(keep, q, BF16(0))
                dz = jnp.where(keep, dz, BF16(0))
            pair_ref[0] = q
            pair_ref[1] = dz
            lse = lse_ref[3 * z + h : 3 * z + h + 1, :]
            delta = delta_ref[3 * z + h : 3 * z + h + 1, :]
            if h != 1:
                dqt_ref[...] = jnp.zeros_like(dqt_ref)

            def one_block(i, _, z=z, h=h, tile=tile, lse=lse, delta=delta):
                at = pl.ds(pl.multiple_of(i * kblock, kblock), kblock)
                kb = k_ref[z, tile, at, :]
                vb = v_ref[z, tile, at, :]
                if h < 2:
                    kb_own = jnp.where(low_k == (h == 0), kb, BF16(0))
                else:
                    kb_own = kb
                visible = kcode_ref[at, :] == qcode_ref[...]
                s = nt(kb, pair_ref[0])
                s = jnp.where(visible, s, NEGATIVE)
                p = jnp.exp(s - lse)
                dp = nt(vb, pair_ref[1])
                ds = (p * (dp - delta)).astype(BF16)
                dv = nn(p.astype(BF16), pair_ref[1])
                dk = nn(ds, pair_ref[0])
                dqt_ref[...] += nn(jnp.transpose(kb_own), ds)
                if h == 1:
                    dt_ref[2, at, :] += dk
                    dt_ref[3, at, :] += dv
                elif h == 0:
                    dt_ref[2, at, :] = dk
                    dt_ref[3, at, :] = dv
                else:
                    dt_ref[1, at, :] = pltpu.roll(dk, HD, 1)
                    dt_ref[4, at, :] = dv
                return 0

            lax.fori_loop(0, keys // kblock, one_block, 0)
            if h >= 1:
                dq = jnp.transpose(dqt_ref[...]) * HD**-0.5
                if h == 1:
                    dt_ref[0, 0:queries, :] = dq
                else:
                    dt_ref[1, 0:queries, :] += dq

        if z == 0:
            xt_ref[...] = jnp.transpose(x_ref[...])
            for copy in copies:
                copy.wait()
        for tile in range(5):
            count = queries if tile == 0 else keys
            t = dt_ref[tile, 0:count, :]
            if tile < 3:
                t = t * cos_ref[0:count, :] - half_swap(t) * sin_ref[0:count, :]
            dbias_ref[z, :, tile * LANES : (tile + 1) * LANES] = jnp.sum(t, axis=0, keepdims=True)
            low_ref[0:count, tile * LANES : (tile + 1) * LANES] = t.astype(BF16)
        dw_ref[z, :, 0:LANES] = nn(
            xt_ref[:, 0:queries], low_ref[0:queries, 0:LANES]
        ).astype(BF16)
        dw_ref[z, :, LANES:] = nn(xt_ref[...], low_ref[:, LANES:]).astype(BF16)
        for i in range(4):
            at = pl.ds(i * block, block)
            part = nt(low_ref[at, LANES:], w_ref[z, :, LANES : 5 * LANES])
            if i < 2:
                part = part + nt(low_ref[at, 0:LANES], w_ref[z, :, 0:LANES])
            if z == 0:
                sums_ref[i] = part
            else:
                target = dx_ref if i % 2 == 0 else dxs_ref
                target[i // 2] = (sums_ref[i] + part).astype(BF16)

    flight = []
    for i in range(min(n_pieces, 4)):
        offset = pl.multiple_of(scal[n_pieces + 5 + i], 32)
        copy = pltpu.make_async_copy(
            dw_ref.at[:, pl.ds(offset, parts_ref.shape[2]), :],
            parts_ref.at[PIECE_ORDER[i] if n_pieces == 8 else 0],
            sems.at[i],
        )
        copy.start()
        flight.append(copy)
    for copy in flight:
        copy.wait()


def attend_back(scal, prows, count, x_full, tables, saved, mixed, dz_own, dz_sib, w_all, chunk):
    cos, sin, qcode, kcode = tables
    q, k, v, lse = saved
    keys, width = x_full.shape
    queries = keys // 2
    block = queries // 2
    parts = (4, 2, 2 * prows, 5 * LANES)
    if count != 8:
        parts = (1, 2, prows, 5 * LANES)
    return pl.pallas_call(
        partial(attend_back_kernel, count, chunk),
        out_shape=(
            shape((2, block, width), BF16),
            shape((2, block, width), BF16),
            shape((2, 1, 5 * LANES), F32),
            shape(parts, BF16),
        ),
        in_specs=[smem()] + [vmem()] * 12 + [anywhere()],
        out_specs=(vmem(),) * 3 + (anywhere(),),
        scratch_shapes=[
            pltpu.VMEM((2, width, 5 * LANES), BF16),
            pltpu.VMEM((width, keys), BF16),
            pltpu.VMEM((2, 2, queries, LANES), BF16),
            pltpu.VMEM((8, queries), F32),
            pltpu.VMEM((5, keys, LANES), F32),
            pltpu.VMEM((LANES, queries), F32),
            pltpu.VMEM((2, queries, LANES), BF16),
            pltpu.VMEM((2, width, 5 * LANES), BF16),
            pltpu.VMEM((keys, 5 * LANES), BF16),
            pltpu.VMEM((4, block, width), F32),
            pltpu.SemaphoreType.DMA((4,)),
        ],
        compiler_params=params(),
        cost_estimate=pl.CostEstimate(
            flops=40_000_000_000, bytes_accessed=20_000_000, transcendentals=8_000_000
        ),
        name="attend_back",
    )(scal, x_full, cos, sin, qcode, kcode, q, k, v, mixed, dz_own, dz_sib, lse, w_all)


def head_tiles(q, k, v, o):
    return jnp.concatenate(
        [
            q[..., :LANES],
            q[..., LANES:],
            k[..., LANES:],
            k[..., :LANES],
            v[..., :LANES],
            v[..., LANES:],
            o[..., LANES:],
            o[..., :LANES],
        ],
        axis=-1,
    )


def head_columns(t):
    q = jnp.concatenate([t[..., 0:128], t[..., 128:192]], axis=-1)
    k = jnp.concatenate([t[..., 256:384], t[..., 192:256]], axis=-1)
    v = jnp.concatenate([t[..., 384:512], t[..., 512:576]], axis=-1)
    return q, k, v


def per_device(
    tokens, w_qkv, b_qkv, w_out, vectors, w_in, b_in, w_back, cotangent, lengths, buckets
):
    layers = w_qkv.shape[0]
    rows, width = tokens.shape
    d = lax.axis_index("dp")
    z = lax.axis_index("mp")
    g, c = d // 2, d % 2

    blocks = []
    for l in range(layers):
        low = w_qkv[l].astype(BF16)
        blocks.append(head_tiles(low[0], low[1], low[2], w_out[l].astype(BF16).T))
        blocks.append(w_in[l].astype(BF16))
        blocks.append(w_back[l].astype(BF16).T)
    blocks = jnp.stack(blocks)
    height = w_qkv.shape[2]
    pieces = 8 if lax.axis_size("dp") == 8 else 1
    piece_rows = height if pieces == 8 else width

    small = jnp.concatenate(
        [
            b_qkv[:, 0],
            b_qkv[:, 1, LANES:],
            b_qkv[:, 1, :LANES],
            b_qkv[:, 2],
            jnp.zeros((layers, HD), F32),
            b_in,
        ],
        axis=-1,
    )
    small = jnp.pad(small, ((0, 8 - layers), (0, 0)))
    slot = LEN_MAX // (3 - buckets)
    meta = jnp.concatenate([slot, lengths[0]]).astype(F32)
    meta = jnp.broadcast_to(jnp.pad(meta, (0, 4))[:, None], (8, LANES))
    exponents = jnp.arange(LANES, dtype=jnp.int32) % (HD // 2)
    frequency = 10000.0 ** (-2.0 * exponents.astype(F32) / HD)[None, :]

    if pieces == 8:
        head, states = forward(blocks, tokens, cotangent, small, meta, frequency, vectors)
        w_all, dy, low, cos, sin, qrow, kcol = head
        grads = backward(w_all, dy, cos, sin, low, qrow, kcol, vectors, states)
        grad_tokens, result, grad_qkv, grad_b_qkv, grad_out, grad_vec, grad_in = grads[:7]
        return (
            result,
            grad_tokens,
            grad_qkv,
            grad_b_qkv,
            grad_out,
            grad_vec,
            grad_in,
            grads[7].reshape(layers, width),
            grads[8],
        )

    head, states = plain_forward(blocks, tokens, cotangent, small, meta, frequency, vectors)
    w_all, gradient, low, cos, sin, qcode, kcode = head
    result = relayout(low)
    gradient = gradient.astype(F32)

    first = jnp.where(c == 0, 1, 2)
    spans = [(g ^ hop) * 2 * height for hop in (0, first, 3 - first, 3)]
    if pieces == 1:
        spans = [jnp.int32(0)] * 4
    column_of = [(z - k) % MP for k in range(MP)]
    own_z = [(z - 2 * c - k) % MP for k in range(2)]
    scal = jnp.stack(row_offsets(g, c, height) + column_of + [2 * c] + spans + own_z)
    scal = scal.astype(jnp.int32)

    masters = []
    vector_grads = []
    in_biases = []
    head_biases = []
    for layer_at in reversed(range(layers)):
        x_full, q, k, v, mixed, mixed_in, lse, r1, r2, e, gp = states[layer_at]
        back = feed_back(
            scal,
            piece_rows,
            pieces,
            gradient,
            r1,
            r2,
            e,
            gp,
            mixed[:rows],
            mixed_in,
            vectors[layer_at],
            w_all,
            3 * layer_at,
        )
        dr1, dz_own, dz_sib, dvec, dbin = back[:5]
        dz_others = core_swap(dz_sib)
        feed_grad = reduce_all(back[5], back[-1])
        dx, dx_sib, dbias, parts = attend_back(
            scal,
            piece_rows,
            pieces,
            x_full.reshape(4 * rows, width),
            (cos, sin, qcode, kcode),
            (q, k, v, lse),
            mixed,
            dz_own,
            dz_others,
            w_all,
            3 * layer_at,
        )
        got = dx.astype(F32) + core_swap(dx_sib).astype(F32)
        gradient = dr1 + got[0] + pair_swap(got[1].astype(BF16)).astype(F32)
        head_grad = reduce_heads(parts)
        masters.insert(0, (feed_grad, head_grad))
        vector_grads.insert(0, dvec)
        in_biases.insert(0, dbin[:, 0])
        head_biases.insert(0, sum_head_biases(dbias[:, 0]))
    grad_tokens = relayout(gradient.astype(BF16)).astype(F32)

    layers_of = jnp.stack(in_biases, axis=1)
    grad_vectors, grad_b_in = sum_vectors(jnp.concatenate(vector_grads), layers_of)
    grad_vectors = grad_vectors.reshape(vectors.shape)
    grad_b_qkv = jnp.stack([jnp.stack(head_columns(b)) for b in head_biases])

    grad_qkv = jnp.stack([jnp.stack(head_columns(m[1])) for m in masters])
    grad_in = jnp.stack([m[0][:, :width] for m in masters])
    grad_back = jnp.stack([m[0][:, width : 2 * width].T for m in masters])
    grad_out = jnp.stack(
        [
            jnp.concatenate(
                [m[0][:, 2 * width + LANES :], m[0][:, 2 * width + HD : 2 * width + LANES]], axis=-1
            ).T
            for m in masters
        ]
    )
    return (
        result,
        grad_tokens,
        grad_qkv,
        grad_b_qkv,
        grad_out,
        grad_vectors,
        grad_in,
        grad_b_in,
        grad_back,
    )


def solution(mesh):
    return jax.shard_map(
        per_device,
        mesh=mesh,
        in_specs=(
            P(("dp", "mp"), None),
            P(None, None, "dp", "mp"),
            P(None, None, "mp"),
            P(None, "mp", "dp"),
            P(),
            P(None, "dp", "mp"),
            P(None, "mp"),
            P(None, "mp", "dp"),
            P(("dp", "mp"), None),
            P("dp", None),
            P("dp"),
        ),
        out_specs=(
            P(("dp", "mp"), None),
            P(("dp", "mp"), None),
            P(None, None, "dp", "mp"),
            P(None, None, "mp"),
            P(None, "mp", "dp"),
            P(),
            P(None, "dp", "mp"),
            P(None, "mp"),
            P(None, "mp", "dp"),
        ),
        check_vma=False,
    )
```

```python
from functools import partial

import jax
import jax.numpy as jnp
from jax import lax
from jax.experimental import pallas as pl
from jax.experimental.pallas import tpu as pltpu
from jax.sharding import PartitionSpec as P

HD = 64
LEN_MAX = 1536
EPSILON = 1e-06
NEGATIVE = -1e30
F32 = jnp.float32
BF16 = jnp.bfloat16
LANES = 128
MP = 4
SPLIT = 2
VMEM_LIMIT = 60 * 1024 * 1024
BACK_LIMIT = 63 * 1024 * 1024


def nn(a, b):
    return lax.dot_general(a, b, (((1,), (0,)), ((), ())), preferred_element_type=F32)


def nt(a, b):
    return lax.dot_general(a, b, (((1,), (1,)), ((), ())), preferred_element_type=F32)


def core_swap(x):
    n = lax.axis_size("dp")
    return lax.ppermute(x, "dp", [(i, i ^ 1) for i in range(n)])


def plane_swap(x, first):
    n = lax.axis_size("dp")
    hops = (2, 4) if first else (4, 2)
    return lax.ppermute(x, "dp", [(i, i ^ hops[i % 2]) for i in range(n)])


def column_shift(x, k):
    return lax.ppermute(x, "mp", [(i, (i + k) % MP) for i in range(MP)])


def pair_swap(x):
    return lax.ppermute(x, "mp", [(i, i ^ 1) for i in range(MP)])


def relayout(x):
    n = lax.axis_size("dp")
    pairs = []
    for d in range(n):
        for z in range(MP):
            if (d % 2) != (z // 2):
                pairs.append((d * MP + z, (d ^ 1) * MP + (z ^ 2)))
            else:
                pairs.append((d * MP + z, d * MP + z))
    return lax.ppermute(x, ("dp", "mp"), pairs)


def turn_columns(x, z):
    return jnp.stack([lax.dynamic_index_in_dim(x, (z - k) % MP, 0, False) for k in range(MP)])


def row_offsets(g, c, rows):
    if lax.axis_size("dp") != 8:
        return [jnp.int32(0)]
    result = []
    for core in (c, 1 - c):
        first = jnp.where(core == 0, 1, 2)
        for hop in (0, first, 3 - first, 3):
            result.append(((g ^ hop) * 2 + core) * rows)
    return result


def send_columns(v):
    total = v[0].astype(F32)
    for k in range(1, MP):
        total = total + column_shift(v[k], -k).astype(F32)
    return total


def reduce_all(keep, away):
    if lax.axis_size("dp") != 8:
        z = lax.axis_index("mp")
        whole = turn_columns(keep[0], z).astype(F32)
        part = lax.psum_scatter(whole, "mp", scatter_dimension=0, tiled=False)
        return lax.psum_scatter(part, "dp", scatter_dimension=0, tiled=True)
    other = core_swap(away)

    def add(i):
        return keep[i].astype(F32) + other[i].astype(F32)

    got = plane_swap(jnp.stack([add(0), add(1)]).astype(BF16), True)
    got_two = plane_swap((add(2) + got[1].astype(F32)).astype(BF16), False)
    v = (add(3) + got[0].astype(F32) + got_two.astype(F32)).astype(BF16)
    return send_columns(v)


def reduce_heads(parts):
    c = lax.axis_index("dp") % 2
    n = lax.axis_size("dp")
    if n != 8:
        z = lax.axis_index("mp")
        wide = jnp.concatenate([parts[0], jnp.zeros_like(parts[0])], axis=0)
        wide = jnp.where(c == 0, wide, jnp.roll(wide, 2, axis=0))
        whole = turn_columns(wide, z).astype(F32)
        part = lax.psum_scatter(whole, "mp", scatter_dimension=0, tiled=False)
        return lax.psum_scatter(part, "dp", scatter_dimension=0, tiled=True)
    got = plane_swap(parts[0:2], True)
    got_two = plane_swap((parts[2].astype(F32) + got[1].astype(F32)).astype(BF16), False)
    v = (parts[3].astype(F32) + got[0].astype(F32) + got_two.astype(F32)).astype(BF16)

    total = column_turn(v[0], 0).astype(F32) + column_turn(v[1], 1).astype(F32)
    rows = total.shape[0] // 2
    kept = lax.dynamic_slice_in_dim(total, c * rows, rows, 0)
    sent = lax.dynamic_slice_in_dim(total, (1 - c) * rows, rows, 0).astype(BF16)
    return kept + core_swap(sent).astype(F32)


def sum_head_biases(v):
    c = lax.axis_index("dp") % 2
    n = lax.axis_size("dp")
    if n != 8:
        z = lax.axis_index("mp")
        zero = jnp.zeros_like(v)
        wide = jnp.where(c == 0, jnp.concatenate([v, zero]), jnp.concatenate([zero, v]))
        total = lax.psum(turn_columns(wide, z), ("dp", "mp"))
        return lax.dynamic_index_in_dim(total, z, 0, False)
    v = v + plane_swap(v, True)
    v = v + plane_swap(v, False)
    total = column_turn(v[0], 0) + column_turn(v[1], 1)
    return total + core_swap(total)


def column_turn(x, k):
    n = lax.axis_size("dp")
    pairs = []
    for d in range(n):
        for z in range(MP):
            pairs.append((d * MP + z, d * MP + (z - k - 2 * (d % 2)) % MP))
    return lax.ppermute(x, ("dp", "mp"), pairs)


def sum_vectors(vectors, columns):
    if lax.axis_size("dp") != 8:
        z = lax.axis_index("mp")
        vectors, columns = lax.psum((vectors, turn_columns(columns, z)), ("dp", "mp"))
        return vectors, lax.dynamic_index_in_dim(columns, z, 0, False)
    n = vectors.shape[0]
    m = columns.shape[1]
    both = jnp.concatenate([vectors, columns.reshape(MP * m, -1)])
    both = both + core_swap(both)
    both = both + plane_swap(both, True)
    both = both + plane_swap(both, False)
    total = both[: n + m]
    for k in range(1, MP):
        at = n + m * (MP - k)
        total = total + column_shift(jnp.concatenate([both[:n], both[at : at + m]]), k)
    return total[:n], total[n:]


def lane_index(shape):
    return lax.broadcasted_iota(jnp.int32, shape, len(shape) - 1)


def half_swap(x):
    lane = lane_index(x.shape)
    return jnp.where(
        lane % HD < HD // 2,
        pltpu.roll(x, LANES - HD // 2, x.ndim - 1),
        pltpu.roll(x, HD // 2, x.ndim - 1),
    )


def norm_parts(r):
    mean = jnp.mean(r, axis=-1, keepdims=True)
    centred = r - mean
    scale = lax.rsqrt(jnp.mean(centred * centred, axis=-1, keepdims=True) + EPSILON)
    return centred * scale, scale


def norm_back(dy, n, scale, gain):
    gdy = dy * gain
    mean_one = jnp.mean(gdy, axis=-1, keepdims=True)
    mean_two = jnp.mean(gdy * n, axis=-1, keepdims=True)
    return (gdy - mean_one - n * mean_two) * scale


def vmem():
    return pl.BlockSpec(memory_space=pltpu.VMEM)


def smem():
    return pl.BlockSpec(memory_space=pltpu.SMEM)


def anywhere():
    return pl.BlockSpec(memory_space=pl.ANY)


def params():
    return pltpu.CompilerParams(vmem_limit_bytes=VMEM_LIMIT)


def shape(dims, dtype):
    return jax.ShapeDtypeStruct(dims, dtype)


def project_rows(i, z, x, w_ref, bias, cos, sin, q_ref, k_ref, v_ref):
    block = x.shape[0]
    at = pl.ds(i * block, block)
    p = nn(x, w_ref[z, :, LANES : 5 * LANES]) + bias[:, LANES:]
    low_half = lane_index((block, LANES)) < HD
    mixed = p[:, 0:LANES]
    mixed = mixed * cos + half_swap(mixed) * sin
    pair = p[:, LANES : 2 * LANES]
    pair = pair * cos + half_swap(pair) * sin
    k_ref[z, 0, at, :] = pair.astype(BF16)
    k_ref[z, 1, at, :] = jnp.where(low_half, pltpu.roll(mixed, HD, 1), 0.0).astype(BF16)
    v_ref[z, 0, at, :] = p[:, 2 * LANES : 3 * LANES].astype(BF16)
    v_ref[z, 1, at, :] = jnp.where(low_half, p[:, 3 * LANES :], 0.0).astype(BF16)
    if i < 2:
        q = nn(x, w_ref[z, :, 0:LANES]) + bias[:, 0:LANES]
        q = q * cos + half_swap(q) * sin
        q_ref[z, 0, at, :] = q.astype(BF16) * BF16(HD**-0.5)
        q_ref[z, 1, at, :] = jnp.where(low_half, mixed, 0.0).astype(BF16) * BF16(HD**-0.5)


def attend_rows(
    i, qblock, qcode_ref, kcode_ref, q_ref, k_ref, v_ref, mixed_ref, lse_cols, between=None
):
    at = pl.ds(pl.multiple_of(i * qblock, qblock), qblock)
    visible = qcode_ref[at, :] == kcode_ref[...]
    low_half = lane_index((qblock, LANES)) < HD
    lane = lane_index((qblock, LANES))
    for z in range(2):
        outs = []
        for h in range(3):
            tile = h // 2
            q = q_ref[z, tile, at, :]
            if h < 2:
                q = jnp.where(low_half == (h == 0), q, BF16(0))
            s = nt(q, k_ref[z, tile])
            s = jnp.where(visible, s, NEGATIVE)
            m = jnp.max(s, axis=-1, keepdims=True)
            p = jnp.exp(s - m)
            l = jnp.sum(p, axis=-1, keepdims=True)
            o = nn(p.astype(BF16), v_ref[z, tile])
            outs.append(o / l)
            lse_cols[at, :] = jnp.where(lane == 3 * z + h, m + jnp.log(l), lse_cols[at, :])
        mixed_ref[at, pl.ds(z * 256, LANES)] = pltpu.roll(outs[2], HD, 1).astype(BF16)
        mixed_ref[at, pl.ds(z * 256 + LANES, LANES)] = jnp.where(
            low_half, outs[0], outs[1]
        ).astype(BF16)
        if between is not None:
            between(z)


def mirrored(z):
    return [z, z + 1 - 2 * (z % 2), (z + 2) % MP, MP - 1 - z]


def head_columns_of(z, c):
    base = (z + 2 * c) % MP
    return [base, base + 1 - 2 * (base % 2)]


def forward_kernel(n_layers, *refs):
    n_in, per_layer = 7, 11
    blocks, tokens, cot, small, meta, frequency, vectors = refs[:n_in]
    w_all, dy_out, low_out, cos_out, sin_out, qrow_out, kcol_out = refs[n_in : n_in + 7]
    saved = [
        refs[n_in + 7 + l * per_layer : n_in + 7 + (l + 1) * per_layer] for l in range(n_layers)
    ]
    (
        xfull,
        mixed_in,
        small_all,
        meta_in,
        wa,
        wo,
        win,
        wback,
        cos_ref,
        sin_ref,
        qcode_ref,
        kcode_ref,
        qrow_ref,
        kcol_ref,
        q_ref,
        k_ref,
        v_ref,
        mixed_ref,
        lse_cols,
        lse_ref,
        stream,
        sum_ref,
        r1_ref,
        low_ref,
        e_ref,
        gp_ref,
        z_send,
        z_recv,
        p_send,
        p_recv,
        c_send,
        c_recv,
        x_send,
        x_recv,
        t_send,
        t_recv,
        l_sem,
        w_sem,
        s_sem,
    ) = refs[n_in + 7 + n_layers * per_layer :]
    rows = stream.shape[0]
    width = stream.shape[1]
    height = blocks.shape[1]
    parts = blocks.shape[0] * SPLIT

    d = lax.axis_index("dp")
    z = lax.axis_index("mp")
    c = d % 2
    x = (d // 2) % 2
    y = d // 4
    flip_x, flip_y = 1 - 2 * x, 1 - 2 * y
    one_x, one_y = x + (1 - c) * flip_x, y + c * flip_y
    two_x, two_y = x + c * flip_x, y + (1 - c) * flip_y

    def device(yy, xx, cc, zz):
        return (yy * 4 + xx * 2 + cc, zz)

    part_rows = height // SPLIT
    planes = ((y, x), (one_y, one_x), (two_y, two_x), (1 - y, 1 - x))

    def rows_of(k, n):
        yy, xx = planes[n]
        start = (yy * 4 + xx * 2 + c) * height + k % SPLIT * part_rows
        return pl.ds(pl.multiple_of(start, 16), part_rows)

    sibling = device(y, x, 1 - c, z)
    first = device(one_y, one_x, c, z)
    second = device(two_y, two_x, c, z)
    pair = device(y, x, c, z + 1 - 2 * (z % 2))
    away = device(y, x, 1 - c, (z + 2) % MP)
    moved = c != z // 2
    mirror = mirrored(z)
    columns = [device(y, x, c, mirror[m]) for m in range(1, MP)]
    barrier = pltpu.get_barrier_semaphore()
    partners = columns + [first, second, sibling, away]
    for partner in partners:
        pl.semaphore_signal(
            barrier, inc=1, device_id=partner, device_id_type=pl.DeviceIdType.MESH
        )
    pl.semaphore_wait(barrier, len(partners))

    def remote(source, target, send, recv, to):
        return pltpu.make_async_remote_copy(
            src_ref=source,
            dst_ref=target,
            send_sem=send,
            recv_sem=recv,
            device_id=to,
            device_id_type=pl.DeviceIdType.MESH,
        )

    sent = []

    def go(make, *at):
        make(*at).start()
        sent.append((make, at))

    def block(k):
        return blocks.at[k // SPLIT, pl.ds(k % SPLIT * part_rows, part_rows)]

    def local_copy(k):
        return pltpu.make_async_copy(block(k), w_all.at[k // SPLIT, z, rows_of(k, 0)], l_sem.at[k])

    def z_copy(k, n):
        if n == 2:
            source = target = w_all.at[k // SPLIT, mirror[2], rows_of(k, 0)]
        else:
            source, target = block(k), w_all.at[k // SPLIT, z, rows_of(k, 0)]
        return remote(
            source, target, z_send.at[k, n], z_recv.at[k, n], columns[1 if n == 1 else 0]
        )

    def p_copy(k, n):
        source = w_all.at[k // SPLIT, :, rows_of(k, 1 if n == 2 else 0)]
        return remote(
            source, source, p_send.at[k, n], p_recv.at[k, n], first if n == 0 else second
        )

    def c_copy(k, n):
        source = w_all.at[k // SPLIT, :, rows_of(k, n)]
        return remote(source, source, c_send.at[k, n], c_recv.at[k, n], sibling)

    def step_send(k):
        local_copy(k).start()
        go(z_copy, k, 1)
        go(z_copy, k, 0)

    def step_across(k):
        z_copy(k, 1).wait_recv()
        go(z_copy, k, 2)

    def step_plane(k):
        local_copy(k).wait()
        z_copy(k, 0).wait_recv()
        z_copy(k, 2).wait_recv()
        go(p_copy, k, 0)
        go(p_copy, k, 1)
        go(c_copy, k, 0)
        if k + 1 < parts:
            step_across(k + 1)
        if k + 2 < parts:
            step_send(k + 2)

    def step_forward(k):
        p_copy(k, 0).wait_recv()
        go(p_copy, k, 2)
        go(c_copy, k, 1)
        p_copy(k, 1).wait_recv()
        go(c_copy, k, 2)

    def step_last(k):
        p_copy(k, 2).wait_recv()
        go(c_copy, k, 3)

    def step_ready(chunk):
        for k in range(chunk * SPLIT, (chunk + 1) * SPLIT):
            for n in range(4):
                c_copy(k, n).wait_recv()

    turns = parts + 2
    position = [0]

    def take(until):
        steps = []
        for n in range(position[0], until):
            if n < 2:
                steps.append(partial(step_plane, n))
            if 0 <= n - 2:
                steps.append(partial(step_last, n - 2))
            if 0 <= n - 1 < parts:
                steps.append(partial(step_forward, n - 1))
            if n == 2:
                steps.append(partial(step_plane, 2))
            if 2 <= n < parts - 1:
                steps.append(partial(step_plane, n + 1))
        position[0] = max(position[0], until)
        return steps

    def run(steps):
        for step in steps:
            step()

    def meta_copy():
        return remote(meta, meta_in, t_send.at[0], t_recv.at[0], sibling)

    def small_copy(s):
        return remote(small, small_all.at[z], t_send.at[3 + s], t_recv.at[3 + s], columns[s])

    step_send(0)
    go(meta_copy)
    for n in range(MP - 1):
        go(small_copy, n)
    token_copy = remote(tokens, xfull.at[0, 0], t_send.at[1], t_recv.at[1], away)
    token_local = pltpu.make_async_copy(tokens, xfull.at[0, 0], l_sem.at[parts])
    step_across(0)

    @pl.when(moved)
    def _():
        token_copy.start()

    @pl.when(jnp.logical_not(moved))
    def _():
        token_local.start()

    step_send(1)
    small_local = pltpu.make_async_copy(small, small_all.at[z], l_sem.at[parts + 1])
    small_local.start()

    meta_copy().wait_recv()
    info = jnp.where(moved, meta_in[...], meta[...])
    slot = info[0:1, :]
    limits = [info[n : n + 1, :] for n in range(1, 4)]
    half = z % 2
    quarters = [2 * c + half, 2 * (1 - c) + half, 2 * c + 1 - half, 2 * (1 - c) + 1 - half]

    def codes(place_all, slot, limits):
        seq = jnp.where(place_all >= slot, 1.0, 0.0) + jnp.where(place_all >= 2.0 * slot, 1.0, 0.0)
        place = place_all - seq * slot
        limit = jnp.where(seq == 0.0, limits[0], jnp.where(seq == 1.0, limits[1], limits[2]))
        return seq, place, jnp.where(place < limit, seq, -1.0)

    sign = jnp.where(lane_index((1, LANES)) % HD < HD // 2, -1.0, 1.0)
    for i in range(4):
        at = pl.ds(i * rows, rows)
        base = quarters[i] * rows
        index = lax.broadcasted_iota(jnp.int32, (rows, LANES), 0) + base
        seq, place, kcode = codes(index.astype(F32), slot, limits)
        angle = place * frequency[...]
        cos_ref[at, :] = jnp.cos(angle)
        sin_ref[at, :] = jnp.sin(angle) * sign
        kcol_ref[at, :] = kcode[:, 0:1]
        if i < 2:
            qcode_ref[at, :] = seq[:, 0:1]
        index = lax.broadcasted_iota(jnp.int32, (1, rows), 1) + base
        seq, place, kcode = codes(
            index.astype(F32), slot[:, 0:1], [limit[:, 0:1] for limit in limits]
        )
        kcode_ref[:, pl.ds(i * rows, rows)] = kcode
        if i < 2:
            qrow_ref[:, pl.ds(i * rows, rows)] = seq

    run(take(1))

    @pl.when(moved)
    def _():
        token_copy.wait_recv()

    @pl.when(jnp.logical_not(moved))
    def _():
        token_local.wait()

    def x_copy(l, n):
        source = xfull.at[l, 2 if n == 2 else 0]
        target = xfull.at[l, (2, 1, 3)[n]]
        return remote(
            source, target, x_send.at[l, n], x_recv.at[l, n], pair if n == 0 else sibling
        )

    def m_copy(l):
        return remote(
            mixed_ref.at[pl.ds(rows, rows)],
            mixed_in.at[l],
            x_send.at[l, 3],
            x_recv.at[l, 3],
            sibling,
        )

    def h_copy(l):
        return remote(low_ref, saved[l][10].at[1], x_send.at[l, 4], x_recv.at[l, 4], sibling)

    def e_copy(l):
        return remote(
            e_ref,
            saved[l][8].at[:, pl.ds(rows, rows), :],
            x_send.at[l, 5],
            x_recv.at[l, 5],
            sibling,
        )

    stores = {}

    def store(name, source, target):
        copy = pltpu.make_async_copy(source, target, s_sem.at[len(stores)])
        copy.start()
        stores[name] = copy

    waited = set()

    def stored(*names):
        for name in names:
            if name in stores and name not in waited:
                waited.add(name)
                stores[name].wait()

    stream[...] = xfull[0, 0].astype(F32)
    store("cos", cos_ref, cos_out)
    store("sin", sin_ref, sin_out)
    store("qrow", qrow_ref, qrow_out)
    store("kcol", kcol_ref, kcol_out)

    cot_copy = remote(cot, dy_out, t_send.at[2], t_recv.at[2], away)
    cot_local = pltpu.make_async_copy(cot, dy_out, l_sem.at[parts + 2])

    def load(source, target, n):
        copy = pltpu.make_async_copy(source, target, w_sem.at[n])
        copy.start()
        return copy

    qblock = 256
    count = 2 * rows // qblock
    own_z = head_columns_of(z, c)
    other_z = [(at + 2) % MP for at in own_z]
    for l in range(n_layers):
        xs, qs, ks, vs, ms, ls, r1s, r2s, es, gps, hs = saved[l]
        last = l - 1
        go(x_copy, l, 0)
        go(x_copy, l, 1)
        if l == 0:
            run(take(2))
            x_copy(l, 0).wait_recv()
            go(x_copy, l, 2)
            run(take(4))
        else:
            run(take(10))
        step_ready(3 * l)
        wa_loads = [
            load(w_all.at[3 * l, own_z[k], :, pl.ds(0, 5 * LANES)], wa.at[k], k) for k in range(2)
        ]
        wo_load = load(w_all.at[3 * l, :, :, pl.ds(4 * LANES, 2 * LANES)], wo, 2)
        if l == 0:

            @pl.when(moved)
            def _():
                cot_copy.start()

            @pl.when(jnp.logical_not(moved))
            def _():
                cot_local.start()

            for s in range(MP - 1):
                small_copy(s).wait_recv()
            small_local.wait()
        else:
            m_copy(last).wait_send()
        stored(("q", last), ("k", last), ("v", last), ("mixed", last), ("lse", last))
        lse_cols[...] = jnp.zeros_like(lse_cols)
        for copy in wa_loads:
            copy.wait()
        for i in range(4):
            if i == 1:
                x_copy(l, 1).wait_recv()
            if i == 2 and l > 0:
                x_copy(l, 0).wait_recv()
                go(x_copy, l, 2)
            if i == 3:
                run(take(5 if l == 0 else 11))
                x_copy(l, 2).wait_recv()
            at = pl.ds(i * rows, rows)
            for k in range(2):
                bias = small_all[own_z[k], pl.ds(l, 1), pl.ds(0, 5 * LANES)]
                project_rows(
                    i, k, xfull[l, i], wa, bias, cos_ref[at, :], sin_ref[at, :], q_ref, k_ref, v_ref
                )
        store(("q", l), q_ref, qs)
        store(("k", l), k_ref, ks)
        store(("v", l), v_ref, vs)
        store(("x", l), xfull.at[l], xs)
        ends = (5, 5, 6, 6, 6, 7) if l == 0 else (11, 12, 12, 12, 13, 13)
        steps = [take(end) for end in ends]

        def one_block(n, _, l=l, steps=steps):
            def between(k):
                for j in range(count):
                    if steps[2 * j + k] or (j, k) in ((1, 1), (2, 0)):

                        @pl.when(n == j)
                        def _(j=j):
                            if (j, k) == (1, 1):
                                m_copy(l).start()
                            run(steps[2 * j + k])
                            if (j, k) == (2, 0):
                                step_ready(3 * l + 1)
                                load(w_all.at[3 * l + 1], win, 3)

            attend_rows(
                count - 1 - n,
                qblock,
                qcode_ref,
                kcode_ref,
                q_ref,
                k_ref,
                v_ref,
                mixed_ref,
                lse_cols,
                between,
            )
            return 0

        lax.fori_loop(0, count, one_block, 0)
        lse_ref[...] = jnp.transpose(lse_cols[...])[0:8, :]
        store(("mixed", l), mixed_ref, ms)
        store(("lse", l), lse_ref, ls)
        win_load = pltpu.make_async_copy(w_all.at[3 * l + 1], win, w_sem.at[3])
        stored(("r1", last), ("r2", last), ("e", last), ("gp", last), ("h", last))
        if l > 0:
            h_copy(last).wait_send()
            e_copy(last).wait_send()
        wo_load.wait()
        m_copy(l).wait_recv()
        a = jnp.zeros((rows, width), F32)
        for k in range(2):
            a = a + nt(mixed_ref[0:rows, k * 256 : k * 256 + 256], wo[own_z[k]])
            a = a + nt(mixed_in[l, :, k * 256 : k * 256 + 256], wo[other_z[k]])
        vec = vectors[l]
        r1 = stream[...] + a + vec[0:1, :]
        r1_ref[...] = r1
        store(("r1", l), r1_ref, r1s)
        n1, _ = norm_parts(r1)
        h = n1 * vec[1:2, :] + vec[2:3, :]
        low_ref[...] = h.astype(BF16)
        store(("h", l), low_ref, hs.at[0])
        h_copy(l).start()
        sum_ref[...] = h + vec[3:4, :]
        win_load.wait()

        def inner(zz, _, l=l):
            u = nn(low_ref[...], win[zz]) + small_all[zz, pl.ds(l, 1), pl.ds(5 * LANES, width)]
            cdf = 0.5 * (1.0 + lax.erf(u * (2.0**-0.5)))
            pdf = jnp.exp(u * u * -0.5) * 0.3989422804014327
            e_ref[zz] = (u * cdf).astype(BF16)
            gp_ref[zz] = (cdf + u * pdf).astype(BF16)
            return 0

        lax.fori_loop(0, 2, inner, 0)
        run(take(8 if l == 0 else turns))
        lax.fori_loop(2, MP - 1, inner, 0)
        step_ready(3 * l + 2)
        wback_load = load(w_all.at[3 * l + 2], wback, 4)
        lax.fori_loop(MP - 1, MP, inner, 0)
        store(("e", l), e_ref, es.at[:, pl.ds(0, rows), :])
        e_copy(l).start()
        store(("gp", l), gp_ref, gps)
        wback_load.wait()

        def outer(zz, _):
            sum_ref[...] += nt(e_ref[zz], wback[zz])
            return 0

        lax.fori_loop(0, MP, outer, 0)
        store(("r2", l), sum_ref, r2s)
        n2, _ = norm_parts(sum_ref[...])
        result = n2 * vec[4:5, :] + vec[5:6, :]
        if l + 1 < n_layers:
            stream[...] = result
            xfull[l + 1, 0] = result.astype(BF16)
        else:
            h_copy(l).wait_send()
            stored(("h", l))
            low_ref[...] = result.astype(BF16)
            store("low", low_ref, low_out)

    m_copy(n_layers - 1).wait_send()
    e_copy(n_layers - 1).wait_send()
    for l in range(n_layers):
        h_copy(l).wait_recv()
        e_copy(l).wait_recv()
    for make, at in sent:
        make(*at).wait_send()
    @pl.when(moved)
    def _():
        token_copy.wait_send()
        cot_copy.wait_send()
        cot_copy.wait_recv()

    @pl.when(jnp.logical_not(moved))
    def _():
        cot_local.wait()

    stored(*stores)


def forward(blocks, tokens, cot, small, meta, frequency, vectors):
    n_layers = vectors.shape[0]
    chunks, height, width = blocks.shape
    rows = tokens.shape[0]
    queries, keys = 2 * rows, 4 * rows
    layer_out = (
        shape((4, rows, width), BF16),
        shape((2, 2, queries, LANES), BF16),
        shape((2, 2, keys, LANES), BF16),
        shape((2, 2, keys, LANES), BF16),
        shape((queries, 512), BF16),
        shape((8, queries), F32),
        shape((rows, width), F32),
        shape((rows, width), F32),
        shape((MP, 2 * rows, width), BF16),
        shape((MP, rows, width), BF16),
        shape((2, rows, width), BF16),
    )
    outs = (
        shape((chunks, MP, 8 * height, width), BF16),
        shape((rows, width), BF16),
        shape((rows, width), BF16),
        shape((keys, LANES), F32),
        shape((keys, LANES), F32),
        shape((1, queries), F32),
        shape((keys, 1), F32),
    ) + layer_out * n_layers
    sem = pltpu.SemaphoreType.DMA
    results = pl.pallas_call(
        partial(forward_kernel, n_layers),
        out_shape=outs,
        in_specs=[anywhere()] * 3 + [vmem()] * 4,
        out_specs=(anywhere(),) * len(outs),
        scratch_shapes=[
            pltpu.VMEM((n_layers, 4, rows, width), BF16),
            pltpu.VMEM((n_layers, rows, 512), BF16),
            pltpu.VMEM((MP,) + small.shape, F32),
            pltpu.VMEM(meta.shape, F32),
            pltpu.VMEM((2, width, 5 * LANES), BF16),
            pltpu.VMEM((MP, width, 2 * LANES), BF16),
            pltpu.VMEM((MP, width, width), BF16),
            pltpu.VMEM((MP, width, width), BF16),
            pltpu.VMEM((keys, LANES), F32),
            pltpu.VMEM((keys, LANES), F32),
            pltpu.VMEM((queries, 1), F32),
            pltpu.VMEM((1, keys), F32),
            pltpu.VMEM((1, queries), F32),
            pltpu.VMEM((keys, 1), F32),
            pltpu.VMEM((2, 2, queries, LANES), BF16),
            pltpu.VMEM((2, 2, keys, LANES), BF16),
            pltpu.VMEM((2, 2, keys, LANES), BF16),
            pltpu.VMEM((queries, 512), BF16),
            pltpu.VMEM((queries, LANES), F32),
            pltpu.VMEM((8, queries), F32),
            pltpu.VMEM((rows, width), F32),
            pltpu.VMEM((rows, width), F32),
            pltpu.VMEM((rows, width), F32),
            pltpu.VMEM((rows, width), BF16),
            pltpu.VMEM((MP, rows, width), BF16),
            pltpu.VMEM((MP, rows, width), BF16),
            sem((chunks * SPLIT, 3)),
            sem((chunks * SPLIT, 3)),
            sem((chunks * SPLIT, 3)),
            sem((chunks * SPLIT, 3)),
            sem((chunks * SPLIT, 4)),
            sem((chunks * SPLIT, 4)),
            sem((n_layers, 6)),
            sem((n_layers, 6)),
            sem((6,)),
            sem((6,)),
            sem((chunks * SPLIT + 3,)),
            sem((5,)),
            sem((5 + 11 * n_layers,)),
        ],
        compiler_params=pltpu.CompilerParams(
            vmem_limit_bytes=VMEM_LIMIT, collective_id=0, has_side_effects=True
        ),
        cost_estimate=pl.CostEstimate(
            flops=100_000_000_000, bytes_accessed=100_000_000, transcendentals=20_000_000
        ),
        name="forward",
    )(blocks, tokens, cot, small, meta, frequency, vectors)
    head = results[:7]
    states = [results[7 + 11 * l : 18 + 11 * l] for l in range(n_layers)]
    return head, states


def place_of(d, z):
    c = d % 2
    x = (d // 2) % 2
    y = d // 4
    flip_x, flip_y = 1 - 2 * x, 1 - 2 * y
    planes = (
        (y, x),
        (y + c * flip_y, x + (1 - c) * flip_x),
        (y + (1 - c) * flip_y, x + c * flip_x),
        (1 - y, 1 - x),
    )
    groups = [2 * yy + xx for yy, xx in planes]

    def device(group, cc, zz):
        return (group * 2 + cc, zz)

    return c, groups, device


def head_back(
    i,
    h,
    kblock,
    q_ref,
    k_ref,
    v_ref,
    dz_ref,
    lse_ref,
    delta_ref,
    qrow_ref,
    kcol_ref,
    pair_ref,
    dqt_ref,
    dt_ref,
):
    tile = h // 2
    keys, queries = k_ref.shape[2], q_ref.shape[2]
    low_q = lane_index((queries, LANES)) < HD
    low_k = lane_index((kblock, LANES)) < HD
    q = q_ref[i, tile]
    dz = dz_ref[i, tile]
    if h < 2:
        keep = low_q == (h == 0)
        q = jnp.where(keep, q, BF16(0))
        dz = jnp.where(keep, dz, BF16(0))
    pair_ref[0] = q
    pair_ref[1] = dz
    lse = lse_ref[3 * i + h : 3 * i + h + 1, :]
    delta = delta_ref[3 * i + h : 3 * i + h + 1, :]
    if h != 1:
        dqt_ref[...] = jnp.zeros_like(dqt_ref)

    def one_block(n, _):
        at = pl.ds(pl.multiple_of(n * kblock, kblock), kblock)
        kb = k_ref[i, tile, at, :]
        vb = v_ref[i, tile, at, :]
        kb_own = jnp.where(low_k == (h == 0), kb, BF16(0)) if h < 2 else kb
        visible = kcol_ref[at, :] == qrow_ref[...]
        s = nt(kb, pair_ref[0])
        s = jnp.where(visible, s, NEGATIVE)
        p = jnp.exp(s - lse)
        dp = nt(vb, pair_ref[1])
        ds = (p * (dp - delta)).astype(BF16)
        dv = nn(p.astype(BF16), pair_ref[1])
        dk = nn(ds, pair_ref[0])
        dqt_ref[...] += nn(jnp.transpose(kb_own), ds)
        if h == 1:
            dt_ref[2, at, :] += dk
            dt_ref[3, at, :] += dv
        elif h == 0:
            dt_ref[2, at, :] = dk
            dt_ref[3, at, :] = dv
        else:
            dt_ref[1, at, :] = pltpu.roll(dk, HD, 1)
            dt_ref[4, at, :] = dv
        return 0

    lax.fori_loop(0, keys // kblock, one_block, 0, unroll=2)
    if h >= 1:
        dq = jnp.transpose(dqt_ref[...]) * HD**-0.5
        if h == 1:
            dt_ref[0, 0:queries, :] = dq
        else:
            dt_ref[1, 0:queries, :] += dq


def head_deltas(i, mixed_ref, dz_ref, delta_ref):
    single = pltpu.roll(mixed_ref[:, i * 256 : i * 256 + LANES].astype(F32), HD, 1)
    pair = mixed_ref[:, i * 256 + LANES : i * 256 + 256].astype(F32)
    prod_one = jnp.transpose(pair * dz_ref[i, 0].astype(F32))
    prod_two = jnp.transpose(single * dz_ref[i, 1].astype(F32))
    delta_ref[3 * i : 3 * i + 1, :] = jnp.sum(prod_one[0:HD], axis=0, keepdims=True)
    delta_ref[3 * i + 1 : 3 * i + 2, :] = jnp.sum(prod_one[HD:], axis=0, keepdims=True)
    delta_ref[3 * i + 2 : 3 * i + 3, :] = jnp.sum(prod_two[0:HD], axis=0, keepdims=True)


def norm_back_rows(acc_ref, r_ref, low_ref, gain):
    rows, width = acc_ref.shape
    step = 32

    def body(i, sums):
        at = pl.ds(pl.multiple_of(i * step, step), step)
        dy = acc_ref[at, :]
        n, scale = norm_parts(r_ref[at, :])
        dr = norm_back(dy, n, scale, gain)
        acc_ref[at, :] = dr
        low_ref[at, :] = dr.astype(BF16)
        return (
            sums[0] + jnp.sum(dy * n, axis=0, keepdims=True),
            sums[1] + jnp.sum(dy, axis=0, keepdims=True),
            sums[2] + jnp.sum(dr, axis=0, keepdims=True),
        )

    zero = jnp.zeros((1, width), F32)
    return lax.fori_loop(0, rows // step, body, (zero, zero, zero))


def backward_kernel(n_layers, *refs):
    n_in, per_layer = 8, 11
    w_all, dy_in, cos_in, sin_in, low_in, qrow_ref, kcol_ref, vectors = refs[:n_in]
    saved = [refs[n_in + l * per_layer : n_in + (l + 1) * per_layer] for l in range(n_layers)]
    at = n_in + n_layers * per_layer
    (
        tokens_out,
        result_out,
        qkv_out,
        bqkv_out,
        outw_out,
        vec_out,
        in_out,
        bin_out,
        back_out,
    ) = refs[at : at + 9]
    (
        pool,
        gp_ref,
        r1_ref,
        r2_ref,
        acc_ref,
        df_ref,
        dfin_ref,
        da_ref,
        dain_ref,
        h_ref,
        turn_ref,
        ht_ref,
        dft_ref,
        du_ref,
        t_ref,
        one_in,
        two_in,
        z_in,
        dwo_ref,
        ta_ref,
        a_one_in,
        a_two_in,
        a_z_in,
        a_c_in,
        a_sum_ref,
        a_out_ref,
        wa,
        q_ref,
        k_ref,
        v_ref,
        mixed_ref,
        lse_ref,
        delta_ref,
        dz_ref,
        dt_ref,
        dqt_ref,
        pair_ref,
        cos_ref,
        sin_ref,
        dxc_in,
        dxp_in,
        back_in,
        v_stage,
        v_in,
        dbin_ref,
        across_ref,
        feed_sum,
        c_send,
        c_recv,
        one_send,
        one_recv,
        two_send,
        two_recv,
        z_send,
        z_recv,
        a_send,
        a_recv,
        x_send,
        x_recv,
        v_send,
        v_recv,
        t_send,
        t_recv,
        w_sem,
        s_sem,
        o_sem,
    ) = refs[at + 9 :]
    part_ref, dxs_ref, dxp_ref = r2_ref, h_ref, df_ref
    rows, width = acc_ref.shape
    height = t_ref.shape[3]
    queries = 2 * rows

    d = lax.axis_index("dp")
    z = lax.axis_index("mp")
    c, groups, device = place_of(d, z)
    sibling = device(groups[0], 1 - c, z)
    first = device(groups[1], c, z)
    second = device(groups[2], c, z)
    away = device(groups[0], 1 - c, (z + 2) % MP)
    pair = device(groups[0], c, z + 1 - 2 * (z % 2))
    mirror = mirrored(z)
    columns = [device(groups[0], c, mirror[m]) for m in range(1, MP)]
    across = columns[1]
    moved = c != z // 2

    barrier = pltpu.get_barrier_semaphore()
    partners = columns + [first, second, sibling, away]
    for partner in partners:
        pl.semaphore_signal(
            barrier, inc=1, device_id=partner, device_id_type=pl.DeviceIdType.MESH
        )

    def remote(source, target, send, recv, to):
        return pltpu.make_async_remote_copy(
            src_ref=source,
            dst_ref=target,
            send_sem=send,
            recv_sem=recv,
            device_id=to,
            device_id_type=pl.DeviceIdType.MESH,
        )

    def column(k):
        base = (z + 2 * (k // 2)) % MP
        return base + (k % 2) * (1 - 2 * (base % 2))

    own_z = head_columns_of(z, c)

    def load(source, target, sem):
        return pltpu.make_async_copy(source, target, sem)

    def early_loads(l):
        _, _, _, _, _, _, r1s, r2s, _, _, hs = saved[l]
        return [
            load(r2s, r2_ref, s_sem.at[0]),
            load(r1s, r1_ref, s_sem.at[1]),
            load(hs, h_ref, s_sem.at[2]),
        ]

    def weight_loads(l, k):
        slot = k % 2
        gps = saved[l][9]
        return [
            load(w_all.at[3 * l + 2, column(k)], pool.at[2 + slot], w_sem.at[slot, 0]),
            load(w_all.at[3 * l + 1, column(k)], pool.at[slot], w_sem.at[slot, 1]),
            load(gps.at[column(k)], gp_ref.at[slot], w_sem.at[slot, 2]),
        ]

    def e_load(l, n):
        slot = n % 2
        es = saved[l][8]
        return load(es.at[column(MP - 1 - n)], pool.at[4 + slot], w_sem.at[slot, 3])

    def late_loads(l):
        _, qs, ks, vs, ms, ls = saved[l][:6]
        return [
            load(qs, q_ref, s_sem.at[3]),
            load(ks, k_ref, s_sem.at[4]),
            load(vs, v_ref, s_sem.at[5]),
            load(ms, mixed_ref, s_sem.at[6]),
            load(ls, lse_ref, s_sem.at[7]),
            load(w_all.at[3 * l, own_z[0]], wa.at[0], s_sem.at[8]),
            load(w_all.at[3 * l, own_z[1]], wa.at[1], s_sem.at[9]),
        ]

    def x_loads(l):
        xs = saved[l][0]
        return [
            load(xs.at[n], pool.at[2 + n // 2, pl.ds(n % 2 * rows, rows)], s_sem.at[14 + n])
            for n in range(4)
        ]

    dy_load = load(dy_in, df_ref, s_sem.at[11])
    table_loads = [load(cos_in, cos_ref, s_sem.at[12]), load(sin_in, sin_ref, s_sem.at[13])]
    dy_load.start()
    for copy in early_loads(n_layers - 1) + [e_load(n_layers - 1, 0)]:
        copy.start()
    for copy in weight_loads(n_layers - 1, 0):
        copy.start()
    for copy in table_loads + late_loads(n_layers - 1):
        copy.start()

    def df_copy(l):
        return remote(df_ref, dfin_ref, c_send.at[l, 0], c_recv.at[l, 0], sibling)

    def da_copy(l):
        return remote(da_ref, dain_ref, c_send.at[l, 1], c_recv.at[l, 1], sibling)

    def du_copy(l, k):
        return remote(
            du_ref.at[k, pl.ds(0, rows)],
            du_ref.at[k, pl.ds(rows, rows)],
            c_send.at[l, 2 + k],
            c_recv.at[l, 2 + k],
            sibling,
        )

    def dxs_copy(l, n):
        return remote(
            dxs_ref.at[n], dxc_in.at[n], c_send.at[l, 6 + n], c_recv.at[l, 6 + n], sibling
        )

    halves = [pl.ds(n * (rows // 2), rows // 2) for n in range(2)]

    def dxp_copy(l, n):
        return remote(
            dxp_ref.at[halves[n]],
            dxp_in.at[l, halves[n]],
            x_send.at[l, n],
            x_recv.at[l, n],
            pair,
        )

    def back_copy(n):
        return remote(
            df_ref.at[halves[n]], back_in.at[halves[n]], t_send.at[2 * n], t_recv.at[2 * n], away
        )

    def one_copy(l, h, k, n):
        return remote(
            t_ref.at[h, k, groups[1 if n == 0 else 3]],
            one_in.at[h, k, n],
            one_send.at[l, h, k, n],
            one_recv.at[l, h, k, n],
            first,
        )

    def two_copy(l, h, k):
        return remote(
            t_ref.at[h, k, groups[2]],
            two_in.at[h, k],
            two_send.at[l, h, k],
            two_recv.at[l, h, k],
            second,
        )

    def z_copy(l, h, k):
        return remote(
            across_ref.at[h] if k == 2 else t_ref.at[h, k, groups[0]],
            z_in.at[l, h, k - 1],
            z_send.at[l, h, k],
            z_recv.at[l, h, k],
            across if k == 2 else pair,
        )

    def span(group):
        return pl.ds(pl.multiple_of(group * 2 * height, 32), 2 * height)

    def a_one_copy(l, i, n):
        return remote(
            ta_ref.at[i, span(groups[1 if n == 0 else 3]), :],
            a_one_in.at[i, n],
            a_send.at[l, i, n],
            a_recv.at[l, i, n],
            first,
        )

    def a_two_copy(l, i):
        return remote(
            ta_ref.at[i, span(groups[2]), :],
            a_two_in.at[i],
            a_send.at[l, i, 2],
            a_recv.at[l, i, 2],
            second,
        )

    def a_z_copy(l, i):
        return remote(
            ta_ref.at[i, span(groups[0]), :],
            a_z_in.at[i],
            a_send.at[l, i, 3],
            a_recv.at[l, i, 3],
            pair if i == 1 else across,
        )

    def a_c_copy(l):
        return remote(a_out_ref, a_c_in.at[l], c_send.at[l, 8], c_recv.at[l, 8], sibling)

    def v_copy(l, n):
        to = (sibling, first, second, columns[0], columns[1], columns[2])[n]
        return remote(
            v_stage.at[l, min(n, 3)], v_in.at[l, n], v_send.at[l, n], v_recv.at[l, n], to
        )

    def step_one(l, h, k):
        for n in range(2):
            one_copy(l, h, k, n).wait_recv()
        g = groups[2]
        t_ref[h, k, g] = (t_ref[h, k, g].astype(F32) + one_in[h, k, 1].astype(F32)).astype(BF16)
        two_copy(l, h, k).start()

    def step_two(l, h, k):
        two_copy(l, h, k).wait_recv()
        g = groups[0]
        total = (
            t_ref[h, k, g].astype(F32) + one_in[h, k, 0].astype(F32) + two_in[h, k].astype(F32)
        )
        if k == 0:
            feed_sum[h] = total
            return
        if k == 2:
            z_copy(l, h, 3).wait_recv()
            if l + 1 < n_layers:
                z_copy(l + 1, h, 2).wait_send()
            across_ref[h] = (total + z_in[l, h, 2].astype(F32)).astype(BF16)
        else:
            t_ref[h, k, g] = total.astype(BF16)
        z_copy(l, h, k).start()

    def step_feed_end(l, h):
        total = feed_sum[h]
        for k in range(1, MP - 1):
            z_copy(l, h, k).wait_recv()
            total = total + z_in[l, h, k - 1].astype(F32)
        if h == 1:
            in_out[l] = total
        else:
            back_out[l] = jnp.transpose(total)

    def feed_sent(l, h):
        for k in range(MP):
            for n in range(2):
                one_copy(l, h, k, n).wait_send()
            two_copy(l, h, k).wait_send()
            if k in (1, 3):
                z_copy(l, h, k).wait_send()

    def step_a_one(l, i):
        for n in range(2):
            a_one_copy(l, i, n).wait_recv()
        at = span(groups[2])
        ta_ref[i, at, :] = (ta_ref[i, at, :].astype(F32) + a_one_in[i, 1].astype(F32)).astype(BF16)
        a_two_copy(l, i).start()

    def step_a_two(l, i):
        a_two_copy(l, i).wait_recv()
        at = span(groups[0])
        total = (
            ta_ref[i, at, :].astype(F32)
            + a_one_in[i, 0].astype(F32)
            + a_two_in[i].astype(F32)
        )
        if i == 1:
            ta_ref[i, at, :] = total.astype(BF16)
            a_z_copy(l, 1).start()
        else:
            a_z_copy(l, 1).wait_recv()
            total = total + a_z_in[1].astype(F32)
            a_sum_ref[...] = total

            @pl.when(c == 1)
            def _():
                ta_ref[i, at, :] = total.astype(BF16)
                a_z_copy(l, 0).start()

    def step_a_z(l):
        @pl.when(c == 1)
        def _():
            a_z_copy(l, 0).wait_recv()
            a_sum_ref[...] = a_z_in[0].astype(F32)

        other = pl.ds(pl.multiple_of((1 - c) * height, 32), height)
        a_out_ref[...] = a_sum_ref[other, :].astype(BF16)
        a_c_copy(l).start()

    def step_a_end(l):
        a_c_copy(l).wait_recv()
        own = pl.ds(pl.multiple_of(c * height, 32), height)
        total = a_sum_ref[own, :] + a_c_in[l].astype(F32)
        tile = [total[:, n * LANES : (n + 1) * LANES] for n in range(6)]
        turned_one = pltpu.roll(tile[1], HD, 1)
        turned_four = pltpu.roll(tile[4], HD, 1)
        for n, (two, one) in enumerate(
            ((tile[0], tile[1]), (tile[2], turned_one), (tile[3], tile[4]))
        ):
            qkv_out[l, n, :, 0:LANES] = two
            qkv_out[l, n, :, LANES:] = one[:, :HD]
        outw_out[l, 0:LANES, :] = jnp.transpose(tile[5])
        outw_out[l, LANES:, :] = jnp.transpose(turned_four)[:HD]

    def a_sent(l, i):
        for n in range(2):
            a_one_copy(l, i, n).wait_send()
        a_two_copy(l, i).wait_send()
        if i == 1:
            a_z_copy(l, 1).wait_send()
        else:

            @pl.when(c == 1)
            def _():
                a_z_copy(l, 0).wait_send()

    def step_v(l, n):
        v_copy(l, n - 1).wait_recv()
        v_stage[l, n] = v_stage[l, n - 1] + v_in[l, n - 1]
        if n < 3:
            v_copy(l, n).start()
        else:
            for s in range(3, 6):
                v_copy(l, s).start()

    def step_v_end(l):
        total = v_stage[l, 3, 0:6, :]
        one = v_stage[l, 3, 6:7, :]
        two = v_stage[l, 3, 10:11, :]
        for s in range(1, MP):
            v_copy(l, 2 + s).wait_recv()
            got = v_in[l, 2 + s]
            total = total + got[0:6, :]
            one = one + got[6 + s : 7 + s, :]
            two = two + got[10 + s : 11 + s, :]
        vec_out[l] = total
        bin_out[l] = one
        turned_one = pltpu.roll(two[:, LANES : 2 * LANES], HD, 1)
        for n, at in enumerate((0, 2, 3)):
            bqkv_out[l, n : n + 1, 0:LANES] = two[:, at * LANES : (at + 1) * LANES]
        bqkv_out[l, 0:1, LANES:] = two[:, LANES : LANES + HD]
        bqkv_out[l, 1:2, LANES:] = turned_one[:, :HD]
        bqkv_out[l, 2:3, LANES:] = two[:, 4 * LANES : 4 * LANES + HD]

    result_copy = remote(low_in, result_out, t_send.at[1], t_recv.at[1], away)
    result_local = pltpu.make_async_copy(low_in, result_out, o_sem.at[1])
    kblock = 256
    for l in reversed(range(n_layers)):
        top = l == n_layers - 1
        vec = vectors[l]
        copies = early_loads(l)
        if top:
            dy_load.wait()
            acc_ref[...] = df_ref[...].astype(F32)
        else:
            for n in range(2):
                dxp_copy(l + 1, n).wait_send()
        for copy in copies:
            copy.wait()
        v_stage[l, 0] = jnp.zeros((16, width), F32)
        sums = norm_back_rows(acc_ref, r2_ref, df_ref, vec[4:5, :])
        v_stage[l, 0, 4:5, :], v_stage[l, 0, 5:6, :], v_stage[l, 0, 3:4, :] = sums
        if top:
            pl.semaphore_wait(barrier, len(partners))
        df_copy(l).start()
        if top:

            @pl.when(moved)
            def _():
                result_copy.start()

            @pl.when(jnp.logical_not(moved))
            def _():
                result_local.start()

        def turned(source, target, half):
            turn_ref[...] = jnp.transpose(source)
            for g in range(4):
                at = pl.ds(pl.multiple_of((2 * g + c) * height, 32), height)
                target[pl.ds(g * height, height), pl.ds(half * rows, rows)] = turn_ref[at, :]

        turned(df_ref[...], dft_ref, 0)
        turned(h_ref[0], ht_ref, 0)
        turned(h_ref[1], ht_ref, 1)
        if not top:
            feed_sent(l + 1, 0)
            step_v(l + 1, 1)
        df_copy(l).wait_recv()
        turned(dfin_ref[...], dft_ref, 1)

        def back_grads(n, _, l=l):
            e_load(l, n).wait()

            @pl.when(n + 1 < MP)
            def _():
                e_load(l, n + 1).start()

            k = MP - 1 - n
            grad = nn(dft_ref[...], pool[4 + n % 2]).astype(BF16)
            t_ref[0, k] = grad.reshape(4, height, width)
            for to in range(2):
                one_copy(l, 0, k, to).start()
            return 0

        lax.fori_loop(0, MP, back_grads, 0)
        if not top:
            for k in range(MP):
                du_copy(l + 1, k).wait_send()

        def inner(k, _, l=l):
            for copy in weight_loads(l, k):
                copy.wait()

            @pl.when(k + 1 < MP)
            def _():
                for copy in weight_loads(l, k + 1):
                    copy.start()

            slot = k % 2
            de = nn(df_ref[...], pool[2 + slot])
            du = de * gp_ref[slot].astype(F32)
            dbin_ref[k] = jnp.sum(du, axis=0, keepdims=True)
            dub = du.astype(BF16)
            du_ref[k, pl.ds(0, rows), :] = dub
            du_copy(l, k).start()
            acc_ref[...] += nt(dub, pool[slot])
            return 0

        lax.fori_loop(0, MP, inner, 0)
        for copy in x_loads(l):
            copy.start()
        for k in range(MP):
            v_stage[l, 0, 6 + k : 7 + k, :] = dbin_ref[k]
        if not top:
            step_a_two(l + 1, 1)
            step_a_one(l + 1, 0)
            for h in range(2):
                step_feed_end(l + 1, h)
            step_v(l + 1, 2)
            da_copy(l + 1).wait_send()
        sums = norm_back_rows(acc_ref, r1_ref, da_ref, vec[1:2, :])
        v_stage[l, 0, 1:2, :], v_stage[l, 0, 2:3, :], v_stage[l, 0, 0:1, :] = sums
        da_copy(l).start()
        for k in (3, 2, 1, 0):
            step_one(l, 0, k)
        if not top:
            feed_sent(l + 1, 1)

        def in_grads(n, _, l=l):
            k = MP - 1 - n
            du_copy(l, k).wait_recv()
            grad = nn(ht_ref[...], du_ref[k]).astype(BF16)
            t_ref[1, k] = grad.reshape(4, height, width)
            for to in range(2):
                one_copy(l, 1, k, to).start()
            return 0

        lax.fori_loop(0, MP, in_grads, 0)
        if not top:
            step_a_two(l + 1, 0)
            step_v(l + 1, 3)
        for copy in late_loads(l):
            copy.wait()
        da_copy(l).wait_recv()
        low_half = lane_index((rows, LANES)) < HD
        for half, source in enumerate((da_ref, dain_ref)):
            at = pl.ds(half * rows, rows)
            for i in range(2):
                dz = nn(source[...], wa[i, :, 4 * LANES :])
                dz_ref[i, 0, at, :] = dz[:, LANES:].astype(BF16)
                dz_ref[i, 1, at, :] = jnp.where(
                    low_half, pltpu.roll(dz[:, :LANES], HD, 1), 0.0
                ).astype(BF16)
            pool[6, :, pl.ds(half * rows, rows)] = jnp.transpose(source[...])
        for i in range(2):
            dwo_ref[i] = nn(pool[6], mixed_ref[:, i * 256 : i * 256 + 256]).astype(BF16)
            head_deltas(i, mixed_ref, dz_ref, delta_ref)
        for copy in x_loads(l):
            copy.wait()
        for half in range(2):
            pool[half] = jnp.transpose(pool[2 + half])
        if top:
            for copy in table_loads:
                copy.wait()
        steps = [[] for _ in range(6)]
        if not top:
            steps[0] = [partial(step_v_end, l + 1), partial(step_a_z, l + 1)]
            steps[1] = [partial(step_a_end, l + 1)]
        steps[0] += [partial(step_two, l, 0, k) for k in (3, 1, 0)]
        steps[1] += [partial(step_one, l, 1, k) for k in (3, 2, 1, 0)]
        steps[2].append(partial(step_two, l, 0, 2))
        steps[3] = [partial(step_two, l, 1, k) for k in (3, 1, 0)]
        steps[5] = [partial(step_two, l, 1, 2), partial(step_a_one, l, 1)]

        def weight_grads(i, l=l, top=top):
            if not top:
                a_sent(l + 1, i)
                if i == 0:
                    a_c_copy(l + 1).wait_send()
            low = [pool.at[2 + 2 * i + half] for half in range(2)]
            ta_ref[i, :, 0:LANES] = nn(pool[0], low[0][:, 0:LANES]).astype(BF16)
            more = nn(pool[0], low[0][:, LANES : 5 * LANES]) + nn(
                pool[1], low[1][:, LANES : 5 * LANES]
            )
            ta_ref[i, :, LANES : 4 * LANES] = more[:, : 3 * LANES].astype(BF16)
            ta_ref[i, :, 4 * LANES : 5 * LANES] = (
                more[:, 3 * LANES :] + dwo_ref[i, :, 0:LANES].astype(F32)
            ).astype(BF16)
            ta_ref[i, :, 5 * LANES :] = dwo_ref[i, :, LANES:]
            for n in range(2):
                a_one_copy(l, i, n).start()

        for turn, i in enumerate((1, 0)):
            for h in range(3):
                head_back(
                    i,
                    h,
                    kblock,
                    q_ref,
                    k_ref,
                    v_ref,
                    dz_ref,
                    lse_ref,
                    delta_ref,
                    qrow_ref,
                    kcol_ref,
                    pair_ref,
                    dqt_ref,
                    dt_ref,
                )
                for step in steps[3 * turn + h]:
                    step()
            for tile in range(5):
                total = jnp.zeros((1, LANES), F32)
                for half in range(1 if tile == 0 else 2):
                    at = pl.ds(half * queries, queries)
                    t = dt_ref[tile, at, :]
                    if tile < 3:
                        t = t * cos_ref[at, :] - half_swap(t) * sin_ref[at, :]
                    total = total + jnp.sum(t, axis=0, keepdims=True)
                    pool[2 + 2 * i + half, :, tile * LANES : (tile + 1) * LANES] = t.astype(BF16)
                for core in range(2):
                    v_stage[
                        l, 0, 10 + 2 * core + i : 11 + 2 * core + i, tile * LANES : (tile + 1) * LANES
                    ] = jnp.where(c == core, total, 0.0)
            if i == 1:
                weight_grads(1)
        v_copy(l, 0).start()

        def spread(n):
            half, at = n // 2, pl.ds((n % 2) * rows, rows)
            total = jnp.zeros((rows, width), F32)
            for i in range(2):
                low = pool.at[2 + 2 * i + half]
                total = total + nt(low[at, LANES : 5 * LANES], wa[i, :, LANES : 5 * LANES])
                if half == 0:
                    total = total + nt(low[at, 0:LANES], wa[i, :, 0:LANES])
            return total

        df_copy(l).wait_send()
        dxs_ref[1] = spread(3).astype(BF16)
        dxs_copy(l, 1).start()
        part_ref[...] = spread(2)
        dxs_copy(l, 1).wait_recv()
        dxp_ref[...] = (part_ref[...] + dxc_in[1].astype(F32)).astype(BF16)
        for n in range(2):
            dxp_copy(l, n).start()
        dxs_ref[0] = spread(1).astype(BF16)
        dxs_copy(l, 0).start()
        acc_ref[...] += spread(0)
        weight_grads(0)
        dxs_copy(l, 0).wait_recv()
        acc_ref[...] += dxc_in[0].astype(F32)
        if l > 0:
            for n in range(2):
                dxs_copy(l, n).wait_send()
            first_loads = early_loads(l - 1) + [e_load(l - 1, 0)] + weight_loads(l - 1, 0)
            for copy in first_loads + late_loads(l - 1):
                copy.start()
        for n in range(2):
            dxp_copy(l, n).wait_recv()
            acc_ref[halves[n], :] += dxp_in[l, halves[n], :].astype(F32)
            if l == 0:
                dxp_copy(0, n).wait_send()
                df_ref[halves[n], :] = acc_ref[halves[n], :].astype(BF16)

                @pl.when(moved)
                def _(n=n):
                    back_copy(n).start()

    step_v(0, 1)
    step_a_two(0, 1)
    for h in range(2):
        step_feed_end(0, h)
    step_a_one(0, 0)
    step_v(0, 2)
    step_a_two(0, 0)
    step_v(0, 3)
    step_v_end(0)

    @pl.when(moved)
    def _():
        for n in range(2):
            back_copy(n).wait_recv()
        acc_ref[...] = back_in[...].astype(F32)

    out_copy = pltpu.make_async_copy(acc_ref, tokens_out, o_sem.at[0])
    out_copy.start()
    step_a_z(0)
    step_a_end(0)
    out_copy.wait()

    @pl.when(moved)
    def _():
        for n in range(2):
            back_copy(n).wait_send()
        result_copy.wait_send()
        result_copy.wait_recv()

    @pl.when(jnp.logical_not(moved))
    def _():
        result_local.wait()

    da_copy(0).wait_send()
    for n in range(2):
        dxs_copy(0, n).wait_send()
    for k in range(MP):
        du_copy(0, k).wait_send()
    for h in range(2):
        feed_sent(0, h)
        z_copy(0, h, 2).wait_send()
    for i in range(2):
        a_sent(0, i)
    a_c_copy(0).wait_send()
    for l in range(n_layers):
        for n in range(6):
            v_copy(l, n).wait_send()


def backward(w_all, dy, cos, sin, low, qrow, kcol, vectors, states):
    n_layers, _, width = vectors.shape
    rows = dy.shape[0]
    height = width // 8
    queries, keys = 2 * rows, 4 * rows
    sem = pltpu.SemaphoreType.DMA
    flat = [array for state in states for array in state]
    return pl.pallas_call(
        partial(backward_kernel, n_layers),
        out_shape=(
            shape((rows, width), F32),
            shape((rows, width), BF16),
            shape((n_layers, 3, height, 3 * HD), F32),
            shape((n_layers, 3, 3 * HD), F32),
            shape((n_layers, 3 * HD, height), F32),
            shape((n_layers, 6, width), F32),
            shape((n_layers, height, width), F32),
            shape((n_layers, 1, width), F32),
            shape((n_layers, width, height), F32),
        ),
        in_specs=[anywhere()] * 5 + [vmem()] * 3 + [anywhere()] * len(flat),
        out_specs=(anywhere(), anywhere()) + (vmem(),) * 7,
        scratch_shapes=[
            pltpu.VMEM((7, width, width), BF16),
            pltpu.VMEM((2, rows, width), BF16),
            pltpu.VMEM((rows, width), F32),
            pltpu.VMEM((rows, width), F32),
            pltpu.VMEM((rows, width), F32),
            pltpu.VMEM((rows, width), BF16),
            pltpu.VMEM((rows, width), BF16),
            pltpu.VMEM((rows, width), BF16),
            pltpu.VMEM((rows, width), BF16),
            pltpu.VMEM((2, rows, width), BF16),
            pltpu.VMEM((width, rows), BF16),
            pltpu.VMEM((4 * height, 2 * rows), BF16),
            pltpu.VMEM((4 * height, 2 * rows), BF16),
            pltpu.VMEM((MP, 2 * rows, width), BF16),
            pltpu.VMEM((2, MP, 4, height, width), BF16),
            pltpu.VMEM((2, MP, 2, height, width), BF16),
            pltpu.VMEM((2, MP, height, width), BF16),
            pltpu.VMEM((n_layers, 2, MP - 1, height, width), BF16),
            pltpu.VMEM((2, width, 2 * LANES), BF16),
            pltpu.VMEM((2, width, width), BF16),
            pltpu.VMEM((2, 2, 2 * height, width), BF16),
            pltpu.VMEM((2, 2 * height, width), BF16),
            pltpu.VMEM((2, 2 * height, width), BF16),
            pltpu.VMEM((n_layers, height, width), BF16),
            pltpu.VMEM((2 * height, width), F32),
            pltpu.VMEM((height, width), BF16),
            pltpu.VMEM((2, width, width), BF16),
            pltpu.VMEM((2, 2, queries, LANES), BF16),
            pltpu.VMEM((2, 2, keys, LANES), BF16),
            pltpu.VMEM((2, 2, keys, LANES), BF16),
            pltpu.VMEM((queries, 512), BF16),
            pltpu.VMEM((8, queries), F32),
            pltpu.VMEM((8, queries), F32),
            pltpu.VMEM((2, 2, queries, LANES), BF16),
            pltpu.VMEM((5, keys, LANES), F32),
            pltpu.VMEM((LANES, queries), F32),
            pltpu.VMEM((2, queries, LANES), BF16),
            pltpu.VMEM((keys, LANES), F32),
            pltpu.VMEM((keys, LANES), F32),
            pltpu.VMEM((2, rows, width), BF16),
            pltpu.VMEM((n_layers, rows, width), BF16),
            pltpu.VMEM((rows, width), BF16),
            pltpu.VMEM((n_layers, 4, 16, width), F32),
            pltpu.VMEM((n_layers, 6, 16, width), F32),
            pltpu.VMEM((MP, 1, width), F32),
            pltpu.VMEM((2, height, width), BF16),
            pltpu.VMEM((2, height, width), F32),
            sem((n_layers, 9)),
            sem((n_layers, 9)),
            sem((n_layers, 2, MP, 2)),
            sem((n_layers, 2, MP, 2)),
            sem((n_layers, 2, MP)),
            sem((n_layers, 2, MP)),
            sem((n_layers, 2, MP)),
            sem((n_layers, 2, MP)),
            sem((n_layers, 2, 4)),
            sem((n_layers, 2, 4)),
            sem((n_layers, 2)),
            sem((n_layers, 2)),
            sem((n_layers, 6)),
            sem((n_layers, 6)),
            sem((3,)),
            sem((3,)),
            sem((2, 4)),
            sem((18,)),
            sem((2,)),
        ],
        compiler_params=pltpu.CompilerParams(
            vmem_limit_bytes=BACK_LIMIT, collective_id=1, has_side_effects=True
        ),
        cost_estimate=pl.CostEstimate(
            flops=200_000_000_000, bytes_accessed=100_000_000, transcendentals=20_000_000
        ),
        name="backward",
    )(w_all, dy, cos, sin, low, qrow, kcol, vectors, *flat)


def attend_kernel(chunk, *refs):
    scal, x_ref, bias_ref, cos_ref, sin_ref, qcode_ref, kcode_ref, w_all = refs[:8]
    q_ref, k_ref, v_ref, mixed_ref, lse_ref, w_ref, lse_cols, sems = refs[8:]
    copies = [
        pltpu.make_async_copy(
            w_all.at[chunk, scal[k], :, pl.ds(0, 5 * LANES)], w_ref.at[k], sems.at[k]
        )
        for k in range(2)
    ]
    for copy in copies:
        copy.start()
    for copy in copies:
        copy.wait()
    rows = x_ref.shape[1]
    for i in range(4):
        at = pl.ds(i * rows, rows)
        for k in range(2):
            project_rows(
                i,
                k,
                x_ref[i],
                w_ref,
                bias_ref[k],
                cos_ref[at, :],
                sin_ref[at, :],
                q_ref,
                k_ref,
                v_ref,
            )
    lse_cols[...] = jnp.zeros_like(lse_cols)

    def one_block(i, _):
        attend_rows(i, 256, qcode_ref, kcode_ref, q_ref, k_ref, v_ref, mixed_ref, lse_cols)
        return 0

    lax.fori_loop(0, 2 * rows // 256, one_block, 0)
    lse_ref[...] = jnp.transpose(lse_cols[...])[0:8, :]


def attend(scal, x_full, bias, tables, qcode, kcode, w_all, chunk):
    cos, sin = tables[:2]
    _, rows, width = x_full.shape
    queries, keys = 2 * rows, 4 * rows
    return pl.pallas_call(
        partial(attend_kernel, chunk),
        out_shape=(
            shape((2, 2, queries, LANES), BF16),
            shape((2, 2, keys, LANES), BF16),
            shape((2, 2, keys, LANES), BF16),
            shape((queries, 512), BF16),
            shape((8, queries), F32),
        ),
        in_specs=[smem()] + [vmem()] * 6 + [anywhere()],
        out_specs=(vmem(),) * 5,
        scratch_shapes=[
            pltpu.VMEM((2, width, 5 * LANES), BF16),
            pltpu.VMEM((queries, LANES), F32),
            pltpu.SemaphoreType.DMA((2,)),
        ],
        compiler_params=params(),
        name="attend",
    )(scal, x_full, bias, cos, sin, qcode, kcode, w_all)


def feed_kernel(chunk, *refs):
    scal, x_ref, own_ref, sib_ref, vec_ref, bin_ref, w_all = refs[:7]
    next_ref, low_ref, r1_ref, r2_ref, e_ref, gp_ref, wo_ref, win_ref, wback_ref, sems = refs[7:]
    copies = [
        pltpu.make_async_copy(
            w_all.at[chunk, :, :, pl.ds(4 * LANES, 2 * LANES)], wo_ref, sems.at[0]
        ),
        pltpu.make_async_copy(w_all.at[chunk + 1], win_ref, sems.at[1]),
        pltpu.make_async_copy(w_all.at[chunk + 2], wback_ref, sems.at[2]),
    ]
    for copy in copies:
        copy.start()
    for copy in copies:
        copy.wait()
    a = jnp.zeros(x_ref.shape, F32)
    for k in range(2):
        a = a + nt(own_ref[:, k * 256 : k * 256 + 256], wo_ref[scal[k]])
        a = a + nt(sib_ref[:, k * 256 : k * 256 + 256], wo_ref[lax.rem(scal[k] + 2, MP)])
    r1 = x_ref[...] + a + vec_ref[0:1, :]
    r1_ref[...] = r1
    n1, _ = norm_parts(r1)
    h = n1 * vec_ref[1:2, :] + vec_ref[2:3, :]
    low_ref[...] = h.astype(BF16)
    r2_ref[...] = h + vec_ref[3:4, :]

    def one(z, _):
        u = nn(low_ref[...], win_ref[z]) + bin_ref[z]
        cdf = 0.5 * (1.0 + lax.erf(u * (2.0**-0.5)))
        pdf = jnp.exp(u * u * -0.5) * 0.3989422804014327
        e = (u * cdf).astype(BF16)
        e_ref[z] = e
        gp_ref[z] = (cdf + u * pdf).astype(BF16)
        r2_ref[...] += nt(e, wback_ref[z])
        return 0

    lax.fori_loop(0, MP, one, 0)
    n2, _ = norm_parts(r2_ref[...])
    result = n2 * vec_ref[4:5, :] + vec_ref[5:6, :]
    next_ref[...] = result
    low_ref[...] = result.astype(BF16)


def feed_forward(scal, x, own, sib, vec, bias_in, w_all, chunk):
    rows, width = x.shape
    return pl.pallas_call(
        partial(feed_kernel, chunk),
        out_shape=(
            shape((rows, width), F32),
            shape((rows, width), BF16),
            shape((rows, width), F32),
            shape((rows, width), F32),
            shape((MP, rows, width), BF16),
            shape((MP, rows, width), BF16),
        ),
        in_specs=[smem()] + [vmem()] * 5 + [anywhere()],
        out_specs=(vmem(),) * 6,
        scratch_shapes=[
            pltpu.VMEM((MP, width, 2 * LANES), BF16),
            pltpu.VMEM((MP, width, width), BF16),
            pltpu.VMEM((MP, width, width), BF16),
            pltpu.SemaphoreType.DMA((3,)),
        ],
        compiler_params=params(),
        name="feed",
    )(scal, x, own, sib, vec, bias_in, w_all)


def plain_forward(blocks, tokens, cot, small, meta, frequency, vectors):
    n_layers = vectors.shape[0]
    rows, width = tokens.shape
    c, z = lax.axis_index("dp") % 2, lax.axis_index("mp")
    w_all = lax.all_gather(blocks, "dp", axis=1, tiled=True)
    w_all = jnp.swapaxes(lax.all_gather(w_all, "mp", axis=0, tiled=False), 0, 1)
    small_all = lax.all_gather(small, "mp", axis=0, tiled=False)
    own_z = jnp.stack([(z - 2 * c - k) % MP for k in range(2)]).astype(jnp.int32)
    info = jnp.where(z // 2 == c, meta, core_swap(meta))
    place = z % 2
    quarters = [2 * c + place, 2 * (1 - c) + place, 2 * c + 1 - place, 2 * (1 - c) + 1 - place]
    positions = jnp.concatenate(
        [q * rows + jnp.arange(rows, dtype=jnp.int32) for q in quarters]
    ).astype(F32)
    slot = info[0, 0]
    seq = jnp.where(positions >= slot, 1.0, 0.0) + jnp.where(positions >= 2.0 * slot, 1.0, 0.0)
    place = positions - seq * slot
    limit = jnp.where(seq == 0.0, info[1, 0], jnp.where(seq == 1.0, info[2, 0], info[3, 0]))
    kcode = jnp.where(place < limit, seq, -1.0)
    qcode = seq[: 2 * rows]
    angles = place[:, None] * frequency
    sign = jnp.where(jnp.arange(LANES) % HD < HD // 2, -1.0, 1.0)
    cos, sin = jnp.cos(angles), jnp.sin(angles) * sign[None, :]
    low = relayout(tokens)
    stream = low.astype(F32)
    states = []
    for l in range(n_layers):
        two = jnp.stack([low, pair_swap(low)])
        others = core_swap(two)
        x_full = jnp.stack([two[0], others[0], two[1], others[1]])
        bias = jnp.stack(
            [
                lax.dynamic_index_in_dim(small_all, own_z[k], 0, False)[l : l + 1, : 5 * LANES]
                for k in range(2)
            ]
        )
        q, k, v, mixed, lse = attend(
            own_z, x_full, bias, (cos, sin), qcode[:, None], kcode[None, :], w_all, 3 * l
        )
        other = core_swap(mixed[rows:])
        stream, low, r1, r2, e, gp = feed_forward(
            own_z,
            stream,
            mixed[:rows],
            other,
            vectors[l],
            small_all[:, l : l + 1, 5 * LANES :],
            w_all,
            3 * l,
        )
        states.append((x_full, q, k, v, mixed, other, lse, r1, r2, e, gp))
    return (w_all, relayout(cot), low, cos, sin, qcode[None, :], kcode[:, None]), states


def feed_back_kernel(n_pieces, rows, chunk, *refs):
    scal, dy_ref, r1_ref, r2_ref, e_ref, gp_ref, own_ref, sib_ref, vec_ref, w_all = refs[:10]
    at = 10
    dr1_ref, dzown_ref, dzsib_ref, dvec_ref, dbin_ref = refs[at : at + 5]
    outs = 2 if n_pieces == 8 else 1
    grads = refs[at + 5 : at + 5 + outs]
    wo_ref, win_ref, wback_ref, df_ref, dft_ref, ht_ref, dw_ref, sems = refs[at + 5 + outs :]
    width = dy_ref.shape[1]
    columns = [scal[n_pieces + k] for k in range(MP)]
    first_z = scal[n_pieces + MP]

    def fetch(source, target, base):
        copies = [
            pltpu.make_async_copy(source(columns[k]), target.at[k], sems.at[base + k])
            for k in range(MP)
        ]
        for copy in copies:
            copy.start()
        return copies

    back_copies = fetch(lambda z: w_all.at[chunk + 2, z], wback_ref, 0)
    in_copies = fetch(lambda z: w_all.at[chunk + 1, z], win_ref, MP)
    out_copies = fetch(
        lambda z: w_all.at[chunk, z, :, pl.ds(4 * LANES, 2 * LANES)], wo_ref, 2 * MP
    )
    dy = dy_ref[...]
    n2, scale2 = norm_parts(r2_ref[...])
    dvec_ref[4:5, :] = jnp.sum(dy * n2, axis=0, keepdims=True)
    dvec_ref[5:6, :] = jnp.sum(dy, axis=0, keepdims=True)
    dr2 = norm_back(dy, n2, scale2, vec_ref[4:5, :])
    dvec_ref[3:4, :] = jnp.sum(dr2, axis=0, keepdims=True)
    dr1_ref[...] = dr2
    df = dr2.astype(BF16)
    df_ref[...] = df
    dft_ref[...] = jnp.transpose(df)
    n1, _ = norm_parts(r1_ref[...])
    h = (n1 * vec_ref[1:2, :] + vec_ref[2:3, :]).astype(BF16)
    ht_ref[...] = jnp.transpose(h)
    for copy in back_copies + in_copies:
        copy.wait()

    def one(z, _):
        de = nn(df_ref[...], wback_ref[z])
        at = scal[n_pieces + z]
        du = de * gp_ref[at].astype(F32)
        dbin_ref[z] = jnp.sum(du, axis=0, keepdims=True)
        dub = du.astype(BF16)
        dr1_ref[...] += nt(dub, win_ref[z])
        dw_ref[z, :, 0:width] = nn(ht_ref[...], dub).astype(BF16)
        dw_ref[z, :, width : 2 * width] = nn(dft_ref[...], e_ref[at]).astype(BF16)
        return 0

    lax.fori_loop(0, MP, one, 0)
    dh = dr1_ref[...]
    n1, scale1 = norm_parts(r1_ref[...])
    dvec_ref[1:2, :] = jnp.sum(dh * n1, axis=0, keepdims=True)
    dvec_ref[2:3, :] = jnp.sum(dh, axis=0, keepdims=True)
    dr1 = norm_back(dh, n1, scale1, vec_ref[1:2, :])
    dvec_ref[0:1, :] = jnp.sum(dr1, axis=0, keepdims=True)
    dr1_ref[...] = dr1
    da = dr1.astype(BF16)
    dft_ref[...] = jnp.transpose(da)
    for copy in out_copies:
        copy.wait()
    used = lane_index((da.shape[0], 2 * LANES)) >= HD
    for z in range(2):
        for mixed_ref, dz_ref, z_at in (
            (own_ref, dzown_ref, first_z + z),
            (sib_ref, dzsib_ref, 2 - first_z + z),
        ):
            part = mixed_ref[:, z * 256 : z * 256 + 256]
            dw_ref[z_at, :, 2 * width :] = nn(dft_ref[...], part).astype(BF16)
            dz = nn(da, wo_ref[z_at])
            dz_ref[:, z * 256 : z * 256 + 256] = jnp.where(used, dz, 0.0).astype(BF16)
    flight = []
    for i in range(n_pieces):
        offset = pl.multiple_of(scal[i], 32)
        target = grads[i // 4].at[PIECE_ORDER[i % 4] if n_pieces == 8 else 0]
        copy = pltpu.make_async_copy(dw_ref.at[:, pl.ds(offset, rows), :], target, sems.at[i])
        copy.start()
        flight.append(copy)
    for copy in flight:
        copy.wait()


PIECE_ORDER = (3, 0, 2, 1)


def feed_back(scal, prows, count, dy, r1, r2, e, gp, own, sib, vec, w_all, chunk):
    rows, width = dy.shape
    lanes = 2 * width + 2 * LANES
    grads = (shape((4, MP, prows, lanes), BF16),) * 2
    if count != 8:
        grads = (shape((1, MP, prows, lanes), BF16),)
    return pl.pallas_call(
        partial(feed_back_kernel, count, prows, chunk),
        out_shape=(
            shape((rows, width), F32),
            shape((rows, 512), BF16),
            shape((rows, 512), BF16),
            shape((6, width), F32),
            shape((MP, 1, width), F32),
            *grads,
        ),
        in_specs=[smem()] + [vmem()] * 8 + [anywhere()],
        out_specs=(vmem(),) * 5 + (anywhere(),) * len(grads),
        scratch_shapes=[
            pltpu.VMEM((MP, width, 2 * LANES), BF16),
            pltpu.VMEM((MP, width, width), BF16),
            pltpu.VMEM((MP, width, width), BF16),
            pltpu.VMEM((rows, width), BF16),
            pltpu.VMEM((width, rows), BF16),
            pltpu.VMEM((width, rows), BF16),
            pltpu.VMEM((MP, width, lanes), BF16),
            pltpu.SemaphoreType.DMA((3 * MP,)),
        ],
        compiler_params=params(),
        cost_estimate=pl.CostEstimate(
            flops=16_000_000_000, bytes_accessed=40_000_000, transcendentals=0
        ),
        name="feed_back",
    )(scal, dy, r1, r2, e, gp, own, sib, vec, w_all)


def attend_back_kernel(n_pieces, chunk, *refs):
    (
        scal,
        x_ref,
        cos_ref,
        sin_ref,
        qcode_ref,
        kcode_ref,
        q_ref,
        k_ref,
        v_ref,
        mixed_ref,
        dzown_ref,
        dzsib_ref,
        lse_ref,
        w_all,
    ) = refs[:14]
    dx_ref, dxs_ref, dbias_ref, parts_ref = refs[14:18]
    (
        w_ref,
        xt_ref,
        dz_ref,
        delta_ref,
        dt_ref,
        dqt_ref,
        pair_ref,
        dw_ref,
        low_ref,
        sums_ref,
        sems,
    ) = refs[18:]
    copies = [
        pltpu.make_async_copy(
            w_all.at[chunk, scal[n_pieces + 9 + k], :, pl.ds(0, 5 * LANES)],
            w_ref.at[k],
            sems.at[k],
        )
        for k in range(2)
    ]
    for copy in copies:
        copy.start()
    keys, width = x_ref.shape
    queries = keys // 2
    block = queries // 2
    for z in range(2):
        for half, source in enumerate((dzown_ref, dzsib_ref)):
            at = pl.ds(half * block, block)
            dz_ref[z, 0, at, :] = source[:, z * 256 + LANES : z * 256 + 256]
            dz_ref[z, 1, at, :] = pltpu.roll(
                source[:, z * 256 : z * 256 + LANES].astype(F32), HD, 1
            ).astype(BF16)
        single = pltpu.roll(mixed_ref[:, z * 256 : z * 256 + LANES].astype(F32), HD, 1)
        pair = mixed_ref[:, z * 256 + LANES : z * 256 + 256].astype(F32)
        prod_one = jnp.transpose(pair * dz_ref[z, 0].astype(F32))
        prod_two = jnp.transpose(single * dz_ref[z, 1].astype(F32))
        delta_ref[3 * z : 3 * z + 1, :] = jnp.sum(prod_one[0:HD], axis=0, keepdims=True)
        delta_ref[3 * z + 1 : 3 * z + 2, :] = jnp.sum(prod_one[HD:], axis=0, keepdims=True)
        delta_ref[3 * z + 2 : 3 * z + 3, :] = jnp.sum(prod_two[0:HD], axis=0, keepdims=True)

    kblock = 256
    low_q = lane_index((queries, LANES)) < HD
    low_k = lane_index((kblock, LANES)) < HD
    for z in range(2):
        for h in range(3):
            tile = h // 2
            q = q_ref[z, tile]
            dz = dz_ref[z, tile]
            if h < 2:
                keep = low_q == (h == 0)
                q = jnp.where(keep, q, BF16(0))
                dz = jnp.where(keep, dz, BF16(0))
            pair_ref[0] = q
            pair_ref[1] = dz
            lse = lse_ref[3 * z + h : 3 * z + h + 1, :]
            delta = delta_ref[3 * z + h : 3 * z + h + 1, :]
            if h != 1:
                dqt_ref[...] = jnp.zeros_like(dqt_ref)

            def one_block(i, _, z=z, h=h, tile=tile, lse=lse, delta=delta):
                at = pl.ds(pl.multiple_of(i * kblock, kblock), kblock)
                kb = k_ref[z, tile, at, :]
                vb = v_ref[z, tile, at, :]
                if h < 2:
                    kb_own = jnp.where(low_k == (h == 0), kb, BF16(0))
                else:
                    kb_own = kb
                visible = kcode_ref[at, :] == qcode_ref[...]
                s = nt(kb, pair_ref[0])
                s = jnp.where(visible, s, NEGATIVE)
                p = jnp.exp(s - lse)
                dp = nt(vb, pair_ref[1])
                ds = (p * (dp - delta)).astype(BF16)
                dv = nn(p.astype(BF16), pair_ref[1])
                dk = nn(ds, pair_ref[0])
                dqt_ref[...] += nn(jnp.transpose(kb_own), ds)
                if h == 1:
                    dt_ref[2, at, :] += dk
                    dt_ref[3, at, :] += dv
                elif h == 0:
                    dt_ref[2, at, :] = dk
                    dt_ref[3, at, :] = dv
                else:
                    dt_ref[1, at, :] = pltpu.roll(dk, HD, 1)
                    dt_ref[4, at, :] = dv
                return 0

            lax.fori_loop(0, keys // kblock, one_block, 0)
            if h >= 1:
                dq = jnp.transpose(dqt_ref[...]) * HD**-0.5
                if h == 1:
                    dt_ref[0, 0:queries, :] = dq
                else:
                    dt_ref[1, 0:queries, :] += dq

        if z == 0:
            xt_ref[...] = jnp.transpose(x_ref[...])
            for copy in copies:
                copy.wait()
        for tile in range(5):
            count = queries if tile == 0 else keys
            t = dt_ref[tile, 0:count, :]
            if tile < 3:
                t = t * cos_ref[0:count, :] - half_swap(t) * sin_ref[0:count, :]
            dbias_ref[z, :, tile * LANES : (tile + 1) * LANES] = jnp.sum(t, axis=0, keepdims=True)
            low_ref[0:count, tile * LANES : (tile + 1) * LANES] = t.astype(BF16)
        dw_ref[z, :, 0:LANES] = nn(
            xt_ref[:, 0:queries], low_ref[0:queries, 0:LANES]
        ).astype(BF16)
        dw_ref[z, :, LANES:] = nn(xt_ref[...], low_ref[:, LANES:]).astype(BF16)
        for i in range(4):
            at = pl.ds(i * block, block)
            part = nt(low_ref[at, LANES:], w_ref[z, :, LANES : 5 * LANES])
            if i < 2:
                part = part + nt(low_ref[at, 0:LANES], w_ref[z, :, 0:LANES])
            if z == 0:
                sums_ref[i] = part
            else:
                target = dx_ref if i % 2 == 0 else dxs_ref
                target[i // 2] = (sums_ref[i] + part).astype(BF16)

    flight = []
    for i in range(min(n_pieces, 4)):
        offset = pl.multiple_of(scal[n_pieces + 5 + i], 32)
        copy = pltpu.make_async_copy(
            dw_ref.at[:, pl.ds(offset, parts_ref.shape[2]), :],
            parts_ref.at[PIECE_ORDER[i] if n_pieces == 8 else 0],
            sems.at[i],
        )
        copy.start()
        flight.append(copy)
    for copy in flight:
        copy.wait()


def attend_back(scal, prows, count, x_full, tables, saved, mixed, dz_own, dz_sib, w_all, chunk):
    cos, sin, qcode, kcode = tables
    q, k, v, lse = saved
    keys, width = x_full.shape
    queries = keys // 2
    block = queries // 2
    parts = (4, 2, 2 * prows, 5 * LANES)
    if count != 8:
        parts = (1, 2, prows, 5 * LANES)
    return pl.pallas_call(
        partial(attend_back_kernel, count, chunk),
        out_shape=(
            shape((2, block, width), BF16),
            shape((2, block, width), BF16),
            shape((2, 1, 5 * LANES), F32),
            shape(parts, BF16),
        ),
        in_specs=[smem()] + [vmem()] * 12 + [anywhere()],
        out_specs=(vmem(),) * 3 + (anywhere(),),
        scratch_shapes=[
            pltpu.VMEM((2, width, 5 * LANES), BF16),
            pltpu.VMEM((width, keys), BF16),
            pltpu.VMEM((2, 2, queries, LANES), BF16),
            pltpu.VMEM((8, queries), F32),
            pltpu.VMEM((5, keys, LANES), F32),
            pltpu.VMEM((LANES, queries), F32),
            pltpu.VMEM((2, queries, LANES), BF16),
            pltpu.VMEM((2, width, 5 * LANES), BF16),
            pltpu.VMEM((keys, 5 * LANES), BF16),
            pltpu.VMEM((4, block, width), F32),
            pltpu.SemaphoreType.DMA((4,)),
        ],
        compiler_params=params(),
        cost_estimate=pl.CostEstimate(
            flops=40_000_000_000, bytes_accessed=20_000_000, transcendentals=8_000_000
        ),
        name="attend_back",
    )(scal, x_full, cos, sin, qcode, kcode, q, k, v, mixed, dz_own, dz_sib, lse, w_all)


def head_tiles(q, k, v, o):
    return jnp.concatenate(
        [
            q[..., :LANES],
            q[..., LANES:],
            k[..., LANES:],
            k[..., :LANES],
            v[..., :LANES],
            v[..., LANES:],
            o[..., LANES:],
            o[..., :LANES],
        ],
        axis=-1,
    )


def head_columns(t):
    q = jnp.concatenate([t[..., 0:128], t[..., 128:192]], axis=-1)
    k = jnp.concatenate([t[..., 256:384], t[..., 192:256]], axis=-1)
    v = jnp.concatenate([t[..., 384:512], t[..., 512:576]], axis=-1)
    return q, k, v


def per_device(
    tokens, w_qkv, b_qkv, w_out, vectors, w_in, b_in, w_back, cotangent, lengths, buckets
):
    layers = w_qkv.shape[0]
    rows, width = tokens.shape
    d = lax.axis_index("dp")
    z = lax.axis_index("mp")
    g, c = d // 2, d % 2

    blocks = []
    for l in range(layers):
        low = w_qkv[l].astype(BF16)
        blocks.append(head_tiles(low[0], low[1], low[2], w_out[l].astype(BF16).T))
        blocks.append(w_in[l].astype(BF16))
        blocks.append(w_back[l].astype(BF16).T)
    blocks = jnp.stack(blocks)
    height = w_qkv.shape[2]
    pieces = 8 if lax.axis_size("dp") == 8 else 1
    piece_rows = height if pieces == 8 else width

    small = jnp.concatenate(
        [
            b_qkv[:, 0],
            b_qkv[:, 1, LANES:],
            b_qkv[:, 1, :LANES],
            b_qkv[:, 2],
            jnp.zeros((layers, HD), F32),
            b_in,
        ],
        axis=-1,
    )
    small = jnp.pad(small, ((0, 8 - layers), (0, 0)))
    slot = LEN_MAX // (3 - buckets)
    meta = jnp.concatenate([slot, lengths[0]]).astype(F32)
    meta = jnp.broadcast_to(jnp.pad(meta, (0, 4))[:, None], (8, LANES))
    exponents = jnp.arange(LANES, dtype=jnp.int32) % (HD // 2)
    frequency = 10000.0 ** (-2.0 * exponents.astype(F32) / HD)[None, :]

    if pieces == 8:
        head, states = forward(blocks, tokens, cotangent, small, meta, frequency, vectors)
        w_all, dy, low, cos, sin, qrow, kcol = head
        grads = backward(w_all, dy, cos, sin, low, qrow, kcol, vectors, states)
        grad_tokens, result, grad_qkv, grad_b_qkv, grad_out, grad_vec, grad_in = grads[:7]
        return (
            result,
            grad_tokens,
            grad_qkv,
            grad_b_qkv,
            grad_out,
            grad_vec,
            grad_in,
            grads[7].reshape(layers, width),
            grads[8],
        )

    head, states = plain_forward(blocks, tokens, cotangent, small, meta, frequency, vectors)
    w_all, gradient, low, cos, sin, qcode, kcode = head
    result = relayout(low)
    gradient = gradient.astype(F32)

    first = jnp.where(c == 0, 1, 2)
    spans = [(g ^ hop) * 2 * height for hop in (0, first, 3 - first, 3)]
    if pieces == 1:
        spans = [jnp.int32(0)] * 4
    column_of = [(z - k) % MP for k in range(MP)]
    own_z = [(z - 2 * c - k) % MP for k in range(2)]
    scal = jnp.stack(row_offsets(g, c, height) + column_of + [2 * c] + spans + own_z)
    scal = scal.astype(jnp.int32)

    masters = []
    vector_grads = []
    in_biases = []
    head_biases = []
    for layer_at in reversed(range(layers)):
        x_full, q, k, v, mixed, mixed_in, lse, r1, r2, e, gp = states[layer_at]
        back = feed_back(
            scal,
            piece_rows,
            pieces,
            gradient,
            r1,
            r2,
            e,
            gp,
            mixed[:rows],
            mixed_in,
            vectors[layer_at],
            w_all,
            3 * layer_at,
        )
        dr1, dz_own, dz_sib, dvec, dbin = back[:5]
        dz_others = core_swap(dz_sib)
        feed_grad = reduce_all(back[5], back[-1])
        dx, dx_sib, dbias, parts = attend_back(
            scal,
            piece_rows,
            pieces,
            x_full.reshape(4 * rows, width),
            (cos, sin, qcode, kcode),
            (q, k, v, lse),
            mixed,
            dz_own,
            dz_others,
            w_all,
            3 * layer_at,
        )
        got = dx.astype(F32) + core_swap(dx_sib).astype(F32)
        gradient = dr1 + got[0] + pair_swap(got[1].astype(BF16)).astype(F32)
        head_grad = reduce_heads(parts)
        masters.insert(0, (feed_grad, head_grad))
        vector_grads.insert(0, dvec)
        in_biases.insert(0, dbin[:, 0])
        head_biases.insert(0, sum_head_biases(dbias[:, 0]))
    grad_tokens = relayout(gradient.astype(BF16)).astype(F32)

    layers_of = jnp.stack(in_biases, axis=1)
    grad_vectors, grad_b_in = sum_vectors(jnp.concatenate(vector_grads), layers_of)
    grad_vectors = grad_vectors.reshape(vectors.shape)
    grad_b_qkv = jnp.stack([jnp.stack(head_columns(b)) for b in head_biases])

    grad_qkv = jnp.stack([jnp.stack(head_columns(m[1])) for m in masters])
    grad_in = jnp.stack([m[0][:, :width] for m in masters])
    grad_back = jnp.stack([m[0][:, width : 2 * width].T for m in masters])
    grad_out = jnp.stack(
        [
            jnp.concatenate(
                [m[0][:, 2 * width + LANES :], m[0][:, 2 * width + HD : 2 * width + LANES]], axis=-1
            ).T
            for m in masters
        ]
    )
    return (
        result,
        grad_tokens,
        grad_qkv,
        grad_b_qkv,
        grad_out,
        grad_vectors,
        grad_in,
        grad_b_in,
        grad_back,
    )


def solution(mesh):
    return jax.shard_map(
        per_device,
        mesh=mesh,
        in_specs=(
            P(("dp", "mp"), None),
            P(None, None, "dp", "mp"),
            P(None, None, "mp"),
            P(None, "mp", "dp"),
            P(),
            P(None, "dp", "mp"),
            P(None, "mp"),
            P(None, "mp", "dp"),
            P(("dp", "mp"), None),
            P("dp", None),
            P("dp"),
        ),
        out_specs=(
            P(("dp", "mp"), None),
            P(("dp", "mp"), None),
            P(None, None, "dp", "mp"),
            P(None, None, "mp"),
            P(None, "mp", "dp"),
            P(),
            P(None, "dp", "mp"),
            P(None, "mp"),
            P(None, "mp", "dp"),
        ),
        check_vma=False,
    )
```
